32 devices in a mesh: seg: 2 (over core), clip: 16 (over z, y, x).
Axes of the slice: x: 2, y: 2, z: 4, core: 2. Of those that a mesh axis runs over, the one named last changes fastest.
Arguments:
- inputs: bfloat16 [64, 16, 49, 2048], P('clip', 'seg'), may hold values from -6 to 6
- clip_counts: int32 [64], P('clip'), may hold values from 8 to 16, as said below
- labels: int32 [64], P('clip'), may hold values from 0 to 173
- master: float32 [9543872], P(('seg', 'clip'))
- first_moment: float32 [9543872], P(('seg', 'clip')), may hold values from -4.7683716e-07 to 4.7683716e-07
- second_moment: float32 [9543872], P(('seg', 'clip')), may hold values from 1.0488405e-16 to 4.195362e-16
Outputs:
- new_master: float32 [9543872], P(('seg', 'clip'))
- new_first: float32 [9543872], P(('seg', 'clip'))
- new_second: float32 [9543872], P(('seg', 'clip'))
- master_low: bfloat16 [9543872], P(('seg', 'clip'))
- input_grad: float32 [64, 16, 49, 2048], P('clip', 'seg')
- grad_norm: float32 [1], replicated
- bias_grad: float32 [174], replicated
The draws below stay inside these ranges and needn't reach their ends.
Inputs may be any that keep to these rules, and one draw needn't show every extreme that they name: `clip_counts`: each clip has 8 or 16 true segments, which fill its first slots; both counts occur.
All inputs are finite; a program needn't handle non-finite values.
Results may differ from the reference program's by a relative error of at most 0.018.
Values may be sent and summed in bfloat16 or wider, within the bound.
A program may use at most 320 MiB of HBM per device.

```python
import math
import jax
import jax.numpy as jnp
from jax import lax

D = 2048
MID = 512
GATE = 128
CLASSES = 174
GRID = 7
HW = 49
SLOTS = 16
STEP = 7
CLIPS = 64
P_PAD = 9543872
N_SEG = 2
N_CLIP = 16


def draw_clip_counts(key, part):
    key = jax.random.fold_in(key, 5)
    picks = jax.random.randint(key, (CLIPS,), 0, 2)
    picks = picks.at[0].set(1).at[1].set(0)
    return (SLOTS // 2 + picks * (SLOTS // 2)).astype(jnp.int32)


def draw_master(key, part):
    key = jax.random.fold_in(key, 9)
    devices = N_SEG * N_CLIP
    norm_width = 2 * MID + D
    block_layout = [(D * MID, D ** (-0.5)), (9 * MID * MID, (9 * MID) ** (-0.5)), (MID * D, MID ** (-0.5)), (MID * GATE, MID ** (-0.5)), (GATE * MID, GATE ** (-0.5))]
    pieces = []
    for index_b in range(2):
        for index_k, (amount, scale) in enumerate(block_layout):
            pieces.append(scale * jax.random.normal(jax.random.fold_in(key, 40 * index_b + index_k), (amount,), jnp.float32))
        pieces.append(1.0 + 0.3 * jax.random.uniform(jax.random.fold_in(key, 40 * index_b + 20), (norm_width,), jnp.float32, -1.0, 1.0))
        pieces.append(0.3 * jax.random.normal(jax.random.fold_in(key, 40 * index_b + 21), (norm_width,), jnp.float32))
    pieces.append(3.0 * D ** (-0.5) * jax.random.normal(jax.random.fold_in(key, 100), (D * CLASSES,), jnp.float32))
    pieces.append(0.3 * jax.random.normal(jax.random.fold_in(key, 101), (CLASSES,), jnp.float32))
    columns = []
    for index_p, values in enumerate(pieces):
        amount = values.shape[0]
        piece_width = (amount + devices - 1) // devices
        filler = 0.02 * jax.random.normal(jax.random.fold_in(key, 200 + index_p), (devices * piece_width - amount,), jnp.float32)
        columns.append(jnp.concatenate([values, filler]).reshape(devices, piece_width))
    return jnp.concatenate(columns, axis=1).reshape(-1)


def with_ends(entries, stream_key, low, top_value):
    shape = entries.shape
    place = [jax.random.randint(jax.random.fold_in(stream_key, axis), (), 0, shape[axis]) for axis in range(len(shape))]
    entries = entries.at[tuple(place)].set(low)
    longest = shape.index(max(shape))
    place[longest] = (place[longest] + 1) % shape[longest]
    return entries.at[tuple(place)].set(top_value)


def block_levels(key, shape, cuts, low, largest):
    level, own = 1.0, jax.random.fold_in(key, 6)
    for dim, blocks in cuts:
        steps = jnp.exp(jax.random.uniform(jax.random.fold_in(own, dim), (blocks,), jnp.float32, low / len(cuts), largest / len(cuts)))
        level = level * jnp.repeat(steps, shape[dim] // blocks).reshape([-1 if axis == dim else 1 for axis in range(len(shape))])
    return level


def normal_values(key, shape, scale, most, cuts=(), kind=jnp.bfloat16):
    drawn = scale * jax.random.normal(key, shape, jnp.float32)
    if cuts:
        drawn = drawn * block_levels(key, shape, cuts, -0.22, 0.18)
    return jnp.clip(drawn, -most, most).astype(kind)


def setup_inputs(seed: int = 0) -> dict:
    keys = jax.random.split(jax.random.key(seed), 7)
    inputs = normal_values(keys[0], (CLIPS, SLOTS, HW, D), 1.0, 6.0, ((0, 16), (1, 2)))
    clip_counts = draw_clip_counts(jax.random.fold_in(keys[6], 71), 0)
    labels = with_ends(jax.random.randint(keys[2], (CLIPS,), 0, CLASSES), jax.random.fold_in(keys[2], 1), 0, CLASSES - 1).astype(jnp.int32)
    master = draw_master(jax.random.fold_in(keys[6], 71), 0)
    first_moment = normal_values(keys[4], (P_PAD,), (0.000111 / P_PAD ** 0.5), 4.76837158203125e-07, ((0, 32),), jnp.float32)
    second_moment = jnp.clip(jnp.exp(math.log(4.19536212868443e-16) - 1.3862944 * jax.random.uniform(keys[5], (P_PAD,), jnp.float32) ** block_levels(keys[5], (P_PAD,), ((0, 32),), -0.2, 0.2)), 1.0488405321711075e-16, 4.19536212868443e-16)
    return dict(inputs=inputs, clip_counts=clip_counts, labels=labels, master=master, first_moment=first_moment, second_moment=second_moment)


@jax.custom_vjp
def low(v):
    return lax.optimization_barrier(v.astype(jnp.bfloat16)).astype(jnp.float32)

@jax.custom_vjp
def low_back(v):
    return v

def low_keep(v):
    return (low(v), None)

def low_pass(kept, grad):
    return (grad,)

def back_keep(v):
    return (v, None)

def back_low(kept, grad):
    return (low(grad),)
low.defvjp(low_keep, low_pass)
low_back.defvjp(back_keep, back_low)
NORM_EPS = 1e-05
CLIP_LIMIT = 0.001
LEARN_RATE = 0.04
WEIGHT_DECAY = 0.05
BETA_ONE = 0.9
BETA_TWO = 0.999
ADAM_EPS = 1e-08
HIGHEST = lax.Precision.HIGHEST

def matmul(left, right):
    return jnp.dot(left, right, precision=HIGHEST, preferred_element_type=jnp.float32)

def layout():
    block_layout = [(D, MID), (9, MID, MID), (MID, D), (MID, GATE), (GATE, MID), (2 * MID + D,), (2 * MID + D,)]
    return block_layout + block_layout + [(D, CLASSES), (CLASSES,)]

def piece_at(flat, devices, position):
    shapes = layout()
    offset = 0
    for index_p in range(position):
        offset = offset + (math.prod(shapes[index_p]) + devices - 1) // devices
    extent = shapes[position]
    amount = math.prod(extent)
    piece_width = (amount + devices - 1) // devices
    shard_rows = flat.reshape(devices, -1)
    return shard_rows[:, offset:offset + piece_width].reshape(-1)[:amount].reshape(extent)

def carve(flat):
    devices = N_SEG * N_CLIP
    return [piece_at(flat, devices, position) for position in range(len(layout()))]

def grid_mean(values):
    leading = values.shape[:-2]
    channels = values.shape[-1]
    grids = values.reshape(leading + (GRID, GRID, channels))
    widths = [(0, 0)] * len(leading) + [(1, 1), (1, 1), (0, 0)]
    padded = jnp.pad(grids, widths)
    total = jnp.zeros_like(grids)
    for index_k in range(9):
        row_start = index_k // 3
        col_start = index_k % 3
        total = total + padded[..., row_start:row_start + GRID, col_start:col_start + GRID, :]
    return (total / 9.0).reshape(values.shape)

def conv_grid(values, kernel):
    grids = values.reshape(-1, GRID, GRID, MID)
    padded = jnp.pad(grids, ((0, 0), (1, 1), (1, 1), (0, 0)))
    total = jnp.zeros((grids.shape[0], GRID, GRID, MID), jnp.float32)
    for index_k in range(9):
        row_start = index_k // 3
        col_start = index_k % 3
        window = padded[:, row_start:row_start + GRID, col_start:col_start + GRID, :]
        total = total + jnp.einsum('nijc,cd->nijd', window, kernel[index_k], precision=HIGHEST, preferred_element_type=jnp.float32)
    return total.reshape(-1, MID)

def batch_norm(values, rows_mask, live_rows, gain, shift):
    mean_val = lax.optimization_barrier(jnp.sum(values * rows_mask, axis=0)) / live_rows
    square = lax.optimization_barrier(jnp.sum(values * values * rows_mask, axis=0)) / live_rows
    variance = square - mean_val * mean_val
    return (values - mean_val) * lax.rsqrt(variance + NORM_EPS) * gain + shift

def bottleneck(flat_in, weights, rows_mask, live_rows, following):
    w_in, w_mid, w_out, w_red, w_exp, gains, shifts = weights
    h_one = low_back(matmul(low(flat_in), w_in))
    a_one = jax.nn.silu(batch_norm(h_one, rows_mask, live_rows, gains[:MID], shifts[:MID]))
    reduced = low_back(low(matmul(low(a_one), w_red))).reshape(CLIPS, SLOTS, HW, GATE)
    later = jnp.concatenate([reduced[:, 1:], jnp.zeros((CLIPS, 1, HW, GATE), jnp.float32)], axis=1)
    change = following[:, :, None, None] * (later - reduced)
    mixed = low_back(low(change + grid_mean(change))).reshape(-1, GATE)
    excite = low_back(matmul(mixed, w_exp))
    gate = jax.nn.sigmoid(excite)
    gated = a_one * (1.0 + gate)
    h_two = low_back(conv_grid(low(gated), w_mid))
    a_two = jax.nn.silu(batch_norm(h_two, rows_mask, live_rows, gains[MID:2 * MID], shifts[MID:2 * MID]))
    h_three = low_back(matmul(low(a_two), w_out))
    pre = batch_norm(h_three, rows_mask, live_rows, gains[2 * MID:], shifts[2 * MID:]) + flat_in
    return jax.nn.silu(pre)

def forward(master_flat, inputs, present, counts_float, onehot):
    pieces = carve(low(master_flat))
    w_cls = pieces[14]
    b_cls = pieces[15]
    rows_mask = jnp.broadcast_to(present[:, :, None], (CLIPS, SLOTS, HW)).reshape(-1, 1)
    live_rows = jnp.sum(rows_mask)
    following = jnp.concatenate([present[:, 1:], jnp.zeros((CLIPS, 1), jnp.float32)], axis=1)
    flowing = inputs.reshape(-1, D)
    for index_b in range(2):
        flowing = bottleneck(flowing, pieces[7 * index_b:7 * index_b + 7], rows_mask, live_rows, following)
    block = flowing.reshape(CLIPS, SLOTS, HW, D)
    pooled = lax.optimization_barrier(jnp.sum(block * present[:, :, None, None], axis=(1, 2))) / (HW * counts_float)[:, None]
    logits = low_back(matmul(low(pooled), w_cls)) + b_cls
    picked = lax.optimization_barrier(jnp.sum(logits * onehot, axis=1))
    return jnp.mean(jax.nn.logsumexp(logits, axis=1) - picked)

def reference(inputs, clip_counts, labels, master, first_moment, second_moment):
    inputs_float = inputs.astype(jnp.float32)
    slot_ids = jnp.arange(SLOTS, dtype=jnp.int32)
    present = (slot_ids[None, :] < clip_counts[:, None]).astype(jnp.float32)
    counts_float = clip_counts.astype(jnp.float32)
    onehot = (labels[:, None] == jnp.arange(CLASSES, dtype=jnp.int32)[None, :]).astype(jnp.float32)

    def objective(flat, data):
        return forward(flat, data, present, counts_float, onehot)
    loss, pullback = jax.vjp(objective, master, inputs_float)
    grad_flat, grad_in = pullback(jnp.ones((), jnp.float32))
    norm = jnp.sqrt(jnp.sum(grad_flat * grad_flat))
    factor = jnp.minimum(1.0, CLIP_LIMIT / (norm + 1e-06))
    clipped = grad_flat * factor
    new_first = BETA_ONE * first_moment + (1.0 - BETA_ONE) * clipped
    new_second = BETA_TWO * second_moment + (1.0 - BETA_TWO) * clipped * clipped
    first_hat = new_first / (1.0 - BETA_ONE ** STEP)
    second_hat = new_second / (1.0 - BETA_TWO ** STEP)
    new_master = master - LEARN_RATE * (first_hat / (jnp.sqrt(second_hat) + ADAM_EPS) + WEIGHT_DECAY * master)
    bias_grad = piece_at(grad_flat, N_SEG * N_CLIP, 15)
    return (new_master, new_first, new_second, new_master.astype(jnp.bfloat16), grad_in, norm.reshape(1), bias_grad)
```

```python
import functools
import math

import jax
import jax.numpy as jnp
from jax import lax
from jax.experimental import pallas as pl
from jax.experimental.pallas import tpu as pltpu
from jax.sharding import PartitionSpec as P

D = 2048
MID = 512
GATE = 128
CLASSES = 174
GRID = 7
HW = 49
STEP = 7
LANES = 128

NORM_EPS = 1e-05
CLIP_LIMIT = 0.001
LEARN_RATE = 0.04
WEIGHT_DECAY = 0.05
BETA_ONE = 0.9
BETA_TWO = 0.999
ADAM_EPS = 1e-08

AXES = ("seg", "clip")
MESH_ID = pl.DeviceIdType.MESH
BF16 = jnp.bfloat16
F32 = jnp.float32


def matmul(left, right):
    return jnp.dot(left, right, preferred_element_type=F32)


def silu_slope(values):
    sig_val = jax.nn.sigmoid(values)
    return sig_val * (1.0 + values * (1.0 - sig_val))


def small_sum_kernel(n_seg, n_clip, inner, x_ref, o_ref, mid, near, far, send_sem, recv_sem):
    seg = lax.axis_index("seg")
    clip = lax.axis_index("clip")
    outer = n_clip // inner
    group = clip // inner
    place = lax.rem(clip, inner)
    n_near = n_seg * inner - 1
    n_far = outer - 1

    def near_peer(i):
        return (
            lax.rem(seg + i // inner, n_seg),
            group * inner + lax.rem(place + lax.rem(i, inner), inner),
        )

    def far_peer(i):
        return (seg, lax.rem(group + i, outer) * inner + place)

    def copy_near(i):
        return pltpu.make_async_remote_copy(
            src_ref=x_ref,
            dst_ref=near.at[i - 1],
            send_sem=send_sem.at[i - 1],
            recv_sem=recv_sem.at[i - 1],
            device_id=near_peer(i),
            device_id_type=MESH_ID,
        )

    def copy_far(i):
        return pltpu.make_async_remote_copy(
            src_ref=mid,
            dst_ref=far.at[i - 1],
            send_sem=send_sem.at[n_near + i - 1],
            recv_sem=recv_sem.at[n_near + i - 1],
            device_id=far_peer(i),
            device_id_type=MESH_ID,
        )

    def repeat(first, last, action):
        if last - first <= 8:
            for i in range(first, last):
                action(i)
        else:

            def body(i, carry):
                action(i)
                return carry

            lax.fori_loop(first, last, body, 0)

    barrier = pltpu.get_barrier_semaphore()

    def greet(peer):
        pl.semaphore_signal(barrier, inc=1, device_id=peer, device_id_type=MESH_ID)

    repeat(1, n_near + 1, lambda i: greet(near_peer(i)))
    repeat(1, n_far + 1, lambda i: greet(far_peer(i)))
    pl.semaphore_wait(barrier, n_near + n_far)
    repeat(1, n_near + 1, lambda i: copy_near(i).start())
    repeat(1, n_near + 1, lambda i: copy_near(i).wait())
    mid[...] = x_ref[...] + jnp.sum(near[...], axis=0)
    repeat(1, n_far + 1, lambda i: copy_far(i).start())
    repeat(1, n_far + 1, lambda i: copy_far(i).wait())
    o_ref[...] = mid[...] + jnp.sum(far[...], axis=0)


def small_sum(values):
    n_seg = lax.axis_size("seg")
    n_clip = lax.axis_size("clip")
    inner = 4 if n_clip % 4 == 0 else 1
    n_near = n_seg * inner - 1
    n_far = n_clip // inner - 1
    rows = values.shape[0]
    return pl.pallas_call(
        functools.partial(small_sum_kernel, n_seg, n_clip, inner),
        out_shape=jax.ShapeDtypeStruct(values.shape, F32),
        in_specs=[pl.BlockSpec(memory_space=pltpu.VMEM)],
        out_specs=pl.BlockSpec(memory_space=pltpu.VMEM),
        scratch_shapes=[
            pltpu.VMEM(values.shape, F32),
            pltpu.VMEM((n_near,) + values.shape, F32),
            pltpu.VMEM((n_far,) + values.shape, F32),
            pltpu.SemaphoreType.DMA((n_near + n_far,)),
            pltpu.SemaphoreType.DMA((n_near + n_far,)),
        ],
        compiler_params=pltpu.CompilerParams(collective_id=rows // 8, has_side_effects=True),
        name="small_sum",
    )(values)


def sum_pair(first, second):
    channels = first.shape[0]
    stacked = jnp.concatenate([first.reshape(-1, LANES), second.reshape(-1, LANES)], axis=0)
    total = small_sum(stacked).reshape(2, channels)
    return total[0], total[1]


def scatter_kernel(n_clip, n_jobs, *refs):
    grads = refs[:n_jobs]
    outs = refs[n_jobs : 2 * n_jobs]
    ones = refs[2 * n_jobs : 3 * n_jobs]
    twos = refs[3 * n_jobs : 4 * n_jobs]
    threes = refs[4 * n_jobs : 5 * n_jobs]
    fours = refs[5 * n_jobs : 6 * n_jobs]
    send_sem, recv_sem = refs[6 * n_jobs :]
    seg = lax.axis_index("seg")
    clip = lax.axis_index("clip")
    depth = n_clip // 4
    z = clip // 4
    y = lax.rem(clip // 2, 2)
    x = lax.rem(clip, 2)
    first = (1 - seg) * y + seg * x
    second = (1 - seg) * x + seg * y
    step = 1 + seg
    jump = 2 - seg
    across_first = (seg, clip + jump * (1 - 2 * first))
    across_second = (seg, clip + step * (1 - 2 * second))
    other = (1 - seg, clip)
    per_job = 1 + 2 + 1 + (depth - 1)

    def along(i):
        return (seg, lax.rem(z + i, depth) * 4 + y * 2 + x)

    barrier = pltpu.get_barrier_semaphore()
    for peer in [other, across_first, across_second] + [along(i) for i in range(1, depth)]:
        pl.semaphore_signal(barrier, inc=1, device_id=peer, device_id_type=MESH_ID)
    pl.semaphore_wait(barrier, depth + 2)

    def remote(job, number, source, target, peer):
        index = job * per_job + number
        return pltpu.make_async_remote_copy(
            src_ref=source,
            dst_ref=target,
            send_sem=send_sem.at[index],
            recv_sem=recv_sem.at[index],
            device_id=peer,
            device_id_type=MESH_ID,
        )

    def core_copy(job):
        return remote(job, 0, grads[job].at[1 - seg], ones[job], other)

    def first_copy(job, k):
        source = ones[job].at[:, jump * (1 - first) + step * k]
        return remote(job, 1 + k, source, twos[job].at[:, k], across_first)

    def second_copy(job):
        return remote(job, 3, twos[job].at[:, 1 - second], threes[job], across_second)

    def line_copy(job, i):
        source = threes[job].at[lax.rem(z + i, depth)]
        return remote(job, 3 + i, source, fours[job].at[i - 1], along(i))

    for job in range(n_jobs):
        core_copy(job).start()
    for job in range(n_jobs):
        core_copy(job).wait()
        one = ones[job]

        def add_one(i, carry, job=job, one=one):
            zz = i // 4
            w = lax.rem(i, 4)
            total = one[zz, w].astype(F32) + grads[job][seg, zz, w].astype(F32)
            one[zz, w] = total.astype(BF16)
            return carry

        lax.fori_loop(0, 4 * depth, add_one, 0)
        for k in range(2):
            first_copy(job, k).start()
    for job in range(n_jobs):
        for k in range(2):
            first_copy(job, k).wait()
        one, two = ones[job], twos[job]

        def add_two(i, carry, one=one, two=two):
            zz = i // 2
            k = lax.rem(i, 2)
            total = two[zz, k].astype(F32) + one[zz, jump * first + step * k].astype(F32)
            two[zz, k] = total.astype(BF16)
            return carry

        lax.fori_loop(0, 2 * depth, add_two, 0)
        second_copy(job).start()
    for job in range(n_jobs):
        second_copy(job).wait()
        two, three = twos[job], threes[job]

        def add_three(zz, carry, two=two, three=three):
            three[zz] = (three[zz].astype(F32) + two[zz, second].astype(F32)).astype(BF16)
            return carry

        lax.fori_loop(0, depth, add_three, 0)
        for i in range(1, depth):
            line_copy(job, i).start()
    for job in range(n_jobs):
        for i in range(1, depth):
            line_copy(job, i).wait()
        total = threes[job][z].astype(F32)
        for i in range(1, depth):
            total = total + fours[job][i - 1].astype(F32)
        outs[job][...] = total


def reduce_scatter(grads):
    n_seg = lax.axis_size("seg")
    n_clip = lax.axis_size("clip")
    fits = n_seg == 2 and n_clip == 16 and all(g.shape[1] % 16 == 0 for g in grads)
    if not fits:
        return [lax.psum_scatter(g, AXES, scatter_dimension=0, tiled=True)[0].astype(F32) for g in grads]
    depth = n_clip // 4
    n_jobs = len(grads)
    sizes = [g.shape[1:] for g in grads]
    shaped = [g.reshape((n_seg, depth, 4) + s) for g, s in zip(grads, sizes)]
    vmem = pl.BlockSpec(memory_space=pltpu.VMEM)
    copies = n_jobs * (depth + 3)
    return pl.pallas_call(
        functools.partial(scatter_kernel, n_clip, n_jobs),
        out_shape=[jax.ShapeDtypeStruct(s, F32) for s in sizes],
        in_specs=[vmem] * n_jobs,
        out_specs=[vmem] * n_jobs,
        scratch_shapes=[pltpu.VMEM((depth, 4) + s, BF16) for s in sizes]
        + [pltpu.VMEM((depth, 2) + s, BF16) for s in sizes]
        + [pltpu.VMEM((depth,) + s, BF16) for s in sizes]
        + [pltpu.VMEM((depth - 1,) + s, BF16) for s in sizes]
        + [pltpu.SemaphoreType.DMA((copies,)), pltpu.SemaphoreType.DMA((copies,))],
        compiler_params=pltpu.CompilerParams(
            collective_id=20, has_side_effects=True, vmem_limit_bytes=60 * 1024 * 1024
        ),
        name="reduce_scatter",
    )(*shaped)


def layout():
    block_layout = [
        (D, MID),
        (9, MID, MID),
        (MID, D),
        (MID, GATE),
        (GATE, MID),
        (2 * MID + D,),
        (2 * MID + D,),
    ]
    return block_layout + block_layout + [(D, CLASSES), (CLASSES,)]


def widths(devices):
    return [(math.prod(extent) + devices - 1) // devices for extent in layout()]


def pad_rows(flat, rows):
    return jnp.pad(flat, (0, rows * LANES - flat.shape[0])).reshape(rows, LANES)


def small_rows(devices):
    wide = widths(devices)
    amount = sum(wide[3:7]) + sum(wide[10:14])
    amount_cls = wide[14] + wide[15]
    return [16 * ((a + 16 * LANES - 1) // (16 * LANES)) for a in (amount, amount_cls)]


def gather_parameters(master):
    devices = lax.axis_size("seg") * lax.axis_size("clip")
    wide = widths(devices)
    starts = [sum(wide[:i]) for i in range(len(wide))]
    low = master.astype(BF16)

    def part(i):
        return low[starts[i] : starts[i] + wide[i]]

    def gather(values):
        return lax.all_gather(values, AXES, axis=0, tiled=True)

    big = {}
    for base in (0, 7):
        for i, columns in ((0, MID), (1, MID), (2, D)):
            big[base + i] = gather(part(base + i).reshape(-1, columns))
    rows, rows_cls = small_rows(devices)
    small = gather(pad_rows(jnp.concatenate([part(i) for i in (3, 4, 5, 6, 10, 11, 12, 13)]), rows))
    small_cls = gather(pad_rows(jnp.concatenate([part(14), part(15)]), rows_cls))
    small = small.reshape(devices, rows * LANES)
    small_cls = small_cls.reshape(devices, rows_cls * LANES)
    shapes = layout()
    pieces = dict(big)

    def take(source, ids):
        offset = 0
        for i in ids:
            amount = math.prod(shapes[i])
            pieces[i] = source[:, offset : offset + wide[i]].reshape(-1)[:amount].reshape(shapes[i])
            offset += wide[i]

    take(small, (3, 4, 5, 6, 10, 11, 12, 13))
    take(small_cls, (14, 15))
    return [pieces[i] for i in range(16)]


def scatter_gradients(grads):
    devices = lax.axis_size("seg") * lax.axis_size("clip")
    wide = widths(devices)
    rows, rows_cls = small_rows(devices)

    def shards(i):
        flat = grads[i].reshape(-1)
        return jnp.pad(flat, (0, devices * wide[i] - flat.shape[0])).reshape(devices, wide[i])

    def pack(ids, n_rows):
        packed = jnp.concatenate([shards(i) for i in ids], axis=1).astype(BF16)
        return jnp.pad(packed, ((0, 0), (0, n_rows * LANES - packed.shape[1]))).reshape(devices, n_rows, LANES)

    smalls = (3, 4, 5, 6, 10, 11, 12, 13)
    jobs = []
    for base in (7, 0):
        for i in (2, 1, 0):
            columns = grads[base + i].shape[-1]
            jobs.append(grads[base + i].astype(BF16).reshape(devices, -1, columns))
    jobs.append(pack(smalls, rows))
    jobs.append(pack((14, 15), rows_cls))
    sums = reduce_scatter(jobs)
    mine = {}
    for k, i in enumerate((9, 8, 7, 2, 1, 0)):
        mine[i] = sums[k].reshape(-1)
    for ids, flat in ((smalls, sums[6].reshape(-1)), ((14, 15), sums[7].reshape(-1))):
        offset = 0
        for i in ids:
            mine[i] = flat[offset : offset + wide[i]]
            offset += wide[i]
    return jnp.concatenate([mine[i] for i in range(16)])


def grid_mean(values):
    channels = values.shape[-1]
    frames = values.shape[1]
    grids = values.reshape(GRID, GRID, frames, channels)
    padded = jnp.pad(grids, ((1, 1), (1, 1), (0, 0), (0, 0)))
    total = padded[:, 0:GRID] + padded[:, 1 : GRID + 1] + padded[:, 2 : GRID + 2]
    total = total[0:GRID] + total[1 : GRID + 1] + total[2 : GRID + 2]
    return (total / 9.0).reshape(values.shape)


def conv(values, kernel, numbers):
    return lax.conv_general_dilated(
        values, kernel, (1, 1), ((1, 1), (1, 1)), dimension_numbers=numbers, preferred_element_type=F32
    )


def norm_forward(values, rows_mask, live_rows, gain, shift):
    masked = values * rows_mask
    sums, squares = sum_pair(jnp.sum(masked, axis=0), jnp.sum(values * masked, axis=0))
    mean_val = sums / live_rows
    variance = squares / live_rows - mean_val * mean_val
    inv_std = lax.rsqrt(variance + NORM_EPS)
    normed = (values - mean_val) * inv_std
    return (normed * gain + shift, normed, inv_std)


def norm_backward(grad_out, normed, inv_std, live_rows, rows_mask, gain):
    part_gain = jnp.sum(grad_out * normed, axis=0)
    part_shift = jnp.sum(grad_out, axis=0)
    total_gain, total_shift = sum_pair(part_gain, part_shift)
    grad_in = gain * inv_std * (grad_out - rows_mask * (total_shift + normed * total_gain) / live_rows)
    return (grad_in, part_gain, part_shift)


def by_slot(values, clips):
    return values.reshape(HW, clips, -1, values.shape[-1])


def gate_forward(reduced, masks):
    following = masks[1][None, :, :, None]
    clips = masks[0].shape[0]
    slots = by_slot(reduced, clips)
    edge = lax.ppermute(slots[:, :, 0], "seg", [(i + 1, i) for i in range(lax.axis_size("seg") - 1)])
    later = jnp.concatenate([slots[:, :, 1:], edge[:, :, None]], axis=2)
    change = (following * (later.astype(F32) - slots.astype(F32))).reshape(reduced.shape)
    return (change + grid_mean(change)).astype(BF16)


def gate_backward(d_mixed, masks):
    present = masks[0][None, :, :, None]
    following = masks[1][None, :, :, None]
    clips = masks[0].shape[0]
    slots = by_slot(d_mixed, clips)
    edge = lax.ppermute(slots[:, :, -1], "seg", [(i, i + 1) for i in range(lax.axis_size("seg") - 1)])
    edge = edge.astype(F32)
    edge = edge + grid_mean(edge)
    wide = d_mixed.astype(F32)
    spread = by_slot(wide + grid_mean(wide), clips)
    earlier = jnp.concatenate([edge[:, :, None], spread[:, :, :-1]], axis=2)
    d_part = present * earlier - following * spread
    return d_part.astype(BF16).reshape(d_mixed.shape)


def block_forward(x_low, x_float, weights, masks, live_rows):
    w_in, w_mid, w_out, w_red, w_exp, gain_low, shift_low = weights
    gains = gain_low.astype(F32)
    shifts = shift_low.astype(F32)
    rows_mask = masks[2]
    frames = x_low.shape[0] // HW
    h_one = matmul(x_low, w_in)
    y_one, normed_one, inv_one = norm_forward(h_one, rows_mask, live_rows, gains[:MID], shifts[:MID])
    a_one = jax.nn.silu(y_one)
    a_one_low = a_one.astype(BF16)
    reduced = matmul(a_one_low, w_red).astype(BF16).reshape(HW, frames, GATE)
    mixed_flat = gate_forward(reduced, masks).reshape(-1, GATE)
    gate = jax.nn.sigmoid(matmul(mixed_flat, w_exp))
    gated = (a_one * (1.0 + gate)).astype(BF16).reshape(GRID, GRID, frames, MID)
    h_two = conv(gated, w_mid.reshape(3, 3, MID, MID), ("HWNC", "HWIO", "HWNC")).reshape(-1, MID)
    y_two, normed_two, inv_two = norm_forward(
        h_two, rows_mask, live_rows, gains[MID : 2 * MID], shifts[MID : 2 * MID]
    )
    a_two_low = jax.nn.silu(y_two).astype(BF16)
    h_three = matmul(a_two_low, w_out)
    y_three, normed_three, inv_three = norm_forward(
        h_three, rows_mask, live_rows, gains[2 * MID :], shifts[2 * MID :]
    )
    pre = y_three + x_float
    kept = (
        x_low,
        a_one,
        a_one_low,
        y_one,
        normed_one,
        inv_one,
        gate,
        mixed_flat,
        gated,
        y_two,
        normed_two,
        inv_two,
        a_two_low,
        normed_three,
        inv_three,
        pre,
    )
    return (jax.nn.silu(pre), kept)


def block_backward(d_out, kept, weights, masks, live_rows):
    w_in, w_mid, w_out, w_red, w_exp, gain_low, shift_low = weights
    gains = gain_low.astype(F32)
    (
        x_low,
        a_one,
        a_one_low,
        y_one,
        normed_one,
        inv_one,
        gate,
        mixed_flat,
        gated,
        y_two,
        normed_two,
        inv_two,
        a_two_low,
        normed_three,
        inv_three,
        pre,
    ) = kept
    rows_mask = masks[2]
    frames = x_low.shape[0] // HW
    d_pre = d_out * silu_slope(pre)
    d_h_three, gain_three, shift_three = norm_backward(
        d_pre, normed_three, inv_three, live_rows, rows_mask, gains[2 * MID :]
    )
    d_h_three_low = d_h_three.astype(BF16)
    g_out = matmul(a_two_low.T, d_h_three_low)
    d_a_two = matmul(d_h_three_low, w_out.T)
    d_y_two = d_a_two * silu_slope(y_two)
    d_h_two, gain_two, shift_two = norm_backward(
        d_y_two, normed_two, inv_two, live_rows, rows_mask, gains[MID : 2 * MID]
    )
    d_h_two_low = d_h_two.astype(BF16).reshape(GRID, GRID, frames, MID)
    g_mid = conv(gated, d_h_two_low, ("HWCN", "HWIO", "HWNC")).reshape(9 * MID, MID)
    turned = jnp.flip(w_mid.reshape(3, 3, MID, MID), (0, 1))
    d_gated = conv(d_h_two_low, turned, ("HWNC", "HWOI", "HWNC")).reshape(-1, MID)
    d_excite = (d_gated * a_one * gate * (1.0 - gate)).astype(BF16)
    g_exp = matmul(mixed_flat.T, d_excite)
    d_mixed = matmul(d_excite, w_exp.T).astype(BF16).reshape(HW, frames, GATE)
    d_reduced_flat = gate_backward(d_mixed, masks).reshape(-1, GATE)
    g_red = matmul(a_one_low.T, d_reduced_flat)
    d_a_one = d_gated * (1.0 + gate) + matmul(d_reduced_flat, w_red.T)
    d_y_one = d_a_one * silu_slope(y_one)
    d_h_one, gain_one, shift_one = norm_backward(
        d_y_one, normed_one, inv_one, live_rows, rows_mask, gains[:MID]
    )
    d_h_one_low = d_h_one.astype(BF16)
    g_in = matmul(x_low.T, d_h_one_low)
    d_x = d_pre + matmul(d_h_one_low, w_in.T)
    grads = [
        g_in,
        g_mid,
        g_out,
        g_red,
        g_exp,
        jnp.concatenate([gain_one, gain_two, gain_three]),
        jnp.concatenate([shift_one, shift_two, shift_three]),
    ]
    return (d_x, grads)


def on_device(inputs, clip_counts, labels, master, first_moment, second_moment):
    seg_count = lax.axis_size("seg")
    pieces = gather_parameters(master)
    first_weights = pieces[0:7]
    second_weights = pieces[7:14]
    w_cls = pieces[14]
    b_cls = pieces[15].astype(F32)
    clip_local, slot_local = inputs.shape[:2]
    frames = clip_local * slot_local
    slot_ids = lax.axis_index("seg") * slot_local + jnp.arange(slot_local, dtype=jnp.int32)
    present = (slot_ids[None, :] < clip_counts[:, None]).astype(F32)
    following = (slot_ids[None, :] + 1 < clip_counts[:, None]).astype(F32)
    rows_mask = jnp.broadcast_to(present.reshape(1, frames), (HW, frames)).reshape(-1, 1)
    masks = (present, following, rows_mask)
    live_part = jnp.full((8, LANES), HW * jnp.sum(present), F32)
    live_rows = small_sum(live_part)[0, 0]
    flat_in = inputs.reshape(frames, HW, D).transpose(1, 0, 2).reshape(-1, D)
    middle, kept_first = block_forward(flat_in, flat_in.astype(F32), first_weights, masks, live_rows)
    final, kept_second = block_forward(middle.astype(BF16), middle, second_weights, masks, live_rows)
    block = final.reshape(HW, clip_local, slot_local, D)
    partial_value = jnp.sum(block * present[None, :, :, None], axis=(0, 2))
    pooled_sum = lax.psum(partial_value.astype(BF16), "seg").astype(F32)
    counts_float = clip_counts.astype(F32)
    pooled = pooled_sum / (HW * counts_float)[:, None]
    pooled_low = pooled.astype(BF16)
    logits = matmul(pooled_low, w_cls) + b_cls
    clips_total = clip_local * lax.axis_size("clip")
    onehot = (labels[:, None] == jnp.arange(CLASSES, dtype=jnp.int32)[None, :]).astype(F32)
    d_logits = (jax.nn.softmax(logits, axis=1) - onehot) / clips_total
    d_lin = d_logits.astype(BF16)
    g_cls = matmul(pooled_low.T, d_lin) / seg_count
    g_bias = jnp.sum(d_logits, axis=0) / seg_count
    d_pooled = matmul(d_lin, w_cls.T)
    scaled = d_pooled / (HW * counts_float)[:, None]
    d_frame = present[:, :, None] * scaled[:, None, :]
    d_block = jnp.broadcast_to(d_frame.reshape(1, frames, D), (HW, frames, D)).reshape(-1, D)
    d_middle, grads_second = block_backward(d_block, kept_second, second_weights, masks, live_rows)
    input_grad, grads_first = block_backward(d_middle, kept_first, first_weights, masks, live_rows)
    grad_mine = scatter_gradients(grads_first + grads_second + [g_cls, g_bias])
    tail = jnp.concatenate(
        [
            jnp.pad(g_bias, (0, 8 * LANES - CLASSES)).reshape(8, LANES),
            jnp.full((8, LANES), jnp.sum(grad_mine * grad_mine), F32),
        ]
    )
    tail = small_sum(tail)
    norm = jnp.sqrt(tail[8, 0])
    bias_grad = tail[:8].reshape(-1)[:CLASSES]
    factor = jnp.minimum(1.0, CLIP_LIMIT / (norm + 1e-06))
    clipped = grad_mine * factor
    new_first = BETA_ONE * first_moment + (1.0 - BETA_ONE) * clipped
    new_second = BETA_TWO * second_moment + (1.0 - BETA_TWO) * clipped * clipped
    first_hat = new_first / (1.0 - BETA_ONE**STEP)
    second_hat = new_second / (1.0 - BETA_TWO**STEP)
    new_master = master - LEARN_RATE * (
        first_hat / (jnp.sqrt(second_hat) + ADAM_EPS) + WEIGHT_DECAY * master
    )
    grid_grad = input_grad.reshape(HW, frames, D).transpose(1, 0, 2)
    return (
        new_master,
        new_first,
        new_second,
        new_master.astype(BF16),
        grid_grad.reshape(inputs.shape),
        norm.reshape(1),
        bias_grad,
    )


def solution(mesh):
    return jax.shard_map(
        on_device,
        mesh=mesh,
        in_specs=(
            P("clip", "seg", None, None),
            P("clip"),
            P("clip"),
            P(AXES),
            P(AXES),
            P(AXES),
        ),
        out_specs=(
            P(AXES),
            P(AXES),
            P(AXES),
            P(AXES),
            P("clip", "seg", None, None),
            P(),
            P(),
        ),
        check_vma=False,
    )
```

```python
import functools
import math

import jax
import jax.numpy as jnp
from jax import lax
from jax.experimental import pallas as pl
from jax.experimental.pallas import tpu as pltpu
from jax.sharding import PartitionSpec as P

D = 2048
MID = 512
GATE = 128
CLASSES = 174
GRID = 7
HW = 49
STEP = 7
LANES = 128

NORM_EPS = 1e-05
CLIP_LIMIT = 0.001
LEARN_RATE = 0.04
WEIGHT_DECAY = 0.05
BETA_ONE = 0.9
BETA_TWO = 0.999
ADAM_EPS = 1e-08

AXES = ("seg", "clip")
MESH_ID = pl.DeviceIdType.MESH
BF16 = jnp.bfloat16
F32 = jnp.float32


def matmul(left, right):
    return jnp.dot(left, right, preferred_element_type=F32)


def silu_slope(values):
    sig_val = jax.nn.sigmoid(values)
    return sig_val * (1.0 + values * (1.0 - sig_val))


def small_sum_kernel(n_seg, n_clip, inner, x_ref, o_ref, mid, near, far, send_sem, recv_sem):
    seg = lax.axis_index("seg")
    clip = lax.axis_index("clip")
    outer = n_clip // inner
    group = clip // inner
    place = lax.rem(clip, inner)
    n_near = n_seg * inner - 1
    n_far = outer - 1

    def near_peer(i):
        return (
            lax.rem(seg + i // inner, n_seg),
            group * inner + lax.rem(place + lax.rem(i, inner), inner),
        )

    def far_peer(i):
        return (seg, lax.rem(group + i, outer) * inner + place)

    def copy_near(i):
        return pltpu.make_async_remote_copy(
            src_ref=x_ref,
            dst_ref=near.at[i - 1],
            send_sem=send_sem.at[i - 1],
            recv_sem=recv_sem.at[i - 1],
            device_id=near_peer(i),
            device_id_type=MESH_ID,
        )

    def copy_far(i):
        return pltpu.make_async_remote_copy(
            src_ref=mid,
            dst_ref=far.at[i - 1],
            send_sem=send_sem.at[n_near + i - 1],
            recv_sem=recv_sem.at[n_near + i - 1],
            device_id=far_peer(i),
            device_id_type=MESH_ID,
        )

    def repeat(first, last, action):
        if last - first <= 8:
            for i in range(first, last):
                action(i)
        else:

            def body(i, carry):
                action(i)
                return carry

            lax.fori_loop(first, last, body, 0)

    barrier = pltpu.get_barrier_semaphore()

    def greet(peer):
        pl.semaphore_signal(barrier, inc=1, device_id=peer, device_id_type=MESH_ID)

    repeat(1, n_near + 1, lambda i: greet(near_peer(i)))
    repeat(1, n_far + 1, lambda i: greet(far_peer(i)))
    pl.semaphore_wait(barrier, n_near + n_far)
    repeat(1, n_near + 1, lambda i: copy_near(i).start())
    repeat(1, n_near + 1, lambda i: copy_near(i).wait())
    mid[...] = x_ref[...] + jnp.sum(near[...], axis=0)
    repeat(1, n_far + 1, lambda i: copy_far(i).start())
    repeat(1, n_far + 1, lambda i: copy_far(i).wait())
    o_ref[...] = mid[...] + jnp.sum(far[...], axis=0)


def small_sum(values):
    n_seg = lax.axis_size("seg")
    n_clip = lax.axis_size("clip")
    inner = 4 if n_clip % 4 == 0 else 1
    n_near = n_seg * inner - 1
    n_far = n_clip // inner - 1
    rows = values.shape[0]
    return pl.pallas_call(
        functools.partial(small_sum_kernel, n_seg, n_clip, inner),
        out_shape=jax.ShapeDtypeStruct(values.shape, F32),
        in_specs=[pl.BlockSpec(memory_space=pltpu.VMEM)],
        out_specs=pl.BlockSpec(memory_space=pltpu.VMEM),
        scratch_shapes=[
            pltpu.VMEM(values.shape, F32),
            pltpu.VMEM((n_near,) + values.shape, F32),
            pltpu.VMEM((n_far,) + values.shape, F32),
            pltpu.SemaphoreType.DMA((n_near + n_far,)),
            pltpu.SemaphoreType.DMA((n_near + n_far,)),
        ],
        compiler_params=pltpu.CompilerParams(collective_id=rows // 8, has_side_effects=True),
        name="small_sum",
    )(values)


def sum_pair(first, second):
    channels = first.shape[0]
    stacked = jnp.concatenate([first.reshape(-1, LANES), second.reshape(-1, LANES)], axis=0)
    total = small_sum(stacked).reshape(2, channels)
    return total[0], total[1]


def scatter_kernel(n_clip, n_jobs, *refs):
    grads = refs[:n_jobs]
    outs = refs[n_jobs : 2 * n_jobs]
    ones = refs[2 * n_jobs : 3 * n_jobs]
    twos = refs[3 * n_jobs : 4 * n_jobs]
    threes = refs[4 * n_jobs : 5 * n_jobs]
    fours = refs[5 * n_jobs : 6 * n_jobs]
    send_sem, recv_sem = refs[6 * n_jobs :]
    seg = lax.axis_index("seg")
    clip = lax.axis_index("clip")
    depth = n_clip // 4
    z = clip // 4
    y = lax.rem(clip // 2, 2)
    x = lax.rem(clip, 2)
    first = (1 - seg) * y + seg * x
    second = (1 - seg) * x + seg * y
    step = 1 + seg
    jump = 2 - seg
    across_first = (seg, clip + jump * (1 - 2 * first))
    across_second = (seg, clip + step * (1 - 2 * second))
    other = (1 - seg, clip)
    per_job = 1 + 2 + 1 + (depth - 1)

    def along(i):
        return (seg, lax.rem(z + i, depth) * 4 + y * 2 + x)

    barrier = pltpu.get_barrier_semaphore()
    for peer in [other, across_first, across_second] + [along(i) for i in range(1, depth)]:
        pl.semaphore_signal(barrier, inc=1, device_id=peer, device_id_type=MESH_ID)
    pl.semaphore_wait(barrier, depth + 2)

    def remote(job, number, source, target, peer):
        index = job * per_job + number
        return pltpu.make_async_remote_copy(
            src_ref=source,
            dst_ref=target,
            send_sem=send_sem.at[index],
            recv_sem=recv_sem.at[index],
            device_id=peer,
            device_id_type=MESH_ID,
        )

    def core_copy(job):
        return remote(job, 0, grads[job].at[1 - seg], ones[job], other)

    def first_copy(job, k):
        source = ones[job].at[:, jump * (1 - first) + step * k]
        return remote(job, 1 + k, source, twos[job].at[:, k], across_first)

    def second_copy(job):
        return remote(job, 3, twos[job].at[:, 1 - second], threes[job], across_second)

    def line_copy(job, i):
        source = threes[job].at[lax.rem(z + i, depth)]
        return remote(job, 3 + i, source, fours[job].at[i - 1], along(i))

    for job in range(n_jobs):
        core_copy(job).start()
    for job in range(n_jobs):
        core_copy(job).wait()
        one = ones[job]

        def add_one(i, carry, job=job, one=one):
            zz = i // 4
            w = lax.rem(i, 4)
            total = one[zz, w].astype(F32) + grads[job][seg, zz, w].astype(F32)
            one[zz, w] = total.astype(BF16)
            return carry

        lax.fori_loop(0, 4 * depth, add_one, 0)
        for k in range(2):
            first_copy(job, k).start()
    for job in range(n_jobs):
        for k in range(2):
            first_copy(job, k).wait()
        one, two = ones[job], twos[job]

        def add_two(i, carry, one=one, two=two):
            zz = i // 2
            k = lax.rem(i, 2)
            total = two[zz, k].astype(F32) + one[zz, jump * first + step * k].astype(F32)
            two[zz, k] = total.astype(BF16)
            return carry

        lax.fori_loop(0, 2 * depth, add_two, 0)
        second_copy(job).start()
    for job in range(n_jobs):
        second_copy(job).wait()
        two, three = twos[job], threes[job]

        def add_three(zz, carry, two=two, three=three):
            three[zz] = (three[zz].astype(F32) + two[zz, second].astype(F32)).astype(BF16)
            return carry

        lax.fori_loop(0, depth, add_three, 0)
        for i in range(1, depth):
            line_copy(job, i).start()
    for job in range(n_jobs):
        for i in range(1, depth):
            line_copy(job, i).wait()
        total = threes[job][z].astype(F32)
        for i in range(1, depth):
            total = total + fours[job][i - 1].astype(F32)
        outs[job][...] = total


def reduce_scatter(grads):
    n_seg = lax.axis_size("seg")
    n_clip = lax.axis_size("clip")
    fits = n_seg == 2 and n_clip == 16 and all(g.shape[1] % 16 == 0 for g in grads)
    if not fits:
        return [lax.psum_scatter(g, AXES, scatter_dimension=0, tiled=True)[0].astype(F32) for g in grads]
    depth = n_clip // 4
    n_jobs = len(grads)
    sizes = [g.shape[1:] for g in grads]
    shaped = [g.reshape((n_seg, depth, 4) + s) for g, s in zip(grads, sizes)]
    vmem = pl.BlockSpec(memory_space=pltpu.VMEM)
    copies = n_jobs * (depth + 3)
    return pl.pallas_call(
        functools.partial(scatter_kernel, n_clip, n_jobs),
        out_shape=[jax.ShapeDtypeStruct(s, F32) for s in sizes],
        in_specs=[vmem] * n_jobs,
        out_specs=[vmem] * n_jobs,
        scratch_shapes=[pltpu.VMEM((depth, 4) + s, BF16) for s in sizes]
        + [pltpu.VMEM((depth, 2) + s, BF16) for s in sizes]
        + [pltpu.VMEM((depth,) + s, BF16) for s in sizes]
        + [pltpu.VMEM((depth - 1,) + s, BF16) for s in sizes]
        + [pltpu.SemaphoreType.DMA((copies,)), pltpu.SemaphoreType.DMA((copies,))],
        compiler_params=pltpu.CompilerParams(
            collective_id=20, has_side_effects=True, vmem_limit_bytes=60 * 1024 * 1024
        ),
        name="reduce_scatter",
    )(*shaped)


def layout():
    block_layout = [
        (D, MID),
        (9, MID, MID),
        (MID, D),
        (MID, GATE),
        (GATE, MID),
        (2 * MID + D,),
        (2 * MID + D,),
    ]
    return block_layout + block_layout + [(D, CLASSES), (CLASSES,)]


def widths(devices):
    return [(math.prod(extent) + devices - 1) // devices for extent in layout()]


def pad_rows(flat, rows):
    return jnp.pad(flat, (0, rows * LANES - flat.shape[0])).reshape(rows, LANES)


def small_rows(devices):
    wide = widths(devices)
    amount = sum(wide[3:7]) + sum(wide[10:14])
    amount_cls = wide[14] + wide[15]
    return [16 * ((a + 16 * LANES - 1) // (16 * LANES)) for a in (amount, amount_cls)]


def gather_parameters(master):
    devices = lax.axis_size("seg") * lax.axis_size("clip")
    wide = widths(devices)
    starts = [sum(wide[:i]) for i in range(len(wide))]
    low = master.astype(BF16)

    def part(i):
        return low[starts[i] : starts[i] + wide[i]]

    def gather(values):
        return lax.all_gather(values, AXES, axis=0, tiled=True)

    big = {}
    for base in (0, 7):
        for i, columns in ((0, MID), (1, MID), (2, D)):
            big[base + i] = gather(part(base + i).reshape(-1, columns))
    rows, rows_cls = small_rows(devices)
    small = gather(pad_rows(jnp.concatenate([part(i) for i in (3, 4, 5, 6, 10, 11, 12, 13)]), rows))
    small_cls = gather(pad_rows(jnp.concatenate([part(14), part(15)]), rows_cls))
    small = small.reshape(devices, rows * LANES)
    small_cls = small_cls.reshape(devices, rows_cls * LANES)
    shapes = layout()
    pieces = dict(big)

    def take(source, ids):
        offset = 0
        for i in ids:
            amount = math.prod(shapes[i])
            pieces[i] = source[:, offset : offset + wide[i]].reshape(-1)[:amount].reshape(shapes[i])
            offset += wide[i]

    take(small, (3, 4, 5, 6, 10, 11, 12, 13))
    take(small_cls, (14, 15))
    return [pieces[i] for i in range(16)]


def scatter_gradients(grads):
    devices = lax.axis_size("seg") * lax.axis_size("clip")
    wide = widths(devices)
    rows, rows_cls = small_rows(devices)

    def shards(i):
        flat = grads[i].reshape(-1)
        return jnp.pad(flat, (0, devices * wide[i] - flat.shape[0])).reshape(devices, wide[i])

    def pack(ids, n_rows):
        packed = jnp.concatenate([shards(i) for i in ids], axis=1).astype(BF16)
        return jnp.pad(packed, ((0, 0), (0, n_rows * LANES - packed.shape[1]))).reshape(devices, n_rows, LANES)

    smalls = (3, 4, 5, 6, 10, 11, 12, 13)
    jobs = []
    for base in (7, 0):
        for i in (2, 1, 0):
            columns = grads[base + i].shape[-1]
            jobs.append(grads[base + i].astype(BF16).reshape(devices, -1, columns))
    jobs.append(pack(smalls, rows))
    jobs.append(pack((14, 15), rows_cls))
    sums = reduce_scatter(jobs)
    mine = {}
    for k, i in enumerate((9, 8, 7, 2, 1, 0)):
        mine[i] = sums[k].reshape(-1)
    for ids, flat in ((smalls, sums[6].reshape(-1)), ((14, 15), sums[7].reshape(-1))):
        offset = 0
        for i in ids:
            mine[i] = flat[offset : offset + wide[i]]
            offset += wide[i]
    return jnp.concatenate([mine[i] for i in range(16)])


def part_of(master, index):
    devices = lax.axis_size("seg") * lax.axis_size("clip")
    wide = widths(devices)
    start = sum(wide[:index])
    return master[start : start + wide[index]]


def norm_table(master, live_part):
    devices = lax.axis_size("seg") * lax.axis_size("clip")
    me = lax.axis_index(AXES)
    width = 2 * MID + D

    def spread(indices, amount):
        parts = jnp.stack([part_of(master, i) for i in indices]).astype(BF16).astype(F32)
        table = jnp.zeros((len(indices), devices, parts.shape[1]), F32)
        table = lax.dynamic_update_slice(table, parts[:, None, :], (0, me, 0))
        return table.reshape(len(indices), -1)[:, :amount]

    norms = spread((5, 6, 12, 13), width).reshape(-1, LANES)
    bias = spread((15,), CLASSES)
    bias = jnp.pad(bias.reshape(-1), (0, 2 * LANES - CLASSES)).reshape(2, LANES)
    live = jnp.full((NORM_ROWS - norms.shape[0] - 2, LANES), live_part, F32)
    return jnp.concatenate([norms, bias, live])


def lanes_first(values):
    lead = values.shape[:-2]
    rows, columns = values.shape[-2:]
    split = values.reshape(lead + (rows, columns // LANES, LANES))
    return jnp.swapaxes(split, -3, -2).reshape(lead + (-1, LANES))


def weight_shards(master):
    devices = lax.axis_size("seg") * lax.axis_size("clip")
    if lax.axis_size("seg") != 2 or devices != SMALL_SHARDS:
        return None
    low = master.astype(BF16)
    shards = {}
    small = []
    for block in range(2):
        base = 7 * block
        shards["in%d" % block] = part_of(low, base).reshape(-1, MID)
        shards["mid%d" % block] = part_of(low, base + 1).reshape(-1, MID)
        shards["out%d" % block] = part_of(low, base + 2).reshape(-1, D)
        small.append(part_of(low, base + 3).reshape(-1, GATE))
        small.append(lanes_first(part_of(low, base + 4).reshape(-1, MID)))
    shards["small"] = jnp.concatenate(small)
    cls = part_of(low, 14).reshape(-1, CLASSES)
    shards["cls"] = jnp.pad(cls, ((0, 0), (0, 2 * LANES - CLASSES)))
    return shards


def whole_weights(master):
    pieces = gather_parameters(master)
    whole = {}
    small = []
    for block in range(2):
        w_in, w_mid, w_out, w_red, w_exp = pieces[7 * block : 7 * block + 5]
        whole["in%d" % block] = w_in
        whole["mid%d" % block] = w_mid.reshape(9 * MID, MID)
        whole["out%d" % block] = w_out
        small.append(w_red.reshape(SMALL_SHARDS, -1, GATE))
        small.append(lanes_first(w_exp.reshape(SMALL_SHARDS, -1, MID)))
    whole["small"] = jnp.concatenate(small, axis=1).reshape(-1, LANES)
    whole["cls"] = jnp.pad(pieces[14], ((0, 0), (0, 2 * LANES - CLASSES)))
    return whole


def grid_mean(values):
    channels = values.shape[-1]
    frames = values.shape[1]
    grids = values.reshape(GRID, GRID, frames, channels)
    padded = jnp.pad(grids, ((1, 1), (1, 1), (0, 0), (0, 0)))
    total = padded[:, 0:GRID] + padded[:, 1 : GRID + 1] + padded[:, 2 : GRID + 2]
    total = total[0:GRID] + total[1 : GRID + 1] + total[2 : GRID + 2]
    return (total / 9.0).reshape(values.shape)


def conv(values, kernel, numbers):
    return lax.conv_general_dilated(
        values, kernel, (1, 1), ((1, 1), (1, 1)), dimension_numbers=numbers, preferred_element_type=F32
    )


class Links:
    def __init__(self, n_seg, n_clip, send_sem, recv_sem):
        self.n_seg = n_seg
        self.n_clip = n_clip
        self.inner = 4
        self.outer = n_clip // 4
        self.seg = lax.axis_index("seg")
        self.clip = lax.axis_index("clip")
        self.group = self.clip // 4
        self.place = lax.rem(self.clip, 4)
        y = self.place // 2
        x = lax.rem(self.place, 2)
        self.first = (1 - self.seg) * y + self.seg * x
        self.second = (1 - self.seg) * x + self.seg * y
        self.step = 1 + self.seg
        self.jump = 2 - self.seg
        self.across_first = (self.seg, self.clip + self.jump * (1 - 2 * self.first))
        self.across_second = (self.seg, self.clip + self.step * (1 - 2 * self.second))
        self.other = (1 - self.seg, self.clip)
        self.send_sem = send_sem
        self.recv_sem = recv_sem
        self.used = 0

    def take(self, count):
        base = self.used
        self.used += count
        return base

    def near_peer(self, i):
        return (
            lax.rem(self.seg + i // 4, self.n_seg),
            self.group * 4 + lax.rem(self.place + lax.rem(i, 4), 4),
        )

    def far_peer(self, i):
        return (self.seg, lax.rem(self.group + i, self.outer) * 4 + self.place)

    def remote(self, index, source, target, peer):
        return pltpu.make_async_remote_copy(
            src_ref=source,
            dst_ref=target,
            send_sem=self.send_sem.at[index],
            recv_sem=self.recv_sem.at[index],
            device_id=peer,
            device_id_type=MESH_ID,
        )

    def local(self, source, target):
        return pltpu.make_async_copy(source, target, self.recv_sem.at[self.take(1)])

    def meet(self):
        barrier = pltpu.get_barrier_semaphore()
        n_near = self.n_seg * 4 - 1
        n_far = self.outer - 1

        def greet(peer):
            pl.semaphore_signal(barrier, inc=1, device_id=peer, device_id_type=MESH_ID)

        repeat(1, n_near + 1, lambda i: greet(self.near_peer(i)))
        repeat(1, n_far + 1, lambda i: greet(self.far_peer(i)))
        pl.semaphore_wait(barrier, n_near + n_far)

    def all_sum(self, source, middle, near, far):
        n_near = self.n_seg * 4 - 1
        n_far = self.outer - 1
        base = self.take(n_near + n_far)

        def close(i):
            return self.remote(base + i - 1, source, near.at[i - 1], self.near_peer(i))

        def distant(i):
            return self.remote(base + n_near + i - 1, middle, far.at[i - 1], self.far_peer(i))

        repeat(1, n_near + 1, lambda i: close(i).start())
        repeat(1, n_near + 1, lambda i: close(i).wait())
        middle[...] = source[...] + jnp.sum(near[...], axis=0)
        repeat(1, n_far + 1, lambda i: distant(i).start())
        repeat(1, n_far + 1, lambda i: distant(i).wait())
        return middle[...] + jnp.sum(far[...], axis=0)


def repeat(first, last, action):
    if last - first <= 8:
        for i in range(first, last):
            action(i)
    else:

        def body(i, carry):
            action(i)
            return carry

        lax.fori_loop(first, last, body, 0)


def sum_scratch(n_seg, n_clip, shape):
    return [
        pltpu.VMEM(shape, F32),
        pltpu.VMEM(shape, F32),
        pltpu.VMEM((n_seg * 4 - 1,) + shape, F32),
        pltpu.VMEM((n_clip // 4 - 1,) + shape, F32),
    ]


class Gather:
    def __init__(self, links, shard, whole):
        depth = links.outer
        whole = whole.reshape((links.n_seg, depth, 4) + shard.shape)
        base = links.take(depth + 3)
        seg, z, place = links.seg, links.group, links.place
        self.own = links.local(shard, whole.at[seg, z, place])
        self.steps = [
            [
                links.remote(base + i - 1, shard, whole.at[seg, z, place], links.far_peer(i))
                for i in range(1, depth)
            ],
            [
                links.remote(
                    base + depth - 1, whole.at[seg, :, place], whole.at[seg, :, place], links.across_second
                )
            ],
            [],
            [links.remote(base + depth + 2, whole.at[seg], whole.at[seg], links.other)],
        ]
        for k in range(2):
            index = links.jump * links.first + links.step * k
            self.steps[2].append(
                links.remote(
                    base + depth + k, whole.at[seg, :, index], whole.at[seg, :, index], links.across_first
                )
            )
        self.at = -1

    def advance(self, last=3):
        if self.at >= 0:
            for copy in self.steps[self.at]:
                copy.wait()
            if self.at == 0:
                self.own.wait()
        self.at += 1
        if self.at == 0:
            self.own.start()
        if self.at <= 3:
            for copy in self.steps[self.at]:
                copy.start()

    def finish(self):
        while self.at <= 3:
            self.advance()


def row_vector(table, start, count):
    return jnp.concatenate([table[start + k : start + k + 1, :] for k in range(count)], axis=1)


def put_rows(target, start, vector, count):
    width = vector.shape[1] // count
    for k in range(count):
        target[start + k : start + k + 1, :] = vector[:, k * width : (k + 1) * width]


def fold(values):
    return jnp.sum(values.reshape(-1, 8, values.shape[-1]), axis=0)


def excite_weights(small, block):
    shards = small.shape[0]
    rows = small[:, 32 * block + 16 : 32 * block + 32].reshape(shards * 16, LANES)
    deep = GATE // shards
    line = lax.broadcasted_iota(jnp.int32, (GATE, shards * 16), 0)
    column = lax.broadcasted_iota(jnp.int32, (GATE, shards * 16), 1)
    parts = []
    for k in range(MID // LANES):
        wanted = (line // deep) * 16 + k * deep + lax.rem(line, deep)
        pick = (column == wanted).astype(F32).astype(BF16)
        parts.append(matmul(pick, rows))
    return jnp.concatenate(parts, axis=1).astype(BF16)


SMALL_SHARDS = 32
NORM_ROWS = 104
BLOCK_NORMS = 48


def forward_kernel(n_seg, n_clip, block, jobs, plan, *refs):
    refs = list(refs)

    def pop(count=1):
        taken = refs[:count]
        del refs[:count]
        return taken if count != 1 else taken[0]

    last = block == 1
    x_hbm, mask, following, norm_in = pop(4)
    shards = dict(zip(jobs, [pop() for _ in jobs]))
    given = dict(zip(plan, [pop() for _ in plan]))
    wholes = dict(zip(jobs, [pop() for _ in jobs]))
    h1_out, low_out, gate_out, mix_out, f_out, h2_out, a2_out, h3_out = pop(8)
    out_hbm, norm_out, st1, st2, st3 = pop(5)
    xv, w_in, w_mid, w_out, small = pop(5)
    h1v, a1v, lowv, rv, edge, dpad, mixv, gatev, fpad, h2v, a2v, h3v = pop(12)
    wide_sum, wide_square, w_exp = pop(3)
    sums = [pop(4) for _ in range(4)]
    pooled = pop() if last else None
    send_sem, recv_sem = pop(2)
    links = Links(n_seg, n_clip, send_sem, recv_sem)
    frames = xv.shape[1]
    live = norm_out if not last else norm_in
    outgoing = []

    def send_out(source, target):
        copy = links.local(source, target)
        copy.start()
        outgoing.append(copy)

    links.meet()
    load_x = links.local(x_hbm, xv)
    load_x.start()
    gathers = {name: Gather(links, shards[name], wholes[name]) for name in jobs}

    def load(name, target):
        if name in gathers:
            gathers[name].finish()
            source = wholes[name]
        else:
            source = given[name]
        copy = links.local(source.reshape(target.shape), target)
        copy.start()
        return copy

    def push(*names):
        for name in names:
            if name in gathers and gathers[name].at <= 3:
                gathers[name].advance()

    own_in = "in%d" % block
    own_mid = "mid%d" % block
    own_out = "out%d" % block
    if not last:
        push(own_in, "small")
        sums[0][0][...] = norm_in[...]
        norm_out[...] = links.all_sum(*sums[0])
        push(own_in, "small", own_mid)
        dpad[...] = jnp.zeros_like(dpad)
        fpad[...] = jnp.zeros_like(fpad)
        push(own_in, "small")
        push(own_in, "small", own_mid, own_out)
    else:
        push(own_mid)
        dpad[...] = jnp.zeros_like(dpad)
        fpad[...] = jnp.zeros_like(fpad)
    wait_in = load(own_in, w_in)
    wait_small = load("small", small)
    wait_in.wait()
    load_x.wait()
    norms = live
    base = BLOCK_NORMS * block
    live_rows = norms[98:99, 0:1]
    half = MID // LANES

    def norm(index, tot, columns, start, out):
        mean = jnp.concatenate([tot[k : k + 1] for k in range(4)], axis=1) / live_rows
        square = jnp.concatenate([tot[4 + k : 5 + k] for k in range(4)], axis=1) / live_rows
        inv = lax.rsqrt(square - mean * mean + NORM_EPS)
        out[0:1, :] = mean
        out[1:2, :] = inv
        gain = row_vector(norms, base + start, columns // LANES)
        shift = row_vector(norms, base + 24 + start, columns // LANES)
        scale = gain * inv
        return scale, shift - mean * scale

    def masked_sums(values):
        shaped = values.reshape(-1, frames, values.shape[-1])
        masked = shaped * mask[...][None]
        return fold(masked), fold(masked * shaped)

    zeros = jnp.zeros((8, MID), F32)

    def first(i, carry):
        part = matmul(xv[pl.ds(GRID * i, GRID)].reshape(GRID * frames, D), w_in[...])
        h1v[pl.ds(GRID * i, GRID)] = part.reshape(GRID, frames, MID)
        one, two = masked_sums(part)
        return (carry[0] + one, carry[1] + two)

    one, two = lax.fori_loop(0, GRID, first, (zeros, zeros))
    send_out(h1v, h1_out)
    push(own_mid, own_out)
    if not last:
        push("in1")
    stat = sums[1][0]
    put_rows(stat, 0, jnp.sum(one, axis=0, keepdims=True), 4)
    put_rows(stat, 4, jnp.sum(two, axis=0, keepdims=True), 4)
    scale_one, shift_one = norm(0, links.all_sum(*sums[1]), MID, 0, st1)
    push(own_mid)
    wait_small.wait()
    w_exp[...] = excite_weights(small, block)
    red = small[:, 32 * block : 32 * block + 16].reshape(MID, GATE)

    def second(i, carry):
        for j in range(GRID):
            y = h1v[GRID * i + j] * scale_one + shift_one
            a = y * jax.nn.sigmoid(y)
            a1v[GRID * i + j] = a
            lowv[GRID * i + j] = a.astype(BF16)
        part = matmul(lowv[pl.ds(GRID * i, GRID)].reshape(GRID * frames, MID), red)
        rv[pl.ds(GRID * i, GRID)] = part.astype(BF16).reshape(GRID, frames, GATE)
        return carry

    lax.fori_loop(0, GRID, second, 0)
    send_out(lowv, low_out)
    swap = links.remote(links.take(1), rv.at[:, 0:16], edge, links.other)
    swap.start()
    if last:
        push(own_mid)
    push(own_out)
    swap.wait()
    clips = frames // 8
    turn = frames - clips
    row = lax.broadcasted_iota(jnp.int32, (frames, GATE), 0)

    def change(i, carry):
        for j in range(GRID):
            now = rv[GRID * i + j].astype(F32)
            rest = edge[GRID * i + j].astype(F32)
            rest = jnp.concatenate([rest] * (frames // 16), axis=0)
            later = jnp.where(row < turn, pltpu.roll(now, turn, 0), pltpu.roll(rest, turn, 0))
            dpad[i + 1, j + 1] = following[...] * (later - now)
        return carry

    lax.fori_loop(0, GRID, change, 0)

    def excite(i, carry):
        for j in range(GRID):
            total = jnp.zeros((frames, GATE), F32)
            for k in range(9):
                total = total + dpad[i + k // 3, j + k % 3]
            mixv[GRID * i + j] = (dpad[i + 1, j + 1] + total / 9.0).astype(BF16)
        e = matmul(mixv[pl.ds(GRID * i, GRID)].reshape(GRID * frames, GATE), w_exp[...])
        e = e.reshape(GRID, frames, MID)
        for j in range(GRID):
            gate = jax.nn.sigmoid(e[j])
            gatev[GRID * i + j] = gate.astype(BF16)
            fpad[i + 1, j + 1] = (a1v[GRID * i + j] * (1.0 + gate)).astype(BF16)
        return carry

    lax.fori_loop(0, GRID, excite, 0)
    send_out(mixv, mix_out)
    send_out(gatev, gate_out)
    send_out(fpad.at[pl.ds(1, GRID), pl.ds(1, GRID)], f_out)
    wait_mid = load(own_mid, w_mid)
    push(own_out, "in1", "cls")
    wait_mid.wait()

    def third(i, carry):
        part = None
        for k in range(9):
            window = fpad[i + k // 3, pl.ds(k % 3, GRID)].reshape(GRID * frames, MID)
            term = matmul(window, w_mid[k])
            part = term if part is None else part + term
        h2v[pl.ds(GRID * i, GRID)] = part.reshape(GRID, frames, MID)
        one, two = masked_sums(part)
        return (carry[0] + one, carry[1] + two)

    one, two = lax.fori_loop(0, GRID, third, (zeros, zeros))
    send_out(h2v, h2_out)
    stat = sums[2][0]
    put_rows(stat, 0, jnp.sum(one, axis=0, keepdims=True), 4)
    put_rows(stat, 4, jnp.sum(two, axis=0, keepdims=True), 4)
    push(own_out)
    scale_two, shift_two = norm(1, links.all_sum(*sums[2]), MID, half, st2)
    wait_out = load(own_out, w_out)
    push("in1", "cls")
    wait_out.wait()
    wide_sum[...] = jnp.zeros_like(wide_sum)
    wide_square[...] = jnp.zeros_like(wide_square)

    def fourth(i, carry):
        for j in range(GRID):
            y = h2v[GRID * i + j] * scale_two + shift_two
            a2v[GRID * i + j] = (y * jax.nn.sigmoid(y)).astype(BF16)
        rows = a2v[pl.ds(GRID * i, GRID)].reshape(GRID * frames, MID)
        for k in range(4):
            part = matmul(rows, w_out[:, k * MID : (k + 1) * MID])
            h3v[pl.ds(GRID * i, GRID), :, k * MID : (k + 1) * MID] = part.astype(BF16).reshape(
                GRID, frames, MID
            )
            one, two = masked_sums(part)
            wide_sum[:, k * MID : (k + 1) * MID] += one
            wide_square[:, k * MID : (k + 1) * MID] += two
        return carry

    lax.fori_loop(0, GRID, fourth, 0)
    send_out(a2v, a2_out)
    send_out(h3v, h3_out)
    push("in1", "cls")
    stat = sums[3][0]
    put_rows(stat, 0, jnp.sum(wide_sum[...], axis=0, keepdims=True), 4)
    put_rows(stat, 4, jnp.sum(wide_square[...], axis=0, keepdims=True), 4)
    scale_three, shift_three = norm(2, links.all_sum(*sums[3]), D, 2 * half, st3)
    push("cls")
    if last:
        pooled[...] = jnp.zeros_like(pooled)
        norm_out[...] = jnp.zeros_like(norm_out)

    def fifth(p, carry):
        for k in range(4):
            span = slice(k * MID, (k + 1) * MID)
            pre = h3v[p, :, span].astype(F32) * scale_three[:, span] + shift_three[:, span]
            pre = pre + xv[p, :, span].astype(F32)
            value = pre * jax.nn.sigmoid(pre)
            if last:
                pooled[:, span] += value * mask[...]
            else:
                xv[p, :, span] = value.astype(BF16)
        return carry

    lax.fori_loop(0, HW, fifth, 0)
    send_out(pooled if last else xv, out_hbm)
    for name in jobs:
        gathers[name].finish()
    for copy in outgoing:
        copy.wait()


def forward_block(block, x, mask, following, norms, shards, given):
    n_seg = lax.axis_size("seg")
    n_clip = lax.axis_size("clip")
    cells, frames, width = x.shape
    jobs = list(shards)
    plan = list(given)
    any_spec = pl.BlockSpec(memory_space=pl.ANY)
    vmem = pl.BlockSpec(memory_space=pltpu.VMEM)
    depth = n_clip // 4

    def grid_shape(columns):
        return (cells, frames, columns)

    last = block == 1
    devices = n_seg * n_clip
    outs = [jax.ShapeDtypeStruct((devices * shards[n].shape[0], shards[n].shape[1]), BF16) for n in jobs]
    outs += [
        jax.ShapeDtypeStruct(grid_shape(MID), F32),
        jax.ShapeDtypeStruct(grid_shape(MID), BF16),
        jax.ShapeDtypeStruct(grid_shape(MID), BF16),
        jax.ShapeDtypeStruct(grid_shape(GATE), BF16),
        jax.ShapeDtypeStruct((GRID, GRID, frames, MID), BF16),
        jax.ShapeDtypeStruct(grid_shape(MID), F32),
        jax.ShapeDtypeStruct(grid_shape(MID), BF16),
        jax.ShapeDtypeStruct(grid_shape(D), BF16),
        jax.ShapeDtypeStruct((frames, D), F32) if last else jax.ShapeDtypeStruct(x.shape, BF16),
        jax.ShapeDtypeStruct(norms.shape, F32),
        jax.ShapeDtypeStruct((8, MID), F32),
        jax.ShapeDtypeStruct((8, MID), F32),
        jax.ShapeDtypeStruct((8, D), F32),
    ]
    out_specs = [any_spec] * (len(jobs) + 9) + [vmem] * 4

    shapes = [(D, MID), (9, MID, MID), (MID, D), (SMALL_SHARDS, 4 * 16, LANES)]
    scratch = [pltpu.VMEM(x.shape, BF16)]
    scratch += [pltpu.VMEM(s, BF16) for s in shapes]
    scratch += [
        pltpu.VMEM(grid_shape(MID), F32),
        pltpu.VMEM(grid_shape(MID), F32),
        pltpu.VMEM(grid_shape(MID), BF16),
        pltpu.VMEM(grid_shape(GATE), BF16),
        pltpu.VMEM((cells, 16, GATE), BF16),
        pltpu.VMEM((GRID + 2, GRID + 2, frames, GATE), F32),
        pltpu.VMEM(grid_shape(GATE), BF16),
        pltpu.VMEM(grid_shape(MID), BF16),
        pltpu.VMEM((GRID + 2, GRID + 2, frames, MID), BF16),
        pltpu.VMEM(grid_shape(MID), F32),
        pltpu.VMEM(grid_shape(MID), BF16),
        pltpu.VMEM(grid_shape(D), BF16),
        pltpu.VMEM((8, D), F32),
        pltpu.VMEM((8, D), F32),
        pltpu.VMEM((GATE, MID), BF16),
    ]
    for shape in (norms.shape, (8, LANES), (8, LANES), (8, MID)):
        scratch += sum_scratch(n_seg, n_clip, shape)
    if last:
        scratch.append(pltpu.VMEM((frames, D), F32))
    count = 4 * (n_seg * 4 + depth) + len(jobs) * (depth + 4) + 32
    scratch += [pltpu.SemaphoreType.DMA((count,)), pltpu.SemaphoreType.DMA((count,))]
    results = pl.pallas_call(
        functools.partial(forward_kernel, n_seg, n_clip, block, jobs, plan),
        out_shape=outs,
        in_specs=[any_spec, vmem, vmem, vmem] + [any_spec] * (len(jobs) + len(plan)),
        out_specs=out_specs,
        scratch_shapes=scratch,
        compiler_params=pltpu.CompilerParams(
            collective_id=30 + block, has_side_effects=True, vmem_limit_bytes=60 * 1024 * 1024
        ),
        name="forward_block",
    )(x, mask, following, norms, *[shards[n] for n in jobs], *[given[n] for n in plan])
    wholes = dict(zip(jobs, results[: len(jobs)]))
    return wholes, results[len(jobs) :]


def norm_backward(grad_out, normed, inv_std, live_rows, rows_mask, gain):
    part_gain = jnp.sum(grad_out * normed, axis=0)
    part_shift = jnp.sum(grad_out, axis=0)
    total_gain, total_shift = sum_pair(part_gain, part_shift)
    grad_in = gain * inv_std * (grad_out - rows_mask * (total_shift + normed * total_gain) / live_rows)
    return (grad_in, part_gain, part_shift)


def gate_backward(d_mixed, masks):
    present = masks[0].T[None, :, :, None]
    following = masks[1].T[None, :, :, None]
    slots = d_mixed.reshape(HW, masks[0].shape[1], masks[0].shape[0], GATE)
    edge = lax.ppermute(slots[:, -1], "seg", [(i, i + 1) for i in range(lax.axis_size("seg") - 1)])
    edge = edge.astype(F32)
    edge = edge + grid_mean(edge)
    wide = d_mixed.astype(F32)
    spread = (wide + grid_mean(wide)).reshape(slots.shape)
    earlier = jnp.concatenate([edge[:, None], spread[:, :-1]], axis=1)
    d_part = present * earlier - following * spread
    return d_part.astype(BF16).reshape(d_mixed.shape)


def block_backward(d_out, x_low, kept, weights, norms, masks, live_rows):
    w_in, w_mid, w_out, w_red, w_exp = weights
    gains, shifts = norms
    h_one, a_one_low, gate, mixed, gated, h_two, a_two_low, h_three, st_one, st_two, st_three = kept
    rows_mask = masks[2]
    frames = x_low.shape[1]
    x_low = x_low.reshape(-1, D)
    normed_three = (h_three.reshape(-1, D).astype(F32) - st_three[0]) * st_three[1]
    pre = normed_three * gains[2 * MID :] + shifts[2 * MID :] + x_low.astype(F32)
    normed_two = (h_two.reshape(-1, MID) - st_two[0]) * st_two[1]
    y_two = normed_two * gains[MID : 2 * MID] + shifts[MID : 2 * MID]
    normed_one = (h_one.reshape(-1, MID) - st_one[0]) * st_one[1]
    y_one = normed_one * gains[:MID] + shifts[:MID]
    a_one = jax.nn.silu(y_one)
    a_one_low = a_one_low.reshape(-1, MID)
    a_two_low = a_two_low.reshape(-1, MID)
    gate = gate.reshape(-1, MID).astype(F32)
    mixed_flat = mixed.reshape(-1, GATE)
    d_pre = d_out * silu_slope(pre)
    d_h_three, gain_three, shift_three = norm_backward(
        d_pre, normed_three, st_three[1], live_rows, rows_mask, gains[2 * MID :]
    )
    d_h_three_low = d_h_three.astype(BF16)
    g_out = matmul(a_two_low.T, d_h_three_low)
    d_a_two = matmul(d_h_three_low, w_out.T)
    d_y_two = d_a_two * silu_slope(y_two)
    d_h_two, gain_two, shift_two = norm_backward(
        d_y_two, normed_two, st_two[1], live_rows, rows_mask, gains[MID : 2 * MID]
    )
    d_h_two_low = d_h_two.astype(BF16).reshape(GRID, GRID, frames, MID)
    g_mid = conv(gated, d_h_two_low, ("HWCN", "HWIO", "HWNC")).reshape(9 * MID, MID)
    turned = jnp.flip(w_mid.reshape(3, 3, MID, MID), (0, 1))
    d_gated = conv(d_h_two_low, turned, ("HWNC", "HWOI", "HWNC")).reshape(-1, MID)
    d_excite = (d_gated * a_one * gate * (1.0 - gate)).astype(BF16)
    g_exp = matmul(mixed_flat.T, d_excite)
    d_mixed = matmul(d_excite, w_exp.T).astype(BF16).reshape(HW, frames, GATE)
    d_reduced_flat = gate_backward(d_mixed, masks).reshape(-1, GATE)
    g_red = matmul(a_one_low.T, d_reduced_flat)
    d_a_one = d_gated * (1.0 + gate) + matmul(d_reduced_flat, w_red.T)
    d_y_one = d_a_one * silu_slope(y_one)
    d_h_one, gain_one, shift_one = norm_backward(
        d_y_one, normed_one, st_one[1], live_rows, rows_mask, gains[:MID]
    )
    d_h_one_low = d_h_one.astype(BF16)
    g_in = matmul(x_low.T, d_h_one_low)
    d_x = d_pre + matmul(d_h_one_low, w_in.T)
    grads = [
        g_in,
        g_mid,
        g_out,
        g_red,
        g_exp,
        jnp.concatenate([gain_one, gain_two, gain_three]),
        jnp.concatenate([shift_one, shift_two, shift_three]),
    ]
    return (d_x, grads)


def on_device(inputs, clip_counts, labels, master, first_moment, second_moment):
    seg_count = lax.axis_size("seg")
    clip_local, slot_local = inputs.shape[:2]
    frames = clip_local * slot_local
    slot_ids = lax.axis_index("seg") * slot_local + jnp.arange(slot_local, dtype=jnp.int32)
    present = (slot_ids[None, :] < clip_counts[:, None]).astype(F32)
    following = (slot_ids[None, :] + 1 < clip_counts[:, None]).astype(F32)
    rows_mask = jnp.broadcast_to(present.T.reshape(1, frames), (HW, frames)).reshape(-1, 1)
    masks = (present, following, rows_mask)
    frame_mask = jnp.broadcast_to(present.T.reshape(frames, 1), (frames, MID))
    frame_following = jnp.broadcast_to(following.T.reshape(frames, 1), (frames, GATE))
    table = norm_table(master, HW * jnp.sum(present))
    x_low = inputs.transpose(2, 1, 0, 3).reshape(HW, frames, D)
    shards = weight_shards(master)
    if shards is None:
        weights = whole_weights(master)
        jobs = ((), ())
    else:
        weights = {}
        jobs = (("in0", "small", "mid0", "out0", "in1"), ("mid1", "out1", "cls"))
    kept = []
    flowing = x_low
    flows = []
    for block in range(2):
        flows.append(flowing)
        names = ("in%d" % block, "small", "mid%d" % block, "out%d" % block)
        given = {name: weights[name] for name in names if name not in jobs[block]}
        gathered, results = forward_block(
            block,
            flowing,
            frame_mask,
            frame_following,
            table,
            {name: shards[name] for name in jobs[block]},
            given,
        )
        weights.update(gathered)
        if block == 0:
            table = results[9]
        kept.append(results[:8] + results[10:])
        flowing = results[8]
    live_rows = table[98, 0]
    small = weights["small"].reshape(SMALL_SHARDS, 4, 16, LANES)
    block_weights = []
    for block in range(2):
        w_exp = small[:, 2 * block + 1].reshape(SMALL_SHARDS, MID // LANES, GATE // SMALL_SHARDS, LANES)
        block_weights.append(
            (
                weights["in%d" % block],
                weights["mid%d" % block],
                weights["out%d" % block],
                small[:, 2 * block].reshape(MID, GATE),
                jnp.swapaxes(w_exp, 1, 2).reshape(GATE, MID),
            )
        )
    tables = [table[BLOCK_NORMS * b : BLOCK_NORMS * (b + 1)].reshape(2, -1) for b in range(2)]
    w_cls = weights["cls"][:, :CLASSES]
    b_cls = table[96:98].reshape(-1)[:CLASSES]
    partial_value = jnp.sum(flowing.reshape(slot_local, clip_local, D), axis=0)
    pooled_sum = lax.psum(partial_value.astype(BF16), "seg").astype(F32)
    counts_float = clip_counts.astype(F32)
    pooled = pooled_sum / (HW * counts_float)[:, None]
    pooled_low = pooled.astype(BF16)
    logits = matmul(pooled_low, w_cls) + b_cls
    clips_total = clip_local * lax.axis_size("clip")
    onehot = (labels[:, None] == jnp.arange(CLASSES, dtype=jnp.int32)[None, :]).astype(F32)
    d_logits = (jax.nn.softmax(logits, axis=1) - onehot) / clips_total
    d_lin = d_logits.astype(BF16)
    g_cls = matmul(pooled_low.T, d_lin) / seg_count
    g_bias = jnp.sum(d_logits, axis=0) / seg_count
    d_pooled = matmul(d_lin, w_cls.T)
    scaled = d_pooled / (HW * counts_float)[:, None]
    d_frame = present.T[:, :, None] * scaled[None]
    d_flow = jnp.broadcast_to(d_frame.reshape(1, frames, D), (HW, frames, D)).reshape(-1, D)
    grads = [None, None]
    for block in (1, 0):
        d_flow, grads[block] = block_backward(
            d_flow, flows[block], kept[block], block_weights[block], tables[block], masks, live_rows
        )
    grad_mine = scatter_gradients(grads[0] + grads[1] + [g_cls, g_bias])
    tail = jnp.concatenate(
        [
            jnp.pad(g_bias, (0, 8 * LANES - CLASSES)).reshape(8, LANES),
            jnp.full((8, LANES), jnp.sum(grad_mine * grad_mine), F32),
        ]
    )
    tail = small_sum(tail)
    norm = jnp.sqrt(tail[8, 0])
    bias_grad = tail[:8].reshape(-1)[:CLASSES]
    factor = jnp.minimum(1.0, CLIP_LIMIT / (norm + 1e-06))
    clipped = grad_mine * factor
    new_first = BETA_ONE * first_moment + (1.0 - BETA_ONE) * clipped
    new_second = BETA_TWO * second_moment + (1.0 - BETA_TWO) * clipped * clipped
    first_hat = new_first / (1.0 - BETA_ONE**STEP)
    second_hat = new_second / (1.0 - BETA_TWO**STEP)
    new_master = master - LEARN_RATE * (
        first_hat / (jnp.sqrt(second_hat) + ADAM_EPS) + WEIGHT_DECAY * master
    )
    grid_grad = d_flow.reshape(HW, slot_local, clip_local, D).transpose(2, 1, 0, 3)
    return (
        new_master,
        new_first,
        new_second,
        new_master.astype(BF16),
        grid_grad.reshape(inputs.shape),
        norm.reshape(1),
        bias_grad,
    )


def solution(mesh):
    return jax.shard_map(
        on_device,
        mesh=mesh,
        in_specs=(
            P("clip", "seg", None, None),
            P("clip"),
            P("clip"),
            P(AXES),
            P(AXES),
            P(AXES),
        ),
        out_specs=(
            P(AXES),
            P(AXES),
            P(AXES),
            P(AXES),
            P("clip", "seg", None, None),
            P(),
            P(),
        ),
        check_vma=False,
    )
```

```python
import functools
import math

import jax
import jax.numpy as jnp
from jax import lax
from jax.experimental import pallas as pl
from jax.experimental.pallas import tpu as pltpu
from jax.sharding import PartitionSpec as P

D = 2048
MID = 512
GATE = 128
CLASSES = 174
GRID = 7
HW = 49
STEP = 7
LANES = 128

NORM_EPS = 1e-05
CLIP_LIMIT = 0.001
LEARN_RATE = 0.04
WEIGHT_DECAY = 0.05
BETA_ONE = 0.9
BETA_TWO = 0.999
ADAM_EPS = 1e-08

AXES = ("seg", "clip")
MESH_ID = pl.DeviceIdType.MESH
BF16 = jnp.bfloat16
F32 = jnp.float32


def matmul(left, right):
    return jnp.dot(left, right, preferred_element_type=F32)


def small_sum_kernel(n_seg, n_clip, inner, x_ref, o_ref, mid, near, far, send_sem, recv_sem):
    seg = lax.axis_index("seg")
    clip = lax.axis_index("clip")
    outer = n_clip // inner
    group = clip // inner
    place = lax.rem(clip, inner)
    n_near = n_seg * inner - 1
    n_far = outer - 1

    def near_peer(i):
        return (
            lax.rem(seg + i // inner, n_seg),
            group * inner + lax.rem(place + lax.rem(i, inner), inner),
        )

    def far_peer(i):
        return (seg, lax.rem(group + i, outer) * inner + place)

    def copy_near(i):
        return pltpu.make_async_remote_copy(
            src_ref=x_ref,
            dst_ref=near.at[i - 1],
            send_sem=send_sem.at[i - 1],
            recv_sem=recv_sem.at[i - 1],
            device_id=near_peer(i),
            device_id_type=MESH_ID,
        )

    def copy_far(i):
        return pltpu.make_async_remote_copy(
            src_ref=mid,
            dst_ref=far.at[i - 1],
            send_sem=send_sem.at[n_near + i - 1],
            recv_sem=recv_sem.at[n_near + i - 1],
            device_id=far_peer(i),
            device_id_type=MESH_ID,
        )

    def repeat(first, last, action):
        if last - first <= 8:
            for i in range(first, last):
                action(i)
        else:

            def body(i, carry):
                action(i)
                return carry

            lax.fori_loop(first, last, body, 0)

    barrier = pltpu.get_barrier_semaphore()

    def greet(peer):
        pl.semaphore_signal(barrier, inc=1, device_id=peer, device_id_type=MESH_ID)

    repeat(1, n_near + 1, lambda i: greet(near_peer(i)))
    repeat(1, n_far + 1, lambda i: greet(far_peer(i)))
    pl.semaphore_wait(barrier, n_near + n_far)
    repeat(1, n_near + 1, lambda i: copy_near(i).start())
    repeat(1, n_near + 1, lambda i: copy_near(i).wait())
    mid[...] = x_ref[...] + jnp.sum(near[...], axis=0)
    repeat(1, n_far + 1, lambda i: copy_far(i).start())
    repeat(1, n_far + 1, lambda i: copy_far(i).wait())
    o_ref[...] = mid[...] + jnp.sum(far[...], axis=0)


def small_sum(values):
    n_seg = lax.axis_size("seg")
    n_clip = lax.axis_size("clip")
    inner = 4 if n_clip % 4 == 0 else 1
    n_near = n_seg * inner - 1
    n_far = n_clip // inner - 1
    rows = values.shape[0]
    return pl.pallas_call(
        functools.partial(small_sum_kernel, n_seg, n_clip, inner),
        out_shape=jax.ShapeDtypeStruct(values.shape, F32),
        in_specs=[pl.BlockSpec(memory_space=pltpu.VMEM)],
        out_specs=pl.BlockSpec(memory_space=pltpu.VMEM),
        scratch_shapes=[
            pltpu.VMEM(values.shape, F32),
            pltpu.VMEM((n_near,) + values.shape, F32),
            pltpu.VMEM((n_far,) + values.shape, F32),
            pltpu.SemaphoreType.DMA((n_near + n_far,)),
            pltpu.SemaphoreType.DMA((n_near + n_far,)),
        ],
        compiler_params=pltpu.CompilerParams(collective_id=rows // 8, has_side_effects=True),
        name="small_sum",
    )(values)


def scatter_kernel(n_clip, n_jobs, *refs):
    grads = refs[:n_jobs]
    outs = refs[n_jobs : 2 * n_jobs]
    ones = refs[2 * n_jobs : 3 * n_jobs]
    twos = refs[3 * n_jobs : 4 * n_jobs]
    threes = refs[4 * n_jobs : 5 * n_jobs]
    fours = refs[5 * n_jobs : 6 * n_jobs]
    send_sem, recv_sem = refs[6 * n_jobs :]
    seg = lax.axis_index("seg")
    clip = lax.axis_index("clip")
    depth = n_clip // 4
    z = clip // 4
    y = lax.rem(clip // 2, 2)
    x = lax.rem(clip, 2)
    first = (1 - seg) * y + seg * x
    second = (1 - seg) * x + seg * y
    step = 1 + seg
    jump = 2 - seg
    across_first = (seg, clip + jump * (1 - 2 * first))
    across_second = (seg, clip + step * (1 - 2 * second))
    other = (1 - seg, clip)
    per_job = 1 + 2 + 1 + (depth - 1)

    def along(i):
        return (seg, lax.rem(z + i, depth) * 4 + y * 2 + x)

    barrier = pltpu.get_barrier_semaphore()
    for peer in [other, across_first, across_second] + [along(i) for i in range(1, depth)]:
        pl.semaphore_signal(barrier, inc=1, device_id=peer, device_id_type=MESH_ID)
    pl.semaphore_wait(barrier, depth + 2)

    def remote(job, number, source, target, peer):
        index = job * per_job + number
        return pltpu.make_async_remote_copy(
            src_ref=source,
            dst_ref=target,
            send_sem=send_sem.at[index],
            recv_sem=recv_sem.at[index],
            device_id=peer,
            device_id_type=MESH_ID,
        )

    def core_copy(job):
        return remote(job, 0, grads[job].at[1 - seg], ones[job], other)

    def first_copy(job, k):
        source = ones[job].at[:, jump * (1 - first) + step * k]
        return remote(job, 1 + k, source, twos[job].at[:, k], across_first)

    def second_copy(job):
        return remote(job, 3, twos[job].at[:, 1 - second], threes[job], across_second)

    def line_copy(job, i):
        source = threes[job].at[lax.rem(z + i, depth)]
        return remote(job, 3 + i, source, fours[job].at[i - 1], along(i))

    for job in range(n_jobs):
        core_copy(job).start()
    for job in range(n_jobs):
        core_copy(job).wait()
        one = ones[job]

        def add_one(i, carry, job=job, one=one):
            zz = i // 4
            w = lax.rem(i, 4)
            total = one[zz, w].astype(F32) + grads[job][seg, zz, w].astype(F32)
            one[zz, w] = total.astype(BF16)
            return carry

        lax.fori_loop(0, 4 * depth, add_one, 0)
        for k in range(2):
            first_copy(job, k).start()
    for job in range(n_jobs):
        for k in range(2):
            first_copy(job, k).wait()
        one, two = ones[job], twos[job]

        def add_two(i, carry, one=one, two=two):
            zz = i // 2
            k = lax.rem(i, 2)
            total = two[zz, k].astype(F32) + one[zz, jump * first + step * k].astype(F32)
            two[zz, k] = total.astype(BF16)
            return carry

        lax.fori_loop(0, 2 * depth, add_two, 0)
        second_copy(job).start()
    for job in range(n_jobs):
        second_copy(job).wait()
        two, three = twos[job], threes[job]

        def add_three(zz, carry, two=two, three=three):
            three[zz] = (three[zz].astype(F32) + two[zz, second].astype(F32)).astype(BF16)
            return carry

        lax.fori_loop(0, depth, add_three, 0)
        for i in range(1, depth):
            line_copy(job, i).start()
    for job in range(n_jobs):
        for i in range(1, depth):
            line_copy(job, i).wait()
        total = threes[job][z].astype(F32)
        for i in range(1, depth):
            total = total + fours[job][i - 1].astype(F32)
        outs[job][...] = total


def reduce_scatter(grads):
    n_seg = lax.axis_size("seg")
    n_clip = lax.axis_size("clip")
    fits = n_seg == 2 and n_clip == 16 and all(g.shape[1] % 16 == 0 for g in grads)
    if not fits:
        return [lax.psum_scatter(g, AXES, scatter_dimension=0, tiled=True)[0].astype(F32) for g in grads]
    depth = n_clip // 4
    n_jobs = len(grads)
    sizes = [g.shape[1:] for g in grads]
    shaped = [g.reshape((n_seg, depth, 4) + s) for g, s in zip(grads, sizes)]
    vmem = pl.BlockSpec(memory_space=pltpu.VMEM)
    copies = n_jobs * (depth + 3)
    return pl.pallas_call(
        functools.partial(scatter_kernel, n_clip, n_jobs),
        out_shape=[jax.ShapeDtypeStruct(s, F32) for s in sizes],
        in_specs=[vmem] * n_jobs,
        out_specs=[vmem] * n_jobs,
        scratch_shapes=[pltpu.VMEM((depth, 4) + s, BF16) for s in sizes]
        + [pltpu.VMEM((depth, 2) + s, BF16) for s in sizes]
        + [pltpu.VMEM((depth,) + s, BF16) for s in sizes]
        + [pltpu.VMEM((depth - 1,) + s, BF16) for s in sizes]
        + [pltpu.SemaphoreType.DMA((copies,)), pltpu.SemaphoreType.DMA((copies,))],
        compiler_params=pltpu.CompilerParams(
            collective_id=20, has_side_effects=True, vmem_limit_bytes=60 * 1024 * 1024
        ),
        name="reduce_scatter",
    )(*shaped)


def layout():
    block_layout = [
        (D, MID),
        (9, MID, MID),
        (MID, D),
        (MID, GATE),
        (GATE, MID),
        (2 * MID + D,),
        (2 * MID + D,),
    ]
    return block_layout + block_layout + [(D, CLASSES), (CLASSES,)]


def widths(devices):
    return [(math.prod(extent) + devices - 1) // devices for extent in layout()]


def pad_rows(flat, rows):
    return jnp.pad(flat, (0, rows * LANES - flat.shape[0])).reshape(rows, LANES)


def small_rows(devices):
    wide = widths(devices)
    amount = sum(wide[3:7]) + sum(wide[10:14])
    amount_cls = wide[14] + wide[15]
    return [16 * ((a + 16 * LANES - 1) // (16 * LANES)) for a in (amount, amount_cls)]


def gather_parameters(master):
    devices = lax.axis_size("seg") * lax.axis_size("clip")
    wide = widths(devices)
    starts = [sum(wide[:i]) for i in range(len(wide))]
    low = master.astype(BF16)

    def part(i):
        return low[starts[i] : starts[i] + wide[i]]

    def gather(values):
        return lax.all_gather(values, AXES, axis=0, tiled=True)

    big = {}
    for base in (0, 7):
        for i, columns in ((0, MID), (1, MID), (2, D)):
            big[base + i] = gather(part(base + i).reshape(-1, columns))
    rows, rows_cls = small_rows(devices)
    small = gather(pad_rows(jnp.concatenate([part(i) for i in (3, 4, 5, 6, 10, 11, 12, 13)]), rows))
    small_cls = gather(pad_rows(jnp.concatenate([part(14), part(15)]), rows_cls))
    small = small.reshape(devices, rows * LANES)
    small_cls = small_cls.reshape(devices, rows_cls * LANES)
    shapes = layout()
    pieces = dict(big)

    def take(source, ids):
        offset = 0
        for i in ids:
            amount = math.prod(shapes[i])
            pieces[i] = source[:, offset : offset + wide[i]].reshape(-1)[:amount].reshape(shapes[i])
            offset += wide[i]

    take(small, (3, 4, 5, 6, 10, 11, 12, 13))
    take(small_cls, (14, 15))
    return [pieces[i] for i in range(16)]


def scatter_gradients(grads):
    devices = lax.axis_size("seg") * lax.axis_size("clip")
    wide = widths(devices)
    rows, rows_cls = small_rows(devices)

    def shards(i):
        flat = grads[i].reshape(-1)
        return jnp.pad(flat, (0, devices * wide[i] - flat.shape[0])).reshape(devices, wide[i])

    def pack(ids, n_rows):
        packed = jnp.concatenate([shards(i) for i in ids], axis=1).astype(BF16)
        return jnp.pad(packed, ((0, 0), (0, n_rows * LANES - packed.shape[1]))).reshape(devices, n_rows, LANES)

    smalls = (3, 4, 5, 6, 10, 11, 12, 13)
    jobs = []
    for base in (7, 0):
        for i in (2, 1, 0):
            columns = grads[base + i].shape[-1]
            jobs.append(grads[base + i].astype(BF16).reshape(devices, -1, columns))
    jobs.append(pack(smalls, rows))
    jobs.append(pack((14, 15), rows_cls))
    sums = reduce_scatter(jobs)
    mine = {}
    for k, i in enumerate((9, 8, 7, 2, 1, 0)):
        mine[i] = sums[k].reshape(-1)
    for ids, flat in ((smalls, sums[6].reshape(-1)), ((14, 15), sums[7].reshape(-1))):
        offset = 0
        for i in ids:
            mine[i] = flat[offset : offset + wide[i]]
            offset += wide[i]
    return jnp.concatenate([mine[i] for i in range(16)])


def part_of(master, index):
    devices = lax.axis_size("seg") * lax.axis_size("clip")
    wide = widths(devices)
    start = sum(wide[:index])
    return master[start : start + wide[index]]


def norm_table(master, live_part):
    devices = lax.axis_size("seg") * lax.axis_size("clip")
    me = lax.axis_index(AXES)
    width = 2 * MID + D

    def spread(indices, amount):
        parts = jnp.stack([part_of(master, i) for i in indices]).astype(BF16).astype(F32)
        table = jnp.zeros((len(indices), devices, parts.shape[1]), F32)
        table = lax.dynamic_update_slice(table, parts[:, None, :], (0, me, 0))
        return table.reshape(len(indices), -1)[:, :amount]

    norms = spread((5, 6, 12, 13), width).reshape(-1, LANES)
    bias = spread((15,), CLASSES)
    bias = jnp.pad(bias.reshape(-1), (0, 2 * LANES - CLASSES)).reshape(2, LANES)
    live = jnp.full((NORM_ROWS - norms.shape[0] - 2, LANES), live_part, F32)
    return jnp.concatenate([norms, bias, live])


def lanes_first(values):
    lead = values.shape[:-2]
    rows, columns = values.shape[-2:]
    split = values.reshape(lead + (rows, columns // LANES, LANES))
    return jnp.swapaxes(split, -3, -2).reshape(lead + (-1, LANES))


def weight_shards(master):
    devices = lax.axis_size("seg") * lax.axis_size("clip")
    if lax.axis_size("seg") != 2 or devices != SMALL_SHARDS:
        return None
    low = master.astype(BF16)
    shards = {}
    small = []
    for block in range(2):
        base = 7 * block
        shards["in%d" % block] = part_of(low, base).reshape(-1, MID)
        shards["mid%d" % block] = part_of(low, base + 1).reshape(-1, MID)
        shards["out%d" % block] = part_of(low, base + 2).reshape(-1, D)
        small.append(part_of(low, base + 3).reshape(-1, GATE))
        small.append(lanes_first(part_of(low, base + 4).reshape(-1, MID)))
    shards["small"] = jnp.concatenate(small)
    cls = part_of(low, 14).reshape(-1, CLASSES)
    shards["cls"] = jnp.pad(cls, ((0, 0), (0, 2 * LANES - CLASSES)))
    return shards


def whole_weights(master):
    pieces = gather_parameters(master)
    whole = {}
    small = []
    for block in range(2):
        w_in, w_mid, w_out, w_red, w_exp = pieces[7 * block : 7 * block + 5]
        whole["in%d" % block] = w_in
        whole["mid%d" % block] = w_mid.reshape(9 * MID, MID)
        whole["out%d" % block] = w_out
        small.append(w_red.reshape(SMALL_SHARDS, -1, GATE))
        small.append(lanes_first(w_exp.reshape(SMALL_SHARDS, -1, MID)))
    whole["small"] = jnp.concatenate(small, axis=1).reshape(-1, LANES)
    whole["cls"] = jnp.pad(pieces[14], ((0, 0), (0, 2 * LANES - CLASSES)))
    return whole


def conv(values, kernel, numbers):
    return lax.conv_general_dilated(
        values, kernel, (1, 1), ((1, 1), (1, 1)), dimension_numbers=numbers, preferred_element_type=F32
    )


class Links:
    def __init__(self, n_seg, n_clip, send_sem, recv_sem):
        self.n_seg = n_seg
        self.n_clip = n_clip
        self.inner = 4
        self.outer = n_clip // 4
        self.seg = lax.axis_index("seg")
        self.clip = lax.axis_index("clip")
        self.group = self.clip // 4
        self.place = lax.rem(self.clip, 4)
        y = self.place // 2
        x = lax.rem(self.place, 2)
        self.first = (1 - self.seg) * y + self.seg * x
        self.second = (1 - self.seg) * x + self.seg * y
        self.step = 1 + self.seg
        self.jump = 2 - self.seg
        self.across_first = (self.seg, self.clip + self.jump * (1 - 2 * self.first))
        self.across_second = (self.seg, self.clip + self.step * (1 - 2 * self.second))
        self.other = (1 - self.seg, self.clip)
        self.send_sem = send_sem
        self.recv_sem = recv_sem
        self.used = 0

    def take(self, count):
        base = self.used
        self.used += count
        return base

    def near_peer(self, i):
        return (
            lax.rem(self.seg + i // 4, self.n_seg),
            self.group * 4 + lax.rem(self.place + lax.rem(i, 4), 4),
        )

    def far_peer(self, i):
        return (self.seg, lax.rem(self.group + i, self.outer) * 4 + self.place)

    def remote(self, index, source, target, peer):
        return pltpu.make_async_remote_copy(
            src_ref=source,
            dst_ref=target,
            send_sem=self.send_sem.at[index],
            recv_sem=self.recv_sem.at[index],
            device_id=peer,
            device_id_type=MESH_ID,
        )

    def local(self, source, target):
        return pltpu.make_async_copy(source, target, self.recv_sem.at[self.take(1)])

    def meet(self):
        barrier = pltpu.get_barrier_semaphore()
        n_near = self.n_seg * 4 - 1
        n_far = self.outer - 1

        def greet(peer):
            pl.semaphore_signal(barrier, inc=1, device_id=peer, device_id_type=MESH_ID)

        repeat(1, n_near + 1, lambda i: greet(self.near_peer(i)))
        repeat(1, n_far + 1, lambda i: greet(self.far_peer(i)))
        pl.semaphore_wait(barrier, n_near + n_far)

    def all_sum(self, source, middle, near, far):
        n_near = self.n_seg * 4 - 1
        n_far = self.outer - 1
        base = self.take(n_near + n_far)

        def close(i):
            return self.remote(base + i - 1, source, near.at[i - 1], self.near_peer(i))

        def distant(i):
            return self.remote(base + n_near + i - 1, middle, far.at[i - 1], self.far_peer(i))

        repeat(1, n_near + 1, lambda i: close(i).start())
        repeat(1, n_near + 1, lambda i: close(i).wait())
        middle[...] = source[...] + jnp.sum(near[...], axis=0)
        repeat(1, n_far + 1, lambda i: distant(i).start())
        repeat(1, n_far + 1, lambda i: distant(i).wait())
        return middle[...] + jnp.sum(far[...], axis=0)


def repeat(first, last, action):
    if last - first <= 8:
        for i in range(first, last):
            action(i)
    else:

        def body(i, carry):
            action(i)
            return carry

        lax.fori_loop(first, last, body, 0)


def sum_scratch(n_seg, n_clip, shape):
    return [
        pltpu.VMEM(shape, F32),
        pltpu.VMEM(shape, F32),
        pltpu.VMEM((n_seg * 4 - 1,) + shape, F32),
        pltpu.VMEM((n_clip // 4 - 1,) + shape, F32),
    ]


class Gather:
    def __init__(self, links, shard, whole):
        depth = links.outer
        whole = whole.reshape((links.n_seg, depth, 4) + shard.shape)
        base = links.take(depth + 3)
        seg, z, place = links.seg, links.group, links.place
        self.own = links.local(shard, whole.at[seg, z, place])
        self.steps = [
            [
                links.remote(base + i - 1, shard, whole.at[seg, z, place], links.far_peer(i))
                for i in range(1, depth)
            ],
            [
                links.remote(
                    base + depth - 1, whole.at[seg, :, place], whole.at[seg, :, place], links.across_second
                )
            ],
            [],
            [links.remote(base + depth + 2, whole.at[seg], whole.at[seg], links.other)],
        ]
        for k in range(2):
            index = links.jump * links.first + links.step * k
            self.steps[2].append(
                links.remote(
                    base + depth + k, whole.at[seg, :, index], whole.at[seg, :, index], links.across_first
                )
            )
        self.at = -1

    def advance(self, last=3):
        if self.at >= 0:
            for copy in self.steps[self.at]:
                copy.wait()
            if self.at == 0:
                self.own.wait()
        self.at += 1
        if self.at == 0:
            self.own.start()
        if self.at <= 3:
            for copy in self.steps[self.at]:
                copy.start()

    def finish(self):
        while self.at <= 3:
            self.advance()


def row_vector(table, start, count):
    return jnp.concatenate([table[start + k : start + k + 1, :] for k in range(count)], axis=1)


def put_rows(target, start, vector, count):
    width = vector.shape[1] // count
    for k in range(count):
        target[start + k : start + k + 1, :] = vector[:, k * width : (k + 1) * width]


def fold(values):
    return jnp.sum(values.reshape(-1, 8, values.shape[-1]), axis=0)


def excite_weights(small, block):
    shards = small.shape[0]
    rows = small[:, 32 * block + 16 : 32 * block + 32].reshape(shards * 16, LANES)
    deep = GATE // shards
    line = lax.broadcasted_iota(jnp.int32, (GATE, shards * 16), 0)
    column = lax.broadcasted_iota(jnp.int32, (GATE, shards * 16), 1)
    parts = []
    for k in range(MID // LANES):
        wanted = (line // deep) * 16 + k * deep + lax.rem(line, deep)
        pick = (column == wanted).astype(F32).astype(BF16)
        parts.append(matmul(pick, rows))
    return jnp.concatenate(parts, axis=1).astype(BF16)


SMALL_SHARDS = 32
NORM_ROWS = 104
BLOCK_NORMS = 48


def forward_kernel(n_seg, n_clip, block, jobs, plan, *refs):
    refs = list(refs)

    def pop(count=1):
        taken = refs[:count]
        del refs[:count]
        return taken if count != 1 else taken[0]

    last = block == 1
    x_hbm, mask, following, norm_in = pop(4)
    shards = dict(zip(jobs, [pop() for _ in jobs]))
    given = dict(zip(plan, [pop() for _ in plan]))
    wholes = dict(zip(jobs, [pop() for _ in jobs]))
    h1_out, low_out, gate_out, mix_out, f_out, h2_out, a2_out, h3_out = pop(8)
    out_hbm, norm_out, st1, st2, st3 = pop(5)
    xv, w_in, w_mid, w_out, small = pop(5)
    h1v, a1v, lowv, rv, edge, dpad, mixv, gatev, fpad, h2v, a2v, h3v = pop(12)
    wide_sum, wide_square, w_exp = pop(3)
    sums = [pop(4) for _ in range(4)]
    pooled = pop() if last else None
    send_sem, recv_sem = pop(2)
    links = Links(n_seg, n_clip, send_sem, recv_sem)
    frames = xv.shape[1]
    live = norm_out if not last else norm_in
    outgoing = []

    def send_out(source, target):
        copy = links.local(source, target)
        copy.start()
        outgoing.append(copy)

    links.meet()
    load_x = links.local(x_hbm, xv)
    load_x.start()
    gathers = {name: Gather(links, shards[name], wholes[name]) for name in jobs}

    def load(name, target):
        if name in gathers:
            gathers[name].finish()
            source = wholes[name]
        else:
            source = given[name]
        copy = links.local(source.reshape(target.shape), target)
        copy.start()
        return copy

    def push(*names):
        for name in names:
            if name in gathers and gathers[name].at <= 3:
                gathers[name].advance()

    own_in = "in%d" % block
    own_mid = "mid%d" % block
    own_out = "out%d" % block
    if not last:
        push(own_in, "small")
        sums[0][0][...] = norm_in[...]
        norm_out[...] = links.all_sum(*sums[0])
        push(own_in, "small", own_mid)
        dpad[...] = jnp.zeros_like(dpad)
        fpad[...] = jnp.zeros_like(fpad)
        push(own_in, "small")
        push(own_in, "small", own_mid, own_out)
    else:
        push(own_mid)
        dpad[...] = jnp.zeros_like(dpad)
        fpad[...] = jnp.zeros_like(fpad)
    wait_in = load(own_in, w_in)
    wait_small = load("small", small)
    wait_in.wait()
    load_x.wait()
    norms = live
    base = BLOCK_NORMS * block
    live_rows = norms[98:99, 0:1]
    half = MID // LANES

    def norm(index, tot, columns, start, out):
        mean = jnp.concatenate([tot[k : k + 1] for k in range(4)], axis=1) / live_rows
        square = jnp.concatenate([tot[4 + k : 5 + k] for k in range(4)], axis=1) / live_rows
        inv = lax.rsqrt(square - mean * mean + NORM_EPS)
        out[0:1, :] = mean
        out[1:2, :] = inv
        gain = row_vector(norms, base + start, columns // LANES)
        shift = row_vector(norms, base + 24 + start, columns // LANES)
        scale = gain * inv
        return scale, shift - mean * scale

    def masked_sums(values):
        shaped = values.reshape(-1, frames, values.shape[-1])
        masked = shaped * mask[...][None]
        return fold(masked), fold(masked * shaped)

    zeros = jnp.zeros((8, MID), F32)

    def first(i, carry):
        part = matmul(xv[pl.ds(GRID * i, GRID)].reshape(GRID * frames, D), w_in[...])
        h1v[pl.ds(GRID * i, GRID)] = part.reshape(GRID, frames, MID)
        one, two = masked_sums(part)
        return (carry[0] + one, carry[1] + two)

    one, two = lax.fori_loop(0, GRID, first, (zeros, zeros))
    send_out(h1v, h1_out)
    push(own_mid, own_out)
    if not last:
        push("in1")
    stat = sums[1][0]
    put_rows(stat, 0, jnp.sum(one, axis=0, keepdims=True), 4)
    put_rows(stat, 4, jnp.sum(two, axis=0, keepdims=True), 4)
    scale_one, shift_one = norm(0, links.all_sum(*sums[1]), MID, 0, st1)
    push(own_mid)
    wait_small.wait()
    w_exp[...] = excite_weights(small, block)
    red = small[:, 32 * block : 32 * block + 16].reshape(MID, GATE)

    def second(i, carry):
        for j in range(GRID):
            y = h1v[GRID * i + j] * scale_one + shift_one
            a = y * jax.nn.sigmoid(y)
            a1v[GRID * i + j] = a
            lowv[GRID * i + j] = a.astype(BF16)
        part = matmul(lowv[pl.ds(GRID * i, GRID)].reshape(GRID * frames, MID), red)
        rv[pl.ds(GRID * i, GRID)] = part.astype(BF16).reshape(GRID, frames, GATE)
        return carry

    lax.fori_loop(0, GRID, second, 0)
    send_out(lowv, low_out)
    swap = links.remote(links.take(1), rv, edge, links.other)
    swap.start()
    if last:
        push(own_mid)
    push(own_out)
    swap.wait()
    row = lax.rem(lax.broadcasted_iota(jnp.int32, (frames, GATE), 0), 8)

    def change(i, carry):
        for j in range(GRID):
            now = rv[GRID * i + j].astype(F32)
            rest = edge[GRID * i + j].astype(F32)
            later = jnp.where(row < 7, pltpu.roll(now, frames - 1, 0), pltpu.roll(rest, 7, 0))
            dpad[i + 1, j + 1] = following[...] * (later - now)
        return carry

    lax.fori_loop(0, GRID, change, 0)

    def excite(i, carry):
        for j in range(GRID):
            total = jnp.zeros((frames, GATE), F32)
            for k in range(9):
                total = total + dpad[i + k // 3, j + k % 3]
            mixv[GRID * i + j] = (dpad[i + 1, j + 1] + total / 9.0).astype(BF16)
        e = matmul(mixv[pl.ds(GRID * i, GRID)].reshape(GRID * frames, GATE), w_exp[...])
        e = e.reshape(GRID, frames, MID)
        for j in range(GRID):
            gate = jax.nn.sigmoid(e[j])
            gatev[GRID * i + j] = gate.astype(BF16)
            fpad[i + 1, j + 1] = (a1v[GRID * i + j] * (1.0 + gate)).astype(BF16)
        return carry

    lax.fori_loop(0, GRID, excite, 0)
    send_out(mixv, mix_out)
    send_out(gatev, gate_out)
    send_out(fpad.at[pl.ds(1, GRID), pl.ds(1, GRID)], f_out)
    wait_mid = load(own_mid, w_mid)
    push(own_out, "in1", "cls")
    wait_mid.wait()

    def third(i, carry):
        part = None
        for k in range(9):
            window = fpad[i + k // 3, pl.ds(k % 3, GRID)].reshape(GRID * frames, MID)
            term = matmul(window, w_mid[k])
            part = term if part is None else part + term
        h2v[pl.ds(GRID * i, GRID)] = part.reshape(GRID, frames, MID)
        one, two = masked_sums(part)
        return (carry[0] + one, carry[1] + two)

    one, two = lax.fori_loop(0, GRID, third, (zeros, zeros))
    send_out(h2v, h2_out)
    stat = sums[2][0]
    put_rows(stat, 0, jnp.sum(one, axis=0, keepdims=True), 4)
    put_rows(stat, 4, jnp.sum(two, axis=0, keepdims=True), 4)
    push(own_out)
    scale_two, shift_two = norm(1, links.all_sum(*sums[2]), MID, half, st2)
    wait_out = load(own_out, w_out)
    push("in1", "cls")
    wait_out.wait()
    wide_sum[...] = jnp.zeros_like(wide_sum)
    wide_square[...] = jnp.zeros_like(wide_square)

    def fourth(i, carry):
        for j in range(GRID):
            y = h2v[GRID * i + j] * scale_two + shift_two
            a2v[GRID * i + j] = (y * jax.nn.sigmoid(y)).astype(BF16)
        rows = a2v[pl.ds(GRID * i, GRID)].reshape(GRID * frames, MID)
        for k in range(4):
            part = matmul(rows, w_out[:, k * MID : (k + 1) * MID])
            h3v[pl.ds(GRID * i, GRID), :, k * MID : (k + 1) * MID] = part.astype(BF16).reshape(
                GRID, frames, MID
            )
            one, two = masked_sums(part)
            wide_sum[:, k * MID : (k + 1) * MID] += one
            wide_square[:, k * MID : (k + 1) * MID] += two
        return carry

    lax.fori_loop(0, GRID, fourth, 0)
    send_out(a2v, a2_out)
    send_out(h3v, h3_out)
    push("in1", "cls")
    stat = sums[3][0]
    put_rows(stat, 0, jnp.sum(wide_sum[...], axis=0, keepdims=True), 4)
    put_rows(stat, 4, jnp.sum(wide_square[...], axis=0, keepdims=True), 4)
    scale_three, shift_three = norm(2, links.all_sum(*sums[3]), D, 2 * half, st3)
    push("cls")
    if last:
        pooled[...] = jnp.zeros_like(pooled)
        norm_out[...] = jnp.zeros_like(norm_out)

    def fifth(p, carry):
        for k in range(4):
            span = slice(k * MID, (k + 1) * MID)
            pre = h3v[p, :, span].astype(F32) * scale_three[:, span] + shift_three[:, span]
            pre = pre + xv[p, :, span].astype(F32)
            value = pre * jax.nn.sigmoid(pre)
            if last:
                pooled[:, span] += value * mask[...]
            else:
                xv[p, :, span] = value.astype(BF16)
        return carry

    lax.fori_loop(0, HW, fifth, 0)
    send_out(pooled if last else xv, out_hbm)
    for name in jobs:
        gathers[name].finish()
    for copy in outgoing:
        copy.wait()


def forward_block(block, x, mask, following, norms, shards, given):
    n_seg = lax.axis_size("seg")
    n_clip = lax.axis_size("clip")
    cells, frames, width = x.shape
    jobs = list(shards)
    plan = list(given)
    any_spec = pl.BlockSpec(memory_space=pl.ANY)
    vmem = pl.BlockSpec(memory_space=pltpu.VMEM)
    depth = n_clip // 4

    def grid_shape(columns):
        return (cells, frames, columns)

    last = block == 1
    devices = n_seg * n_clip
    outs = [jax.ShapeDtypeStruct((devices * shards[n].shape[0], shards[n].shape[1]), BF16) for n in jobs]
    outs += [
        jax.ShapeDtypeStruct(grid_shape(MID), F32),
        jax.ShapeDtypeStruct(grid_shape(MID), BF16),
        jax.ShapeDtypeStruct(grid_shape(MID), BF16),
        jax.ShapeDtypeStruct(grid_shape(GATE), BF16),
        jax.ShapeDtypeStruct((GRID, GRID, frames, MID), BF16),
        jax.ShapeDtypeStruct(grid_shape(MID), F32),
        jax.ShapeDtypeStruct(grid_shape(MID), BF16),
        jax.ShapeDtypeStruct(grid_shape(D), BF16),
        jax.ShapeDtypeStruct((frames, D), F32) if last else jax.ShapeDtypeStruct(x.shape, BF16),
        jax.ShapeDtypeStruct(norms.shape, F32),
        jax.ShapeDtypeStruct((8, MID), F32),
        jax.ShapeDtypeStruct((8, MID), F32),
        jax.ShapeDtypeStruct((8, D), F32),
    ]
    out_specs = [any_spec] * (len(jobs) + 9) + [vmem] * 4

    shapes = [(D, MID), (9, MID, MID), (MID, D), (SMALL_SHARDS, 4 * 16, LANES)]
    scratch = [pltpu.VMEM(x.shape, BF16)]
    scratch += [pltpu.VMEM(s, BF16) for s in shapes]
    scratch += [
        pltpu.VMEM(grid_shape(MID), F32),
        pltpu.VMEM(grid_shape(MID), F32),
        pltpu.VMEM(grid_shape(MID), BF16),
        pltpu.VMEM(grid_shape(GATE), BF16),
        pltpu.VMEM(grid_shape(GATE), BF16),
        pltpu.VMEM((GRID + 2, GRID + 2, frames, GATE), F32),
        pltpu.VMEM(grid_shape(GATE), BF16),
        pltpu.VMEM(grid_shape(MID), BF16),
        pltpu.VMEM((GRID + 2, GRID + 2, frames, MID), BF16),
        pltpu.VMEM(grid_shape(MID), F32),
        pltpu.VMEM(grid_shape(MID), BF16),
        pltpu.VMEM(grid_shape(D), BF16),
        pltpu.VMEM((8, D), F32),
        pltpu.VMEM((8, D), F32),
        pltpu.VMEM((GATE, MID), BF16),
    ]
    for shape in (norms.shape, (8, LANES), (8, LANES), (8, MID)):
        scratch += sum_scratch(n_seg, n_clip, shape)
    if last:
        scratch.append(pltpu.VMEM((frames, D), F32))
    count = 4 * (n_seg * 4 + depth) + len(jobs) * (depth + 4) + 32
    scratch += [pltpu.SemaphoreType.DMA((count,)), pltpu.SemaphoreType.DMA((count,))]
    results = pl.pallas_call(
        functools.partial(forward_kernel, n_seg, n_clip, block, jobs, plan),
        out_shape=outs,
        in_specs=[any_spec, vmem, vmem, vmem] + [any_spec] * (len(jobs) + len(plan)),
        out_specs=out_specs,
        scratch_shapes=scratch,
        compiler_params=pltpu.CompilerParams(
            collective_id=30 + block, has_side_effects=True, vmem_limit_bytes=60 * 1024 * 1024
        ),
        name="forward_block",
    )(x, mask, following, norms, *[shards[n] for n in jobs], *[given[n] for n in plan])
    wholes = dict(zip(jobs, results[: len(jobs)]))
    return wholes, results[len(jobs) :]


def backward_kernel(n_seg, n_clip, block, *refs):
    refs = list(refs)

    def pop(count=1):
        taken = refs[:count]
        del refs[:count]
        return taken if count != 1 else taken[0]

    last = block == 1
    h3_hbm, x_hbm, d_in, h2_hbm, h1_hbm, gate_hbm = pop(6)
    in_hbm, mid_hbm, out_hbm, small_hbm = pop(4)
    norms, st1, st2, st3, mask, present, following = pop(7)
    dh3_out, dh2_out, de_out, dr_out, dh1_out, dx_out, norm_grads = pop(7)
    dv, h3v, xv, h2v, h1v, gatev, dyv, pad2, dsv, edge, pad_s, pad_e = pop(12)
    drv, dh1v, w_in, w_mid, w_out, small, w_exp = pop(7)
    sum_gain, sum_shift = pop(2)
    sums = [pop(4) for _ in range(3)]
    send_sem, recv_sem = pop(2)
    links = Links(n_seg, n_clip, send_sem, recv_sem)
    frames = xv.shape[1]
    outgoing = []

    def send_out(source, target):
        copy = links.local(source, target)
        copy.start()
        outgoing.append(copy)

    def load(source, target):
        copy = links.local(source.reshape(target.shape), target)
        copy.start()
        return copy

    loads_one = [load(h3_hbm, h3v), load(x_hbm, xv)]
    if not last:
        loads_one.append(load(d_in, dv))
    loads_two = [load(out_hbm, w_out), load(h2_hbm, h2v)]
    loads_three = [load(mid_hbm, w_mid), load(h1_hbm, h1v), load(gate_hbm, gatev), load(small_hbm, small)]
    loads_four = [load(in_hbm, w_in)]
    links.meet()
    base = BLOCK_NORMS * block
    live_rows = norms[98:99, 0:1]
    half = MID // LANES
    pad2[...] = jnp.zeros_like(pad2)
    pad_s[...] = jnp.zeros_like(pad_s)
    pad_e[...] = jnp.zeros_like(pad_e)
    sum_gain[...] = jnp.zeros_like(sum_gain)
    sum_shift[...] = jnp.zeros_like(sum_shift)

    def vectors(start, columns, stats):
        gain = row_vector(norms, base + start, columns // LANES)
        shift = row_vector(norms, base + 24 + start, columns // LANES)
        return gain, shift, stats[0:1, :], stats[1:2, :]

    def totals(index, start, columns, gain_rows, shift_rows):
        stat = sums[index][0]
        put_rows(stat, 0, jnp.sum(gain_rows, axis=0, keepdims=True), 4)
        put_rows(stat, 4, jnp.sum(shift_rows, axis=0, keepdims=True), 4)
        tot = links.all_sum(*sums[index])
        gain = jnp.concatenate([tot[k : k + 1] for k in range(4)], axis=1)
        shift = jnp.concatenate([tot[4 + k : 5 + k] for k in range(4)], axis=1)
        put_rows(norm_grads, start, gain, columns // LANES)
        put_rows(norm_grads, 24 + start, shift, columns // LANES)
        return gain / live_rows, shift / live_rows

    def slope_of(values):
        sig = jax.nn.sigmoid(values)
        return sig, sig * (1.0 + values * (1.0 - sig))

    def dot_t(left, right):
        return lax.dot_general(left, right, (((1,), (1,)), ((), ())), preferred_element_type=F32)

    for copy in loads_one:
        copy.wait()
    gain3, shift3, mean3, inv3 = vectors(2 * half, D, st3)

    def first(p, carry):
        for k in range(4):
            span = slice(k * MID, (k + 1) * MID)
            n = (h3v[p, :, span].astype(F32) - mean3[:, span]) * inv3[:, span]
            pre = n * gain3[:, span] + shift3[:, span] + xv[p, :, span].astype(F32)
            grad = d_in[:, span] if last else dv[p, :, span]
            grad = grad * slope_of(pre)[1]
            dv[p, :, span] = grad
            sum_gain[:, span] += fold(grad * n)
            sum_shift[:, span] += fold(grad)
        return carry

    lax.fori_loop(0, HW, first, 0)
    part_gain, part_shift = totals(0, 2 * half, D, sum_gain[...], sum_shift[...])
    factor3 = gain3 * inv3
    for copy in loads_two:
        copy.wait()
    gain2, shift2, mean2, inv2 = vectors(half, MID, st2)
    zeros = jnp.zeros((8, MID), F32)

    def second(i, carry):
        for j in range(GRID):
            p = GRID * i + j
            for k in range(4):
                span = slice(k * MID, (k + 1) * MID)
                n = (h3v[p, :, span].astype(F32) - mean3[:, span]) * inv3[:, span]
                rest = mask[...] * (part_shift[:, span] + n * part_gain[:, span])
                h3v[p, :, span] = (factor3[:, span] * (dv[p, :, span] - rest)).astype(BF16)
        d_a = dot_t(h3v[pl.ds(GRID * i, GRID)].reshape(GRID * frames, D), w_out[...])
        d_a = d_a.reshape(GRID, frames, MID)
        one, two = carry
        for j in range(GRID):
            n = (h2v[GRID * i + j] - mean2) * inv2
            grad = d_a[j] * slope_of(n * gain2 + shift2)[1]
            dyv[GRID * i + j] = grad
            one = one + fold(grad * n)
            two = two + fold(grad)
        return (one, two)

    one, two = lax.fori_loop(0, GRID, second, (zeros, zeros))
    send_out(h3v, dh3_out)
    part_gain2, part_shift2 = totals(1, half, MID, one, two)
    factor2 = gain2 * inv2

    def third(i, carry):
        for j in range(GRID):
            p = GRID * i + j
            n = (h2v[p] - mean2) * inv2
            rest = mask[...] * (part_shift2 + n * part_gain2)
            pad2[i + 1, j + 1] = (factor2 * (dyv[p] - rest)).astype(BF16)
        return carry

    lax.fori_loop(0, GRID, third, 0)
    send_out(pad2.at[pl.ds(1, GRID), pl.ds(1, GRID)], dh2_out)
    for copy in loads_three:
        copy.wait()
    w_exp[...] = excite_weights(small, block)
    red = small[:, 32 * block : 32 * block + 16].reshape(MID, GATE)
    gain1, shift1, mean1, inv1 = vectors(0, MID, st1)

    def fourth(i, carry):
        part = None
        for k in range(9):
            window = pad2[i + 2 - k // 3, pl.ds(2 - k % 3, GRID)].reshape(GRID * frames, MID)
            term = dot_t(window, w_mid[k])
            part = term if part is None else part + term
        part = part.reshape(GRID, frames, MID)
        for j in range(GRID):
            p = GRID * i + j
            y = (h1v[p] - mean1) * inv1 * gain1 + shift1
            a = y * jax.nn.sigmoid(y)
            gate = gatev[p].astype(F32)
            dyv[p] = part[j] * (1.0 + gate)
            gatev[p] = (part[j] * a * gate * (1.0 - gate)).astype(BF16)
        d_s = dot_t(gatev[pl.ds(GRID * i, GRID)].reshape(GRID * frames, MID), w_exp[...])
        d_s = d_s.astype(BF16).reshape(GRID, frames, GATE)
        dsv[pl.ds(GRID * i, GRID)] = d_s
        for j in range(GRID):
            pad_s[i + 1, j + 1] = d_s[j].astype(F32)
        return carry

    lax.fori_loop(0, GRID, fourth, 0)
    swap = links.remote(links.take(1), dsv, edge, links.other)
    swap.start()
    send_out(gatev, de_out)
    swap.wait()

    def unpack(i, carry):
        for j in range(GRID):
            pad_e[i + 1, j + 1] = edge[GRID * i + j].astype(F32)
        return carry

    lax.fori_loop(0, GRID, unpack, 0)
    row = lax.rem(lax.broadcasted_iota(jnp.int32, (frames, GATE), 0), 8)
    from_other = links.seg.astype(F32)

    def fifth(i, carry):
        for j in range(GRID):
            near = jnp.zeros((frames, GATE), F32)
            far = jnp.zeros((frames, GATE), F32)
            for k in range(9):
                near = near + pad_s[i + k // 3, j + k % 3]
                far = far + pad_e[i + k // 3, j + k % 3]
            near = pad_s[i + 1, j + 1] + near / 9.0
            far = (pad_e[i + 1, j + 1] + far / 9.0) * from_other
            earlier = jnp.where(row > 0, pltpu.roll(near, 1, 0), pltpu.roll(far, frames - 7, 0))
            drv[GRID * i + j] = (present[...] * earlier - following[...] * near).astype(BF16)
        d_a = dot_t(drv[pl.ds(GRID * i, GRID)].reshape(GRID * frames, GATE), red)
        d_a = d_a.reshape(GRID, frames, MID)
        one, two = carry
        for j in range(GRID):
            p = GRID * i + j
            n = (h1v[p] - mean1) * inv1
            grad = (dyv[p] + d_a[j]) * slope_of(n * gain1 + shift1)[1]
            dyv[p] = grad
            one = one + fold(grad * n)
            two = two + fold(grad)
        return (one, two)

    one, two = lax.fori_loop(0, GRID, fifth, (zeros, zeros))
    send_out(drv, dr_out)
    part_gain1, part_shift1 = totals(2, 0, MID, one, two)
    factor1 = gain1 * inv1
    for copy in loads_four:
        copy.wait()

    def sixth(i, carry):
        for j in range(GRID):
            p = GRID * i + j
            n = (h1v[p] - mean1) * inv1
            rest = mask[...] * (part_shift1 + n * part_gain1)
            dh1v[p] = (factor1 * (dyv[p] - rest)).astype(BF16)
        rows = dh1v[pl.ds(GRID * i, GRID)].reshape(GRID * frames, MID)
        for k in range(4):
            span = slice(k * MID, (k + 1) * MID)
            part = dot_t(rows, w_in[span, :])
            dv[pl.ds(GRID * i, GRID), :, span] += part.reshape(GRID, frames, MID)
        return carry

    lax.fori_loop(0, GRID, sixth, 0)
    send_out(dh1v, dh1_out)
    send_out(dv, dx_out)
    for copy in outgoing:
        copy.wait()


def backward_block(block, h3, x, d_in, h2, h1, gate, weights, norms, stats, masks):
    n_seg = lax.axis_size("seg")
    n_clip = lax.axis_size("clip")
    cells, frames, width = x.shape
    any_spec = pl.BlockSpec(memory_space=pl.ANY)
    vmem = pl.BlockSpec(memory_space=pltpu.VMEM)
    last = block == 1

    def grid_shape(columns):
        return (cells, frames, columns)

    outs = [
        jax.ShapeDtypeStruct(grid_shape(D), BF16),
        jax.ShapeDtypeStruct((GRID, GRID, frames, MID), BF16),
        jax.ShapeDtypeStruct(grid_shape(MID), BF16),
        jax.ShapeDtypeStruct(grid_shape(GATE), BF16),
        jax.ShapeDtypeStruct(grid_shape(MID), BF16),
        jax.ShapeDtypeStruct(grid_shape(D), F32),
        jax.ShapeDtypeStruct((BLOCK_NORMS, LANES), F32),
    ]
    scratch = [
        pltpu.VMEM(grid_shape(D), F32),
        pltpu.VMEM(grid_shape(D), BF16),
        pltpu.VMEM(grid_shape(D), BF16),
        pltpu.VMEM(grid_shape(MID), F32),
        pltpu.VMEM(grid_shape(MID), F32),
        pltpu.VMEM(grid_shape(MID), BF16),
        pltpu.VMEM(grid_shape(MID), F32),
        pltpu.VMEM((GRID + 2, GRID + 2, frames, MID), BF16),
        pltpu.VMEM(grid_shape(GATE), BF16),
        pltpu.VMEM(grid_shape(GATE), BF16),
        pltpu.VMEM((GRID + 2, GRID + 2, frames, GATE), F32),
        pltpu.VMEM((GRID + 2, GRID + 2, frames, GATE), F32),
        pltpu.VMEM(grid_shape(GATE), BF16),
        pltpu.VMEM(grid_shape(MID), BF16),
        pltpu.VMEM((D, MID), BF16),
        pltpu.VMEM((9, MID, MID), BF16),
        pltpu.VMEM((MID, D), BF16),
        pltpu.VMEM((SMALL_SHARDS, 64, LANES), BF16),
        pltpu.VMEM((GATE, MID), BF16),
        pltpu.VMEM((8, D), F32),
        pltpu.VMEM((8, D), F32),
    ]
    for shape in ((8, MID), (8, LANES), (8, LANES)):
        scratch += sum_scratch(n_seg, n_clip, shape)
    count = 3 * (n_seg * 4 + n_clip // 4) + 32
    scratch += [pltpu.SemaphoreType.DMA((count,)), pltpu.SemaphoreType.DMA((count,))]
    d_spec = vmem if last else any_spec
    return pl.pallas_call(
        functools.partial(backward_kernel, n_seg, n_clip, block),
        out_shape=outs,
        in_specs=[any_spec, any_spec, d_spec] + [any_spec] * 7 + [vmem] * 7,
        out_specs=[any_spec] * 6 + [vmem],
        scratch_shapes=scratch,
        compiler_params=pltpu.CompilerParams(
            collective_id=40 + block, has_side_effects=True, vmem_limit_bytes=62 * 1024 * 1024
        ),
        name="backward_block",
    )(h3, x, d_in, h2, h1, gate, *weights, norms, *stats, *masks)


def weight_gradients(x, kept, steps):
    gated, a_low, mixed, a_two = kept
    d_three, d_two, d_excite, d_reduced, d_one = steps
    return [
        matmul(x.reshape(-1, D).T, d_one.reshape(-1, MID)),
        conv(gated, d_two, ("HWCN", "HWIO", "HWNC")).reshape(9 * MID, MID),
        matmul(a_two.reshape(-1, MID).T, d_three.reshape(-1, D)),
        matmul(a_low.reshape(-1, MID).T, d_reduced.reshape(-1, GATE)),
        matmul(mixed.reshape(-1, GATE).T, d_excite.reshape(-1, MID)),
    ]


def on_device(inputs, clip_counts, labels, master, first_moment, second_moment):
    seg_count = lax.axis_size("seg")
    clip_local, slot_local = inputs.shape[:2]
    frames = clip_local * slot_local
    slot_ids = lax.axis_index("seg") * slot_local + jnp.arange(slot_local, dtype=jnp.int32)
    present = (slot_ids[None, :] < clip_counts[:, None]).astype(F32)
    following = (slot_ids[None, :] + 1 < clip_counts[:, None]).astype(F32)
    frame_mask = jnp.broadcast_to(present.reshape(frames, 1), (frames, MID))
    frame_following = jnp.broadcast_to(following.reshape(frames, 1), (frames, GATE))
    table = norm_table(master, HW * jnp.sum(present))
    x_low = inputs.reshape(frames, HW, D).transpose(1, 0, 2)
    shards = weight_shards(master)
    if shards is None:
        weights = whole_weights(master)
        jobs = ((), ())
    else:
        weights = {}
        jobs = (("in0", "small", "mid0", "out0", "in1"), ("mid1", "out1", "cls"))
    kept = []
    flowing = x_low
    flows = []
    for block in range(2):
        flows.append(flowing)
        names = ("in%d" % block, "small", "mid%d" % block, "out%d" % block)
        given = {name: weights[name] for name in names if name not in jobs[block]}
        gathered, results = forward_block(
            block,
            flowing,
            frame_mask,
            frame_following,
            table,
            {name: shards[name] for name in jobs[block]},
            given,
        )
        weights.update(gathered)
        if block == 0:
            table = results[9]
        kept.append(results[:8] + results[10:])
        flowing = results[8]
    w_cls = weights["cls"][:, :CLASSES]
    b_cls = table[96:98].reshape(-1)[:CLASSES]
    partial_value = jnp.sum(flowing.reshape(clip_local, slot_local, D), axis=1)
    pooled_sum = lax.psum(partial_value.astype(BF16), "seg").astype(F32)
    counts_float = clip_counts.astype(F32)
    pooled = pooled_sum / (HW * counts_float)[:, None]
    pooled_low = pooled.astype(BF16)
    logits = matmul(pooled_low, w_cls) + b_cls
    clips_total = clip_local * lax.axis_size("clip")
    onehot = (labels[:, None] == jnp.arange(CLASSES, dtype=jnp.int32)[None, :]).astype(F32)
    d_logits = (jax.nn.softmax(logits, axis=1) - onehot) / clips_total
    d_lin = d_logits.astype(BF16)
    g_cls = matmul(pooled_low.T, d_lin) / seg_count
    g_bias = jnp.sum(d_logits, axis=0) / seg_count
    d_pooled = matmul(d_lin, w_cls.T)
    scaled = d_pooled / (HW * counts_float)[:, None]
    d_flow = (present[:, :, None] * scaled[:, None]).reshape(frames, D)
    masks = (frame_mask, frame_mask[:, :GATE], frame_following)
    grads = [None, None]
    for block in (1, 0):
        h_one, a_low, gate, mixed, gated, h_two, a_two, h_three, st_one, st_two, st_three = kept[block]
        *steps, d_flow, norm_sums = backward_block(
            block,
            h_three,
            flows[block],
            d_flow,
            h_two,
            h_one,
            gate,
            [weights[name + str(block)] for name in ("in", "mid", "out")] + [weights["small"]],
            table,
            (st_one, st_two, st_three),
            masks,
        )
        grads[block] = weight_gradients(flows[block], (gated, a_low, mixed, a_two), steps)
        devices = seg_count * lax.axis_size("clip")
        grads[block] += [norm_sums[:24].reshape(-1) / devices, norm_sums[24:].reshape(-1) / devices]
    grad_mine = scatter_gradients(grads[0] + grads[1] + [g_cls, g_bias])
    tail = jnp.concatenate(
        [
            jnp.pad(g_bias, (0, 8 * LANES - CLASSES)).reshape(8, LANES),
            jnp.full((8, LANES), jnp.sum(grad_mine * grad_mine), F32),
        ]
    )
    tail = small_sum(tail)
    norm = jnp.sqrt(tail[8, 0])
    bias_grad = tail[:8].reshape(-1)[:CLASSES]
    factor = jnp.minimum(1.0, CLIP_LIMIT / (norm + 1e-06))
    clipped = grad_mine * factor
    new_first = BETA_ONE * first_moment + (1.0 - BETA_ONE) * clipped
    new_second = BETA_TWO * second_moment + (1.0 - BETA_TWO) * clipped * clipped
    first_hat = new_first / (1.0 - BETA_ONE**STEP)
    second_hat = new_second / (1.0 - BETA_TWO**STEP)
    new_master = master - LEARN_RATE * (
        first_hat / (jnp.sqrt(second_hat) + ADAM_EPS) + WEIGHT_DECAY * master
    )
    grid_grad = d_flow.transpose(1, 0, 2).reshape(inputs.shape)
    return (
        new_master,
        new_first,
        new_second,
        new_master.astype(BF16),
        grid_grad.reshape(inputs.shape),
        norm.reshape(1),
        bias_grad,
    )


def solution(mesh):
    return jax.shard_map(
        on_device,
        mesh=mesh,
        in_specs=(
            P("clip", "seg", None, None),
            P("clip"),
            P("clip"),
            P(AXES),
            P(AXES),
            P(AXES),
        ),
        out_specs=(
            P(AXES),
            P(AXES),
            P(AXES),
            P(AXES),
            P("clip", "seg", None, None),
            P(),
            P(),
        ),
        check_vma=False,
    )
```

```python
import functools
import math

import jax
import jax.numpy as jnp
from jax import lax
from jax.experimental import pallas as pl
from jax.experimental.pallas import tpu as pltpu
from jax.sharding import PartitionSpec as P

D = 2048
MID = 512
GATE = 128
CLASSES = 174
GRID = 7
HW = 49
STEP = 7
LANES = 128

NORM_EPS = 1e-05
CLIP_LIMIT = 0.001
LEARN_RATE = 0.04
WEIGHT_DECAY = 0.05
BETA_ONE = 0.9
BETA_TWO = 0.999
ADAM_EPS = 1e-08

AXES = ("seg", "clip")
MESH_ID = pl.DeviceIdType.MESH
BF16 = jnp.bfloat16
F32 = jnp.float32


def matmul(left, right):
    return jnp.dot(left, right, preferred_element_type=F32)


def layout():
    block_layout = [
        (D, MID),
        (9, MID, MID),
        (MID, D),
        (MID, GATE),
        (GATE, MID),
        (2 * MID + D,),
        (2 * MID + D,),
    ]
    return block_layout + block_layout + [(D, CLASSES), (CLASSES,)]


def widths(devices):
    return [(math.prod(extent) + devices - 1) // devices for extent in layout()]


def pad_rows(flat, rows):
    return jnp.pad(flat, (0, rows * LANES - flat.shape[0])).reshape(rows, LANES)


def small_rows(devices):
    wide = widths(devices)
    amount = sum(wide[3:7]) + sum(wide[10:14])
    amount_cls = wide[14] + wide[15]
    return [16 * ((a + 16 * LANES - 1) // (16 * LANES)) for a in (amount, amount_cls)]


def gather_parameters(master):
    devices = lax.axis_size("seg") * lax.axis_size("clip")
    wide = widths(devices)
    starts = [sum(wide[:i]) for i in range(len(wide))]
    low = master.astype(BF16)

    def part(i):
        return low[starts[i] : starts[i] + wide[i]]

    def gather(values):
        return lax.all_gather(values, AXES, axis=0, tiled=True)

    big = {}
    for base in (0, 7):
        for i, columns in ((0, MID), (1, MID), (2, D)):
            big[base + i] = gather(part(base + i).reshape(-1, columns))
    rows, rows_cls = small_rows(devices)
    small = gather(pad_rows(jnp.concatenate([part(i) for i in (3, 4, 5, 6, 10, 11, 12, 13)]), rows))
    small_cls = gather(pad_rows(jnp.concatenate([part(14), part(15)]), rows_cls))
    small = small.reshape(devices, rows * LANES)
    small_cls = small_cls.reshape(devices, rows_cls * LANES)
    shapes = layout()
    pieces = dict(big)

    def take(source, ids):
        offset = 0
        for i in ids:
            amount = math.prod(shapes[i])
            pieces[i] = source[:, offset : offset + wide[i]].reshape(-1)[:amount].reshape(shapes[i])
            offset += wide[i]

    take(small, (3, 4, 5, 6, 10, 11, 12, 13))
    take(small_cls, (14, 15))
    return [pieces[i] for i in range(16)]


def part_of(master, index):
    devices = lax.axis_size("seg") * lax.axis_size("clip")
    wide = widths(devices)
    start = sum(wide[:index])
    return master[start : start + wide[index]]


def norm_rows(vectors):
    rows = jnp.stack([jnp.pad(v, ((0, 0), (0, LANES - v.shape[1]))) for v in vectors], axis=1)
    return jnp.pad(rows, ((0, 0), (0, 16 - rows.shape[1]), (0, 0)))


def lanes_first(values):
    lead = values.shape[:-2]
    rows, columns = values.shape[-2:]
    split = values.reshape(lead + (rows, columns // LANES, LANES))
    return jnp.swapaxes(split, -3, -2).reshape(lead + (-1, LANES))


def split_rows(target, kind, block, pieces, rows):
    size = rows.shape[1] // pieces
    for k, name in enumerate(piece_names(kind, block, pieces)):
        target[name] = rows[:, k * size : (k + 1) * size].reshape(-1, MID)


def piece_names(kind, block, pieces):
    return [kind + "abc"[k] + str(block) for k in range(pieces)]


def weight_names(block):
    return piece_names("in", block, 2) + piece_names("mid", block, 3) + ["out%d" % block, "small"]


def weight_shards(master):
    devices = lax.axis_size("seg") * lax.axis_size("clip")
    if lax.axis_size("seg") != 2 or devices != SMALL_SHARDS:
        return None
    low = master.astype(BF16)
    shards = {}
    small = []
    for block in range(2):
        base = 7 * block
        split_rows(shards, "in", block, 2, part_of(low, base).reshape(1, -1, MID))
        split_rows(shards, "mid", block, 3, part_of(low, base + 1).reshape(1, -1, MID))
        shards["out%d" % block] = part_of(low, base + 2).reshape(-1, D)
        small.append(part_of(low, base + 3).reshape(-1, GATE))
        small.append(lanes_first(part_of(low, base + 4).reshape(-1, MID)))
    small.append(norm_rows([part_of(low, i)[None] for i in (5, 6, 12, 13, 15)])[0])
    shards["small"] = jnp.concatenate(small)
    cls = part_of(low, 14).reshape(-1, CLASSES)
    shards["cls"] = jnp.pad(cls, ((0, 0), (0, 2 * LANES - CLASSES)))
    return shards


def whole_weights(master):
    pieces = gather_parameters(master)
    whole = {}
    small = []
    for block in range(2):
        w_in, w_mid, w_out, w_red, w_exp = pieces[7 * block : 7 * block + 5]
        split_rows(whole, "in", block, 2, w_in.reshape(SMALL_SHARDS, -1, MID))
        split_rows(whole, "mid", block, 3, w_mid.reshape(SMALL_SHARDS, -1, MID))
        whole["out%d" % block] = w_out
        small.append(w_red.reshape(SMALL_SHARDS, -1, GATE))
        small.append(lanes_first(w_exp.reshape(SMALL_SHARDS, -1, MID)))
    vectors = [pieces[i].reshape(SMALL_SHARDS, -1) for i in (5, 6, 12, 13)]
    bias = jnp.pad(pieces[15], (0, 6 * SMALL_SHARDS - CLASSES)).reshape(SMALL_SHARDS, 6)
    small.append(norm_rows(vectors + [bias]))
    whole["small"] = jnp.concatenate(small, axis=1).reshape(-1, LANES)
    whole["cls"] = jnp.pad(pieces[14], ((0, 0), (0, 2 * LANES - CLASSES)))
    return whole


def scatter_gradients(grads):
    devices = lax.axis_size("seg") * lax.axis_size("clip")
    wide = widths(devices)
    columns = []
    for values, width in zip(grads, wide):
        flat = values.reshape(-1)
        columns.append(jnp.pad(flat, (0, devices * width - flat.shape[0])).reshape(devices, width))
    packed = jnp.concatenate(columns, axis=1)
    return lax.psum_scatter(packed, AXES, scatter_dimension=0, tiled=True)[0]


def conv(values, kernel, numbers):
    return lax.conv_general_dilated(
        values, kernel, (1, 1), ((1, 1), (1, 1)), dimension_numbers=numbers, preferred_element_type=F32
    )


class Links:
    def __init__(self, n_seg, n_clip, send_sem, recv_sem):
        self.n_seg = n_seg
        self.n_clip = n_clip
        self.inner = 4
        self.outer = n_clip // 4
        self.seg = lax.axis_index("seg")
        self.clip = lax.axis_index("clip")
        self.group = self.clip // 4
        self.place = lax.rem(self.clip, 4)
        y = self.place // 2
        x = lax.rem(self.place, 2)
        self.first = (1 - self.seg) * y + self.seg * x
        self.second = (1 - self.seg) * x + self.seg * y
        self.step = 1 + self.seg
        self.jump = 2 - self.seg
        self.across_first = (self.seg, self.clip + self.jump * (1 - 2 * self.first))
        self.across_second = (self.seg, self.clip + self.step * (1 - 2 * self.second))
        self.other = (1 - self.seg, self.clip)
        self.send_sem = send_sem
        self.recv_sem = recv_sem
        self.used = 0

    def take(self, count):
        base = self.used
        self.used += count
        return base

    def near_peer(self, i):
        return (
            lax.rem(self.seg + i // 4, self.n_seg),
            self.group * 4 + lax.rem(self.place + lax.rem(i, 4), 4),
        )

    def far_peer(self, i):
        return (self.seg, lax.rem(self.group + i, self.outer) * 4 + self.place)

    def remote(self, index, source, target, peer):
        return pltpu.make_async_remote_copy(
            src_ref=source,
            dst_ref=target,
            send_sem=self.send_sem.at[index],
            recv_sem=self.recv_sem.at[index],
            device_id=peer,
            device_id_type=MESH_ID,
        )

    def local(self, source, target):
        return pltpu.make_async_copy(source, target, self.recv_sem.at[self.take(1)])

    def meet(self):
        barrier = pltpu.get_barrier_semaphore()
        n_near = self.n_seg * 4 - 1
        n_far = self.outer - 1

        def greet(peer):
            pl.semaphore_signal(barrier, inc=1, device_id=peer, device_id_type=MESH_ID)

        repeat(1, n_near + 1, lambda i: greet(self.near_peer(i)))
        repeat(1, n_far + 1, lambda i: greet(self.far_peer(i)))
        pl.semaphore_wait(barrier, n_near + n_far)

    def all_sum(self, source, middle, near, far, between=lambda: None):
        n_near = self.n_seg * 4 - 1
        n_far = self.outer - 1
        base = self.take(n_near + n_far)

        def close(i):
            return self.remote(base + i - 1, source, near.at[i - 1], self.near_peer(i))

        def distant(i):
            return self.remote(base + n_near + i - 1, middle, far.at[i - 1], self.far_peer(i))

        repeat(1, n_near + 1, lambda i: close(i).start())
        repeat(1, n_near + 1, lambda i: close(i).wait())
        middle[...] = source[...] + jnp.sum(near[...], axis=0)
        repeat(1, n_far + 1, lambda i: distant(i).start())
        between()
        repeat(1, n_far + 1, lambda i: distant(i).wait())
        return middle[...] + jnp.sum(far[...], axis=0)


def repeat(first, last, action):
    if last - first <= 8:
        for i in range(first, last):
            action(i)
    else:

        def body(i, carry):
            action(i)
            return carry

        lax.fori_loop(first, last, body, 0)


def sum_scratch(n_seg, n_clip, shape):
    return [
        pltpu.VMEM(shape, F32),
        pltpu.VMEM(shape, F32),
        pltpu.VMEM((n_seg * 4 - 1,) + shape, F32),
        pltpu.VMEM((n_clip // 4 - 1,) + shape, F32),
    ]


class Gather:
    def __init__(self, links, shard, whole):
        depth = links.outer
        whole = whole.reshape((links.n_seg, depth, 4) + shard.shape)
        base = links.take(depth + 3)
        seg, z, place = links.seg, links.group, links.place
        self.own = links.local(shard, whole.at[seg, z, place])
        self.steps = [
            [
                links.remote(base + i - 1, shard, whole.at[seg, z, place], links.far_peer(i))
                for i in range(1, depth)
            ],
            [
                links.remote(
                    base + depth - 1, whole.at[seg, :, place], whole.at[seg, :, place], links.across_second
                )
            ],
            [],
            [links.remote(base + depth + 2, whole.at[seg], whole.at[seg], links.other)],
        ]
        for k in range(2):
            index = links.jump * links.first + links.step * k
            self.steps[2].append(
                links.remote(
                    base + depth + k, whole.at[seg, :, index], whole.at[seg, :, index], links.across_first
                )
            )
        self.at = -1

    def advance(self, last=3):
        if self.at >= 0:
            for copy in self.steps[self.at]:
                copy.wait()
            if self.at == 0:
                self.own.wait()
        self.at += 1
        if self.at == 0:
            self.own.start()
        if self.at <= 3:
            for copy in self.steps[self.at]:
                copy.start()

    def finish(self):
        while self.at <= 3:
            self.advance()


def row_vector(table, row, start, count):
    return jnp.concatenate([table[start + k, row : row + 1, :] for k in range(count)], axis=1)


def build_table(small, table):
    lane = lax.broadcasted_iota(jnp.int32, (8, LANES), 1)
    for q in range(SMALL_SHARDS // 4):
        rows = [small[4 * q + j, 64:80, :].astype(F32)[:8] for j in range(4)]
        one = pltpu.roll(rows[1], 96, 1)
        two = pltpu.roll(rows[2], 64, 1)
        three = pltpu.roll(rows[3], 32, 1)
        table[3 * q] = jnp.where(lane < 96, rows[0], one)
        table[3 * q + 1] = jnp.where(lane < 64, one, two)
        table[3 * q + 2] = jnp.where(lane < 32, two, three)


def put_rows(target, start, vector, count):
    width = vector.shape[1] // count
    for k in range(count):
        target[start + k : start + k + 1, :] = vector[:, k * width : (k + 1) * width]


def fold(values):
    return jnp.sum(values.reshape(-1, 8, values.shape[-1]), axis=0)


def excite_pick(shards, k):
    deep = GATE // shards
    line = lax.broadcasted_iota(jnp.int32, (GATE, shards * 16), 0)
    column = lax.broadcasted_iota(jnp.int32, (GATE, shards * 16), 1)
    wanted = (line // deep) * 16 + k * deep + lax.rem(line, deep)
    return (column == wanted).astype(F32).astype(BF16)


def excite_weights(small, block):
    shards = small.shape[0]
    rows = small[:, 32 * block + 16 : 32 * block + 32].reshape(shards * 16, LANES)
    parts = [matmul(excite_pick(shards, k), rows) for k in range(MID // LANES)]
    return jnp.concatenate(parts, axis=1).astype(BF16)


SMALL_SHARDS = 32
TABLE = ((2 * MID + D) // LANES + 1, 8, LANES)


JOBS = (
    ("ina0", "inb0", "small", "mida0", "midb0", "midc0", "out0", "ina1", "inb1", "mida1", "midb1", "midc1"),
    ("out1", "cls"),
)
PUSHES = (
    {
        "start": "ina0 small",
        "dpad": "ina0 small inb0",
        "fpad": "ina0 small inb0",
        "warm": "ina0 small inb0 mida0",
        "load": "inb0 mida0 midb0",
        "ready": "mida0 midb0 midc0",
        "first": "mida0 midb0 midc0 out0",
        "far1": "midb0 midc0 out0",
        "sum1": "midc0 out0 ina1",
        "second": "out0 ina1 inb1",
        "excite": "ina1 inb1 mida1",
        "third": "ina1 inb1 mida1 midb1",
        "far2": "inb1 mida1 midb1 midc1",
        "sum2": "mida1 midb1 midc1",
        "fourth": "midb1 midc1",
        "sum3": "midc1",
    },
    {
        "start": "out1",
        "first": "out1 cls",
        "sum1": "out1 cls",
        "second": "out1 cls",
        "excite": "cls",
    },
)


def forward_kernel(n_seg, n_clip, block, jobs, plan, *refs):
    refs = list(refs)

    def pop(count=1):
        taken = refs[:count]
        del refs[:count]
        return taken if count != 1 else taken[0]

    last = block == 1
    x_hbm, mask, following, table_in = pop(4)
    shards = dict(zip(jobs, [pop() for _ in jobs]))
    given = dict(zip(plan, [pop() for _ in plan]))
    wholes = dict(zip(jobs, [pop() for _ in jobs]))
    h1_out, low_out, gate_out, mix_out, f_out, h2_out, a2_out, h3_out = pop(8)
    out_hbm, table_out, st1, st2, st3 = pop(5)
    xv, w_in, w_mid, w_out, small = pop(5)
    h1v, a1v, lowv, rv, edge, dpad, mixv, gatev, fpad, h2v, a2v, h3v = pop(12)
    wide_sum, wide_square, w_exp = pop(3)
    sums = [pop(4) for _ in range(3)]
    pooled = pop() if last else None
    send_sem, recv_sem = pop(2)
    links = Links(n_seg, n_clip, send_sem, recv_sem)
    frames = xv.shape[1]
    table = table_in if last else table_out
    outgoing = []

    def send_out(source, target):
        copy = links.local(source, target)
        copy.start()
        outgoing.append(copy)

    links.meet()
    load_x = links.local(x_hbm, xv)
    load_x.start()
    gathers = {name: Gather(links, shards[name], wholes[name]) for name in jobs}

    def load(name, target):
        if name in gathers:
            gathers[name].finish()
            source = wholes[name]
        else:
            source = given[name]
        copy = links.local(source.reshape(target.shape), target)
        copy.start()
        return copy

    def push(point):
        for name in PUSHES[block].get(point, "").split():
            if name in gathers and gathers[name].at <= 3:
                gathers[name].advance()

    own_out = "out%d" % block

    def load_pieces(kind, count, target):
        rows = target.shape[0] // SMALL_SHARDS
        size = rows // count
        wide = target.reshape(SMALL_SHARDS, rows, MID)
        return [
            load(name, wide.at[:, k * size : (k + 1) * size])
            for k, name in enumerate(piece_names(kind, block, count))
        ]

    push("start")
    dpad[...] = jnp.zeros_like(dpad)
    push("dpad")
    fpad[...] = jnp.zeros_like(fpad)
    push("fpad")
    push("warm")
    push("load")
    waits = load_pieces("in", 2, w_in) + [load("small", small)]
    push("ready")
    for copy in waits:
        copy.wait()
    load_x.wait()
    if last:
        table_out[...] = table_in[...]
    else:
        table_out[...] = jnp.zeros_like(table_out)
        build_table(small, table_out)
    half = MID // LANES

    def norm(index, tot, columns, start, out):
        live_rows = table[TABLE[0] - 1, 0:1, 0:1]
        mean = jnp.concatenate([tot[k : k + 1] for k in range(4)], axis=1) / live_rows
        square = jnp.concatenate([tot[4 + k : 5 + k] for k in range(4)], axis=1) / live_rows
        inv = lax.rsqrt(square - mean * mean + NORM_EPS)
        out[0:1, :] = mean
        out[1:2, :] = inv
        gain = row_vector(table, 2 * block, start, columns // LANES)
        shift = row_vector(table, 2 * block + 1, start, columns // LANES)
        scale = gain * inv
        return scale, shift - mean * scale

    def masked_sums(values):
        shaped = values.reshape(-1, frames, values.shape[-1])
        masked = shaped * mask[...][None]
        return fold(masked), fold(masked * shaped)

    zeros = jnp.zeros((8, MID), F32)

    def first(i, carry):
        part = matmul(xv[pl.ds(GRID * i, GRID)].reshape(GRID * frames, D), w_in[...])
        h1v[pl.ds(GRID * i, GRID)] = part.reshape(GRID, frames, MID)
        one, two = masked_sums(part)
        return (carry[0] + one, carry[1] + two)

    one, two = lax.fori_loop(0, GRID, first, (zeros, zeros))
    send_out(h1v, h1_out)
    push("first")
    stat = sums[0][0]
    put_rows(stat, 0, jnp.sum(one, axis=0, keepdims=True), 4)
    put_rows(stat, 4, jnp.sum(two, axis=0, keepdims=True), 4)
    stat[8:16, :] = jnp.broadcast_to(HW * jnp.sum(mask[:, :LANES], axis=0, keepdims=True), (8, LANES))
    total = links.all_sum(*sums[0], lambda: push("far1"))
    if not last:
        table_out[TABLE[0] - 1] = total[8:16]
    scale_one, shift_one = norm(0, total, MID, 0, st1)
    push("sum1")
    w_exp[...] = excite_weights(small, block)
    red = small[:, 32 * block : 32 * block + 16].reshape(MID, GATE)

    def second(i, carry):
        for j in range(GRID):
            y = h1v[GRID * i + j] * scale_one + shift_one
            a = y * jax.nn.sigmoid(y)
            a1v[GRID * i + j] = a
            lowv[GRID * i + j] = a.astype(BF16)
        part = matmul(lowv[pl.ds(GRID * i, GRID)].reshape(GRID * frames, MID), red)
        rv[pl.ds(GRID * i, GRID)] = part.astype(BF16).reshape(GRID, frames, GATE)
        return carry

    lax.fori_loop(0, GRID, second, 0)
    send_out(lowv, low_out)
    swap = links.remote(links.take(1), rv, edge, links.other)
    swap.start()
    push("second")
    swap.wait()
    row = lax.rem(lax.broadcasted_iota(jnp.int32, (frames, GATE), 0), 8)

    def change(i, carry):
        for j in range(GRID):
            now = rv[GRID * i + j].astype(F32)
            rest = edge[GRID * i + j].astype(F32)
            later = jnp.where(row < 7, pltpu.roll(now, frames - 1, 0), pltpu.roll(rest, 7, 0))
            dpad[i + 1, j + 1] = following[...] * (later - now)
        return carry

    lax.fori_loop(0, GRID, change, 0)
    push("change")

    def excite(i, carry):
        for j in range(GRID):
            total = jnp.zeros((frames, GATE), F32)
            for k in range(9):
                total = total + dpad[i + k // 3, j + k % 3]
            mixv[GRID * i + j] = (dpad[i + 1, j + 1] + total / 9.0).astype(BF16)
        e = matmul(mixv[pl.ds(GRID * i, GRID)].reshape(GRID * frames, GATE), w_exp[...])
        e = e.reshape(GRID, frames, MID)
        for j in range(GRID):
            gate = jax.nn.sigmoid(e[j])
            gatev[GRID * i + j] = gate.astype(BF16)
            fpad[i + 1, j + 1] = (a1v[GRID * i + j] * (1.0 + gate)).astype(BF16)
        return carry

    lax.fori_loop(0, GRID, excite, 0)
    send_out(mixv, mix_out)
    send_out(gatev, gate_out)
    send_out(fpad.at[pl.ds(1, GRID), pl.ds(1, GRID)], f_out)
    wait_mid = load_pieces("mid", 3, w_mid)
    push("excite")
    for copy in wait_mid:
        copy.wait()

    def third(i, carry):
        part = None
        for k in range(9):
            window = fpad[i + k // 3, pl.ds(k % 3, GRID)].reshape(GRID * frames, MID)
            term = matmul(window, w_mid[k * MID : (k + 1) * MID])
            part = term if part is None else part + term
        h2v[pl.ds(GRID * i, GRID)] = part.reshape(GRID, frames, MID)
        one, two = masked_sums(part)
        return (carry[0] + one, carry[1] + two)

    one, two = lax.fori_loop(0, GRID, third, (zeros, zeros))
    send_out(h2v, h2_out)
    stat = sums[1][0]
    put_rows(stat, 0, jnp.sum(one, axis=0, keepdims=True), 4)
    put_rows(stat, 4, jnp.sum(two, axis=0, keepdims=True), 4)
    push("third")
    total = links.all_sum(*sums[1], lambda: push("far2"))
    scale_two, shift_two = norm(1, total, MID, half, st2)
    wait_out = load(own_out, w_out)
    push("sum2")
    wait_out.wait()
    wide_sum[...] = jnp.zeros_like(wide_sum)
    wide_square[...] = jnp.zeros_like(wide_square)

    def fourth(i, carry):
        for j in range(GRID):
            y = h2v[GRID * i + j] * scale_two + shift_two
            a2v[GRID * i + j] = (y * jax.nn.sigmoid(y)).astype(BF16)
        rows = a2v[pl.ds(GRID * i, GRID)].reshape(GRID * frames, MID)
        for k in range(4):
            part = matmul(rows, w_out[:, k * MID : (k + 1) * MID])
            h3v[pl.ds(GRID * i, GRID), :, k * MID : (k + 1) * MID] = part.astype(BF16).reshape(
                GRID, frames, MID
            )
            one, two = masked_sums(part)
            wide_sum[:, k * MID : (k + 1) * MID] += one
            wide_square[:, k * MID : (k + 1) * MID] += two
        return carry

    lax.fori_loop(0, GRID, fourth, 0)
    send_out(a2v, a2_out)
    send_out(h3v, h3_out)
    push("fourth")
    stat = sums[2][0]
    put_rows(stat, 0, jnp.sum(wide_sum[...], axis=0, keepdims=True), 4)
    put_rows(stat, 4, jnp.sum(wide_square[...], axis=0, keepdims=True), 4)
    scale_three, shift_three = norm(2, links.all_sum(*sums[2]), D, 2 * half, st3)
    push("sum3")
    if last:
        pooled[...] = jnp.zeros_like(pooled)

    def fifth(p, carry):
        for k in range(4):
            span = slice(k * MID, (k + 1) * MID)
            pre = h3v[p, :, span].astype(F32) * scale_three[:, span] + shift_three[:, span]
            pre = pre + xv[p, :, span].astype(F32)
            value = pre * jax.nn.sigmoid(pre)
            if last:
                pooled[:, span] += value * mask[...]
            else:
                xv[p, :, span] = value.astype(BF16)
        return carry

    lax.fori_loop(0, HW, fifth, 0)
    send_out(pooled if last else xv, out_hbm)
    for name in jobs:
        gathers[name].finish()
    for copy in outgoing:
        copy.wait()


def forward_block(block, x, mask, following, table, shards, given):
    n_seg = lax.axis_size("seg")
    n_clip = lax.axis_size("clip")
    cells, frames, width = x.shape
    jobs = list(shards)
    plan = list(given)
    any_spec = pl.BlockSpec(memory_space=pl.ANY)
    vmem = pl.BlockSpec(memory_space=pltpu.VMEM)
    depth = n_clip // 4

    def grid_shape(columns):
        return (cells, frames, columns)

    last = block == 1
    devices = n_seg * n_clip
    outs = [jax.ShapeDtypeStruct((devices * shards[n].shape[0], shards[n].shape[1]), BF16) for n in jobs]
    outs += [
        jax.ShapeDtypeStruct(grid_shape(MID), F32),
        jax.ShapeDtypeStruct(grid_shape(MID), BF16),
        jax.ShapeDtypeStruct(grid_shape(MID), BF16),
        jax.ShapeDtypeStruct(grid_shape(GATE), BF16),
        jax.ShapeDtypeStruct((GRID, GRID, frames, MID), BF16),
        jax.ShapeDtypeStruct(grid_shape(MID), F32),
        jax.ShapeDtypeStruct(grid_shape(MID), BF16),
        jax.ShapeDtypeStruct(grid_shape(D), BF16),
        jax.ShapeDtypeStruct((frames, D), F32) if last else jax.ShapeDtypeStruct(x.shape, BF16),
        jax.ShapeDtypeStruct(TABLE, F32),
        jax.ShapeDtypeStruct((8, MID), F32),
        jax.ShapeDtypeStruct((8, MID), F32),
        jax.ShapeDtypeStruct((8, D), F32),
    ]
    out_specs = [any_spec] * (len(jobs) + 9) + [vmem] * 4

    shapes = [(D, MID), (9 * MID, MID), (MID, D), (SMALL_SHARDS, 80, LANES)]
    scratch = [pltpu.VMEM(x.shape, BF16)]
    scratch += [pltpu.VMEM(s, BF16) for s in shapes]
    scratch += [
        pltpu.VMEM(grid_shape(MID), F32),
        pltpu.VMEM(grid_shape(MID), F32),
        pltpu.VMEM(grid_shape(MID), BF16),
        pltpu.VMEM(grid_shape(GATE), BF16),
        pltpu.VMEM(grid_shape(GATE), BF16),
        pltpu.VMEM((GRID + 2, GRID + 2, frames, GATE), F32),
        pltpu.VMEM(grid_shape(GATE), BF16),
        pltpu.VMEM(grid_shape(MID), BF16),
        pltpu.VMEM((GRID + 2, GRID + 2, frames, MID), BF16),
        pltpu.VMEM(grid_shape(MID), F32),
        pltpu.VMEM(grid_shape(MID), BF16),
        pltpu.VMEM(grid_shape(D), BF16),
        pltpu.VMEM((8, D), F32),
        pltpu.VMEM((8, D), F32),
        pltpu.VMEM((GATE, MID), BF16),
    ]
    for shape in ((16, LANES), (8, LANES), (8, MID)):
        scratch += sum_scratch(n_seg, n_clip, shape)
    if last:
        scratch.append(pltpu.VMEM((frames, D), F32))
    count = 4 * (n_seg * 4 + depth) + len(jobs) * (depth + 4) + 32
    scratch += [pltpu.SemaphoreType.DMA((count,)), pltpu.SemaphoreType.DMA((count,))]
    results = pl.pallas_call(
        functools.partial(forward_kernel, n_seg, n_clip, block, jobs, plan),
        out_shape=outs,
        in_specs=[any_spec, vmem, vmem, vmem] + [any_spec] * (len(jobs) + len(plan)),
        out_specs=out_specs,
        scratch_shapes=scratch,
        compiler_params=pltpu.CompilerParams(
            collective_id=30 + block, has_side_effects=True, vmem_limit_bytes=60 * 1024 * 1024
        ),
        name="forward_block",
    )(x, mask, following, table, *[shards[n] for n in jobs], *[given[n] for n in plan])
    wholes = dict(zip(jobs, results[: len(jobs)]))
    return wholes, results[len(jobs) :]


def backward_kernel(n_seg, n_clip, block, *refs):
    refs = list(refs)

    def pop(count=1):
        taken = refs[:count]
        del refs[:count]
        return taken if count != 1 else taken[0]

    last = block == 1
    h3_hbm, x_hbm, d_in, h2_hbm, h1_hbm, gate_hbm = pop(6)
    in_a, in_b, mid_a, mid_b, mid_c, out_hbm, small_hbm = pop(7)
    table, st1, st2, st3, mask, present, following = pop(7)
    dh3_out, dh2_out, de_out, dr_out, dh1_out, dx_out, norm_grads = pop(7)
    dv, h3v, xv, h2v, h1v, gatev, dyv, pad2, dsv, edge, pad_s, pad_e = pop(12)
    drv, dh1v, w_in, w_mid, w_out, small, w_exp = pop(7)
    sum_gain, sum_shift = pop(2)
    sums = [pop(4) for _ in range(3)]
    send_sem, recv_sem = pop(2)
    links = Links(n_seg, n_clip, send_sem, recv_sem)
    frames = xv.shape[1]
    outgoing = []

    def send_out(source, target):
        copy = links.local(source, target)
        copy.start()
        outgoing.append(copy)

    def load(source, target):
        copy = links.local(source.reshape(target.shape), target)
        copy.start()
        return copy

    loads_one = [load(h3_hbm, h3v), load(x_hbm, xv)]
    if not last:
        loads_one.append(load(d_in, dv))
    loads_two = [load(out_hbm, w_out), load(h2_hbm, h2v)]
    loads_three = [load(h1_hbm, h1v), load(gate_hbm, gatev), load(small_hbm, small)]
    loads_four = []
    for parts, target, waits in (
        ((mid_a, mid_b, mid_c), w_mid, loads_three),
        ((in_a, in_b), w_in, loads_four),
    ):
        rows = target.shape[0] // SMALL_SHARDS
        size = rows // len(parts)
        wide = target.reshape(SMALL_SHARDS, rows, MID)
        for k, source in enumerate(parts):
            waits.append(load(source, wide.at[:, k * size : (k + 1) * size]))
    links.meet()
    live_rows = table[TABLE[0] - 1, 0:1, 0:1]
    half = MID // LANES
    pad2[...] = jnp.zeros_like(pad2)
    pad_s[...] = jnp.zeros_like(pad_s)
    pad_e[...] = jnp.zeros_like(pad_e)
    sum_gain[...] = jnp.zeros_like(sum_gain)
    sum_shift[...] = jnp.zeros_like(sum_shift)

    def vectors(start, columns, stats):
        gain = row_vector(table, 2 * block, start, columns // LANES)
        shift = row_vector(table, 2 * block + 1, start, columns // LANES)
        return gain, shift, stats[0:1, :], stats[1:2, :]

    def totals(index, start, columns, gain_rows, shift_rows):
        stat = sums[index][0]
        put_rows(stat, 0, jnp.sum(gain_rows, axis=0, keepdims=True), 4)
        put_rows(stat, 4, jnp.sum(shift_rows, axis=0, keepdims=True), 4)
        tot = links.all_sum(*sums[index])
        gain = jnp.concatenate([tot[k : k + 1] for k in range(4)], axis=1)
        shift = jnp.concatenate([tot[4 + k : 5 + k] for k in range(4)], axis=1)
        put_rows(norm_grads, start, gain, columns // LANES)
        put_rows(norm_grads, 24 + start, shift, columns // LANES)
        return gain / live_rows, shift / live_rows

    def slope_of(values):
        sig = jax.nn.sigmoid(values)
        return sig, sig * (1.0 + values * (1.0 - sig))

    def dot_t(left, right):
        return lax.dot_general(left, right, (((1,), (1,)), ((), ())), preferred_element_type=F32)

    for copy in loads_one:
        copy.wait()
    gain3, shift3, mean3, inv3 = vectors(2 * half, D, st3)

    def first(p, carry):
        for k in range(4):
            span = slice(k * MID, (k + 1) * MID)
            n = (h3v[p, :, span].astype(F32) - mean3[:, span]) * inv3[:, span]
            pre = n * gain3[:, span] + shift3[:, span] + xv[p, :, span].astype(F32)
            grad = d_in[:, span] if last else dv[p, :, span]
            grad = grad * slope_of(pre)[1]
            dv[p, :, span] = grad
            sum_gain[:, span] += fold(grad * n)
            sum_shift[:, span] += fold(grad)
        return carry

    lax.fori_loop(0, HW, first, 0)
    part_gain, part_shift = totals(0, 2 * half, D, sum_gain[...], sum_shift[...])
    factor3 = gain3 * inv3
    for copy in loads_two:
        copy.wait()
    gain2, shift2, mean2, inv2 = vectors(half, MID, st2)
    zeros = jnp.zeros((8, MID), F32)

    def second(i, carry):
        for j in range(GRID):
            p = GRID * i + j
            for k in range(4):
                span = slice(k * MID, (k + 1) * MID)
                n = (h3v[p, :, span].astype(F32) - mean3[:, span]) * inv3[:, span]
                rest = mask[...] * (part_shift[:, span] + n * part_gain[:, span])
                h3v[p, :, span] = (factor3[:, span] * (dv[p, :, span] - rest)).astype(BF16)
        d_a = dot_t(h3v[pl.ds(GRID * i, GRID)].reshape(GRID * frames, D), w_out[...])
        d_a = d_a.reshape(GRID, frames, MID)
        one, two = carry
        for j in range(GRID):
            n = (h2v[GRID * i + j] - mean2) * inv2
            grad = d_a[j] * slope_of(n * gain2 + shift2)[1]
            dyv[GRID * i + j] = grad
            one = one + fold(grad * n)
            two = two + fold(grad)
        return (one, two)

    one, two = lax.fori_loop(0, GRID, second, (zeros, zeros))
    send_out(h3v, dh3_out)
    part_gain2, part_shift2 = totals(1, half, MID, one, two)
    factor2 = gain2 * inv2

    def third(i, carry):
        for j in range(GRID):
            p = GRID * i + j
            n = (h2v[p] - mean2) * inv2
            rest = mask[...] * (part_shift2 + n * part_gain2)
            pad2[i + 1, j + 1] = (factor2 * (dyv[p] - rest)).astype(BF16)
        return carry

    lax.fori_loop(0, GRID, third, 0)
    send_out(pad2.at[pl.ds(1, GRID), pl.ds(1, GRID)], dh2_out)
    for copy in loads_three:
        copy.wait()
    w_exp[...] = excite_weights(small, block)
    red = small[:, 32 * block : 32 * block + 16].reshape(MID, GATE)
    gain1, shift1, mean1, inv1 = vectors(0, MID, st1)

    def fourth(i, carry):
        part = None
        for k in range(9):
            window = pad2[i + 2 - k // 3, pl.ds(2 - k % 3, GRID)].reshape(GRID * frames, MID)
            term = dot_t(window, w_mid[k * MID : (k + 1) * MID])
            part = term if part is None else part + term
        part = part.reshape(GRID, frames, MID)
        for j in range(GRID):
            p = GRID * i + j
            y = (h1v[p] - mean1) * inv1 * gain1 + shift1
            a = y * jax.nn.sigmoid(y)
            gate = gatev[p].astype(F32)
            dyv[p] = part[j] * (1.0 + gate)
            gatev[p] = (part[j] * a * gate * (1.0 - gate)).astype(BF16)
        d_s = dot_t(gatev[pl.ds(GRID * i, GRID)].reshape(GRID * frames, MID), w_exp[...])
        d_s = d_s.astype(BF16).reshape(GRID, frames, GATE)
        dsv[pl.ds(GRID * i, GRID)] = d_s
        for j in range(GRID):
            pad_s[i + 1, j + 1] = d_s[j].astype(F32)
        return carry

    lax.fori_loop(0, GRID, fourth, 0)
    swap = links.remote(links.take(1), dsv, edge, links.other)
    swap.start()
    send_out(gatev, de_out)
    swap.wait()

    def unpack(i, carry):
        for j in range(GRID):
            pad_e[i + 1, j + 1] = edge[GRID * i + j].astype(F32)
        return carry

    lax.fori_loop(0, GRID, unpack, 0)
    row = lax.rem(lax.broadcasted_iota(jnp.int32, (frames, GATE), 0), 8)
    from_other = links.seg.astype(F32)

    def fifth(i, carry):
        for j in range(GRID):
            near = jnp.zeros((frames, GATE), F32)
            far = jnp.zeros((frames, GATE), F32)
            for k in range(9):
                near = near + pad_s[i + k // 3, j + k % 3]
                far = far + pad_e[i + k // 3, j + k % 3]
            near = pad_s[i + 1, j + 1] + near / 9.0
            far = (pad_e[i + 1, j + 1] + far / 9.0) * from_other
            earlier = jnp.where(row > 0, pltpu.roll(near, 1, 0), pltpu.roll(far, frames - 7, 0))
            drv[GRID * i + j] = (present[...] * earlier - following[...] * near).astype(BF16)
        d_a = dot_t(drv[pl.ds(GRID * i, GRID)].reshape(GRID * frames, GATE), red)
        d_a = d_a.reshape(GRID, frames, MID)
        one, two = carry
        for j in range(GRID):
            p = GRID * i + j
            n = (h1v[p] - mean1) * inv1
            grad = (dyv[p] + d_a[j]) * slope_of(n * gain1 + shift1)[1]
            dyv[p] = grad
            one = one + fold(grad * n)
            two = two + fold(grad)
        return (one, two)

    one, two = lax.fori_loop(0, GRID, fifth, (zeros, zeros))
    send_out(drv, dr_out)
    part_gain1, part_shift1 = totals(2, 0, MID, one, two)
    factor1 = gain1 * inv1
    for copy in loads_four:
        copy.wait()

    def sixth(i, carry):
        for j in range(GRID):
            p = GRID * i + j
            n = (h1v[p] - mean1) * inv1
            rest = mask[...] * (part_shift1 + n * part_gain1)
            dh1v[p] = (factor1 * (dyv[p] - rest)).astype(BF16)
        rows = dh1v[pl.ds(GRID * i, GRID)].reshape(GRID * frames, MID)
        for k in range(4):
            span = slice(k * MID, (k + 1) * MID)
            part = dot_t(rows, w_in[span, :])
            dv[pl.ds(GRID * i, GRID), :, span] += part.reshape(GRID, frames, MID)
        dx_copy(i).start()
        return carry

    dx_base = links.take(GRID)

    def dx_copy(i):
        rows = pl.ds(GRID * i, GRID)
        return pltpu.make_async_copy(dv.at[rows], dx_out.at[rows], links.recv_sem.at[dx_base + i])

    lax.fori_loop(0, GRID, sixth, 0)
    send_out(dh1v, dh1_out)
    for i in range(GRID):
        dx_copy(i).wait()
    for copy in outgoing:
        copy.wait()


def backward_block(block, h3, x, d_in, h2, h1, gate, weights, table, stats, masks):
    n_seg = lax.axis_size("seg")
    n_clip = lax.axis_size("clip")
    cells, frames, width = x.shape
    any_spec = pl.BlockSpec(memory_space=pl.ANY)
    vmem = pl.BlockSpec(memory_space=pltpu.VMEM)
    last = block == 1

    def grid_shape(columns):
        return (cells, frames, columns)

    outs = [
        jax.ShapeDtypeStruct(grid_shape(D), BF16),
        jax.ShapeDtypeStruct((GRID, GRID, frames, MID), BF16),
        jax.ShapeDtypeStruct(grid_shape(MID), BF16),
        jax.ShapeDtypeStruct(grid_shape(GATE), BF16),
        jax.ShapeDtypeStruct(grid_shape(MID), BF16),
        jax.ShapeDtypeStruct(grid_shape(D), F32),
        jax.ShapeDtypeStruct((48, LANES), F32),
    ]
    scratch = [
        pltpu.VMEM(grid_shape(D), F32),
        pltpu.VMEM(grid_shape(D), BF16),
        pltpu.VMEM(grid_shape(D), BF16),
        pltpu.VMEM(grid_shape(MID), F32),
        pltpu.VMEM(grid_shape(MID), F32),
        pltpu.VMEM(grid_shape(MID), BF16),
        pltpu.VMEM(grid_shape(MID), F32),
        pltpu.VMEM((GRID + 2, GRID + 2, frames, MID), BF16),
        pltpu.VMEM(grid_shape(GATE), BF16),
        pltpu.VMEM(grid_shape(GATE), BF16),
        pltpu.VMEM((GRID + 2, GRID + 2, frames, GATE), F32),
        pltpu.VMEM((GRID + 2, GRID + 2, frames, GATE), F32),
        pltpu.VMEM(grid_shape(GATE), BF16),
        pltpu.VMEM(grid_shape(MID), BF16),
        pltpu.VMEM((D, MID), BF16),
        pltpu.VMEM((9 * MID, MID), BF16),
        pltpu.VMEM((MID, D), BF16),
        pltpu.VMEM((SMALL_SHARDS, 80, LANES), BF16),
        pltpu.VMEM((GATE, MID), BF16),
        pltpu.VMEM((8, D), F32),
        pltpu.VMEM((8, D), F32),
    ]
    for shape in ((8, MID), (8, LANES), (8, LANES)):
        scratch += sum_scratch(n_seg, n_clip, shape)
    count = 3 * (n_seg * 4 + n_clip // 4) + 40
    scratch += [pltpu.SemaphoreType.DMA((count,)), pltpu.SemaphoreType.DMA((count,))]
    d_spec = vmem if last else any_spec
    return pl.pallas_call(
        functools.partial(backward_kernel, n_seg, n_clip, block),
        out_shape=outs,
        in_specs=[any_spec, any_spec, d_spec] + [any_spec] * 10 + [vmem] * 7,
        out_specs=[any_spec] * 6 + [vmem],
        scratch_shapes=scratch,
        compiler_params=pltpu.CompilerParams(
            collective_id=40 + block, has_side_effects=True, vmem_limit_bytes=62 * 1024 * 1024
        ),
        name="backward_block",
    )(h3, x, d_in, h2, h1, gate, *weights, table, *stats, *masks)


class Scatter:
    def __init__(self, links, grad, rows, buffers, finish):
        self.links = links
        self.grad = grad
        self.rows = rows
        self.one, self.two, self.three, self.four = buffers
        self.finish = finish
        self.depth = links.outer
        self.base = links.take(self.depth + 3)
        self.at = -1

    def copies(self):
        links, base, depth = self.links, self.base, self.depth
        if self.at == 0:
            source = self.grad.at[1 - links.seg, :, :, self.rows]
            return [links.remote(base, source, self.one, links.other)]
        if self.at == 1:
            found = []
            for k in range(2):
                source = self.one.at[:, links.jump * (1 - links.first) + links.step * k]
                found.append(links.remote(base + 1 + k, source, self.two.at[:, k], links.across_first))
            return found
        if self.at == 2:
            source = self.two.at[:, 1 - links.second]
            return [links.remote(base + 3, source, self.three, links.across_second)]
        found = []
        for i in range(1, depth):
            source = self.three.at[lax.rem(links.group + i, depth)]
            found.append(links.remote(base + 3 + i, source, self.four.at[i - 1], links.far_peer(i)))
        return found

    def add(self):
        links, depth = self.links, self.depth
        one, two, three, four = self.one, self.two, self.three, self.four
        if self.at == 0:

            def add_one(i, carry):
                z = i // 4
                w = lax.rem(i, 4)
                total = one[z, w].astype(F32) + self.grad[links.seg, z, w, self.rows].astype(F32)
                one[z, w] = total.astype(BF16)
                return carry

            lax.fori_loop(0, 4 * depth, add_one, 0)
        elif self.at == 1:

            def add_two(i, carry):
                z = i // 2
                k = lax.rem(i, 2)
                kept = one[z, links.jump * links.first + links.step * k]
                two[z, k] = (two[z, k].astype(F32) + kept.astype(F32)).astype(BF16)
                return carry

            lax.fori_loop(0, 2 * depth, add_two, 0)
        elif self.at == 2:

            def add_three(z, carry):
                three[z] = (three[z].astype(F32) + two[z, links.second].astype(F32)).astype(BF16)
                return carry

            lax.fori_loop(0, depth, add_three, 0)
        else:
            total = three[links.group].astype(F32)
            for i in range(1, depth):
                total = total + four[i - 1].astype(F32)
            self.finish(total)

    def advance(self):
        if self.at > 3:
            return
        if self.at >= 0:
            for copy in self.copies():
                copy.wait()
            self.add()
        self.at += 1
        if self.at <= 3:
            for copy in self.copies():
                copy.start()


SCATTERED = {
    "cls": (64, 2 * LANES),
    "out1": (16, D),
    "mida1": (48, MID),
    "midb1": (48, MID),
    "midc1": (48, MID),
    "in1": (64, MID),
    "out0": (16, D),
    "mida0": (48, MID),
    "midb0": (48, MID),
    "midc0": (48, MID),
    "in0": (64, MID),
    "small": (80, LANES),
}


def gradient_kernel(n_seg, n_clip, *refs):
    refs = list(refs)

    def pop(count=1):
        taken = refs[:count]
        del refs[:count]
        return taken if count != 1 else taken[0]

    sources = [pop(10) for _ in range(2)]
    cls_hbm, norm_rows_in, bias = pop(3)
    out_refs = {}
    for block in (0, 1):
        out_refs["in%d" % block], out_refs["mid%d" % block], out_refs["out%d" % block] = pop(3)
    out_refs["small"], out_refs["cls"], tail = pop(3)
    big3, bigx, mid_a2, mid_d2, mid_d1, mid_low, mid_de, thin_dr, thin_s, fpad = pop(10)
    g_in, g_mid, g_out, g_small, g_cls, squares = pop(6)
    sums = pop(4)
    buffers = {name: pop(4) for name in SCATTERED}
    send_sem, recv_sem = pop(2)
    links = Links(n_seg, n_clip, send_sem, recv_sem)
    cells, frames = bigx.shape[0], bigx.shape[1]
    rows_all = cells * frames
    devices = SMALL_SHARDS

    def load(source, target):
        copy = links.local(source.reshape(target.shape), target)
        copy.start()
        return copy

    interior = fpad.at[pl.ds(1, GRID), pl.ds(1, GRID)]
    names = ("x", "d1", "f", "d2", "a2", "d3", "low", "dr", "s", "de")
    targets = dict(zip(names, (bigx, mid_d1, interior, mid_d2, mid_a2, big3, mid_low, thin_dr, thin_s, mid_de)))
    hbm = [dict(zip(names, source)) for source in sources]

    def fetch(block, *keys):
        return [load(hbm[block][key], targets[key]) for key in keys]

    waits = {
        "out": fetch(1, "a2", "d3"),
        "small": fetch(1, "low", "dr", "s", "de"),
    }
    load_cls = load(cls_hbm, g_cls)
    fpad[...] = jnp.zeros_like(fpad)
    waits["mid"] = fetch(1, "f", "d2")
    waits["in"] = fetch(1, "x", "d1")
    links.meet()
    squares[...] = jnp.zeros_like(squares)

    def folded(ref, rows):
        return ref.reshape(n_seg, links.outer, 4, rows, ref.shape[-1])

    grads = {"cls": g_cls, "small": g_small}
    jobs = {}

    def make(name):
        kind = name[:-1] if name not in ("cls", "small") else name
        block = name[-1]
        rows, columns = SCATTERED[name]
        start = 0
        if kind.startswith("mid"):
            ref, shard_rows = g_mid, 3 * rows
            start = rows * "abc".index(kind[3])
            out = out_refs["mid" + block]
        else:
            ref = {"in": g_in, "out": g_out, "small": g_small, "cls": g_cls}[kind]
            shard_rows = rows
            out = out_refs[kind + block if kind in ("in", "out") else kind]

        def finish(total):
            out[start : start + rows, :] = total
            squares[:, :columns] += fold(total * total)

        jobs[name] = Scatter(links, folded(ref, shard_rows), pl.ds(start, rows), buffers[name], finish)

    for name in SCATTERED:
        make(name)

    def push(*wanted):
        for name in wanted:
            jobs[name].advance()

    def dot_tn(left, right):
        return lax.dot_general(left, right, (((0,), (0,)), ((), ())), preferred_element_type=F32)

    def ready(kind):
        for copy in waits[kind]:
            copy.wait()

    def task_out():
        ready("out")

        def body(k, carry):
            span = pl.ds(pl.multiple_of(k * MID, MID), MID)
            part = dot_tn(mid_a2[...].reshape(rows_all, MID), big3[:, :, span].reshape(rows_all, MID))
            g_out[:, span] = part.astype(BF16)
            return carry

        lax.fori_loop(0, D // MID, body, 0)

    def task_in():
        ready("in")

        def body(k, carry):
            span = pl.ds(pl.multiple_of(k * MID, MID), MID)
            part = dot_tn(bigx[:, :, span].reshape(rows_all, MID), mid_d1[...].reshape(rows_all, MID))
            g_in[span, :] = part.astype(BF16)
            return carry

        lax.fori_loop(0, D // MID, body, 0)

    def task_mid(first, last):
        if first == 0:
            ready("mid")

        def body(k, carry):
            window = fpad[pl.ds(k // 3, GRID), pl.ds(lax.rem(k, 3), GRID)].reshape(rows_all, MID)
            part = dot_tn(window, mid_d2[...].reshape(rows_all, MID))
            g_mid[pl.ds(pl.multiple_of(k * MID, MID), MID), :] = part.astype(BF16)
            return carry

        lax.fori_loop(first, last, body, 0)

    def task_small(block):
        ready("small")
        part = dot_tn(mid_low[...].reshape(rows_all, MID), thin_dr[...].reshape(rows_all, GATE))
        g_small[:, 32 * block : 32 * block + 16, :] = part.astype(BF16).reshape(devices, 16, LANES)
        part = dot_tn(thin_s[...].reshape(rows_all, GATE), mid_de[...].reshape(rows_all, MID)).astype(BF16)
        rows = jnp.zeros((devices * 16, LANES), F32)
        for k in range(MID // LANES):
            rows = rows + dot_tn(excite_pick(devices, k), part[:, k * LANES : (k + 1) * LANES])
        g_small[:, 32 * block + 16 : 32 * block + 32, :] = rows.astype(BF16).reshape(devices, 16, LANES)

    g_small[:, 64:80, :] = norm_rows_in[...]
    load_cls.wait()
    push("cls")
    task_out()
    push("cls", "out1")
    waits["out"] = fetch(0, "a2", "d3")
    task_mid(0, 4)
    push("cls", "out1")
    task_mid(4, 9)
    push("cls", "out1", "mida1", "midb1")
    waits["mid"] = fetch(0, "f", "d2")
    task_small(1)
    waits["small"] = fetch(0, "low", "dr", "s", "de")
    push("out1", "mida1", "midc1")
    task_in()
    push("cls", "out1", "midb1", "mida1", "in1")
    waits["in"] = fetch(0, "x", "d1")
    task_out()
    push("midc1", "midb1", "mida1", "in1", "out0")
    task_mid(0, 4)
    push("mida1", "midc1", "midb1", "in1", "out0")
    task_mid(4, 9)
    push("midb1", "midc1", "in1", "out0", "mida0", "midb0")
    task_small(0)
    push("midc1", "in1", "out0", "mida0", "midc0")
    task_in()
    push("out0", "midb0", "mida0", "in0")
    push("midc0", "midb0", "mida0", "in0", "small")
    push("mida0", "midc0", "midb0", "in0", "small")
    push("midb0", "midc0", "in0", "small")
    push("midc0", "in0", "small")
    for name in SCATTERED:
        while jobs[name].at <= 3:
            jobs[name].advance()
    total = jnp.sum(jnp.sum(squares[...], axis=0, keepdims=True), axis=1, keepdims=True)
    sums[0][0:8, :] = bias[...]
    sums[0][8:16, :] = jnp.broadcast_to(total, (8, LANES))
    tail[...] = links.all_sum(*sums)


def gradient_sums(sources, g_cls, norm_rows_in, bias):
    n_seg = lax.axis_size("seg")
    n_clip = lax.axis_size("clip")
    depth = n_clip // 4
    cells, frames, width = sources[0][0].shape
    any_spec = pl.BlockSpec(memory_space=pl.ANY)
    vmem = pl.BlockSpec(memory_space=pltpu.VMEM)

    def grid_shape(columns):
        return pltpu.VMEM((cells, frames, columns), BF16)

    outs = []
    for block in (0, 1):
        outs += [(64, MID), (144, MID), (16, D)]
    outs += [(80, LANES), (64, 2 * LANES), (16, LANES)]
    scratch = [grid_shape(D), grid_shape(D)] + [grid_shape(MID)] * 5 + [grid_shape(GATE)] * 2
    scratch += [
        pltpu.VMEM((GRID + 2, GRID + 2, frames, MID), BF16),
        pltpu.VMEM((D, MID), BF16),
        pltpu.VMEM((9 * MID, MID), BF16),
        pltpu.VMEM((MID, D), BF16),
        pltpu.VMEM((SMALL_SHARDS, 80, LANES), BF16),
        pltpu.VMEM((D, 2 * LANES), BF16),
        pltpu.VMEM((8, D), F32),
    ]
    scratch += sum_scratch(n_seg, n_clip, (16, LANES))
    for shape in SCATTERED.values():
        for lead in ((depth, 4), (depth, 2), (depth,), (depth - 1,)):
            scratch.append(pltpu.VMEM(lead + shape, BF16))
    count = n_seg * 4 + depth + len(SCATTERED) * (depth + 3) + 40
    scratch += [pltpu.SemaphoreType.DMA((count,)), pltpu.SemaphoreType.DMA((count,))]
    return pl.pallas_call(
        functools.partial(gradient_kernel, n_seg, n_clip),
        out_shape=[jax.ShapeDtypeStruct(s, F32) for s in outs],
        in_specs=[any_spec] * 21 + [vmem, vmem],
        out_specs=[vmem] * len(outs),
        scratch_shapes=scratch,
        compiler_params=pltpu.CompilerParams(
            collective_id=50, has_side_effects=True, vmem_limit_bytes=62 * 1024 * 1024
        ),
        name="gradient_sums",
    )(*sources[0], *sources[1], g_cls, norm_rows_in, bias)


def weight_gradients(x, d_one, gated, d_two, a_two, d_three, a_low, d_reduced, mixed, d_excite):
    return [
        matmul(x.reshape(-1, D).T, d_one.reshape(-1, MID)),
        conv(gated, d_two, ("HWCN", "HWIO", "HWNC")).reshape(9 * MID, MID),
        matmul(a_two.reshape(-1, MID).T, d_three.reshape(-1, D)),
        matmul(a_low.reshape(-1, MID).T, d_reduced.reshape(-1, GATE)),
        matmul(mixed.reshape(-1, GATE).T, d_excite.reshape(-1, MID)),
    ]


def on_device(inputs, clip_counts, labels, master, first_moment, second_moment):
    seg_count = lax.axis_size("seg")
    clip_local, slot_local = inputs.shape[:2]
    frames = clip_local * slot_local
    slot_ids = lax.axis_index("seg") * slot_local + jnp.arange(slot_local, dtype=jnp.int32)
    present = (slot_ids[None, :] < clip_counts[:, None]).astype(F32)
    following = (slot_ids[None, :] + 1 < clip_counts[:, None]).astype(F32)
    frame_mask = jnp.broadcast_to(present.reshape(frames, 1), (frames, MID))
    frame_following = jnp.broadcast_to(following.reshape(frames, 1), (frames, GATE))
    table = jnp.zeros(TABLE, F32)
    x_low = inputs.reshape(frames, HW, D).transpose(1, 0, 2)
    shards = weight_shards(master)
    if shards is None:
        weights = whole_weights(master)
        jobs = ((), ())
    else:
        weights = {}
        jobs = JOBS
    kept = []
    flowing = x_low
    flows = []
    for block in range(2):
        flows.append(flowing)
        given = {name: weights[name] for name in weight_names(block) if name not in jobs[block]}
        gathered, results = forward_block(
            block,
            flowing,
            frame_mask,
            frame_following,
            table,
            {name: shards[name] for name in jobs[block]},
            given,
        )
        weights.update(gathered)
        if block == 0:
            table = results[9]
        kept.append(results[:8] + results[10:])
        flowing = results[8]
    w_cls = weights["cls"][:, :CLASSES]
    bias_row = 64 + 4
    b_cls = weights["small"].reshape(SMALL_SHARDS, 80, LANES)[:, bias_row, :6].reshape(-1)[:CLASSES].astype(F32)
    partial_value = jnp.sum(flowing.reshape(clip_local, slot_local, D), axis=1)
    pooled_sum = lax.psum(partial_value.astype(BF16), "seg").astype(F32)
    counts_float = clip_counts.astype(F32)
    pooled = pooled_sum / (HW * counts_float)[:, None]
    pooled_low = pooled.astype(BF16)
    logits = matmul(pooled_low, w_cls) + b_cls
    clips_total = clip_local * lax.axis_size("clip")
    onehot = (labels[:, None] == jnp.arange(CLASSES, dtype=jnp.int32)[None, :]).astype(F32)
    d_logits = (jax.nn.softmax(logits, axis=1) - onehot) / clips_total
    d_lin = d_logits.astype(BF16)
    g_cls = matmul(pooled_low.T, d_lin) / seg_count
    g_bias = jnp.sum(d_logits, axis=0) / seg_count
    d_pooled = matmul(d_lin, w_cls.T)
    scaled = d_pooled / (HW * counts_float)[:, None]
    d_flow = (present[:, :, None] * scaled[:, None]).reshape(frames, D)
    masks = (frame_mask, frame_mask[:, :GATE], frame_following)
    sources = [None, None]
    norm_grads = [None, None]
    for block in (1, 0):
        h_one, a_low, gate, mixed, gated, h_two, a_two, h_three, st_one, st_two, st_three = kept[block]
        *steps, d_flow, norm_sums = backward_block(
            block,
            h_three,
            flows[block],
            d_flow,
            h_two,
            h_one,
            gate,
            [weights[name] for name in weight_names(block)],
            table,
            (st_one, st_two, st_three),
            masks,
        )
        sources[block] = (flows[block], steps[4], gated, steps[1], a_two, steps[0], a_low, steps[3], mixed, steps[2])
        norm_grads[block] = [norm_sums[:24].reshape(-1), norm_sums[24:].reshape(-1)]
    devices = seg_count * lax.axis_size("clip")
    bias_rows = jnp.pad(g_bias, (0, 8 * LANES - CLASSES)).reshape(8, LANES)
    if shards is None:
        grads = []
        for block in (0, 1):
            grads += weight_gradients(*sources[block]) + [v / devices for v in norm_grads[block]]
        grad_mine = scatter_gradients(grads + [g_cls, g_bias])
        square = jnp.full((8, LANES), jnp.sum(grad_mine * grad_mine), F32)
        tail = lax.psum(jnp.concatenate([bias_rows, square]), AXES)
    else:
        vectors = [v.reshape(SMALL_SHARDS, -1) / devices for b in (0, 1) for v in norm_grads[b]]
        padded = jnp.pad(g_bias, (0, 6 * SMALL_SHARDS - CLASSES)).reshape(SMALL_SHARDS, 6)
        extra = norm_rows(vectors + [padded]).astype(BF16)
        cls_low = jnp.pad(g_cls.astype(BF16), ((0, 0), (0, 2 * LANES - CLASSES)))
        *sums, tail = gradient_sums(sources, cls_low, extra, bias_rows)
        mine = []
        small = sums[6]
        for block in (0, 1):
            mine += [v.reshape(-1) for v in sums[3 * block : 3 * block + 3]]
            mine.append(small[32 * block : 32 * block + 16].reshape(-1))
            turned = small[32 * block + 16 : 32 * block + 32].reshape(MID // LANES, -1, LANES)
            mine.append(jnp.swapaxes(turned, 0, 1).reshape(-1))
            mine.append(small[64 + 2 * block, :96])
            mine.append(small[65 + 2 * block, :96])
        mine += [sums[7][:, :CLASSES].reshape(-1), small[68, :6]]
        grad_mine = jnp.concatenate(mine)
    norm = jnp.sqrt(tail[8, 0])
    bias_grad = tail[:8].reshape(-1)[:CLASSES]
    factor = jnp.minimum(1.0, CLIP_LIMIT / (norm + 1e-06))
    clipped = grad_mine * factor
    new_first = BETA_ONE * first_moment + (1.0 - BETA_ONE) * clipped
    new_second = BETA_TWO * second_moment + (1.0 - BETA_TWO) * clipped * clipped
    first_hat = new_first / (1.0 - BETA_ONE**STEP)
    second_hat = new_second / (1.0 - BETA_TWO**STEP)
    new_master = master - LEARN_RATE * (
        first_hat / (jnp.sqrt(second_hat) + ADAM_EPS) + WEIGHT_DECAY * master
    )
    grid_grad = d_flow.transpose(1, 0, 2).reshape(inputs.shape)
    return (
        new_master,
        new_first,
        new_second,
        new_master.astype(BF16),
        grid_grad.reshape(inputs.shape),
        norm.reshape(1),
        bias_grad,
    )


def solution(mesh):
    return jax.shard_map(
        on_device,
        mesh=mesh,
        in_specs=(
            P("clip", "seg", None, None),
            P("clip"),
            P("clip"),
            P(AXES),
            P(AXES),
            P(AXES),
        ),
        out_specs=(
            P(AXES),
            P(AXES),
            P(AXES),
            P(AXES),
            P("clip", "seg", None, None),
            P(),
            P(),
        ),
        check_vma=False,
    )
```

```python
import functools
import math

import jax
import jax.numpy as jnp
from jax import lax
from jax.experimental import pallas as pl
from jax.experimental.pallas import tpu as pltpu
from jax.sharding import PartitionSpec as P

D = 2048
MID = 512
GATE = 128
CLASSES = 174
GRID = 7
HW = 49
STEP = 7
LANES = 128

NORM_EPS = 1e-05
CLIP_LIMIT = 0.001
LEARN_RATE = 0.04
WEIGHT_DECAY = 0.05
BETA_ONE = 0.9
BETA_TWO = 0.999
ADAM_EPS = 1e-08

AXES = ("seg", "clip")
MESH_ID = pl.DeviceIdType.MESH
BF16 = jnp.bfloat16
F32 = jnp.float32


def matmul(left, right):
    return jnp.dot(left, right, preferred_element_type=F32)


def layout():
    block_layout = [
        (D, MID),
        (9, MID, MID),
        (MID, D),
        (MID, GATE),
        (GATE, MID),
        (2 * MID + D,),
        (2 * MID + D,),
    ]
    return block_layout + block_layout + [(D, CLASSES), (CLASSES,)]


def widths(devices):
    return [(math.prod(extent) + devices - 1) // devices for extent in layout()]


def pad_rows(flat, rows):
    return jnp.pad(flat, (0, rows * LANES - flat.shape[0])).reshape(rows, LANES)


def small_rows(devices):
    wide = widths(devices)
    amount = sum(wide[3:7]) + sum(wide[10:14])
    amount_cls = wide[14] + wide[15]
    return [16 * ((a + 16 * LANES - 1) // (16 * LANES)) for a in (amount, amount_cls)]


def gather_parameters(master):
    devices = lax.axis_size("seg") * lax.axis_size("clip")
    wide = widths(devices)
    starts = [sum(wide[:i]) for i in range(len(wide))]
    low = master.astype(BF16)

    def part(i):
        return low[starts[i] : starts[i] + wide[i]]

    def gather(values):
        return lax.all_gather(values, AXES, axis=0, tiled=True)

    big = {}
    for base in (0, 7):
        for i, columns in ((0, MID), (1, MID), (2, D)):
            big[base + i] = gather(part(base + i).reshape(-1, columns))
    rows, rows_cls = small_rows(devices)
    small = gather(pad_rows(jnp.concatenate([part(i) for i in (3, 4, 5, 6, 10, 11, 12, 13)]), rows))
    small_cls = gather(pad_rows(jnp.concatenate([part(14), part(15)]), rows_cls))
    small = small.reshape(devices, rows * LANES)
    small_cls = small_cls.reshape(devices, rows_cls * LANES)
    shapes = layout()
    pieces = dict(big)

    def take(source, ids):
        offset = 0
        for i in ids:
            amount = math.prod(shapes[i])
            pieces[i] = source[:, offset : offset + wide[i]].reshape(-1)[:amount].reshape(shapes[i])
            offset += wide[i]

    take(small, (3, 4, 5, 6, 10, 11, 12, 13))
    take(small_cls, (14, 15))
    return [pieces[i] for i in range(16)]


def part_of(master, index):
    devices = lax.axis_size("seg") * lax.axis_size("clip")
    wide = widths(devices)
    start = sum(wide[:index])
    return master[start : start + wide[index]]


def norm_rows(vectors):
    rows = jnp.stack([jnp.pad(v, ((0, 0), (0, LANES - v.shape[1]))) for v in vectors], axis=1)
    return jnp.pad(rows, ((0, 0), (0, 16 - rows.shape[1]), (0, 0)))


def lanes_first(values):
    lead = values.shape[:-2]
    rows, columns = values.shape[-2:]
    split = values.reshape(lead + (rows, columns // LANES, LANES))
    return jnp.swapaxes(split, -3, -2).reshape(lead + (-1, LANES))


def split_rows(target, kind, block, pieces, rows):
    size = rows.shape[1] // pieces
    for k, name in enumerate(piece_names(kind, block, pieces)):
        target[name] = rows[:, k * size : (k + 1) * size].reshape(-1, MID)


def piece_names(kind, block, pieces):
    return [kind + "abc"[k] + str(block) for k in range(pieces)]


def weight_names(block):
    return piece_names("in", block, 2) + piece_names("mid", block, 3) + ["out%d" % block, "small"]


def weight_shards(master):
    devices = lax.axis_size("seg") * lax.axis_size("clip")
    if lax.axis_size("seg") != 2 or devices != SMALL_SHARDS:
        return None
    low = master.astype(BF16)
    shards = {}
    small = []
    for block in range(2):
        base = 7 * block
        split_rows(shards, "in", block, 2, part_of(low, base).reshape(1, -1, MID))
        split_rows(shards, "mid", block, 3, part_of(low, base + 1).reshape(1, -1, MID))
        shards["out%d" % block] = part_of(low, base + 2).reshape(-1, D)
        small.append(part_of(low, base + 3).reshape(-1, GATE))
        small.append(lanes_first(part_of(low, base + 4).reshape(-1, MID)))
    small.append(norm_rows([part_of(low, i)[None] for i in (5, 6, 12, 13, 15)])[0])
    shards["small"] = jnp.concatenate(small)
    cls = part_of(low, 14).reshape(-1, CLASSES)
    shards["cls"] = jnp.pad(cls, ((0, 0), (0, 2 * LANES - CLASSES)))
    return shards


def whole_weights(master):
    pieces = gather_parameters(master)
    whole = {}
    small = []
    for block in range(2):
        w_in, w_mid, w_out, w_red, w_exp = pieces[7 * block : 7 * block + 5]
        split_rows(whole, "in", block, 2, w_in.reshape(SMALL_SHARDS, -1, MID))
        split_rows(whole, "mid", block, 3, w_mid.reshape(SMALL_SHARDS, -1, MID))
        whole["out%d" % block] = w_out
        small.append(w_red.reshape(SMALL_SHARDS, -1, GATE))
        small.append(lanes_first(w_exp.reshape(SMALL_SHARDS, -1, MID)))
    vectors = [pieces[i].reshape(SMALL_SHARDS, -1) for i in (5, 6, 12, 13)]
    bias = jnp.pad(pieces[15], (0, 6 * SMALL_SHARDS - CLASSES)).reshape(SMALL_SHARDS, 6)
    small.append(norm_rows(vectors + [bias]))
    whole["small"] = jnp.concatenate(small, axis=1).reshape(-1, LANES)
    whole["cls"] = jnp.pad(pieces[14], ((0, 0), (0, 2 * LANES - CLASSES)))
    return whole


def scatter_gradients(grads):
    devices = lax.axis_size("seg") * lax.axis_size("clip")
    wide = widths(devices)
    columns = []
    for values, width in zip(grads, wide):
        flat = values.reshape(-1)
        columns.append(jnp.pad(flat, (0, devices * width - flat.shape[0])).reshape(devices, width))
    packed = jnp.concatenate(columns, axis=1)
    return lax.psum_scatter(packed, AXES, scatter_dimension=0, tiled=True)[0]


def conv(values, kernel, numbers):
    return lax.conv_general_dilated(
        values, kernel, (1, 1), ((1, 1), (1, 1)), dimension_numbers=numbers, preferred_element_type=F32
    )


class Links:
    def __init__(self, n_seg, n_clip, send_sem, recv_sem):
        self.n_seg = n_seg
        self.n_clip = n_clip
        self.inner = 4
        self.outer = n_clip // 4
        self.seg = lax.axis_index("seg")
        self.clip = lax.axis_index("clip")
        self.group = self.clip // 4
        self.place = lax.rem(self.clip, 4)
        y = self.place // 2
        x = lax.rem(self.place, 2)
        self.first = (1 - self.seg) * y + self.seg * x
        self.second = (1 - self.seg) * x + self.seg * y
        self.step = 1 + self.seg
        self.jump = 2 - self.seg
        self.across_first = (self.seg, self.clip + self.jump * (1 - 2 * self.first))
        self.across_second = (self.seg, self.clip + self.step * (1 - 2 * self.second))
        self.other = (1 - self.seg, self.clip)
        self.send_sem = send_sem
        self.recv_sem = recv_sem
        self.used = 0

    def take(self, count):
        base = self.used
        self.used += count
        return base

    def near_peer(self, i):
        return (
            lax.rem(self.seg + i // 4, self.n_seg),
            self.group * 4 + lax.rem(self.place + lax.rem(i, 4), 4),
        )

    def far_peer(self, i):
        return (self.seg, lax.rem(self.group + i, self.outer) * 4 + self.place)

    def remote(self, index, source, target, peer):
        return pltpu.make_async_remote_copy(
            src_ref=source,
            dst_ref=target,
            send_sem=self.send_sem.at[index],
            recv_sem=self.recv_sem.at[index],
            device_id=peer,
            device_id_type=MESH_ID,
        )

    def local(self, source, target):
        return pltpu.make_async_copy(source, target, self.recv_sem.at[self.take(1)])

    def meet(self):
        barrier = pltpu.get_barrier_semaphore()
        n_near = self.n_seg * 4 - 1
        n_far = self.outer - 1

        def greet(peer):
            pl.semaphore_signal(barrier, inc=1, device_id=peer, device_id_type=MESH_ID)

        repeat(1, n_near + 1, lambda i: greet(self.near_peer(i)))
        repeat(1, n_far + 1, lambda i: greet(self.far_peer(i)))
        pl.semaphore_wait(barrier, n_near + n_far)

    def sum_near(self, source, middle, near, far):
        n_near = self.n_seg * 4 - 1
        n_far = self.outer - 1
        base = self.take(n_near + n_far)

        def close(i):
            return self.remote(base + i - 1, source, near.at[i - 1], self.near_peer(i))

        def distant(i):
            return self.remote(base + n_near + i - 1, middle, far.at[i - 1], self.far_peer(i))

        repeat(1, n_near + 1, lambda i: close(i).start())
        repeat(1, n_near + 1, lambda i: close(i).wait())
        middle[...] = source[...] + jnp.sum(near[...], axis=0)
        repeat(1, n_far + 1, lambda i: distant(i).start())

        def rest():
            repeat(1, n_far + 1, lambda i: distant(i).wait())
            return middle[...] + jnp.sum(far[...], axis=0)

        return rest

    def all_sum(self, source, middle, near, far):
        return self.sum_near(source, middle, near, far)()


def repeat(first, last, action):
    if last - first <= 8:
        for i in range(first, last):
            action(i)
    else:

        def body(i, carry):
            action(i)
            return carry

        lax.fori_loop(first, last, body, 0)


def sum_scratch(n_seg, n_clip, shape):
    return [
        pltpu.VMEM(shape, F32),
        pltpu.VMEM(shape, F32),
        pltpu.VMEM((n_seg * 4 - 1,) + shape, F32),
        pltpu.VMEM((n_clip // 4 - 1,) + shape, F32),
    ]


class Gather:
    def __init__(self, links, shard, whole):
        depth = links.outer
        whole = whole.reshape((links.n_seg, depth, 4) + shard.shape)
        base = links.take(depth + 3)
        seg, z, place = links.seg, links.group, links.place
        self.own = links.local(shard, whole.at[seg, z, place])
        self.steps = [
            [
                links.remote(base + i - 1, shard, whole.at[seg, z, place], links.far_peer(i))
                for i in range(1, depth)
            ],
            [
                links.remote(
                    base + depth - 1, whole.at[seg, :, place], whole.at[seg, :, place], links.across_second
                )
            ],
            [],
            [links.remote(base + depth + 2, whole.at[seg], whole.at[seg], links.other)],
        ]
        for k in range(2):
            index = links.jump * links.first + links.step * k
            self.steps[2].append(
                links.remote(
                    base + depth + k, whole.at[seg, :, index], whole.at[seg, :, index], links.across_first
                )
            )
        self.at = -1

    def advance(self, last=3):
        if self.at >= 0:
            for copy in self.steps[self.at]:
                copy.wait()
            if self.at == 0:
                self.own.wait()
        self.at += 1
        if self.at == 0:
            self.own.start()
        if self.at <= 3:
            for copy in self.steps[self.at]:
                copy.start()

    def finish(self):
        while self.at <= 3:
            self.advance()


def row_vector(table, row, start, count):
    return jnp.concatenate([table[start + k, row : row + 1, :] for k in range(count)], axis=1)


def build_table(small, table):
    lane = lax.broadcasted_iota(jnp.int32, (8, LANES), 1)
    for q in range(SMALL_SHARDS // 4):
        rows = [small[4 * q + j, 64:80, :].astype(F32)[:8] for j in range(4)]
        one = pltpu.roll(rows[1], 96, 1)
        two = pltpu.roll(rows[2], 64, 1)
        three = pltpu.roll(rows[3], 32, 1)
        table[3 * q] = jnp.where(lane < 96, rows[0], one)
        table[3 * q + 1] = jnp.where(lane < 64, one, two)
        table[3 * q + 2] = jnp.where(lane < 32, two, three)


def put_rows(target, start, vector, count):
    width = vector.shape[1] // count
    for k in range(count):
        target[start + k : start + k + 1, :] = vector[:, k * width : (k + 1) * width]


def fold(values):
    return jnp.sum(values.reshape(-1, 8, values.shape[-1]), axis=0)


def excite_pick(shards, k):
    deep = GATE // shards
    line = lax.broadcasted_iota(jnp.int32, (GATE, shards * 16), 0)
    column = lax.broadcasted_iota(jnp.int32, (GATE, shards * 16), 1)
    wanted = (line // deep) * 16 + k * deep + lax.rem(line, deep)
    return (column == wanted).astype(F32).astype(BF16)


def excite_weights(small, block):
    shards = small.shape[0]
    rows = small[:, 32 * block + 16 : 32 * block + 32].reshape(shards * 16, LANES)
    parts = [matmul(excite_pick(shards, k), rows) for k in range(MID // LANES)]
    return jnp.concatenate(parts, axis=1).astype(BF16)


SMALL_SHARDS = 32
TABLE = ((2 * MID + D) // LANES + 1, 8, LANES)


STAGES = (
    (
        "ina0", "small", "inb0", "mida0", "@dpad", "@fpad", "ina0", "midb0", "small", "ina0", "midc0", "inb0",
        "small", "ina0", "out0", "mida0", "inb0", "small", "ina0", "midb0", "mida0", "ina1", "small", "inb0",
        "inb1", "midc0", "midb0", "mida1", "inb0", "@first", "midb1", "mida0", "midc0", "out0", "@near1", "mida0",
        "midc1", "midb0", "ina1", "inb1", "@far1", "midb0", "midc0", "out0", "ina1", "mida1", "@second", "inb1",
        "@swap", "@excite", "midc0", "midb1", "@third", "out0", "ina1", "mida1", "midc1", "@near2", "out0", "ina1",
        "inb1", "midb1", "@far2", "mida1", "midc1", "@fourth", "inb1", "mida1", "midb1", "@near3", "midc1",
        "@far3", "midb1", "@fifth", "midc1",
    ),
    (
        "out1", "@dpad", "@fpad", "@first", "cls", "@near1", "out1", "@far1", "cls", "@second", "@swap", "out1",
        "@excite", "cls", "@third", "out1", "@near2", "cls", "@far2", "out1", "@fourth", "cls", "@near3", "@far3",
        "@fifth",
    ),
)
JOBS = tuple(tuple(dict.fromkeys(item for item in order if item[0] != "@")) for order in STAGES)


def forward_kernel(n_seg, n_clip, block, jobs, plan, *refs):
    refs = list(refs)

    def pop(count=1):
        taken = refs[:count]
        del refs[:count]
        return taken if count != 1 else taken[0]

    last = block == 1
    x_hbm, mask, following, table_in = pop(4)
    shards = dict(zip(jobs, [pop() for _ in jobs]))
    given = dict(zip(plan, [pop() for _ in plan]))
    wholes = dict(zip(jobs, [pop() for _ in jobs]))
    h1_out, low_out, gate_out, mix_out, f_out, h2_out, a2_out, h3_out = pop(8)
    out_hbm, table_out, st1, st2, st3 = pop(5)
    xv, w_in, w_mid, w_out, small = pop(5)
    h1v, a1v, lowv, rv, edge, dpad, mixv, gatev, fpad, h2v, a2v, h3v = pop(12)
    wide_sum, wide_square, w_exp = pop(3)
    sums = [pop(4) for _ in range(3)]
    pooled = pop() if last else None
    send_sem, recv_sem = pop(2)
    links = Links(n_seg, n_clip, send_sem, recv_sem)
    frames = xv.shape[1]
    table = table_in if last else table_out
    outgoing = []

    def send_out(source, target):
        copy = links.local(source, target)
        copy.start()
        outgoing.append(copy)

    links.meet()
    load_x = links.local(x_hbm, xv)
    load_x.start()
    gathers = {name: Gather(links, shards[name], wholes[name]) for name in jobs}

    targets = {"out%d" % block: w_out, "small": small}
    for kind, target, count in (("in", w_in, 2), ("mid", w_mid, 3)):
        rows = target.shape[0] // SMALL_SHARDS
        size = rows // count
        wide = target.reshape(SMALL_SHARDS, rows, MID)
        for k, name in enumerate(piece_names(kind, block, count)):
            targets[name] = wide.at[:, k * size : (k + 1) * size]
    loads = {}

    def load(name):
        source = wholes[name] if name in gathers else given[name]
        loads[name] = links.local(source.reshape(targets[name].shape), targets[name])
        loads[name].start()

    def push(name):
        if gathers[name].at <= 3:
            gathers[name].advance()
            if gathers[name].at > 3 and name in targets:
                load(name)

    def need(*names):
        for name in names:
            while name not in loads:
                push(name)
        for name in names:
            loads[name].wait()

    for name in weight_names(block):
        if name not in gathers:
            load(name)
    table = table_in if last else table_out
    half = MID // LANES

    def norm(index, tot, columns, start, out):
        live_rows = table[TABLE[0] - 1, 0:1, 0:1]
        mean = jnp.concatenate([tot[k : k + 1] for k in range(4)], axis=1) / live_rows
        square = jnp.concatenate([tot[4 + k : 5 + k] for k in range(4)], axis=1) / live_rows
        inv = lax.rsqrt(square - mean * mean + NORM_EPS)
        out[0:1, :] = mean
        out[1:2, :] = inv
        gain = row_vector(table, 2 * block, start, columns // LANES)
        shift = row_vector(table, 2 * block + 1, start, columns // LANES)
        scale = gain * inv
        return scale, shift - mean * scale

    def masked_sums(values):
        shaped = values.reshape(-1, frames, values.shape[-1])
        masked = shaped * mask[...][None]
        return fold(masked), fold(masked * shaped)

    zeros = jnp.zeros((8, MID), F32)
    kept = {}

    def first(i, carry):
        part = matmul(xv[pl.ds(GRID * i, GRID)].reshape(GRID * frames, D), w_in[...])
        h1v[pl.ds(GRID * i, GRID)] = part.reshape(GRID, frames, MID)
        one, two = masked_sums(part)
        return (carry[0] + one, carry[1] + two)

    def put_sums(index, one, two):
        stat = sums[index][0]
        put_rows(stat, 0, jnp.sum(one, axis=0, keepdims=True), 4)
        put_rows(stat, 4, jnp.sum(two, axis=0, keepdims=True), 4)
        return stat

    def stage_dpad():
        dpad[...] = jnp.zeros_like(dpad)

    def stage_fpad():
        fpad[...] = jnp.zeros_like(fpad)
        if last:
            table_out[...] = table_in[...]
        else:
            table_out[...] = jnp.zeros_like(table_out)

    def stage_first():
        need(*piece_names("in", block, 2))
        load_x.wait()
        stat = put_sums(0, *lax.fori_loop(0, GRID, first, (zeros, zeros)))
        present = HW * jnp.sum(mask[:, :LANES], axis=0, keepdims=True)
        stat[8:16, :] = jnp.broadcast_to(present, (8, LANES))
        send_out(h1v, h1_out)

    def stage_near1():
        kept["rest"] = links.sum_near(*sums[0])

    def stage_far1():
        need("small")
        total = kept["rest"]()
        if not last:
            build_table(small, table_out)
            table_out[TABLE[0] - 1] = total[8:16]
        kept["one"] = norm(0, total, MID, 0, st1)

    def second(i, carry):
        for j in range(GRID):
            y = h1v[GRID * i + j] * kept["one"][0] + kept["one"][1]
            a = y * jax.nn.sigmoid(y)
            a1v[GRID * i + j] = a
            lowv[GRID * i + j] = a.astype(BF16)
        part = matmul(lowv[pl.ds(GRID * i, GRID)].reshape(GRID * frames, MID), kept["red"])
        rv[pl.ds(GRID * i, GRID)] = part.astype(BF16).reshape(GRID, frames, GATE)
        return carry

    def stage_second():
        w_exp[...] = excite_weights(small, block)
        kept["red"] = small[:, 32 * block : 32 * block + 16].reshape(MID, GATE)
        lax.fori_loop(0, GRID, second, 0)
        send_out(lowv, low_out)
        kept["swap"] = links.remote(links.take(1), rv, edge, links.other)
        kept["swap"].start()

    row = lax.rem(lax.broadcasted_iota(jnp.int32, (frames, GATE), 0), 8)

    def change(i, carry):
        for j in range(GRID):
            now = rv[GRID * i + j].astype(F32)
            rest = edge[GRID * i + j].astype(F32)
            later = jnp.where(row < 7, pltpu.roll(now, frames - 1, 0), pltpu.roll(rest, 7, 0))
            dpad[i + 1, j + 1] = following[...] * (later - now)
        return carry

    def stage_swap():
        kept["swap"].wait()
        lax.fori_loop(0, GRID, change, 0)

    def excite(i, carry):
        for j in range(GRID):
            total = jnp.zeros((frames, GATE), F32)
            for k in range(9):
                total = total + dpad[i + k // 3, j + k % 3]
            mixv[GRID * i + j] = (dpad[i + 1, j + 1] + total / 9.0).astype(BF16)
        e = matmul(mixv[pl.ds(GRID * i, GRID)].reshape(GRID * frames, GATE), w_exp[...])
        e = e.reshape(GRID, frames, MID)
        for j in range(GRID):
            gate = jax.nn.sigmoid(e[j])
            gatev[GRID * i + j] = gate.astype(BF16)
            fpad[i + 1, j + 1] = (a1v[GRID * i + j] * (1.0 + gate)).astype(BF16)
        return carry

    def stage_excite():
        lax.fori_loop(0, GRID, excite, 0)
        send_out(mixv, mix_out)
        send_out(gatev, gate_out)
        send_out(fpad.at[pl.ds(1, GRID), pl.ds(1, GRID)], f_out)

    def third(i, carry):
        part = None
        for k in range(9):
            window = fpad[i + k // 3, pl.ds(k % 3, GRID)].reshape(GRID * frames, MID)
            term = matmul(window, w_mid[k * MID : (k + 1) * MID])
            part = term if part is None else part + term
        h2v[pl.ds(GRID * i, GRID)] = part.reshape(GRID, frames, MID)
        one, two = masked_sums(part)
        return (carry[0] + one, carry[1] + two)

    def stage_third():
        need(*piece_names("mid", block, 3))
        put_sums(1, *lax.fori_loop(0, GRID, third, (zeros, zeros)))
        send_out(h2v, h2_out)

    def stage_near2():
        kept["rest"] = links.sum_near(*sums[1])

    def stage_far2():
        kept["two"] = norm(1, kept["rest"](), MID, half, st2)
        wide_sum[...] = jnp.zeros_like(wide_sum)
        wide_square[...] = jnp.zeros_like(wide_square)

    def fourth(i, carry):
        for j in range(GRID):
            y = h2v[GRID * i + j] * kept["two"][0] + kept["two"][1]
            a2v[GRID * i + j] = (y * jax.nn.sigmoid(y)).astype(BF16)
        rows = a2v[pl.ds(GRID * i, GRID)].reshape(GRID * frames, MID)
        for k in range(4):
            part = matmul(rows, w_out[:, k * MID : (k + 1) * MID])
            h3v[pl.ds(GRID * i, GRID), :, k * MID : (k + 1) * MID] = part.astype(BF16).reshape(
                GRID, frames, MID
            )
            one, two = masked_sums(part)
            wide_sum[:, k * MID : (k + 1) * MID] += one
            wide_square[:, k * MID : (k + 1) * MID] += two
        return carry

    def stage_fourth():
        need("out%d" % block)
        lax.fori_loop(0, GRID, fourth, 0)
        put_sums(2, wide_sum[...], wide_square[...])
        send_out(a2v, a2_out)
        send_out(h3v, h3_out)

    def stage_near3():
        kept["rest"] = links.sum_near(*sums[2])

    def stage_far3():
        kept["three"] = norm(2, kept["rest"](), D, 2 * half, st3)
        if last:
            pooled[...] = jnp.zeros_like(pooled)

    def fifth(p, carry):
        for k in range(4):
            span = slice(k * MID, (k + 1) * MID)
            scale, shift = kept["three"]
            pre = h3v[p, :, span].astype(F32) * scale[:, span] + shift[:, span]
            pre = pre + xv[p, :, span].astype(F32)
            value = pre * jax.nn.sigmoid(pre)
            if last:
                pooled[:, span] += value * mask[...]
            else:
                xv[p, :, span] = value.astype(BF16)
        return carry

    def stage_fifth():
        lax.fori_loop(0, HW, fifth, 0)
        send_out(pooled if last else xv, out_hbm)

    stages = {
        "dpad": stage_dpad,
        "fpad": stage_fpad,
        "first": stage_first,
        "near1": stage_near1,
        "far1": stage_far1,
        "second": stage_second,
        "swap": stage_swap,
        "excite": stage_excite,
        "third": stage_third,
        "near2": stage_near2,
        "far2": stage_far2,
        "fourth": stage_fourth,
        "near3": stage_near3,
        "far3": stage_far3,
        "fifth": stage_fifth,
    }
    for item in STAGES[block]:
        if item[0] == "@":
            with jax.named_scope(item[1:]):
                stages[item[1:]]()
        elif item in gathers:
            push(item)
    for name in jobs:
        gathers[name].finish()
    for copy in outgoing:
        copy.wait()


def forward_block(block, x, mask, following, table, shards, given):
    n_seg = lax.axis_size("seg")
    n_clip = lax.axis_size("clip")
    cells, frames, width = x.shape
    jobs = list(shards)
    plan = list(given)
    any_spec = pl.BlockSpec(memory_space=pl.ANY)
    vmem = pl.BlockSpec(memory_space=pltpu.VMEM)
    depth = n_clip // 4

    def grid_shape(columns):
        return (cells, frames, columns)

    last = block == 1
    devices = n_seg * n_clip
    outs = [jax.ShapeDtypeStruct((devices * shards[n].shape[0], shards[n].shape[1]), BF16) for n in jobs]
    outs += [
        jax.ShapeDtypeStruct(grid_shape(MID), F32),
        jax.ShapeDtypeStruct(grid_shape(MID), BF16),
        jax.ShapeDtypeStruct(grid_shape(MID), BF16),
        jax.ShapeDtypeStruct(grid_shape(GATE), BF16),
        jax.ShapeDtypeStruct((GRID, GRID, frames, MID), BF16),
        jax.ShapeDtypeStruct(grid_shape(MID), F32),
        jax.ShapeDtypeStruct(grid_shape(MID), BF16),
        jax.ShapeDtypeStruct(grid_shape(D), BF16),
        jax.ShapeDtypeStruct((frames, D), F32) if last else jax.ShapeDtypeStruct(x.shape, BF16),
        jax.ShapeDtypeStruct(TABLE, F32),
        jax.ShapeDtypeStruct((8, MID), F32),
        jax.ShapeDtypeStruct((8, MID), F32),
        jax.ShapeDtypeStruct((8, D), F32),
    ]
    out_specs = [any_spec] * (len(jobs) + 9) + [vmem] * 4

    shapes = [(D, MID), (9 * MID, MID), (MID, D), (SMALL_SHARDS, 80, LANES)]
    scratch = [pltpu.VMEM(x.shape, BF16)]
    scratch += [pltpu.VMEM(s, BF16) for s in shapes]
    scratch += [
        pltpu.VMEM(grid_shape(MID), F32),
        pltpu.VMEM(grid_shape(MID), F32),
        pltpu.VMEM(grid_shape(MID), BF16),
        pltpu.VMEM(grid_shape(GATE), BF16),
        pltpu.VMEM(grid_shape(GATE), BF16),
        pltpu.VMEM((GRID + 2, GRID + 2, frames, GATE), F32),
        pltpu.VMEM(grid_shape(GATE), BF16),
        pltpu.VMEM(grid_shape(MID), BF16),
        pltpu.VMEM((GRID + 2, GRID + 2, frames, MID), BF16),
        pltpu.VMEM(grid_shape(MID), F32),
        pltpu.VMEM(grid_shape(MID), BF16),
        pltpu.VMEM(grid_shape(D), BF16),
        pltpu.VMEM((8, D), F32),
        pltpu.VMEM((8, D), F32),
        pltpu.VMEM((GATE, MID), BF16),
    ]
    for shape in ((16, LANES), (8, LANES), (8, MID)):
        scratch += sum_scratch(n_seg, n_clip, shape)
    if last:
        scratch.append(pltpu.VMEM((frames, D), F32))
    count = 4 * (n_seg * 4 + depth) + len(jobs) * (depth + 4) + 32
    scratch += [pltpu.SemaphoreType.DMA((count,)), pltpu.SemaphoreType.DMA((count,))]
    results = pl.pallas_call(
        functools.partial(forward_kernel, n_seg, n_clip, block, jobs, plan),
        out_shape=outs,
        in_specs=[any_spec, vmem, vmem, vmem] + [any_spec] * (len(jobs) + len(plan)),
        out_specs=out_specs,
        scratch_shapes=scratch,
        compiler_params=pltpu.CompilerParams(
            collective_id=30 + block, has_side_effects=True, vmem_limit_bytes=60 * 1024 * 1024
        ),
        name="forward_block",
    )(x, mask, following, table, *[shards[n] for n in jobs], *[given[n] for n in plan])
    wholes = dict(zip(jobs, results[: len(jobs)]))
    return wholes, results[len(jobs) :]


def backward_kernel(n_seg, n_clip, block, *refs):
    refs = list(refs)

    def pop(count=1):
        taken = refs[:count]
        del refs[:count]
        return taken if count != 1 else taken[0]

    last = block == 1
    h3_hbm, x_hbm, d_in, h2_hbm, h1_hbm, gate_hbm = pop(6)
    in_a, in_b, mid_a, mid_b, mid_c, out_hbm, small_hbm = pop(7)
    table, st1, st2, st3, mask, present, following = pop(7)
    dh3_out, dh2_out, de_out, dr_out, dh1_out, dx_out, norm_grads = pop(7)
    dv, h3v, xv, h2v, h1v, gatev, dyv, pad2, dsv, edge, pad_s, pad_e = pop(12)
    drv, dh1v, w_in, w_mid, w_out, small, w_exp = pop(7)
    sum_gain, sum_shift = pop(2)
    sums = [pop(4) for _ in range(3)]
    send_sem, recv_sem = pop(2)
    links = Links(n_seg, n_clip, send_sem, recv_sem)
    frames = xv.shape[1]
    outgoing = []

    def send_out(source, target):
        copy = links.local(source, target)
        copy.start()
        outgoing.append(copy)

    def load(source, target):
        copy = links.local(source.reshape(target.shape), target)
        copy.start()
        return copy

    loads_one = [load(h3_hbm, h3v), load(x_hbm, xv)]
    if not last:
        loads_one.append(load(d_in, dv))
    loads_two = [load(out_hbm, w_out), load(h2_hbm, h2v)]
    loads_three = [load(h1_hbm, h1v), load(gate_hbm, gatev), load(small_hbm, small)]
    loads_four = []
    for parts, target, waits in (
        ((mid_a, mid_b, mid_c), w_mid, loads_three),
        ((in_a, in_b), w_in, loads_four),
    ):
        rows = target.shape[0] // SMALL_SHARDS
        size = rows // len(parts)
        wide = target.reshape(SMALL_SHARDS, rows, MID)
        for k, source in enumerate(parts):
            waits.append(load(source, wide.at[:, k * size : (k + 1) * size]))
    links.meet()
    live_rows = table[TABLE[0] - 1, 0:1, 0:1]
    half = MID // LANES
    pad2[...] = jnp.zeros_like(pad2)
    pad_s[...] = jnp.zeros_like(pad_s)
    pad_e[...] = jnp.zeros_like(pad_e)
    sum_gain[...] = jnp.zeros_like(sum_gain)
    sum_shift[...] = jnp.zeros_like(sum_shift)

    def vectors(start, columns, stats):
        gain = row_vector(table, 2 * block, start, columns // LANES)
        shift = row_vector(table, 2 * block + 1, start, columns // LANES)
        return gain, shift, stats[0:1, :], stats[1:2, :]

    def totals(index, start, columns, gain_rows, shift_rows):
        stat = sums[index][0]
        put_rows(stat, 0, jnp.sum(gain_rows, axis=0, keepdims=True), 4)
        put_rows(stat, 4, jnp.sum(shift_rows, axis=0, keepdims=True), 4)
        tot = links.all_sum(*sums[index])
        gain = jnp.concatenate([tot[k : k + 1] for k in range(4)], axis=1)
        shift = jnp.concatenate([tot[4 + k : 5 + k] for k in range(4)], axis=1)
        put_rows(norm_grads, start, gain, columns // LANES)
        put_rows(norm_grads, 24 + start, shift, columns // LANES)
        return gain / live_rows, shift / live_rows

    def slope_of(values):
        sig = jax.nn.sigmoid(values)
        return sig, sig * (1.0 + values * (1.0 - sig))

    def dot_t(left, right):
        return lax.dot_general(left, right, (((1,), (1,)), ((), ())), preferred_element_type=F32)

    for copy in loads_one:
        copy.wait()
    gain3, shift3, mean3, inv3 = vectors(2 * half, D, st3)

    def first(p, carry):
        for k in range(4):
            span = slice(k * MID, (k + 1) * MID)
            n = (h3v[p, :, span].astype(F32) - mean3[:, span]) * inv3[:, span]
            pre = n * gain3[:, span] + shift3[:, span] + xv[p, :, span].astype(F32)
            grad = d_in[:, span] if last else dv[p, :, span]
            grad = grad * slope_of(pre)[1]
            dv[p, :, span] = grad
            sum_gain[:, span] += fold(grad * n)
            sum_shift[:, span] += fold(grad)
        return carry

    lax.fori_loop(0, HW, first, 0)
    part_gain, part_shift = totals(0, 2 * half, D, sum_gain[...], sum_shift[...])
    factor3 = gain3 * inv3
    for copy in loads_two:
        copy.wait()
    gain2, shift2, mean2, inv2 = vectors(half, MID, st2)
    zeros = jnp.zeros((8, MID), F32)

    def second(i, carry):
        for j in range(GRID):
            p = GRID * i + j
            for k in range(4):
                span = slice(k * MID, (k + 1) * MID)
                n = (h3v[p, :, span].astype(F32) - mean3[:, span]) * inv3[:, span]
                rest = mask[...] * (part_shift[:, span] + n * part_gain[:, span])
                h3v[p, :, span] = (factor3[:, span] * (dv[p, :, span] - rest)).astype(BF16)
        d_a = dot_t(h3v[pl.ds(GRID * i, GRID)].reshape(GRID * frames, D), w_out[...])
        d_a = d_a.reshape(GRID, frames, MID)
        one, two = carry
        for j in range(GRID):
            n = (h2v[GRID * i + j] - mean2) * inv2
            grad = d_a[j] * slope_of(n * gain2 + shift2)[1]
            dyv[GRID * i + j] = grad
            one = one + fold(grad * n)
            two = two + fold(grad)
        return (one, two)

    one, two = lax.fori_loop(0, GRID, second, (zeros, zeros))
    send_out(h3v, dh3_out)
    part_gain2, part_shift2 = totals(1, half, MID, one, two)
    factor2 = gain2 * inv2

    def third(i, carry):
        for j in range(GRID):
            p = GRID * i + j
            n = (h2v[p] - mean2) * inv2
            rest = mask[...] * (part_shift2 + n * part_gain2)
            pad2[i + 1, j + 1] = (factor2 * (dyv[p] - rest)).astype(BF16)
        return carry

    lax.fori_loop(0, GRID, third, 0)
    send_out(pad2.at[pl.ds(1, GRID), pl.ds(1, GRID)], dh2_out)
    for copy in loads_three:
        copy.wait()
    w_exp[...] = excite_weights(small, block)
    red = small[:, 32 * block : 32 * block + 16].reshape(MID, GATE)
    gain1, shift1, mean1, inv1 = vectors(0, MID, st1)

    def fourth(i, carry):
        part = None
        for k in range(9):
            window = pad2[i + 2 - k // 3, pl.ds(2 - k % 3, GRID)].reshape(GRID * frames, MID)
            term = dot_t(window, w_mid[k * MID : (k + 1) * MID])
            part = term if part is None else part + term
        part = part.reshape(GRID, frames, MID)
        for j in range(GRID):
            p = GRID * i + j
            y = (h1v[p] - mean1) * inv1 * gain1 + shift1
            a = y * jax.nn.sigmoid(y)
            gate = gatev[p].astype(F32)
            dyv[p] = part[j] * (1.0 + gate)
            gatev[p] = (part[j] * a * gate * (1.0 - gate)).astype(BF16)
        d_s = dot_t(gatev[pl.ds(GRID * i, GRID)].reshape(GRID * frames, MID), w_exp[...])
        d_s = d_s.astype(BF16).reshape(GRID, frames, GATE)
        dsv[pl.ds(GRID * i, GRID)] = d_s
        for j in range(GRID):
            pad_s[i + 1, j + 1] = d_s[j].astype(F32)
        return carry

    lax.fori_loop(0, GRID, fourth, 0)
    swap = links.remote(links.take(1), dsv, edge, links.other)
    swap.start()
    send_out(gatev, de_out)
    swap.wait()

    def unpack(i, carry):
        for j in range(GRID):
            pad_e[i + 1, j + 1] = edge[GRID * i + j].astype(F32)
        return carry

    lax.fori_loop(0, GRID, unpack, 0)
    row = lax.rem(lax.broadcasted_iota(jnp.int32, (frames, GATE), 0), 8)
    from_other = links.seg.astype(F32)

    def fifth(i, carry):
        for j in range(GRID):
            near = jnp.zeros((frames, GATE), F32)
            far = jnp.zeros((frames, GATE), F32)
            for k in range(9):
                near = near + pad_s[i + k // 3, j + k % 3]
                far = far + pad_e[i + k // 3, j + k % 3]
            near = pad_s[i + 1, j + 1] + near / 9.0
            far = (pad_e[i + 1, j + 1] + far / 9.0) * from_other
            earlier = jnp.where(row > 0, pltpu.roll(near, 1, 0), pltpu.roll(far, frames - 7, 0))
            drv[GRID * i + j] = (present[...] * earlier - following[...] * near).astype(BF16)
        d_a = dot_t(drv[pl.ds(GRID * i, GRID)].reshape(GRID * frames, GATE), red)
        d_a = d_a.reshape(GRID, frames, MID)
        one, two = carry
        for j in range(GRID):
            p = GRID * i + j
            n = (h1v[p] - mean1) * inv1
            grad = (dyv[p] + d_a[j]) * slope_of(n * gain1 + shift1)[1]
            dyv[p] = grad
            one = one + fold(grad * n)
            two = two + fold(grad)
        return (one, two)

    one, two = lax.fori_loop(0, GRID, fifth, (zeros, zeros))
    send_out(drv, dr_out)
    part_gain1, part_shift1 = totals(2, 0, MID, one, two)
    factor1 = gain1 * inv1
    for copy in loads_four:
        copy.wait()

    def sixth(i, carry):
        for j in range(GRID):
            p = GRID * i + j
            n = (h1v[p] - mean1) * inv1
            rest = mask[...] * (part_shift1 + n * part_gain1)
            dh1v[p] = (factor1 * (dyv[p] - rest)).astype(BF16)
        rows = dh1v[pl.ds(GRID * i, GRID)].reshape(GRID * frames, MID)
        for k in range(4):
            span = slice(k * MID, (k + 1) * MID)
            part = dot_t(rows, w_in[span, :])
            dv[pl.ds(GRID * i, GRID), :, span] += part.reshape(GRID, frames, MID)
        dx_copy(i).start()
        return carry

    dx_base = links.take(GRID)

    def dx_copy(i):
        rows = pl.ds(GRID * i, GRID)
        return pltpu.make_async_copy(dv.at[rows], dx_out.at[rows], links.recv_sem.at[dx_base + i])

    lax.fori_loop(0, GRID, sixth, 0)
    send_out(dh1v, dh1_out)
    for i in range(GRID):
        dx_copy(i).wait()
    for copy in outgoing:
        copy.wait()


def backward_block(block, h3, x, d_in, h2, h1, gate, weights, table, stats, masks):
    n_seg = lax.axis_size("seg")
    n_clip = lax.axis_size("clip")
    cells, frames, width = x.shape
    any_spec = pl.BlockSpec(memory_space=pl.ANY)
    vmem = pl.BlockSpec(memory_space=pltpu.VMEM)
    last = block == 1

    def grid_shape(columns):
        return (cells, frames, columns)

    outs = [
        jax.ShapeDtypeStruct(grid_shape(D), BF16),
        jax.ShapeDtypeStruct((GRID, GRID, frames, MID), BF16),
        jax.ShapeDtypeStruct(grid_shape(MID), BF16),
        jax.ShapeDtypeStruct(grid_shape(GATE), BF16),
        jax.ShapeDtypeStruct(grid_shape(MID), BF16),
        jax.ShapeDtypeStruct(grid_shape(D), F32),
        jax.ShapeDtypeStruct((48, LANES), F32),
    ]
    scratch = [
        pltpu.VMEM(grid_shape(D), F32),
        pltpu.VMEM(grid_shape(D), BF16),
        pltpu.VMEM(grid_shape(D), BF16),
        pltpu.VMEM(grid_shape(MID), F32),
        pltpu.VMEM(grid_shape(MID), F32),
        pltpu.VMEM(grid_shape(MID), BF16),
        pltpu.VMEM(grid_shape(MID), F32),
        pltpu.VMEM((GRID + 2, GRID + 2, frames, MID), BF16),
        pltpu.VMEM(grid_shape(GATE), BF16),
        pltpu.VMEM(grid_shape(GATE), BF16),
        pltpu.VMEM((GRID + 2, GRID + 2, frames, GATE), F32),
        pltpu.VMEM((GRID + 2, GRID + 2, frames, GATE), F32),
        pltpu.VMEM(grid_shape(GATE), BF16),
        pltpu.VMEM(grid_shape(MID), BF16),
        pltpu.VMEM((D, MID), BF16),
        pltpu.VMEM((9 * MID, MID), BF16),
        pltpu.VMEM((MID, D), BF16),
        pltpu.VMEM((SMALL_SHARDS, 80, LANES), BF16),
        pltpu.VMEM((GATE, MID), BF16),
        pltpu.VMEM((8, D), F32),
        pltpu.VMEM((8, D), F32),
    ]
    for shape in ((8, MID), (8, LANES), (8, LANES)):
        scratch += sum_scratch(n_seg, n_clip, shape)
    count = 3 * (n_seg * 4 + n_clip // 4) + 40
    scratch += [pltpu.SemaphoreType.DMA((count,)), pltpu.SemaphoreType.DMA((count,))]
    d_spec = vmem if last else any_spec
    return pl.pallas_call(
        functools.partial(backward_kernel, n_seg, n_clip, block),
        out_shape=outs,
        in_specs=[any_spec, any_spec, d_spec] + [any_spec] * 10 + [vmem] * 7,
        out_specs=[any_spec] * 6 + [vmem],
        scratch_shapes=scratch,
        compiler_params=pltpu.CompilerParams(
            collective_id=40 + block, has_side_effects=True, vmem_limit_bytes=62 * 1024 * 1024
        ),
        name="backward_block",
    )(h3, x, d_in, h2, h1, gate, *weights, table, *stats, *masks)


class Scatter:
    def __init__(self, links, grad, rows, buffers, finish):
        self.links = links
        self.grad = grad
        self.rows = rows
        self.one, self.two, self.three, self.four = buffers
        self.finish = finish
        self.depth = links.outer
        self.base = links.take(self.depth + 3)
        self.at = -1

    def copies(self):
        links, base, depth = self.links, self.base, self.depth
        if self.at == 0:
            source = self.grad.at[1 - links.seg, :, :, self.rows]
            return [links.remote(base, source, self.one, links.other)]
        if self.at == 1:
            found = []
            for k in range(2):
                source = self.one.at[:, links.jump * (1 - links.first) + links.step * k]
                found.append(links.remote(base + 1 + k, source, self.two.at[:, k], links.across_first))
            return found
        if self.at == 2:
            source = self.two.at[:, 1 - links.second]
            return [links.remote(base + 3, source, self.three, links.across_second)]
        found = []
        for i in range(1, depth):
            source = self.three.at[lax.rem(links.group + i, depth)]
            found.append(links.remote(base + 3 + i, source, self.four.at[i - 1], links.far_peer(i)))
        return found

    def add(self):
        links, depth = self.links, self.depth
        one, two, three, four = self.one, self.two, self.three, self.four
        if self.at == 0:

            def add_one(i, carry):
                z = i // 4
                w = lax.rem(i, 4)
                total = one[z, w].astype(F32) + self.grad[links.seg, z, w, self.rows].astype(F32)
                one[z, w] = total.astype(BF16)
                return carry

            lax.fori_loop(0, 4 * depth, add_one, 0)
        elif self.at == 1:

            def add_two(i, carry):
                z = i // 2
                k = lax.rem(i, 2)
                kept = one[z, links.jump * links.first + links.step * k]
                two[z, k] = (two[z, k].astype(F32) + kept.astype(F32)).astype(BF16)
                return carry

            lax.fori_loop(0, 2 * depth, add_two, 0)
        elif self.at == 2:

            def add_three(z, carry):
                three[z] = (three[z].astype(F32) + two[z, links.second].astype(F32)).astype(BF16)
                return carry

            lax.fori_loop(0, depth, add_three, 0)
        else:
            total = three[links.group].astype(F32)
            for i in range(1, depth):
                total = total + four[i - 1].astype(F32)
            self.finish(total)

    def advance(self):
        if self.at > 3:
            return
        if self.at >= 0:
            for copy in self.copies():
                copy.wait()
            self.add()
        self.at += 1
        if self.at <= 3:
            for copy in self.copies():
                copy.start()


SCATTERED = {
    "cls": (64, 2 * LANES),
    "out1": (16, D),
    "mida1": (48, MID),
    "midb1": (48, MID),
    "midc1": (48, MID),
    "in1": (64, MID),
    "out0": (16, D),
    "mida0": (48, MID),
    "midb0": (48, MID),
    "midc0": (48, MID),
    "in0": (64, MID),
    "small": (80, LANES),
}


ORDER = (
    "cls", "@out1a", "@out1b", "out1", "cls", "@in1a", "in1", "@in1b", "out1", "cls", "@mid1a", "in1", "@mid1b",
    "mida1", "midb1", "midc1", "@mid1c", "cls", "out1", "mida1", "@small1", "@in0a", "in0", "in1", "@in0b", "cls",
    "out1", "midb1", "midc1", "@mid0a", "mida1", "@mid0b", "mida0", "midb0", "midc0", "out1", "in1", "@mid0c",
    "midb1", "@small0", "small", "in0", "@out0a", "midc1", "mida1", "in1", "@out0b", "out0", "midb1", "mida0",
    "mida1", "out0", "in0", "midc1", "midb1", "mida0", "midc1", "midb0", "out0", "in0", "mida0", "midc0", "midb0",
    "in0", "out0", "small", "mida0", "midc0", "midb0", "small", "out0", "midc0", "small", "midb0", "midc0",
    "small",
)


ORDER_FIRST = "out1a"


def gradient_kernel(n_seg, n_clip, *refs):
    refs = list(refs)

    def pop(count=1):
        taken = refs[:count]
        del refs[:count]
        return taken if count != 1 else taken[0]

    sources = [pop(10) for _ in range(2)]
    cls_hbm, norm_rows_in, bias = pop(3)
    out_refs = {}
    for block in (0, 1):
        out_refs["in%d" % block], out_refs["mid%d" % block], out_refs["out%d" % block] = pop(3)
    out_refs["small"], out_refs["cls"], tail = pop(3)
    big3, bigx, mid_a2, mid_d2, mid_d1, mid_low, mid_de, thin_dr, thin_s, fpad = pop(10)
    g_in, g_mid, g_out, g_small, g_cls, squares = pop(6)
    sums = pop(4)
    buffers = {name: pop(4) for name in SCATTERED}
    send_sem, recv_sem = pop(2)
    links = Links(n_seg, n_clip, send_sem, recv_sem)
    cells, frames = bigx.shape[0], bigx.shape[1]
    rows_all = cells * frames
    devices = SMALL_SHARDS

    def load(source, target):
        copy = links.local(source.reshape(target.shape), target)
        copy.start()
        return copy

    interior = fpad.at[pl.ds(1, GRID), pl.ds(1, GRID)]
    names = ("x", "d1", "f", "d2", "a2", "d3", "low", "dr", "s", "de")
    targets = dict(zip(names, (bigx, mid_d1, interior, mid_d2, mid_a2, big3, mid_low, thin_dr, thin_s, mid_de)))
    hbm = [dict(zip(names, source)) for source in sources]

    def fetch(block, *keys):
        return [load(hbm[block][key], targets[key]) for key in keys]

    operands = {
        "out": ("a2", "d3"),
        "in": ("x", "d1"),
        "mid": ("f", "d2"),
        "small": ("low", "dr", "s", "de"),
    }
    load_cls = load(cls_hbm, g_cls)
    waits = {"out": fetch(1, *operands["out"])}
    fpad[...] = jnp.zeros_like(fpad)
    links.meet()
    squares[...] = jnp.zeros_like(squares)

    def folded(ref, rows):
        return ref.reshape(n_seg, links.outer, 4, rows, ref.shape[-1])

    grads = {"cls": g_cls, "small": g_small}
    jobs = {}

    def make(name):
        kind = name[:-1] if name not in ("cls", "small") else name
        block = name[-1]
        rows, columns = SCATTERED[name]
        start = 0
        if kind.startswith("mid"):
            ref, shard_rows = g_mid, 3 * rows
            start = rows * "abc".index(kind[3])
            out = out_refs["mid" + block]
        else:
            ref = {"in": g_in, "out": g_out, "small": g_small, "cls": g_cls}[kind]
            shard_rows = rows
            out = out_refs[kind + block if kind in ("in", "out") else kind]

        def finish(total):
            out[start : start + rows, :] = total
            squares[:, :columns] += fold(total * total)

        jobs[name] = Scatter(links, folded(ref, shard_rows), pl.ds(start, rows), buffers[name], finish)

    for name in SCATTERED:
        make(name)

    def push(*wanted):
        for name in wanted:
            jobs[name].advance()

    def dot_tn(left, right):
        return lax.dot_general(left, right, (((0,), (0,)), ((), ())), preferred_element_type=F32)

    turn = 1 - links.seg

    def task_out(first, last):
        def body(k, carry):
            span = pl.ds(pl.multiple_of(k * MID, MID), MID)
            part = dot_tn(mid_a2[...].reshape(rows_all, MID), big3[:, :, span].reshape(rows_all, MID))
            g_out[:, span] = part.astype(BF16)
            return carry

        lax.fori_loop(first, last, body, 0)

    def task_in(first, last):
        def body(i, carry):
            k = i + turn * (3 - 2 * i)
            span = pl.ds(pl.multiple_of(k * MID, MID), MID)
            part = dot_tn(bigx[:, :, span].reshape(rows_all, MID), mid_d1[...].reshape(rows_all, MID))
            g_in[span, :] = part.astype(BF16)
            return carry

        lax.fori_loop(first, last, body, 0)

    def task_mid(first, last):
        def body(i, carry):
            k = i + turn * (8 - 2 * i)
            window = fpad[pl.ds(k // 3, GRID), pl.ds(lax.rem(k, 3), GRID)].reshape(rows_all, MID)
            part = dot_tn(window, mid_d2[...].reshape(rows_all, MID))
            g_mid[pl.ds(pl.multiple_of(k * MID, MID), MID), :] = part.astype(BF16)
            return carry

        lax.fori_loop(first, last, body, 0)

    def task_small(block):
        part = dot_tn(mid_low[...].reshape(rows_all, MID), thin_dr[...].reshape(rows_all, GATE))
        g_small[:, 32 * block : 32 * block + 16, :] = part.astype(BF16).reshape(devices, 16, LANES)
        part = dot_tn(thin_s[...].reshape(rows_all, GATE), mid_de[...].reshape(rows_all, MID)).astype(BF16)
        rows = jnp.zeros((devices * 16, LANES), F32)
        for k in range(MID // LANES):
            rows = rows + dot_tn(excite_pick(devices, k), part[:, k * LANES : (k + 1) * LANES])
        g_small[:, 32 * block + 16 : 32 * block + 32, :] = rows.astype(BF16).reshape(devices, 16, LANES)

    def run(piece):
        letter = piece[-1] if piece[-1] in "abc" else ""
        kind, block = piece[: len(piece) - 1 - len(letter)], int(piece[len(piece) - 1 - len(letter)])
        part = "abc".index(letter) if letter else 0
        if part == 0:
            for copy in waits[kind]:
                copy.wait()
            if block == 0 and kind != "small":
                for name in SCATTERED:
                    if name.startswith(kind) and name[-1] == "1":
                        while jobs[name].at < 1:
                            jobs[name].advance()
        if kind == "mid":
            task_mid(3 * part, 3 * part + 3)
        elif kind == "in":
            task_in(2 * part, 2 * part + 2)
        elif kind == "out":
            task_out(2 * part, 2 * part + 2)
        else:
            task_small(block)
        if block == 1 and part == {"mid": 2, "in": 1, "out": 1, "small": 0}[kind]:
            waits[kind] = fetch(0, *operands[kind])
        if block == 1 and piece == ORDER_FIRST:
            for other in ("in", "mid", "small"):
                waits[other] = fetch(1, *operands[other])

    g_small[:, 64:80, :] = norm_rows_in[...]
    load_cls.wait()
    for item in ORDER:
        if item[0] == "@":
            with jax.named_scope("product"):
                run(item[1:])
        else:
            push(item)
    for name in SCATTERED:
        while jobs[name].at <= 3:
            jobs[name].advance()
    total = jnp.sum(jnp.sum(squares[...], axis=0, keepdims=True), axis=1, keepdims=True)
    sums[0][0:8, :] = bias[...]
    sums[0][8:16, :] = jnp.broadcast_to(total, (8, LANES))
    tail[...] = links.all_sum(*sums)


def gradient_sums(sources, g_cls, norm_rows_in, bias):
    n_seg = lax.axis_size("seg")
    n_clip = lax.axis_size("clip")
    depth = n_clip // 4
    cells, frames, width = sources[0][0].shape
    any_spec = pl.BlockSpec(memory_space=pl.ANY)
    vmem = pl.BlockSpec(memory_space=pltpu.VMEM)

    def grid_shape(columns):
        return pltpu.VMEM((cells, frames, columns), BF16)

    outs = []
    for block in (0, 1):
        outs += [(64, MID), (144, MID), (16, D)]
    outs += [(80, LANES), (64, 2 * LANES), (16, LANES)]
    scratch = [grid_shape(D), grid_shape(D)] + [grid_shape(MID)] * 5 + [grid_shape(GATE)] * 2
    scratch += [
        pltpu.VMEM((GRID + 2, GRID + 2, frames, MID), BF16),
        pltpu.VMEM((D, MID), BF16),
        pltpu.VMEM((9 * MID, MID), BF16),
        pltpu.VMEM((MID, D), BF16),
        pltpu.VMEM((SMALL_SHARDS, 80, LANES), BF16),
        pltpu.VMEM((D, 2 * LANES), BF16),
        pltpu.VMEM((8, D), F32),
    ]
    scratch += sum_scratch(n_seg, n_clip, (16, LANES))
    for shape in SCATTERED.values():
        for lead in ((depth, 4), (depth, 2), (depth,), (depth - 1,)):
            scratch.append(pltpu.VMEM(lead + shape, BF16))
    count = n_seg * 4 + depth + len(SCATTERED) * (depth + 3) + 40
    scratch += [pltpu.SemaphoreType.DMA((count,)), pltpu.SemaphoreType.DMA((count,))]
    return pl.pallas_call(
        functools.partial(gradient_kernel, n_seg, n_clip),
        out_shape=[jax.ShapeDtypeStruct(s, F32) for s in outs],
        in_specs=[any_spec] * 21 + [vmem, vmem],
        out_specs=[vmem] * len(outs),
        scratch_shapes=scratch,
        compiler_params=pltpu.CompilerParams(
            collective_id=50, has_side_effects=True, vmem_limit_bytes=62 * 1024 * 1024
        ),
        name="gradient_sums",
    )(*sources[0], *sources[1], g_cls, norm_rows_in, bias)


def weight_gradients(x, d_one, gated, d_two, a_two, d_three, a_low, d_reduced, mixed, d_excite):
    return [
        matmul(x.reshape(-1, D).T, d_one.reshape(-1, MID)),
        conv(gated, d_two, ("HWCN", "HWIO", "HWNC")).reshape(9 * MID, MID),
        matmul(a_two.reshape(-1, MID).T, d_three.reshape(-1, D)),
        matmul(a_low.reshape(-1, MID).T, d_reduced.reshape(-1, GATE)),
        matmul(mixed.reshape(-1, GATE).T, d_excite.reshape(-1, MID)),
    ]


def on_device(inputs, clip_counts, labels, master, first_moment, second_moment):
    seg_count = lax.axis_size("seg")
    clip_local, slot_local = inputs.shape[:2]
    frames = clip_local * slot_local
    slot_ids = lax.axis_index("seg") * slot_local + jnp.arange(slot_local, dtype=jnp.int32)
    present = (slot_ids[None, :] < clip_counts[:, None]).astype(F32)
    following = (slot_ids[None, :] + 1 < clip_counts[:, None]).astype(F32)
    frame_mask = jnp.broadcast_to(present.reshape(frames, 1), (frames, MID))
    frame_following = jnp.broadcast_to(following.reshape(frames, 1), (frames, GATE))
    table = jnp.zeros(TABLE, F32)
    x_low = inputs.reshape(frames, HW, D).transpose(1, 0, 2)
    shards = weight_shards(master)
    if shards is None:
        weights = whole_weights(master)
        jobs = ((), ())
    else:
        weights = {}
        jobs = JOBS
    kept = []
    flowing = x_low
    flows = []
    for block in range(2):
        flows.append(flowing)
        given = {name: weights[name] for name in weight_names(block) if name not in jobs[block]}
        gathered, results = forward_block(
            block,
            flowing,
            frame_mask,
            frame_following,
            table,
            {name: shards[name] for name in jobs[block]},
            given,
        )
        weights.update(gathered)
        if block == 0:
            table = results[9]
        kept.append(results[:8] + results[10:])
        flowing = results[8]
    w_cls = weights["cls"][:, :CLASSES]
    bias_row = 64 + 4
    b_cls = weights["small"].reshape(SMALL_SHARDS, 80, LANES)[:, bias_row, :6].reshape(-1)[:CLASSES].astype(F32)
    partial_value = jnp.sum(flowing.reshape(clip_local, slot_local, D), axis=1)
    pooled_sum = lax.psum(partial_value.astype(BF16), "seg").astype(F32)
    counts_float = clip_counts.astype(F32)
    pooled = pooled_sum / (HW * counts_float)[:, None]
    pooled_low = pooled.astype(BF16)
    logits = matmul(pooled_low, w_cls) + b_cls
    clips_total = clip_local * lax.axis_size("clip")
    onehot = (labels[:, None] == jnp.arange(CLASSES, dtype=jnp.int32)[None, :]).astype(F32)
    d_logits = (jax.nn.softmax(logits, axis=1) - onehot) / clips_total
    d_lin = d_logits.astype(BF16)
    g_cls = matmul(pooled_low.T, d_lin) / seg_count
    g_bias = jnp.sum(d_logits, axis=0) / seg_count
    d_pooled = matmul(d_lin, w_cls.T)
    scaled = d_pooled / (HW * counts_float)[:, None]
    d_flow = (present[:, :, None] * scaled[:, None]).reshape(frames, D)
    masks = (frame_mask, frame_mask[:, :GATE], frame_following)
    sources = [None, None]
    norm_grads = [None, None]
    for block in (1, 0):
        h_one, a_low, gate, mixed, gated, h_two, a_two, h_three, st_one, st_two, st_three = kept[block]
        *steps, d_flow, norm_sums = backward_block(
            block,
            h_three,
            flows[block],
            d_flow,
            h_two,
            h_one,
            gate,
            [weights[name] for name in weight_names(block)],
            table,
            (st_one, st_two, st_three),
            masks,
        )
        sources[block] = (flows[block], steps[4], gated, steps[1], a_two, steps[0], a_low, steps[3], mixed, steps[2])
        norm_grads[block] = [norm_sums[:24].reshape(-1), norm_sums[24:].reshape(-1)]
    devices = seg_count * lax.axis_size("clip")
    bias_rows = jnp.pad(g_bias, (0, 8 * LANES - CLASSES)).reshape(8, LANES)
    if shards is None:
        grads = []
        for block in (0, 1):
            grads += weight_gradients(*sources[block]) + [v / devices for v in norm_grads[block]]
        grad_mine = scatter_gradients(grads + [g_cls, g_bias])
        square = jnp.full((8, LANES), jnp.sum(grad_mine * grad_mine), F32)
        tail = lax.psum(jnp.concatenate([bias_rows, square]), AXES)
    else:
        vectors = [v.reshape(SMALL_SHARDS, -1) / devices for b in (0, 1) for v in norm_grads[b]]
        padded = jnp.pad(g_bias, (0, 6 * SMALL_SHARDS - CLASSES)).reshape(SMALL_SHARDS, 6)
        extra = norm_rows(vectors + [padded]).astype(BF16)
        cls_low = jnp.pad(g_cls.astype(BF16), ((0, 0), (0, 2 * LANES - CLASSES)))
        *sums, tail = gradient_sums(sources, cls_low, extra, bias_rows)
        mine = []
        small = sums[6]
        for block in (0, 1):
            mine += [v.reshape(-1) for v in sums[3 * block : 3 * block + 3]]
            mine.append(small[32 * block : 32 * block + 16].reshape(-1))
            turned = small[32 * block + 16 : 32 * block + 32].reshape(MID // LANES, -1, LANES)
            mine.append(jnp.swapaxes(turned, 0, 1).reshape(-1))
            mine.append(small[64 + 2 * block, :96])
            mine.append(small[65 + 2 * block, :96])
        mine += [sums[7][:, :CLASSES].reshape(-1), small[68, :6]]
        grad_mine = jnp.concatenate(mine)
    norm = jnp.sqrt(tail[8, 0])
    bias_grad = tail[:8].reshape(-1)[:CLASSES]
    factor = jnp.minimum(1.0, CLIP_LIMIT / (norm + 1e-06))
    clipped = grad_mine * factor
    new_first = BETA_ONE * first_moment + (1.0 - BETA_ONE) * clipped
    new_second = BETA_TWO * second_moment + (1.0 - BETA_TWO) * clipped * clipped
    first_hat = new_first / (1.0 - BETA_ONE**STEP)
    second_hat = new_second / (1.0 - BETA_TWO**STEP)
    new_master = master - LEARN_RATE * (
        first_hat / (jnp.sqrt(second_hat) + ADAM_EPS) + WEIGHT_DECAY * master
    )
    grid_grad = d_flow.transpose(1, 0, 2).reshape(inputs.shape)
    return (
        new_master,
        new_first,
        new_second,
        new_master.astype(BF16),
        grid_grad.reshape(inputs.shape),
        norm.reshape(1),
        bias_grad,
    )


def solution(mesh):
    return jax.shard_map(
        on_device,
        mesh=mesh,
        in_specs=(
            P("clip", "seg", None, None),
            P("clip"),
            P("clip"),
            P(AXES),
            P(AXES),
            P(AXES),
        ),
        out_specs=(
            P(AXES),
            P(AXES),
            P(AXES),
            P(AXES),
            P("clip", "seg", None, None),
            P(),
            P(),
        ),
        check_vma=False,
    )
```

```python
import functools
import math

import jax
import jax.numpy as jnp
from jax import lax
from jax.experimental import pallas as pl
from jax.experimental.pallas import tpu as pltpu
from jax.sharding import PartitionSpec as P

D = 2048
MID = 512
GATE = 128
CLASSES = 174
GRID = 7
HW = 49
STEP = 7
LANES = 128

NORM_EPS = 1e-05
CLIP_LIMIT = 0.001
LEARN_RATE = 0.04
WEIGHT_DECAY = 0.05
BETA_ONE = 0.9
BETA_TWO = 0.999
ADAM_EPS = 1e-08

AXES = ("seg", "clip")
MESH_ID = pl.DeviceIdType.MESH
BF16 = jnp.bfloat16
F32 = jnp.float32


def matmul(left, right):
    return jnp.dot(left, right, preferred_element_type=F32)


def layout():
    block_layout = [
        (D, MID),
        (9, MID, MID),
        (MID, D),
        (MID, GATE),
        (GATE, MID),
        (2 * MID + D,),
        (2 * MID + D,),
    ]
    return block_layout + block_layout + [(D, CLASSES), (CLASSES,)]


def widths(devices):
    return [(math.prod(extent) + devices - 1) // devices for extent in layout()]


def pad_rows(flat, rows):
    return jnp.pad(flat, (0, rows * LANES - flat.shape[0])).reshape(rows, LANES)


def small_rows(devices):
    wide = widths(devices)
    amount = sum(wide[3:7]) + sum(wide[10:14])
    amount_cls = wide[14] + wide[15]
    return [16 * ((a + 16 * LANES - 1) // (16 * LANES)) for a in (amount, amount_cls)]


def gather_parameters(master):
    devices = lax.axis_size("seg") * lax.axis_size("clip")
    wide = widths(devices)
    starts = [sum(wide[:i]) for i in range(len(wide))]
    low = master.astype(BF16)

    def part(i):
        return low[starts[i] : starts[i] + wide[i]]

    def gather(values):
        return lax.all_gather(values, AXES, axis=0, tiled=True)

    big = {}
    for base in (0, 7):
        for i, columns in ((0, MID), (1, MID), (2, D)):
            big[base + i] = gather(part(base + i).reshape(-1, columns))
    rows, rows_cls = small_rows(devices)
    small = gather(pad_rows(jnp.concatenate([part(i) for i in (3, 4, 5, 6, 10, 11, 12, 13)]), rows))
    small_cls = gather(pad_rows(jnp.concatenate([part(14), part(15)]), rows_cls))
    small = small.reshape(devices, rows * LANES)
    small_cls = small_cls.reshape(devices, rows_cls * LANES)
    shapes = layout()
    pieces = dict(big)

    def take(source, ids):
        offset = 0
        for i in ids:
            amount = math.prod(shapes[i])
            pieces[i] = source[:, offset : offset + wide[i]].reshape(-1)[:amount].reshape(shapes[i])
            offset += wide[i]

    take(small, (3, 4, 5, 6, 10, 11, 12, 13))
    take(small_cls, (14, 15))
    return [pieces[i] for i in range(16)]


def part_of(master, index):
    devices = lax.axis_size("seg") * lax.axis_size("clip")
    wide = widths(devices)
    start = sum(wide[:index])
    return master[start : start + wide[index]]


def norm_rows(vectors):
    rows = jnp.stack([jnp.pad(v, ((0, 0), (0, LANES - v.shape[1]))) for v in vectors], axis=1)
    return jnp.pad(rows, ((0, 0), (0, 16 - rows.shape[1]), (0, 0)))


def lanes_first(values):
    lead = values.shape[:-2]
    rows, columns = values.shape[-2:]
    split = values.reshape(lead + (rows, columns // LANES, LANES))
    return jnp.swapaxes(split, -3, -2).reshape(lead + (-1, LANES))


def split_rows(target, kind, block, pieces, rows):
    size = rows.shape[1] // pieces
    for k, name in enumerate(piece_names(kind, block, pieces)):
        target[name] = rows[:, k * size : (k + 1) * size].reshape(-1, MID)


def piece_names(kind, block, pieces):
    return [kind + "abc"[k] + str(block) for k in range(pieces)]


def weight_names(block):
    return piece_names("in", block, 2) + piece_names("mid", block, 3) + ["out%d" % block, "small"]


def weight_shards(master):
    devices = lax.axis_size("seg") * lax.axis_size("clip")
    if lax.axis_size("seg") != 2 or devices != SMALL_SHARDS:
        return None
    low = master.astype(BF16)
    shards = {}
    small = []
    for block in range(2):
        base = 7 * block
        split_rows(shards, "in", block, 2, part_of(low, base).reshape(1, -1, MID))
        split_rows(shards, "mid", block, 3, part_of(low, base + 1).reshape(1, -1, MID))
        shards["out%d" % block] = part_of(low, base + 2).reshape(-1, D)
        small.append(part_of(low, base + 3).reshape(-1, GATE))
        small.append(lanes_first(part_of(low, base + 4).reshape(-1, MID)))
    small.append(norm_rows([part_of(low, i)[None] for i in (5, 6, 12, 13, 15)])[0])
    shards["small"] = jnp.concatenate(small)
    cls = part_of(low, 14).reshape(-1, CLASSES)
    shards["cls"] = jnp.pad(cls, ((0, 0), (0, 2 * LANES - CLASSES)))
    return shards


def whole_weights(master):
    pieces = gather_parameters(master)
    whole = {}
    small = []
    for block in range(2):
        w_in, w_mid, w_out, w_red, w_exp = pieces[7 * block : 7 * block + 5]
        split_rows(whole, "in", block, 2, w_in.reshape(SMALL_SHARDS, -1, MID))
        split_rows(whole, "mid", block, 3, w_mid.reshape(SMALL_SHARDS, -1, MID))
        whole["out%d" % block] = w_out
        small.append(w_red.reshape(SMALL_SHARDS, -1, GATE))
        small.append(lanes_first(w_exp.reshape(SMALL_SHARDS, -1, MID)))
    vectors = [pieces[i].reshape(SMALL_SHARDS, -1) for i in (5, 6, 12, 13)]
    bias = jnp.pad(pieces[15], (0, 6 * SMALL_SHARDS - CLASSES)).reshape(SMALL_SHARDS, 6)
    small.append(norm_rows(vectors + [bias]))
    whole["small"] = jnp.concatenate(small, axis=1).reshape(-1, LANES)
    whole["cls"] = jnp.pad(pieces[14], ((0, 0), (0, 2 * LANES - CLASSES)))
    return whole


def scatter_gradients(grads):
    devices = lax.axis_size("seg") * lax.axis_size("clip")
    wide = widths(devices)
    columns = []
    for values, width in zip(grads, wide):
        flat = values.reshape(-1)
        columns.append(jnp.pad(flat, (0, devices * width - flat.shape[0])).reshape(devices, width))
    packed = jnp.concatenate(columns, axis=1)
    return lax.psum_scatter(packed, AXES, scatter_dimension=0, tiled=True)[0]


def conv(values, kernel, numbers):
    return lax.conv_general_dilated(
        values, kernel, (1, 1), ((1, 1), (1, 1)), dimension_numbers=numbers, preferred_element_type=F32
    )


class Links:
    def __init__(self, n_seg, n_clip, send_sem, recv_sem):
        self.n_seg = n_seg
        self.n_clip = n_clip
        self.inner = 4
        self.outer = n_clip // 4
        self.seg = lax.axis_index("seg")
        self.clip = lax.axis_index("clip")
        self.group = self.clip // 4
        self.place = lax.rem(self.clip, 4)
        y = self.place // 2
        x = lax.rem(self.place, 2)
        self.first = (1 - self.seg) * y + self.seg * x
        self.second = (1 - self.seg) * x + self.seg * y
        self.step = 1 + self.seg
        self.jump = 2 - self.seg
        self.across_first = (self.seg, self.clip + self.jump * (1 - 2 * self.first))
        self.across_second = (self.seg, self.clip + self.step * (1 - 2 * self.second))
        self.other = (1 - self.seg, self.clip)
        self.send_sem = send_sem
        self.recv_sem = recv_sem
        self.used = 0

    def take(self, count):
        base = self.used
        self.used += count
        return base

    def near_peer(self, i):
        return (
            lax.rem(self.seg + i // 4, self.n_seg),
            self.group * 4 + lax.rem(self.place + lax.rem(i, 4), 4),
        )

    def far_peer(self, i):
        return (self.seg, lax.rem(self.group + i, self.outer) * 4 + self.place)

    def remote(self, index, source, target, peer):
        return pltpu.make_async_remote_copy(
            src_ref=source,
            dst_ref=target,
            send_sem=self.send_sem.at[index],
            recv_sem=self.recv_sem.at[index],
            device_id=peer,
            device_id_type=MESH_ID,
        )

    def local(self, source, target):
        return pltpu.make_async_copy(source, target, self.recv_sem.at[self.take(1)])

    def meet(self):
        barrier = pltpu.get_barrier_semaphore()
        n_near = self.n_seg * 4 - 1
        n_far = self.outer - 1

        def greet(peer):
            pl.semaphore_signal(barrier, inc=1, device_id=peer, device_id_type=MESH_ID)

        repeat(1, n_near + 1, lambda i: greet(self.near_peer(i)))
        repeat(1, n_far + 1, lambda i: greet(self.far_peer(i)))
        pl.semaphore_wait(barrier, n_near + n_far)

    def sum_near(self, source, middle, near, far):
        n_near = self.n_seg * 4 - 1
        n_far = self.outer - 1
        base = self.take(n_near + n_far)

        def close(i):
            return self.remote(base + i - 1, source, near.at[i - 1], self.near_peer(i))

        def distant(i):
            return self.remote(base + n_near + i - 1, middle, far.at[i - 1], self.far_peer(i))

        repeat(1, n_near + 1, lambda i: close(i).start())
        repeat(1, n_near + 1, lambda i: close(i).wait())
        middle[...] = source[...] + jnp.sum(near[...], axis=0)
        repeat(1, n_far + 1, lambda i: distant(i).start())

        def rest():
            repeat(1, n_far + 1, lambda i: distant(i).wait())
            return middle[...] + jnp.sum(far[...], axis=0)

        return rest

    def all_sum(self, source, middle, near, far):
        return self.sum_near(source, middle, near, far)()


def repeat(first, last, action):
    if last - first <= 8:
        for i in range(first, last):
            action(i)
    else:

        def body(i, carry):
            action(i)
            return carry

        lax.fori_loop(first, last, body, 0)


def sum_scratch(n_seg, n_clip, shape):
    return [
        pltpu.VMEM(shape, F32),
        pltpu.VMEM(shape, F32),
        pltpu.VMEM((n_seg * 4 - 1,) + shape, F32),
        pltpu.VMEM((n_clip // 4 - 1,) + shape, F32),
    ]


class Gather:
    def __init__(self, links, shard, whole):
        depth = links.outer
        whole = whole.reshape((links.n_seg, depth, 4) + shard.shape)
        base = links.take(depth + 3)
        seg, z, place = links.seg, links.group, links.place
        self.own = links.local(shard, whole.at[seg, z, place])
        self.steps = [
            [
                links.remote(base + i - 1, shard, whole.at[seg, z, place], links.far_peer(i))
                for i in range(1, depth)
            ],
            [
                links.remote(
                    base + depth - 1, whole.at[seg, :, place], whole.at[seg, :, place], links.across_second
                )
            ],
            [],
            [links.remote(base + depth + 2, whole.at[seg], whole.at[seg], links.other)],
        ]
        for k in range(2):
            index = links.jump * links.first + links.step * k
            self.steps[2].append(
                links.remote(
                    base + depth + k, whole.at[seg, :, index], whole.at[seg, :, index], links.across_first
                )
            )
        self.at = -1

    def advance(self, last=3):
        if self.at >= 0:
            for copy in self.steps[self.at]:
                copy.wait()
            if self.at == 0:
                self.own.wait()
        self.at += 1
        if self.at == 0:
            self.own.start()
        if self.at <= 3:
            for copy in self.steps[self.at]:
                copy.start()

    def finish(self):
        while self.at <= 3:
            self.advance()


def row_vector(table, row, start, count):
    return jnp.concatenate([table[start + k, row : row + 1, :] for k in range(count)], axis=1)


def build_table(small, table):
    lane = lax.broadcasted_iota(jnp.int32, (8, LANES), 1)
    for q in range(SMALL_SHARDS // 4):
        rows = [small[4 * q + j, 64:80, :].astype(F32)[:8] for j in range(4)]
        one = pltpu.roll(rows[1], 96, 1)
        two = pltpu.roll(rows[2], 64, 1)
        three = pltpu.roll(rows[3], 32, 1)
        table[3 * q] = jnp.where(lane < 96, rows[0], one)
        table[3 * q + 1] = jnp.where(lane < 64, one, two)
        table[3 * q + 2] = jnp.where(lane < 32, two, three)


def put_rows(target, start, vector, count):
    width = vector.shape[1] // count
    for k in range(count):
        target[start + k : start + k + 1, :] = vector[:, k * width : (k + 1) * width]


def fold(values):
    return jnp.sum(values.reshape(-1, 8, values.shape[-1]), axis=0)


def excite_pick(shards, k):
    deep = GATE // shards
    line = lax.broadcasted_iota(jnp.int32, (GATE, shards * 16), 0)
    column = lax.broadcasted_iota(jnp.int32, (GATE, shards * 16), 1)
    wanted = (line // deep) * 16 + k * deep + lax.rem(line, deep)
    return (column == wanted).astype(F32).astype(BF16)


def excite_weights(small, block):
    shards = small.shape[0]
    rows = small[:, 32 * block + 16 : 32 * block + 32].reshape(shards * 16, LANES)
    parts = [matmul(excite_pick(shards, k), rows) for k in range(MID // LANES)]
    return jnp.concatenate(parts, axis=1).astype(BF16)


SMALL_SHARDS = 32
TABLE = ((2 * MID + D) // LANES + 1, 8, LANES)


STAGES = (
    (
        "ina0", "small", "inb0", "mida0", "@dpad", "@fpad", "ina0", "midb0", "small", "ina0", "midc0", "inb0",
        "small", "ina0", "out0", "mida0", "inb0", "small", "ina0", "midb0", "mida0", "ina1", "small", "inb0",
        "inb1", "midc0", "midb0", "mida1", "inb0", "@first", "midb1", "mida0", "midc0", "out0", "@near1", "mida0",
        "midc1", "midb0", "ina1", "inb1", "@far1", "midb0", "midc0", "out0", "ina1", "mida1", "@second", "inb1",
        "@swap", "@excite", "midc0", "midb1", "@third", "out0", "ina1", "mida1", "midc1", "@near2", "out0", "ina1",
        "inb1", "midb1", "@far2", "mida1", "midc1", "@fourth", "inb1", "mida1", "midb1", "@near3", "midc1",
        "@far3", "midb1", "@fifth", "midc1",
    ),
    (
        "out1", "@dpad", "@fpad", "@first", "cls", "@near1", "out1", "@far1", "cls", "@second", "@swap", "out1",
        "@excite", "cls", "@third", "out1", "@near2", "cls", "@far2", "out1", "@fourth", "cls", "@near3", "@far3",
        "@fifth",
    ),
)
JOBS = tuple(tuple(dict.fromkeys(item for item in order if item[0] != "@")) for order in STAGES)


def forward_kernel(n_seg, n_clip, block, jobs, plan, *refs):
    refs = list(refs)

    def pop(count=1):
        taken = refs[:count]
        del refs[:count]
        return taken if count != 1 else taken[0]

    last = block == 1
    x_hbm, mask, following, table_in = pop(4)
    shards = dict(zip(jobs, [pop() for _ in jobs]))
    given = dict(zip(plan, [pop() for _ in plan]))
    wholes = dict(zip(jobs, [pop() for _ in jobs]))
    h1_out, low_out, gate_out, mix_out, f_out, h2_out, a2_out, h3_out = pop(8)
    out_hbm, table_out, st1, st2, st3 = pop(5)
    xv, w_in, w_mid, w_out, small = pop(5)
    h1v, a1v, lowv, rv, edge, dpad, mixv, gatev, fpad, h2v, a2v, h3v = pop(12)
    wide_sum, wide_square, w_exp = pop(3)
    sums = [pop(4) for _ in range(3)]
    pooled = pop() if last else None
    send_sem, recv_sem = pop(2)
    links = Links(n_seg, n_clip, send_sem, recv_sem)
    frames = xv.shape[1]
    table = table_in if last else table_out
    outgoing = []

    def send_out(source, target):
        copy = links.local(source, target)
        copy.start()
        outgoing.append(copy)

    links.meet()
    load_x = links.local(x_hbm, xv)
    load_x.start()
    gathers = {name: Gather(links, shards[name], wholes[name]) for name in jobs}

    targets = {"out%d" % block: w_out, "small": small}
    for kind, target, count in (("in", w_in, 2), ("mid", w_mid, 3)):
        rows = target.shape[0] // SMALL_SHARDS
        size = rows // count
        wide = target.reshape(SMALL_SHARDS, rows, MID)
        for k, name in enumerate(piece_names(kind, block, count)):
            targets[name] = wide.at[:, k * size : (k + 1) * size]
    loads = {}

    def load(name):
        source = wholes[name] if name in gathers else given[name]
        loads[name] = links.local(source.reshape(targets[name].shape), targets[name])
        loads[name].start()

    def push(name):
        if gathers[name].at <= 3:
            gathers[name].advance()
            if gathers[name].at > 3 and name in targets:
                load(name)

    def need(*names):
        for name in names:
            while name not in loads:
                push(name)
        for name in names:
            loads[name].wait()

    for name in weight_names(block):
        if name not in gathers:
            load(name)
    table = table_in if last else table_out
    half = MID // LANES

    def norm(index, tot, columns, start, out):
        live_rows = table[TABLE[0] - 1, 0:1, 0:1]
        mean = jnp.concatenate([tot[k : k + 1] for k in range(4)], axis=1) / live_rows
        square = jnp.concatenate([tot[4 + k : 5 + k] for k in range(4)], axis=1) / live_rows
        inv = lax.rsqrt(square - mean * mean + NORM_EPS)
        out[0:1, :] = mean
        out[1:2, :] = inv
        gain = row_vector(table, 2 * block, start, columns // LANES)
        shift = row_vector(table, 2 * block + 1, start, columns // LANES)
        scale = gain * inv
        return scale, shift - mean * scale

    def masked_sums(values):
        shaped = values.reshape(-1, frames, values.shape[-1])
        masked = shaped * mask[...][None]
        return fold(masked), fold(masked * shaped)

    zeros = jnp.zeros((8, MID), F32)
    kept = {}

    def first(i, carry):
        part = matmul(xv[pl.ds(GRID * i, GRID)].reshape(GRID * frames, D), w_in[...])
        h1v[pl.ds(GRID * i, GRID)] = part.reshape(GRID, frames, MID)
        one, two = masked_sums(part)
        return (carry[0] + one, carry[1] + two)

    def put_sums(index, one, two):
        stat = sums[index][0]
        put_rows(stat, 0, jnp.sum(one, axis=0, keepdims=True), 4)
        put_rows(stat, 4, jnp.sum(two, axis=0, keepdims=True), 4)
        return stat

    def stage_dpad():
        dpad[...] = jnp.zeros_like(dpad)

    def stage_fpad():
        fpad[...] = jnp.zeros_like(fpad)
        if last:
            table_out[...] = table_in[...]
        else:
            table_out[...] = jnp.zeros_like(table_out)

    def stage_first():
        need(*piece_names("in", block, 2))
        load_x.wait()
        stat = put_sums(0, *lax.fori_loop(0, GRID, first, (zeros, zeros)))
        present = HW * jnp.sum(mask[:, :LANES], axis=0, keepdims=True)
        stat[8:16, :] = jnp.broadcast_to(present, (8, LANES))
        send_out(h1v, h1_out)

    def stage_near1():
        kept["rest"] = links.sum_near(*sums[0])

    def stage_far1():
        need("small")
        total = kept["rest"]()
        if not last:
            build_table(small, table_out)
            table_out[TABLE[0] - 1] = total[8:16]
        kept["one"] = norm(0, total, MID, 0, st1)

    def second(i, carry):
        for j in range(GRID):
            y = h1v[GRID * i + j] * kept["one"][0] + kept["one"][1]
            a = y * jax.nn.sigmoid(y)
            a1v[GRID * i + j] = a
            lowv[GRID * i + j] = a.astype(BF16)
        part = matmul(lowv[pl.ds(GRID * i, GRID)].reshape(GRID * frames, MID), kept["red"])
        rv[pl.ds(GRID * i, GRID)] = part.astype(BF16).reshape(GRID, frames, GATE)
        return carry

    def stage_second():
        w_exp[...] = excite_weights(small, block)
        kept["red"] = small[:, 32 * block : 32 * block + 16].reshape(MID, GATE)
        lax.fori_loop(0, GRID, second, 0)
        send_out(lowv, low_out)
        kept["swap"] = links.remote(links.take(1), rv, edge, links.other)
        kept["swap"].start()

    row = lax.rem(lax.broadcasted_iota(jnp.int32, (frames, GATE), 0), 8)

    def change(i, carry):
        for j in range(GRID):
            now = rv[GRID * i + j].astype(F32)
            rest = edge[GRID * i + j].astype(F32)
            later = jnp.where(row < 7, pltpu.roll(now, frames - 1, 0), pltpu.roll(rest, 7, 0))
            dpad[i + 1, j + 1] = following[...] * (later - now)
        return carry

    def stage_swap():
        kept["swap"].wait()
        lax.fori_loop(0, GRID, change, 0)

    def excite(i, carry):
        for j in range(GRID):
            total = jnp.zeros((frames, GATE), F32)
            for k in range(9):
                total = total + dpad[i + k // 3, j + k % 3]
            mixv[GRID * i + j] = (dpad[i + 1, j + 1] + total / 9.0).astype(BF16)
        e = matmul(mixv[pl.ds(GRID * i, GRID)].reshape(GRID * frames, GATE), w_exp[...])
        e = e.reshape(GRID, frames, MID)
        for j in range(GRID):
            gate = jax.nn.sigmoid(e[j])
            gatev[GRID * i + j] = gate.astype(BF16)
            fpad[i + 1, j + 1] = (a1v[GRID * i + j] * (1.0 + gate)).astype(BF16)
        return carry

    def stage_excite():
        lax.fori_loop(0, GRID, excite, 0)
        send_out(mixv, mix_out)
        send_out(gatev, gate_out)
        send_out(fpad.at[pl.ds(1, GRID), pl.ds(1, GRID)], f_out)

    def third(i, carry):
        part = None
        for k in range(9):
            window = fpad[i + k // 3, pl.ds(k % 3, GRID)].reshape(GRID * frames, MID)
            term = matmul(window, w_mid[k * MID : (k + 1) * MID])
            part = term if part is None else part + term
        h2v[pl.ds(GRID * i, GRID)] = part.reshape(GRID, frames, MID)
        one, two = masked_sums(part)
        return (carry[0] + one, carry[1] + two)

    def stage_third():
        need(*piece_names("mid", block, 3))
        put_sums(1, *lax.fori_loop(0, GRID, third, (zeros, zeros)))
        send_out(h2v, h2_out)

    def stage_near2():
        kept["rest"] = links.sum_near(*sums[1])

    def stage_far2():
        kept["two"] = norm(1, kept["rest"](), MID, half, st2)
        wide_sum[...] = jnp.zeros_like(wide_sum)
        wide_square[...] = jnp.zeros_like(wide_square)

    def fourth(i, carry):
        for j in range(GRID):
            y = h2v[GRID * i + j] * kept["two"][0] + kept["two"][1]
            a2v[GRID * i + j] = (y * jax.nn.sigmoid(y)).astype(BF16)
        rows = a2v[pl.ds(GRID * i, GRID)].reshape(GRID * frames, MID)
        for k in range(4):
            part = matmul(rows, w_out[:, k * MID : (k + 1) * MID])
            h3v[pl.ds(GRID * i, GRID), :, k * MID : (k + 1) * MID] = part.astype(BF16).reshape(
                GRID, frames, MID
            )
            one, two = masked_sums(part)
            wide_sum[:, k * MID : (k + 1) * MID] += one
            wide_square[:, k * MID : (k + 1) * MID] += two
        return carry

    def stage_fourth():
        need("out%d" % block)
        lax.fori_loop(0, GRID, fourth, 0)
        put_sums(2, wide_sum[...], wide_square[...])
        send_out(a2v, a2_out)
        send_out(h3v, h3_out)

    def stage_near3():
        kept["rest"] = links.sum_near(*sums[2])

    def stage_far3():
        kept["three"] = norm(2, kept["rest"](), D, 2 * half, st3)
        if last:
            pooled[...] = jnp.zeros_like(pooled)

    def fifth(p, carry):
        for k in range(4):
            span = slice(k * MID, (k + 1) * MID)
            scale, shift = kept["three"]
            pre = h3v[p, :, span].astype(F32) * scale[:, span] + shift[:, span]
            pre = pre + xv[p, :, span].astype(F32)
            value = pre * jax.nn.sigmoid(pre)
            if last:
                pooled[:, span] += value * mask[...]
            else:
                xv[p, :, span] = value.astype(BF16)
        return carry

    def stage_fifth():
        lax.fori_loop(0, HW, fifth, 0)
        send_out(pooled if last else xv, out_hbm)

    stages = {
        "dpad": stage_dpad,
        "fpad": stage_fpad,
        "first": stage_first,
        "near1": stage_near1,
        "far1": stage_far1,
        "second": stage_second,
        "swap": stage_swap,
        "excite": stage_excite,
        "third": stage_third,
        "near2": stage_near2,
        "far2": stage_far2,
        "fourth": stage_fourth,
        "near3": stage_near3,
        "far3": stage_far3,
        "fifth": stage_fifth,
    }
    for item in STAGES[block]:
        if item[0] == "@":
            with jax.named_scope(item[1:]):
                stages[item[1:]]()
        elif item in gathers:
            push(item)
    for name in jobs:
        gathers[name].finish()
    for copy in outgoing:
        copy.wait()


def forward_block(block, x, mask, following, table, shards, given):
    n_seg = lax.axis_size("seg")
    n_clip = lax.axis_size("clip")
    cells, frames, width = x.shape
    jobs = list(shards)
    plan = list(given)
    any_spec = pl.BlockSpec(memory_space=pl.ANY)
    vmem = pl.BlockSpec(memory_space=pltpu.VMEM)
    depth = n_clip // 4

    def grid_shape(columns):
        return (cells, frames, columns)

    last = block == 1
    devices = n_seg * n_clip
    outs = [jax.ShapeDtypeStruct((devices * shards[n].shape[0], shards[n].shape[1]), BF16) for n in jobs]
    outs += [
        jax.ShapeDtypeStruct(grid_shape(MID), F32),
        jax.ShapeDtypeStruct(grid_shape(MID), BF16),
        jax.ShapeDtypeStruct(grid_shape(MID), BF16),
        jax.ShapeDtypeStruct(grid_shape(GATE), BF16),
        jax.ShapeDtypeStruct((GRID, GRID, frames, MID), BF16),
        jax.ShapeDtypeStruct(grid_shape(MID), F32),
        jax.ShapeDtypeStruct(grid_shape(MID), BF16),
        jax.ShapeDtypeStruct(grid_shape(D), BF16),
        jax.ShapeDtypeStruct((frames, D), F32) if last else jax.ShapeDtypeStruct(x.shape, BF16),
        jax.ShapeDtypeStruct(TABLE, F32),
        jax.ShapeDtypeStruct((8, MID), F32),
        jax.ShapeDtypeStruct((8, MID), F32),
        jax.ShapeDtypeStruct((8, D), F32),
    ]
    out_specs = [any_spec] * (len(jobs) + 9) + [vmem] * 4

    shapes = [(D, MID), (9 * MID, MID), (MID, D), (SMALL_SHARDS, 80, LANES)]
    scratch = [pltpu.VMEM(x.shape, BF16)]
    scratch += [pltpu.VMEM(s, BF16) for s in shapes]
    scratch += [
        pltpu.VMEM(grid_shape(MID), F32),
        pltpu.VMEM(grid_shape(MID), F32),
        pltpu.VMEM(grid_shape(MID), BF16),
        pltpu.VMEM(grid_shape(GATE), BF16),
        pltpu.VMEM(grid_shape(GATE), BF16),
        pltpu.VMEM((GRID + 2, GRID + 2, frames, GATE), F32),
        pltpu.VMEM(grid_shape(GATE), BF16),
        pltpu.VMEM(grid_shape(MID), BF16),
        pltpu.VMEM((GRID + 2, GRID + 2, frames, MID), BF16),
        pltpu.VMEM(grid_shape(MID), F32),
        pltpu.VMEM(grid_shape(MID), BF16),
        pltpu.VMEM(grid_shape(D), BF16),
        pltpu.VMEM((8, D), F32),
        pltpu.VMEM((8, D), F32),
        pltpu.VMEM((GATE, MID), BF16),
    ]
    for shape in ((16, LANES), (8, LANES), (8, MID)):
        scratch += sum_scratch(n_seg, n_clip, shape)
    if last:
        scratch.append(pltpu.VMEM((frames, D), F32))
    count = 4 * (n_seg * 4 + depth) + len(jobs) * (depth + 4) + 32
    scratch += [pltpu.SemaphoreType.DMA((count,)), pltpu.SemaphoreType.DMA((count,))]
    results = pl.pallas_call(
        functools.partial(forward_kernel, n_seg, n_clip, block, jobs, plan),
        out_shape=outs,
        in_specs=[any_spec, vmem, vmem, vmem] + [any_spec] * (len(jobs) + len(plan)),
        out_specs=out_specs,
        scratch_shapes=scratch,
        compiler_params=pltpu.CompilerParams(
            collective_id=30 + block, has_side_effects=True, vmem_limit_bytes=60 * 1024 * 1024
        ),
        name="forward_block",
    )(x, mask, following, table, *[shards[n] for n in jobs], *[given[n] for n in plan])
    wholes = dict(zip(jobs, results[: len(jobs)]))
    return wholes, results[len(jobs) :]


def backward_kernel(n_seg, n_clip, block, *refs):
    refs = list(refs)

    def pop(count=1):
        taken = refs[:count]
        del refs[:count]
        return taken if count != 1 else taken[0]

    last = block == 1
    h3_hbm, x_hbm, d_in, h2_hbm, h1_hbm, gate_hbm = pop(6)
    in_a, in_b, mid_a, mid_b, mid_c, out_hbm, small_hbm = pop(7)
    table, st1, st2, st3, mask, present, following = pop(7)
    dh3_out, dh2_out, de_out, dr_out, dh1_out, dx_out, norm_grads = pop(7)
    dv, h3v, xv, h2v, h1v, gatev, dyv, pad2, dsv, edge, pad_s, pad_e = pop(12)
    drv, dh1v, w_in, w_mid, w_out, small, w_exp = pop(7)
    sum_gain, sum_shift = pop(2)
    sums = [pop(4) for _ in range(3)]
    send_sem, recv_sem = pop(2)
    links = Links(n_seg, n_clip, send_sem, recv_sem)
    frames = xv.shape[1]
    outgoing = []

    def send_out(source, target):
        copy = links.local(source, target)
        copy.start()
        outgoing.append(copy)

    def load(source, target):
        copy = links.local(source.reshape(target.shape), target)
        copy.start()
        return copy

    streams = [(h3_hbm, h3v), (x_hbm, xv)]
    if not last:
        streams.append((d_in, dv))
    wide_base = links.take(len(streams) * GRID)

    def wide_copies(i):
        rows = pl.ds(GRID * i, GRID)
        return [
            pltpu.make_async_copy(source.at[rows], target.at[rows], links.recv_sem.at[wide_base + GRID * k + i])
            for k, (source, target) in enumerate(streams)
        ]

    for i in range(GRID):
        for copy in wide_copies(i):
            copy.start()
    loads_two = [load(out_hbm, w_out), load(h2_hbm, h2v)]
    loads_three = [load(h1_hbm, h1v), load(gate_hbm, gatev), load(small_hbm, small)]
    loads_four = []
    for parts, target, waits in (
        ((mid_a, mid_b, mid_c), w_mid, loads_three),
        ((in_a, in_b), w_in, loads_four),
    ):
        rows = target.shape[0] // SMALL_SHARDS
        size = rows // len(parts)
        wide = target.reshape(SMALL_SHARDS, rows, MID)
        for k, source in enumerate(parts):
            waits.append(load(source, wide.at[:, k * size : (k + 1) * size]))
    links.meet()
    live_rows = table[TABLE[0] - 1, 0:1, 0:1]
    half = MID // LANES
    pad2[...] = jnp.zeros_like(pad2)
    pad_s[...] = jnp.zeros_like(pad_s)
    pad_e[...] = jnp.zeros_like(pad_e)
    sum_gain[...] = jnp.zeros_like(sum_gain)
    sum_shift[...] = jnp.zeros_like(sum_shift)

    def vectors(start, columns, stats):
        gain = row_vector(table, 2 * block, start, columns // LANES)
        shift = row_vector(table, 2 * block + 1, start, columns // LANES)
        return gain, shift, stats[0:1, :], stats[1:2, :]

    def totals(index, start, columns, gain_rows, shift_rows):
        stat = sums[index][0]
        put_rows(stat, 0, jnp.sum(gain_rows, axis=0, keepdims=True), 4)
        put_rows(stat, 4, jnp.sum(shift_rows, axis=0, keepdims=True), 4)
        tot = links.all_sum(*sums[index])
        gain = jnp.concatenate([tot[k : k + 1] for k in range(4)], axis=1)
        shift = jnp.concatenate([tot[4 + k : 5 + k] for k in range(4)], axis=1)
        put_rows(norm_grads, start, gain, columns // LANES)
        put_rows(norm_grads, 24 + start, shift, columns // LANES)
        return gain / live_rows, shift / live_rows

    def slope_of(values):
        sig = jax.nn.sigmoid(values)
        return sig, sig * (1.0 + values * (1.0 - sig))

    def dot_t(left, right):
        return lax.dot_general(left, right, (((1,), (1,)), ((), ())), preferred_element_type=F32)

    gain3, shift3, mean3, inv3 = vectors(2 * half, D, st3)

    def first_rows(i, carry):
        for copy in wide_copies(i):
            copy.wait()
        return lax.fori_loop(GRID * i, GRID * i + GRID, first, carry)

    def first(p, carry):
        for k in range(4):
            span = slice(k * MID, (k + 1) * MID)
            n = (h3v[p, :, span].astype(F32) - mean3[:, span]) * inv3[:, span]
            pre = n * gain3[:, span] + shift3[:, span] + xv[p, :, span].astype(F32)
            grad = d_in[:, span] if last else dv[p, :, span]
            grad = grad * slope_of(pre)[1]
            dv[p, :, span] = grad
            sum_gain[:, span] += fold(grad * n)
            sum_shift[:, span] += fold(grad)
        return carry

    lax.fori_loop(0, GRID, first_rows, 0)
    part_gain, part_shift = totals(0, 2 * half, D, sum_gain[...], sum_shift[...])
    factor3 = gain3 * inv3
    for copy in loads_two:
        copy.wait()
    gain2, shift2, mean2, inv2 = vectors(half, MID, st2)
    zeros = jnp.zeros((8, MID), F32)

    def second(i, carry):
        for j in range(GRID):
            p = GRID * i + j
            for k in range(4):
                span = slice(k * MID, (k + 1) * MID)
                n = (h3v[p, :, span].astype(F32) - mean3[:, span]) * inv3[:, span]
                rest = mask[...] * (part_shift[:, span] + n * part_gain[:, span])
                h3v[p, :, span] = (factor3[:, span] * (dv[p, :, span] - rest)).astype(BF16)
        d_a = dot_t(h3v[pl.ds(GRID * i, GRID)].reshape(GRID * frames, D), w_out[...])
        d_a = d_a.reshape(GRID, frames, MID)
        one, two = carry
        for j in range(GRID):
            n = (h2v[GRID * i + j] - mean2) * inv2
            grad = d_a[j] * slope_of(n * gain2 + shift2)[1]
            dyv[GRID * i + j] = grad
            one = one + fold(grad * n)
            two = two + fold(grad)
        return (one, two)

    one, two = lax.fori_loop(0, GRID, second, (zeros, zeros))
    send_out(h3v, dh3_out)
    part_gain2, part_shift2 = totals(1, half, MID, one, two)
    factor2 = gain2 * inv2

    def third(i, carry):
        for j in range(GRID):
            p = GRID * i + j
            n = (h2v[p] - mean2) * inv2
            rest = mask[...] * (part_shift2 + n * part_gain2)
            pad2[i + 1, j + 1] = (factor2 * (dyv[p] - rest)).astype(BF16)
        return carry

    lax.fori_loop(0, GRID, third, 0)
    send_out(pad2.at[pl.ds(1, GRID), pl.ds(1, GRID)], dh2_out)
    for copy in loads_three:
        copy.wait()
    w_exp[...] = excite_weights(small, block)
    red = small[:, 32 * block : 32 * block + 16].reshape(MID, GATE)
    gain1, shift1, mean1, inv1 = vectors(0, MID, st1)

    def fourth(i, carry):
        part = None
        for k in range(9):
            window = pad2[i + 2 - k // 3, pl.ds(2 - k % 3, GRID)].reshape(GRID * frames, MID)
            term = dot_t(window, w_mid[k * MID : (k + 1) * MID])
            part = term if part is None else part + term
        part = part.reshape(GRID, frames, MID)
        for j in range(GRID):
            p = GRID * i + j
            y = (h1v[p] - mean1) * inv1 * gain1 + shift1
            a = y * jax.nn.sigmoid(y)
            gate = gatev[p].astype(F32)
            dyv[p] = part[j] * (1.0 + gate)
            gatev[p] = (part[j] * a * gate * (1.0 - gate)).astype(BF16)
        d_s = dot_t(gatev[pl.ds(GRID * i, GRID)].reshape(GRID * frames, MID), w_exp[...])
        d_s = d_s.astype(BF16).reshape(GRID, frames, GATE)
        dsv[pl.ds(GRID * i, GRID)] = d_s
        for j in range(GRID):
            pad_s[i + 1, j + 1] = d_s[j].astype(F32)
        return carry

    lax.fori_loop(0, GRID, fourth, 0)
    swap = links.remote(links.take(1), dsv, edge, links.other)
    swap.start()
    send_out(gatev, de_out)
    swap.wait()

    def unpack(i, carry):
        for j in range(GRID):
            pad_e[i + 1, j + 1] = edge[GRID * i + j].astype(F32)
        return carry

    lax.fori_loop(0, GRID, unpack, 0)
    row = lax.rem(lax.broadcasted_iota(jnp.int32, (frames, GATE), 0), 8)
    from_other = links.seg.astype(F32)

    def fifth(i, carry):
        for j in range(GRID):
            near = jnp.zeros((frames, GATE), F32)
            far = jnp.zeros((frames, GATE), F32)
            for k in range(9):
                near = near + pad_s[i + k // 3, j + k % 3]
                far = far + pad_e[i + k // 3, j + k % 3]
            near = pad_s[i + 1, j + 1] + near / 9.0
            far = (pad_e[i + 1, j + 1] + far / 9.0) * from_other
            earlier = jnp.where(row > 0, pltpu.roll(near, 1, 0), pltpu.roll(far, frames - 7, 0))
            drv[GRID * i + j] = (present[...] * earlier - following[...] * near).astype(BF16)
        d_a = dot_t(drv[pl.ds(GRID * i, GRID)].reshape(GRID * frames, GATE), red)
        d_a = d_a.reshape(GRID, frames, MID)
        one, two = carry
        for j in range(GRID):
            p = GRID * i + j
            n = (h1v[p] - mean1) * inv1
            grad = (dyv[p] + d_a[j]) * slope_of(n * gain1 + shift1)[1]
            dyv[p] = grad
            one = one + fold(grad * n)
            two = two + fold(grad)
        return (one, two)

    one, two = lax.fori_loop(0, GRID, fifth, (zeros, zeros))
    send_out(drv, dr_out)
    part_gain1, part_shift1 = totals(2, 0, MID, one, two)
    factor1 = gain1 * inv1
    for copy in loads_four:
        copy.wait()

    def sixth(i, carry):
        for j in range(GRID):
            p = GRID * i + j
            n = (h1v[p] - mean1) * inv1
            rest = mask[...] * (part_shift1 + n * part_gain1)
            dh1v[p] = (factor1 * (dyv[p] - rest)).astype(BF16)
        rows = dh1v[pl.ds(GRID * i, GRID)].reshape(GRID * frames, MID)
        for k in range(4):
            span = slice(k * MID, (k + 1) * MID)
            part = dot_t(rows, w_in[span, :])
            dv[pl.ds(GRID * i, GRID), :, span] += part.reshape(GRID, frames, MID)
        dx_copy(i).start()
        return carry

    dx_base = links.take(GRID)

    def dx_copy(i):
        rows = pl.ds(GRID * i, GRID)
        return pltpu.make_async_copy(dv.at[rows], dx_out.at[rows], links.recv_sem.at[dx_base + i])

    lax.fori_loop(0, GRID, sixth, 0)
    send_out(dh1v, dh1_out)
    for i in range(GRID):
        dx_copy(i).wait()
    for copy in outgoing:
        copy.wait()


def backward_block(block, h3, x, d_in, h2, h1, gate, weights, table, stats, masks):
    n_seg = lax.axis_size("seg")
    n_clip = lax.axis_size("clip")
    cells, frames, width = x.shape
    any_spec = pl.BlockSpec(memory_space=pl.ANY)
    vmem = pl.BlockSpec(memory_space=pltpu.VMEM)
    last = block == 1

    def grid_shape(columns):
        return (cells, frames, columns)

    outs = [
        jax.ShapeDtypeStruct(grid_shape(D), BF16),
        jax.ShapeDtypeStruct((GRID, GRID, frames, MID), BF16),
        jax.ShapeDtypeStruct(grid_shape(MID), BF16),
        jax.ShapeDtypeStruct(grid_shape(GATE), BF16),
        jax.ShapeDtypeStruct(grid_shape(MID), BF16),
        jax.ShapeDtypeStruct(grid_shape(D), F32),
        jax.ShapeDtypeStruct((48, LANES), F32),
    ]
    scratch = [
        pltpu.VMEM(grid_shape(D), F32),
        pltpu.VMEM(grid_shape(D), BF16),
        pltpu.VMEM(grid_shape(D), BF16),
        pltpu.VMEM(grid_shape(MID), F32),
        pltpu.VMEM(grid_shape(MID), F32),
        pltpu.VMEM(grid_shape(MID), BF16),
        pltpu.VMEM(grid_shape(MID), F32),
        pltpu.VMEM((GRID + 2, GRID + 2, frames, MID), BF16),
        pltpu.VMEM(grid_shape(GATE), BF16),
        pltpu.VMEM(grid_shape(GATE), BF16),
        pltpu.VMEM((GRID + 2, GRID + 2, frames, GATE), F32),
        pltpu.VMEM((GRID + 2, GRID + 2, frames, GATE), F32),
        pltpu.VMEM(grid_shape(GATE), BF16),
        pltpu.VMEM(grid_shape(MID), BF16),
        pltpu.VMEM((D, MID), BF16),
        pltpu.VMEM((9 * MID, MID), BF16),
        pltpu.VMEM((MID, D), BF16),
        pltpu.VMEM((SMALL_SHARDS, 80, LANES), BF16),
        pltpu.VMEM((GATE, MID), BF16),
        pltpu.VMEM((8, D), F32),
        pltpu.VMEM((8, D), F32),
    ]
    for shape in ((8, MID), (8, LANES), (8, LANES)):
        scratch += sum_scratch(n_seg, n_clip, shape)
    count = 3 * (n_seg * 4 + n_clip // 4) + 64
    scratch += [pltpu.SemaphoreType.DMA((count,)), pltpu.SemaphoreType.DMA((count,))]
    d_spec = vmem if last else any_spec
    return pl.pallas_call(
        functools.partial(backward_kernel, n_seg, n_clip, block),
        out_shape=outs,
        in_specs=[any_spec, any_spec, d_spec] + [any_spec] * 10 + [vmem] * 7,
        out_specs=[any_spec] * 6 + [vmem],
        scratch_shapes=scratch,
        compiler_params=pltpu.CompilerParams(
            collective_id=40 + block, has_side_effects=True, vmem_limit_bytes=62 * 1024 * 1024
        ),
        name="backward_block",
    )(h3, x, d_in, h2, h1, gate, *weights, table, *stats, *masks)


class Scatter:
    def __init__(self, links, grad, rows, buffers, finish):
        self.links = links
        self.grad = grad
        self.rows = rows
        self.one, self.two, self.three, self.four = buffers
        self.finish = finish
        self.depth = links.outer
        self.base = links.take(self.depth + 3)
        self.at = -1

    def copies(self):
        links, base, depth = self.links, self.base, self.depth
        if self.at == 0:
            source = self.grad.at[1 - links.seg, :, :, self.rows]
            return [links.remote(base, source, self.one, links.other)]
        if self.at == 1:
            found = []
            for k in range(2):
                source = self.one.at[:, links.jump * (1 - links.first) + links.step * k]
                found.append(links.remote(base + 1 + k, source, self.two.at[:, k], links.across_first))
            return found
        if self.at == 2:
            source = self.two.at[:, 1 - links.second]
            return [links.remote(base + 3, source, self.three, links.across_second)]
        found = []
        for i in range(1, depth):
            source = self.three.at[lax.rem(links.group + i, depth)]
            found.append(links.remote(base + 3 + i, source, self.four.at[i - 1], links.far_peer(i)))
        return found

    def add(self):
        links, depth = self.links, self.depth
        one, two, three, four = self.one, self.two, self.three, self.four
        if self.at == 0:

            def add_one(i, carry):
                z = i // 4
                w = lax.rem(i, 4)
                total = one[z, w].astype(F32) + self.grad[links.seg, z, w, self.rows].astype(F32)
                one[z, w] = total.astype(BF16)
                return carry

            lax.fori_loop(0, 4 * depth, add_one, 0)
        elif self.at == 1:

            def add_two(i, carry):
                z = i // 2
                k = lax.rem(i, 2)
                kept = one[z, links.jump * links.first + links.step * k]
                two[z, k] = (two[z, k].astype(F32) + kept.astype(F32)).astype(BF16)
                return carry

            lax.fori_loop(0, 2 * depth, add_two, 0)
        elif self.at == 2:

            def add_three(z, carry):
                three[z] = (three[z].astype(F32) + two[z, links.second].astype(F32)).astype(BF16)
                return carry

            lax.fori_loop(0, depth, add_three, 0)
        else:
            total = three[links.group].astype(F32)
            for i in range(1, depth):
                total = total + four[i - 1].astype(F32)
            self.finish(total)

    def advance(self):
        if self.at > 3:
            return
        if self.at >= 0:
            for copy in self.copies():
                copy.wait()
            self.add()
        self.at += 1
        if self.at <= 3:
            for copy in self.copies():
                copy.start()


SCATTERED = {
    "cls": (64, 2 * LANES),
    "out1": (16, D),
    "mida1": (48, MID),
    "midb1": (48, MID),
    "midc1": (48, MID),
    "in1": (64, MID),
    "out0": (16, D),
    "mida0": (48, MID),
    "midb0": (48, MID),
    "midc0": (48, MID),
    "in0": (64, MID),
    "small": (80, LANES),
}


FLAT_MID = 256
FLAT_OUT = 832
FLAT_SMALL = 1088
FLAT_ROWS = 1122
FLAT_CLS = 2243
ORDER = (
    "cls", "@out1a", "@out1b", "out1", "cls", "@in1a", "in1", "@in1b", "out1", "cls", "@mid1a", "in1", "@mid1b",
    "mida1", "midb1", "midc1", "@mid1c", "cls", "out1", "mida1", "@small1", "@in0a", "in0", "in1", "@in0b", "cls",
    "out1", "midb1", "midc1", "@mid0a", "mida1", "@mid0b", "mida0", "midb0", "midc0", "out1", "in1", "@mid0c",
    "midb1", "@small0", "small", "in0", "@out0a", "midc1", "mida1", "in1", "@out0b", "out0", "midb1", "mida0",
    "mida1", "out0", "in0", "midc1", "midb1", "mida0", "midc1", "midb0", "out0", "in0", "mida0", "midc0", "midb0",
    "in0", "out0", "small", "mida0", "midc0", "midb0", "small", "out0", "midc0", "small", "midb0", "midc0",
    "small",
)


ORDER_FIRST = "out1a"


def gradient_kernel(n_seg, n_clip, *refs):
    refs = list(refs)

    def pop(count=1):
        taken = refs[:count]
        del refs[:count]
        return taken if count != 1 else taken[0]

    sources = [pop(10) for _ in range(2)]
    cls_hbm, norm_rows_in, bias = pop(3)
    flat, tail = pop(2)
    big3, bigx, mid_a2, mid_d2, mid_d1, mid_low, mid_de, thin_dr, thin_s, fpad = pop(10)
    g_in, g_mid, g_out, g_small, g_cls, squares, turned = pop(7)
    sums = pop(4)
    buffers = {name: pop(4) for name in SCATTERED}
    send_sem, recv_sem = pop(2)
    links = Links(n_seg, n_clip, send_sem, recv_sem)
    cells, frames = bigx.shape[0], bigx.shape[1]
    rows_all = cells * frames
    devices = SMALL_SHARDS

    def load(source, target):
        copy = links.local(source.reshape(target.shape), target)
        copy.start()
        return copy

    interior = fpad.at[pl.ds(1, GRID), pl.ds(1, GRID)]
    names = ("x", "d1", "f", "d2", "a2", "d3", "low", "dr", "s", "de")
    targets = dict(zip(names, (bigx, mid_d1, interior, mid_d2, mid_a2, big3, mid_low, thin_dr, thin_s, mid_de)))
    hbm = [dict(zip(names, source)) for source in sources]

    def fetch(block, *keys):
        return [load(hbm[block][key], targets[key]) for key in keys]

    operands = {
        "out": ("a2", "d3"),
        "in": ("x", "d1"),
        "mid": ("f", "d2"),
        "small": ("low", "dr", "s", "de"),
    }
    load_cls = load(cls_hbm, g_cls)
    waits = {"out": fetch(1, *operands["out"])}
    fpad[...] = jnp.zeros_like(fpad)
    links.meet()
    squares[...] = jnp.zeros_like(squares)

    def folded(ref, rows):
        return ref.reshape(n_seg, links.outer, 4, rows, ref.shape[-1])

    grads = {"cls": g_cls, "small": g_small}
    jobs = {}

    def put(block, first, values, stride=1):
        count = values.shape[0]
        if block == 0:
            flat[pl.ds(first, count, stride), :] = values
        else:
            turned[pl.ds(first + 8, count, stride), :] = pltpu.roll(values, 64, 1)

    def put_small(total):
        lane = lax.broadcasted_iota(jnp.int32, (1, LANES), 1)
        for block in range(2):
            rows = total[32 * block : 32 * block + 32]
            put(block, FLAT_SMALL, rows[:16])
            for k in range(4):
                put(block, FLAT_SMALL + 16 + k, rows[16 + 4 * k : 20 + 4 * k], 4)
            gain = total[64 + 2 * block : 65 + 2 * block]
            shift = pltpu.roll(total[65 + 2 * block : 66 + 2 * block], 96, 1)
            put(block, FLAT_SMALL + 32, jnp.where(lane < 96, gain, shift))
            put(block, FLAT_SMALL + 33, shift)
        flat[FLAT_CLS + 87 : FLAT_CLS + 88, :] = total[68:69]

    def put_classifier(total):
        lane = lax.broadcasted_iota(jnp.int32, (1, LANES), 1)
        flat[FLAT_CLS:, :] = jnp.zeros_like(flat[FLAT_CLS:, :])
        for i in range(total.shape[0]):
            line, by = divmod(CLASSES * i, LANES)
            line += FLAT_CLS
            low, high = total[i : i + 1, :LANES], total[i : i + 1, LANES:]
            if by:
                low, high = pltpu.roll(low, by, 1), pltpu.roll(high, by, 1)
            here = lane >= by
            flat[line : line + 1, :] += jnp.where(here, low, 0.0)
            flat[line + 1 : line + 2, :] += jnp.where(here, high, low)
            if by + CLASSES - LANES > LANES:
                flat[line + 2 : line + 3, :] += jnp.where(here, 0.0, high)

    def make(name):
        kind = name[:-1] if name not in ("cls", "small") else name
        block = name[-1]
        rows, columns = SCATTERED[name]
        start = rows * "abc".index(kind[3]) if kind.startswith("mid") else 0
        ref = {"in": g_in, "out": g_out, "small": g_small, "cls": g_cls}.get(kind, g_mid)
        shard_rows = 3 * rows if kind.startswith("mid") else rows

        def finish(total):
            squares[:, :columns] += fold(total * total)
            if kind == "cls":
                put_classifier(total)
            elif kind == "small":
                put_small(total)
            else:
                lines = columns // LANES
                first = {"in": 0, "out": FLAT_OUT}.get(kind, FLAT_MID) + start * lines
                for k in range(lines):
                    put(int(block), first + k, total[:, k * LANES : (k + 1) * LANES], lines)

        jobs[name] = Scatter(links, folded(ref, shard_rows), pl.ds(start, rows), buffers[name], finish)

    for name in SCATTERED:
        make(name)

    def push(*wanted):
        for name in wanted:
            jobs[name].advance()

    def dot_tn(left, right):
        return lax.dot_general(left, right, (((0,), (0,)), ((), ())), preferred_element_type=F32)

    turn = 1 - links.seg

    def task_out(first, last):
        def body(k, carry):
            span = pl.ds(pl.multiple_of(k * MID, MID), MID)
            part = dot_tn(mid_a2[...].reshape(rows_all, MID), big3[:, :, span].reshape(rows_all, MID))
            g_out[:, span] = part.astype(BF16)
            return carry

        lax.fori_loop(first, last, body, 0)

    def task_in(first, last):
        def body(i, carry):
            k = i + turn * (3 - 2 * i)
            span = pl.ds(pl.multiple_of(k * MID, MID), MID)
            part = dot_tn(bigx[:, :, span].reshape(rows_all, MID), mid_d1[...].reshape(rows_all, MID))
            g_in[span, :] = part.astype(BF16)
            return carry

        lax.fori_loop(first, last, body, 0)

    def task_mid(first, last):
        def body(i, carry):
            k = i + turn * (8 - 2 * i)
            window = fpad[pl.ds(k // 3, GRID), pl.ds(lax.rem(k, 3), GRID)].reshape(rows_all, MID)
            part = dot_tn(window, mid_d2[...].reshape(rows_all, MID))
            g_mid[pl.ds(pl.multiple_of(k * MID, MID), MID), :] = part.astype(BF16)
            return carry

        lax.fori_loop(first, last, body, 0)

    def task_small(block):
        part = dot_tn(mid_low[...].reshape(rows_all, MID), thin_dr[...].reshape(rows_all, GATE))
        g_small[:, 32 * block : 32 * block + 16, :] = part.astype(BF16).reshape(devices, 16, LANES)
        part = dot_tn(thin_s[...].reshape(rows_all, GATE), mid_de[...].reshape(rows_all, MID)).astype(BF16)
        rows = jnp.zeros((devices * 16, LANES), F32)
        for k in range(MID // LANES):
            rows = rows + dot_tn(excite_pick(devices, k), part[:, k * LANES : (k + 1) * LANES])
        g_small[:, 32 * block + 16 : 32 * block + 32, :] = rows.astype(BF16).reshape(devices, 16, LANES)

    def run(piece):
        letter = piece[-1] if piece[-1] in "abc" else ""
        kind, block = piece[: len(piece) - 1 - len(letter)], int(piece[len(piece) - 1 - len(letter)])
        part = "abc".index(letter) if letter else 0
        if part == 0:
            for copy in waits[kind]:
                copy.wait()
            if block == 0 and kind != "small":
                for name in SCATTERED:
                    if name.startswith(kind) and name[-1] == "1":
                        while jobs[name].at < 1:
                            jobs[name].advance()
        if kind == "mid":
            task_mid(3 * part, 3 * part + 3)
        elif kind == "in":
            task_in(2 * part, 2 * part + 2)
        elif kind == "out":
            task_out(2 * part, 2 * part + 2)
        else:
            task_small(block)
        if block == 1 and part == {"mid": 2, "in": 1, "out": 1, "small": 0}[kind]:
            waits[kind] = fetch(0, *operands[kind])
        if block == 1 and piece == ORDER_FIRST:
            for other in ("in", "mid", "small"):
                waits[other] = fetch(1, *operands[other])

    g_small[:, 64:80, :] = norm_rows_in[...]
    load_cls.wait()
    for item in ORDER:
        if item[0] == "@":
            with jax.named_scope("product"):
                run(item[1:])
        else:
            push(item)
    for name in SCATTERED:
        while jobs[name].at <= 3:
            jobs[name].advance()
    lane = lax.broadcasted_iota(jnp.int32, (FLAT_ROWS, LANES), 1)
    now, before = turned[8 : 8 + FLAT_ROWS, :], turned[7 : 7 + FLAT_ROWS, :]
    old = flat[FLAT_SMALL + 33 : FLAT_SMALL + 34, :]
    flat[FLAT_ROWS - 1 : 2 * FLAT_ROWS - 1, :] = jnp.where(lane < 64, before, now)
    flat[FLAT_ROWS - 1 : FLAT_ROWS, :] = jnp.where(lane[:1] < 64, old, now[:1])
    total = jnp.sum(jnp.sum(squares[...], axis=0, keepdims=True), axis=1, keepdims=True)
    sums[0][0:8, :] = bias[...]
    sums[0][8:16, :] = jnp.broadcast_to(total, (8, LANES))
    tail[...] = links.all_sum(*sums)


def gradient_sums(sources, g_cls, norm_rows_in, bias):
    n_seg = lax.axis_size("seg")
    n_clip = lax.axis_size("clip")
    depth = n_clip // 4
    cells, frames, width = sources[0][0].shape
    any_spec = pl.BlockSpec(memory_space=pl.ANY)
    vmem = pl.BlockSpec(memory_space=pltpu.VMEM)

    def grid_shape(columns):
        return pltpu.VMEM((cells, frames, columns), BF16)

    outs = [(FLAT_CLS + 93, LANES), (16, LANES)]
    scratch = [grid_shape(D), grid_shape(D)] + [grid_shape(MID)] * 5 + [grid_shape(GATE)] * 2
    scratch += [
        pltpu.VMEM((GRID + 2, GRID + 2, frames, MID), BF16),
        pltpu.VMEM((D, MID), BF16),
        pltpu.VMEM((9 * MID, MID), BF16),
        pltpu.VMEM((MID, D), BF16),
        pltpu.VMEM((SMALL_SHARDS, 80, LANES), BF16),
        pltpu.VMEM((D, 2 * LANES), BF16),
        pltpu.VMEM((8, D), F32),
        pltpu.VMEM((FLAT_ROWS + 14, LANES), F32),
    ]
    scratch += sum_scratch(n_seg, n_clip, (16, LANES))
    for shape in SCATTERED.values():
        for lead in ((depth, 4), (depth, 2), (depth,), (depth - 1,)):
            scratch.append(pltpu.VMEM(lead + shape, BF16))
    count = n_seg * 4 + depth + len(SCATTERED) * (depth + 3) + 40
    scratch += [pltpu.SemaphoreType.DMA((count,)), pltpu.SemaphoreType.DMA((count,))]
    return pl.pallas_call(
        functools.partial(gradient_kernel, n_seg, n_clip),
        out_shape=[jax.ShapeDtypeStruct(s, F32) for s in outs],
        in_specs=[any_spec] * 21 + [vmem, vmem],
        out_specs=[vmem] * len(outs),
        scratch_shapes=scratch,
        compiler_params=pltpu.CompilerParams(
            collective_id=50, has_side_effects=True, vmem_limit_bytes=62 * 1024 * 1024
        ),
        name="gradient_sums",
    )(*sources[0], *sources[1], g_cls, norm_rows_in, bias)


def weight_gradients(x, d_one, gated, d_two, a_two, d_three, a_low, d_reduced, mixed, d_excite):
    return [
        matmul(x.reshape(-1, D).T, d_one.reshape(-1, MID)),
        conv(gated, d_two, ("HWCN", "HWIO", "HWNC")).reshape(9 * MID, MID),
        matmul(a_two.reshape(-1, MID).T, d_three.reshape(-1, D)),
        matmul(a_low.reshape(-1, MID).T, d_reduced.reshape(-1, GATE)),
        matmul(mixed.reshape(-1, GATE).T, d_excite.reshape(-1, MID)),
    ]


def on_device(inputs, clip_counts, labels, master, first_moment, second_moment):
    seg_count = lax.axis_size("seg")
    clip_local, slot_local = inputs.shape[:2]
    frames = clip_local * slot_local
    slot_ids = lax.axis_index("seg") * slot_local + jnp.arange(slot_local, dtype=jnp.int32)
    present = (slot_ids[None, :] < clip_counts[:, None]).astype(F32)
    following = (slot_ids[None, :] + 1 < clip_counts[:, None]).astype(F32)
    frame_mask = jnp.broadcast_to(present.reshape(frames, 1), (frames, MID))
    frame_following = jnp.broadcast_to(following.reshape(frames, 1), (frames, GATE))
    table = jnp.zeros(TABLE, F32)
    x_low = inputs.reshape(frames, HW, D).transpose(1, 0, 2)
    shards = weight_shards(master)
    if shards is None:
        weights = whole_weights(master)
        jobs = ((), ())
    else:
        weights = {}
        jobs = JOBS
    kept = []
    flowing = x_low
    flows = []
    for block in range(2):
        flows.append(flowing)
        given = {name: weights[name] for name in weight_names(block) if name not in jobs[block]}
        gathered, results = forward_block(
            block,
            flowing,
            frame_mask,
            frame_following,
            table,
            {name: shards[name] for name in jobs[block]},
            given,
        )
        weights.update(gathered)
        if block == 0:
            table = results[9]
        kept.append(results[:8] + results[10:])
        flowing = results[8]
    w_cls = weights["cls"][:, :CLASSES]
    bias_row = 64 + 4
    b_cls = weights["small"].reshape(SMALL_SHARDS, 80, LANES)[:, bias_row, :6].reshape(-1)[:CLASSES].astype(F32)
    partial_value = jnp.sum(flowing.reshape(clip_local, slot_local, D), axis=1)
    pooled_sum = lax.psum(partial_value.astype(BF16), "seg").astype(F32)
    counts_float = clip_counts.astype(F32)
    pooled = pooled_sum / (HW * counts_float)[:, None]
    pooled_low = pooled.astype(BF16)
    logits = matmul(pooled_low, w_cls) + b_cls
    clips_total = clip_local * lax.axis_size("clip")
    onehot = (labels[:, None] == jnp.arange(CLASSES, dtype=jnp.int32)[None, :]).astype(F32)
    d_logits = (jax.nn.softmax(logits, axis=1) - onehot) / clips_total
    d_lin = d_logits.astype(BF16)
    g_cls = matmul(pooled_low.T, d_lin) / seg_count
    g_bias = jnp.sum(d_logits, axis=0) / seg_count
    d_pooled = matmul(d_lin, w_cls.T)
    scaled = d_pooled / (HW * counts_float)[:, None]
    d_flow = (present[:, :, None] * scaled[:, None]).reshape(frames, D)
    masks = (frame_mask, frame_mask[:, :GATE], frame_following)
    sources = [None, None]
    norm_grads = [None, None]
    for block in (1, 0):
        h_one, a_low, gate, mixed, gated, h_two, a_two, h_three, st_one, st_two, st_three = kept[block]
        *steps, d_flow, norm_sums = backward_block(
            block,
            h_three,
            flows[block],
            d_flow,
            h_two,
            h_one,
            gate,
            [weights[name] for name in weight_names(block)],
            table,
            (st_one, st_two, st_three),
            masks,
        )
        sources[block] = (flows[block], steps[4], gated, steps[1], a_two, steps[0], a_low, steps[3], mixed, steps[2])
        norm_grads[block] = [norm_sums[:24].reshape(-1), norm_sums[24:].reshape(-1)]
    devices = seg_count * lax.axis_size("clip")
    bias_rows = jnp.pad(g_bias, (0, 8 * LANES - CLASSES)).reshape(8, LANES)
    if shards is None:
        grads = []
        for block in (0, 1):
            grads += weight_gradients(*sources[block]) + [v / devices for v in norm_grads[block]]
        grad_mine = scatter_gradients(grads + [g_cls, g_bias])
        square = jnp.full((8, LANES), jnp.sum(grad_mine * grad_mine), F32)
        tail = lax.psum(jnp.concatenate([bias_rows, square]), AXES)
    else:
        vectors = [v.reshape(SMALL_SHARDS, -1) / devices for b in (0, 1) for v in norm_grads[b]]
        padded = jnp.pad(g_bias, (0, 6 * SMALL_SHARDS - CLASSES)).reshape(SMALL_SHARDS, 6)
        extra = norm_rows(vectors + [padded]).astype(BF16)
        cls_low = jnp.pad(g_cls.astype(BF16), ((0, 0), (0, 2 * LANES - CLASSES)))
        flat, tail = gradient_sums(sources, cls_low, extra, bias_rows)
        grad_mine = flat.reshape(-1)[: master.shape[0]]
    norm = jnp.sqrt(tail[8, 0])
    bias_grad = tail[:8].reshape(-1)[:CLASSES]
    factor = jnp.minimum(1.0, CLIP_LIMIT / (norm + 1e-06))
    clipped = grad_mine * factor
    new_first = BETA_ONE * first_moment + (1.0 - BETA_ONE) * clipped
    new_second = BETA_TWO * second_moment + (1.0 - BETA_TWO) * clipped * clipped
    first_hat = new_first / (1.0 - BETA_ONE**STEP)
    second_hat = new_second / (1.0 - BETA_TWO**STEP)
    new_master = master - LEARN_RATE * (
        first_hat / (jnp.sqrt(second_hat) + ADAM_EPS) + WEIGHT_DECAY * master
    )
    grid_grad = d_flow.transpose(1, 0, 2).reshape(inputs.shape)
    return (
        new_master,
        new_first,
        new_second,
        new_master.astype(BF16),
        grid_grad.reshape(inputs.shape),
        norm.reshape(1),
        bias_grad,
    )


def solution(mesh):
    return jax.shard_map(
        on_device,
        mesh=mesh,
        in_specs=(
            P("clip", "seg", None, None),
            P("clip"),
            P("clip"),
            P(AXES),
            P(AXES),
            P(AXES),
        ),
        out_specs=(
            P(AXES),
            P(AXES),
            P(AXES),
            P(AXES),
            P("clip", "seg", None, None),
            P(),
            P(),
        ),
        check_vma=False,
    )
```

```python
import functools
import math

import jax
import jax.numpy as jnp
from jax import lax
from jax.experimental import pallas as pl
from jax.experimental.pallas import tpu as pltpu
from jax.sharding import PartitionSpec as P

D = 2048
MID = 512
GATE = 128
CLASSES = 174
GRID = 7
HW = 49
STEP = 7
LANES = 128

NORM_EPS = 1e-05
CLIP_LIMIT = 0.001
LEARN_RATE = 0.04
WEIGHT_DECAY = 0.05
BETA_ONE = 0.9
BETA_TWO = 0.999
ADAM_EPS = 1e-08

AXES = ("seg", "clip")
MESH_ID = pl.DeviceIdType.MESH
BF16 = jnp.bfloat16
F32 = jnp.float32


def matmul(left, right):
    return jnp.dot(left, right, preferred_element_type=F32)


def layout():
    block_layout = [
        (D, MID),
        (9, MID, MID),
        (MID, D),
        (MID, GATE),
        (GATE, MID),
        (2 * MID + D,),
        (2 * MID + D,),
    ]
    return block_layout + block_layout + [(D, CLASSES), (CLASSES,)]


def widths(devices):
    return [(math.prod(extent) + devices - 1) // devices for extent in layout()]


def pad_rows(flat, rows):
    return jnp.pad(flat, (0, rows * LANES - flat.shape[0])).reshape(rows, LANES)


def small_rows(devices):
    wide = widths(devices)
    amount = sum(wide[3:7]) + sum(wide[10:14])
    amount_cls = wide[14] + wide[15]
    return [16 * ((a + 16 * LANES - 1) // (16 * LANES)) for a in (amount, amount_cls)]


def gather_parameters(master):
    devices = lax.axis_size("seg") * lax.axis_size("clip")
    wide = widths(devices)
    starts = [sum(wide[:i]) for i in range(len(wide))]
    low = master.astype(BF16)

    def part(i):
        return low[starts[i] : starts[i] + wide[i]]

    def gather(values):
        return lax.all_gather(values, AXES, axis=0, tiled=True)

    big = {}
    for base in (0, 7):
        for i, columns in ((0, MID), (1, MID), (2, D)):
            big[base + i] = gather(part(base + i).reshape(-1, columns))
    rows, rows_cls = small_rows(devices)
    small = gather(pad_rows(jnp.concatenate([part(i) for i in (3, 4, 5, 6, 10, 11, 12, 13)]), rows))
    small_cls = gather(pad_rows(jnp.concatenate([part(14), part(15)]), rows_cls))
    small = small.reshape(devices, rows * LANES)
    small_cls = small_cls.reshape(devices, rows_cls * LANES)
    shapes = layout()
    pieces = dict(big)

    def take(source, ids):
        offset = 0
        for i in ids:
            amount = math.prod(shapes[i])
            pieces[i] = source[:, offset : offset + wide[i]].reshape(-1)[:amount].reshape(shapes[i])
            offset += wide[i]

    take(small, (3, 4, 5, 6, 10, 11, 12, 13))
    take(small_cls, (14, 15))
    return [pieces[i] for i in range(16)]


def part_of(master, index):
    devices = lax.axis_size("seg") * lax.axis_size("clip")
    wide = widths(devices)
    start = sum(wide[:index])
    return master[start : start + wide[index]]


def norm_rows(vectors):
    rows = jnp.stack([jnp.pad(v, ((0, 0), (0, LANES - v.shape[1]))) for v in vectors], axis=1)
    return jnp.pad(rows, ((0, 0), (0, 16 - rows.shape[1]), (0, 0)))


def lanes_first(values):
    lead = values.shape[:-2]
    rows, columns = values.shape[-2:]
    split = values.reshape(lead + (rows, columns // LANES, LANES))
    return jnp.swapaxes(split, -3, -2).reshape(lead + (-1, LANES))


def split_rows(target, kind, block, pieces, rows):
    size = rows.shape[1] // pieces
    for k, name in enumerate(piece_names(kind, block, pieces)):
        target[name] = rows[:, k * size : (k + 1) * size].reshape(-1, MID)


def piece_names(kind, block, pieces):
    return [kind + "abc"[k] + str(block) for k in range(pieces)]


def weight_names(block):
    return piece_names("in", block, 2) + piece_names("mid", block, 3) + ["out%d" % block, "small"]


def weight_shards(master):
    devices = lax.axis_size("seg") * lax.axis_size("clip")
    if lax.axis_size("seg") != 2 or devices != SMALL_SHARDS:
        return None
    low = master.astype(BF16)
    shards = {}
    small = []
    for block in range(2):
        base = 7 * block
        split_rows(shards, "in", block, 2, part_of(low, base).reshape(1, -1, MID))
        split_rows(shards, "mid", block, 3, part_of(low, base + 1).reshape(1, -1, MID))
        shards["out%d" % block] = part_of(low, base + 2).reshape(-1, D)
        small.append(part_of(low, base + 3).reshape(-1, GATE))
        small.append(lanes_first(part_of(low, base + 4).reshape(-1, MID)))
    small.append(norm_rows([part_of(low, i)[None] for i in (5, 6, 12, 13, 15)])[0])
    shards["small"] = jnp.concatenate(small)
    cls = part_of(low, 14).reshape(-1, CLASSES)
    shards["cls"] = jnp.pad(cls, ((0, 0), (0, 2 * LANES - CLASSES)))
    return shards


def whole_weights(master):
    pieces = gather_parameters(master)
    whole = {}
    small = []
    for block in range(2):
        w_in, w_mid, w_out, w_red, w_exp = pieces[7 * block : 7 * block + 5]
        split_rows(whole, "in", block, 2, w_in.reshape(SMALL_SHARDS, -1, MID))
        split_rows(whole, "mid", block, 3, w_mid.reshape(SMALL_SHARDS, -1, MID))
        whole["out%d" % block] = w_out
        small.append(w_red.reshape(SMALL_SHARDS, -1, GATE))
        small.append(lanes_first(w_exp.reshape(SMALL_SHARDS, -1, MID)))
    vectors = [pieces[i].reshape(SMALL_SHARDS, -1) for i in (5, 6, 12, 13)]
    bias = jnp.pad(pieces[15], (0, 6 * SMALL_SHARDS - CLASSES)).reshape(SMALL_SHARDS, 6)
    small.append(norm_rows(vectors + [bias]))
    whole["small"] = jnp.concatenate(small, axis=1).reshape(-1, LANES)
    whole["cls"] = jnp.pad(pieces[14], ((0, 0), (0, 2 * LANES - CLASSES)))
    return whole


def scatter_gradients(grads):
    devices = lax.axis_size("seg") * lax.axis_size("clip")
    wide = widths(devices)
    columns = []
    for values, width in zip(grads, wide):
        flat = values.reshape(-1)
        columns.append(jnp.pad(flat, (0, devices * width - flat.shape[0])).reshape(devices, width))
    packed = jnp.concatenate(columns, axis=1)
    return lax.psum_scatter(packed, AXES, scatter_dimension=0, tiled=True)[0]


def conv(values, kernel, numbers):
    return lax.conv_general_dilated(
        values, kernel, (1, 1), ((1, 1), (1, 1)), dimension_numbers=numbers, preferred_element_type=F32
    )


class Links:
    def __init__(self, n_seg, n_clip, send_sem, recv_sem):
        self.n_seg = n_seg
        self.n_clip = n_clip
        self.inner = 4
        self.outer = n_clip // 4
        self.seg = lax.axis_index("seg")
        self.clip = lax.axis_index("clip")
        self.group = self.clip // 4
        self.place = lax.rem(self.clip, 4)
        y = self.place // 2
        x = lax.rem(self.place, 2)
        self.first = (1 - self.seg) * y + self.seg * x
        self.second = (1 - self.seg) * x + self.seg * y
        self.step = 1 + self.seg
        self.jump = 2 - self.seg
        self.across_first = (self.seg, self.clip + self.jump * (1 - 2 * self.first))
        self.across_second = (self.seg, self.clip + self.step * (1 - 2 * self.second))
        self.other = (1 - self.seg, self.clip)
        self.send_sem = send_sem
        self.recv_sem = recv_sem
        self.used = 0

    def take(self, count):
        base = self.used
        self.used += count
        return base

    def near_peer(self, i):
        return (
            lax.rem(self.seg + i // 4, self.n_seg),
            self.group * 4 + lax.rem(self.place + lax.rem(i, 4), 4),
        )

    def far_peer(self, i):
        return (self.seg, lax.rem(self.group + i, self.outer) * 4 + self.place)

    def remote(self, index, source, target, peer):
        return pltpu.make_async_remote_copy(
            src_ref=source,
            dst_ref=target,
            send_sem=self.send_sem.at[index],
            recv_sem=self.recv_sem.at[index],
            device_id=peer,
            device_id_type=MESH_ID,
        )

    def local(self, source, target):
        return pltpu.make_async_copy(source, target, self.recv_sem.at[self.take(1)])

    def meet(self):
        barrier = pltpu.get_barrier_semaphore()
        n_near = self.n_seg * 4 - 1
        n_far = self.outer - 1

        def greet(peer):
            pl.semaphore_signal(barrier, inc=1, device_id=peer, device_id_type=MESH_ID)

        repeat(1, n_near + 1, lambda i: greet(self.near_peer(i)))
        repeat(1, n_far + 1, lambda i: greet(self.far_peer(i)))
        pl.semaphore_wait(barrier, n_near + n_far)

    def sum_near(self, source, middle, near, far):
        n_near = self.n_seg * 4 - 1
        n_far = self.outer - 1
        base = self.take(n_near + n_far)

        def close(i):
            return self.remote(base + i - 1, source, near.at[i - 1], self.near_peer(i))

        def distant(i):
            return self.remote(base + n_near + i - 1, middle, far.at[i - 1], self.far_peer(i))

        repeat(1, n_near + 1, lambda i: close(i).start())
        repeat(1, n_near + 1, lambda i: close(i).wait())
        middle[...] = source[...] + jnp.sum(near[...], axis=0)
        repeat(1, n_far + 1, lambda i: distant(i).start())

        def rest():
            repeat(1, n_far + 1, lambda i: distant(i).wait())
            return middle[...] + jnp.sum(far[...], axis=0)

        return rest

    def all_sum(self, source, middle, near, far):
        return self.sum_near(source, middle, near, far)()


def repeat(first, last, action):
    if last - first <= 8:
        for i in range(first, last):
            action(i)
    else:

        def body(i, carry):
            action(i)
            return carry

        lax.fori_loop(first, last, body, 0)


def sum_scratch(n_seg, n_clip, shape):
    return [
        pltpu.VMEM(shape, F32),
        pltpu.VMEM(shape, F32),
        pltpu.VMEM((n_seg * 4 - 1,) + shape, F32),
        pltpu.VMEM((n_clip // 4 - 1,) + shape, F32),
    ]


class Gather:
    def __init__(self, links, shard, whole):
        depth = links.outer
        whole = whole.reshape((links.n_seg, depth, 4) + shard.shape)
        base = links.take(depth + 3)
        seg, z, place = links.seg, links.group, links.place
        self.own = links.local(shard, whole.at[seg, z, place])
        self.steps = [
            [
                links.remote(base + i - 1, shard, whole.at[seg, z, place], links.far_peer(i))
                for i in range(1, depth)
            ],
            [
                links.remote(
                    base + depth - 1, whole.at[seg, :, place], whole.at[seg, :, place], links.across_second
                )
            ],
            [],
            [links.remote(base + depth + 2, whole.at[seg], whole.at[seg], links.other)],
        ]
        for k in range(2):
            index = links.jump * links.first + links.step * k
            self.steps[2].append(
                links.remote(
                    base + depth + k, whole.at[seg, :, index], whole.at[seg, :, index], links.across_first
                )
            )
        self.at = -1

    def advance(self, last=3):
        if self.at >= 0:
            for copy in self.steps[self.at]:
                copy.wait()
            if self.at == 0:
                self.own.wait()
        self.at += 1
        if self.at == 0:
            self.own.start()
        if self.at <= 3:
            for copy in self.steps[self.at]:
                copy.start()

    def finish(self):
        while self.at <= 3:
            self.advance()


def row_vector(table, row, start, count):
    return jnp.concatenate([table[start + k, row : row + 1, :] for k in range(count)], axis=1)


def build_table(small, table):
    lane = lax.broadcasted_iota(jnp.int32, (8, LANES), 1)
    for q in range(SMALL_SHARDS // 4):
        rows = [small[4 * q + j, 64:80, :].astype(F32)[:8] for j in range(4)]
        one = pltpu.roll(rows[1], 96, 1)
        two = pltpu.roll(rows[2], 64, 1)
        three = pltpu.roll(rows[3], 32, 1)
        table[3 * q] = jnp.where(lane < 96, rows[0], one)
        table[3 * q + 1] = jnp.where(lane < 64, one, two)
        table[3 * q + 2] = jnp.where(lane < 32, two, three)


def put_rows(target, start, vector, count):
    width = vector.shape[1] // count
    for k in range(count):
        target[start + k : start + k + 1, :] = vector[:, k * width : (k + 1) * width]


def fold(values):
    return jnp.sum(values.reshape(-1, 8, values.shape[-1]), axis=0)


def excite_pick(shards, k):
    deep = GATE // shards
    line = lax.broadcasted_iota(jnp.int32, (GATE, shards * 16), 0)
    column = lax.broadcasted_iota(jnp.int32, (GATE, shards * 16), 1)
    wanted = (line // deep) * 16 + k * deep + lax.rem(line, deep)
    return (column == wanted).astype(F32).astype(BF16)


def excite_weights(small, block):
    shards = small.shape[0]
    rows = small[:, 32 * block + 16 : 32 * block + 32].reshape(shards * 16, LANES)
    parts = [matmul(excite_pick(shards, k), rows) for k in range(MID // LANES)]
    return jnp.concatenate(parts, axis=1).astype(BF16)


SMALL_SHARDS = 32
SLOTS_HERE = 8
TABLE = ((2 * MID + D) // LANES + 1, 8, LANES)


STAGES = (
    (
        "ina0", "small", "inb0", "mida0", "@dpad", "@fpad", "ina0", "midb0", "small", "ina0", "midc0", "inb0",
        "small", "ina0", "out0", "mida0", "inb0", "small", "ina0", "midb0", "mida0", "ina1", "small", "inb0",
        "inb1", "midc0", "midb0", "mida1", "inb0", "@first", "midb1", "mida0", "midc0", "out0", "@near1", "mida0",
        "midc1", "midb0", "ina1", "inb1", "@far1", "midb0", "midc0", "out0", "ina1", "mida1", "@second", "inb1",
        "@swap", "@excite", "midc0", "midb1", "@third", "out0", "ina1", "mida1", "midc1", "@near2", "out0", "ina1",
        "inb1", "midb1", "@far2", "mida1", "midc1", "@fourth", "inb1", "mida1", "midb1", "@near3", "midc1",
        "@far3", "midb1", "@fifth", "midc1",
    ),
    (
        "out1", "@dpad", "@fpad", "@first", "cls", "@near1", "out1", "@far1", "cls", "@second", "@swap", "out1",
        "@excite", "cls", "@third", "out1", "@near2", "cls", "@far2", "out1", "@fourth", "cls", "@near3", "@far3",
        "@fifth",
    ),
)
JOBS = tuple(tuple(dict.fromkeys(item for item in order if item[0] != "@")) for order in STAGES)


def forward_kernel(n_seg, n_clip, block, jobs, plan, *refs):
    refs = list(refs)

    def pop(count=1):
        taken = refs[:count]
        del refs[:count]
        return taken if count != 1 else taken[0]

    last = block == 1
    x_hbm, mask, following, table_in = pop(4)
    share, chosen = pop(2) if last else (None, None)
    shards = dict(zip(jobs, [pop() for _ in jobs]))
    given = dict(zip(plan, [pop() for _ in plan]))
    wholes = dict(zip(jobs, [pop() for _ in jobs]))
    h1_out, low_out, gate_out, mix_out, f_out, h2_out, a2_out, h3_out = pop(8)
    out_hbm, table_out, st1, st2, st3 = pop(5)
    g_cls, g_bias = pop(2) if last else (None, None)
    xv, w_in, w_mid, w_out, small = pop(5)
    h1v, a1v, lowv, rv, edge, dpad, mixv, gatev, fpad, h2v, a2v, h3v = pop(12)
    wide_sum, wide_square, w_exp = pop(3)
    sums = [pop(4) for _ in range(3)]
    pooled, clip_sums, clip_other, w_cls = pop(4) if last else [None] * 4
    send_sem, recv_sem = pop(2)
    links = Links(n_seg, n_clip, send_sem, recv_sem)
    frames = xv.shape[1]
    table = table_in if last else table_out
    outgoing = []

    def send_out(source, target):
        copy = links.local(source, target)
        copy.start()
        outgoing.append(copy)

    links.meet()
    x_base = links.take(GRID)

    def load_x(i):
        rows = pl.ds(GRID * i, GRID)
        return pltpu.make_async_copy(x_hbm.at[rows], xv.at[rows], links.recv_sem.at[x_base + i])

    for i in range(GRID):
        load_x(i).start()
    gathers = {name: Gather(links, shards[name], wholes[name]) for name in jobs}

    targets = {"out%d" % block: w_out, "small": small}
    if last:
        targets["cls"] = w_cls
    for kind, target, count in (("in", w_in, 2), ("mid", w_mid, 3)):
        rows = target.shape[0] // SMALL_SHARDS
        size = rows // count
        wide = target.reshape(SMALL_SHARDS, rows, MID)
        for k, name in enumerate(piece_names(kind, block, count)):
            targets[name] = wide.at[:, k * size : (k + 1) * size]
    loads = {}

    def load(name):
        source = wholes[name] if name in gathers else given[name]
        loads[name] = links.local(source.reshape(targets[name].shape), targets[name])
        loads[name].start()

    def push(name):
        if gathers[name].at <= 3:
            gathers[name].advance()
            if gathers[name].at > 3 and name in targets:
                load(name)

    def need(*names):
        for name in names:
            while name not in loads:
                push(name)
        for name in names:
            loads[name].wait()

    for name in targets:
        if name not in gathers:
            load(name)
    table = table_in if last else table_out
    half = MID // LANES

    def norm(index, tot, columns, start, out):
        live_rows = table[TABLE[0] - 1, 0:1, 0:1]
        mean = jnp.concatenate([tot[k : k + 1] for k in range(4)], axis=1) / live_rows
        square = jnp.concatenate([tot[4 + k : 5 + k] for k in range(4)], axis=1) / live_rows
        inv = lax.rsqrt(square - mean * mean + NORM_EPS)
        out[0:1, :] = mean
        out[1:2, :] = inv
        gain = row_vector(table, 2 * block, start, columns // LANES)
        shift = row_vector(table, 2 * block + 1, start, columns // LANES)
        scale = gain * inv
        return scale, shift - mean * scale

    def masked_sums(values):
        shaped = values.reshape(-1, frames, values.shape[-1])
        masked = shaped * mask[...][None]
        return fold(masked), fold(masked * shaped)

    zeros = jnp.zeros((8, MID), F32)
    kept = {}

    def first(i, carry):
        load_x(i).wait()
        part = matmul(xv[pl.ds(GRID * i, GRID)].reshape(GRID * frames, D), w_in[...])
        h1v[pl.ds(GRID * i, GRID)] = part.reshape(GRID, frames, MID)
        one, two = masked_sums(part)
        return (carry[0] + one, carry[1] + two)

    def put_sums(index, one, two):
        stat = sums[index][0]
        put_rows(stat, 0, jnp.sum(one, axis=0, keepdims=True), 4)
        put_rows(stat, 4, jnp.sum(two, axis=0, keepdims=True), 4)
        return stat

    def stage_dpad():
        dpad[...] = jnp.zeros_like(dpad)

    def stage_fpad():
        fpad[...] = jnp.zeros_like(fpad)
        if last:
            table_out[...] = table_in[...]
        else:
            table_out[...] = jnp.zeros_like(table_out)

    def stage_first():
        need(*piece_names("in", block, 2))
        stat = put_sums(0, *lax.fori_loop(0, GRID, first, (zeros, zeros)))
        present = HW * jnp.sum(mask[:, :LANES], axis=0, keepdims=True)
        stat[8:16, :] = jnp.broadcast_to(present, (8, LANES))
        send_out(h1v, h1_out)

    def stage_near1():
        kept["rest"] = links.sum_near(*sums[0])

    def stage_far1():
        need("small")
        total = kept["rest"]()
        if not last:
            build_table(small, table_out)
            table_out[TABLE[0] - 1] = total[8:16]
        kept["one"] = norm(0, total, MID, 0, st1)

    def second(i, carry):
        for j in range(GRID):
            y = h1v[GRID * i + j] * kept["one"][0] + kept["one"][1]
            a = y * jax.nn.sigmoid(y)
            a1v[GRID * i + j] = a
            lowv[GRID * i + j] = a.astype(BF16)
        part = matmul(lowv[pl.ds(GRID * i, GRID)].reshape(GRID * frames, MID), kept["red"])
        rv[pl.ds(GRID * i, GRID)] = part.astype(BF16).reshape(GRID, frames, GATE)
        return carry

    def stage_second():
        w_exp[...] = excite_weights(small, block)
        kept["red"] = small[:, 32 * block : 32 * block + 16].reshape(MID, GATE)
        lax.fori_loop(0, GRID, second, 0)
        send_out(lowv, low_out)
        kept["swap"] = links.remote(links.take(1), rv, edge, links.other)
        kept["swap"].start()

    row = lax.rem(lax.broadcasted_iota(jnp.int32, (frames, GATE), 0), 8)

    def change(i, carry):
        for j in range(GRID):
            now = rv[GRID * i + j].astype(F32)
            rest = edge[GRID * i + j].astype(F32)
            later = jnp.where(row < 7, pltpu.roll(now, frames - 1, 0), pltpu.roll(rest, 7, 0))
            dpad[i + 1, j + 1] = following[...] * (later - now)
        return carry

    def stage_swap():
        kept["swap"].wait()
        lax.fori_loop(0, GRID, change, 0)

    def excite(i, carry):
        for j in range(GRID):
            total = jnp.zeros((frames, GATE), F32)
            for k in range(9):
                total = total + dpad[i + k // 3, j + k % 3]
            mixv[GRID * i + j] = (dpad[i + 1, j + 1] + total / 9.0).astype(BF16)
        e = matmul(mixv[pl.ds(GRID * i, GRID)].reshape(GRID * frames, GATE), w_exp[...])
        e = e.reshape(GRID, frames, MID)
        for j in range(GRID):
            gate = jax.nn.sigmoid(e[j])
            gatev[GRID * i + j] = gate.astype(BF16)
            fpad[i + 1, j + 1] = (a1v[GRID * i + j] * (1.0 + gate)).astype(BF16)
        return carry

    def stage_excite():
        lax.fori_loop(0, GRID, excite, 0)
        send_out(mixv, mix_out)
        send_out(gatev, gate_out)
        send_out(fpad.at[pl.ds(1, GRID), pl.ds(1, GRID)], f_out)

    def third(i, carry):
        part = None
        for k in range(9):
            window = fpad[i + k // 3, pl.ds(k % 3, GRID)].reshape(GRID * frames, MID)
            term = matmul(window, w_mid[k * MID : (k + 1) * MID])
            part = term if part is None else part + term
        h2v[pl.ds(GRID * i, GRID)] = part.reshape(GRID, frames, MID)
        one, two = masked_sums(part)
        return (carry[0] + one, carry[1] + two)

    def stage_third():
        need(*piece_names("mid", block, 3))
        put_sums(1, *lax.fori_loop(0, GRID, third, (zeros, zeros)))
        send_out(h2v, h2_out)

    def stage_near2():
        kept["rest"] = links.sum_near(*sums[1])

    def stage_far2():
        kept["two"] = norm(1, kept["rest"](), MID, half, st2)
        wide_sum[...] = jnp.zeros_like(wide_sum)
        wide_square[...] = jnp.zeros_like(wide_square)

    def fourth(i, carry):
        for j in range(GRID):
            y = h2v[GRID * i + j] * kept["two"][0] + kept["two"][1]
            a2v[GRID * i + j] = (y * jax.nn.sigmoid(y)).astype(BF16)
        rows = a2v[pl.ds(GRID * i, GRID)].reshape(GRID * frames, MID)
        for k in range(4):
            part = matmul(rows, w_out[:, k * MID : (k + 1) * MID])
            h3v[pl.ds(GRID * i, GRID), :, k * MID : (k + 1) * MID] = part.astype(BF16).reshape(
                GRID, frames, MID
            )
            one, two = masked_sums(part)
            wide_sum[:, k * MID : (k + 1) * MID] += one
            wide_square[:, k * MID : (k + 1) * MID] += two
        return carry

    def stage_fourth():
        need("out%d" % block)
        lax.fori_loop(0, GRID, fourth, 0)
        put_sums(2, wide_sum[...], wide_square[...])
        send_out(a2v, a2_out)
        send_out(h3v, h3_out)

    def stage_near3():
        kept["rest"] = links.sum_near(*sums[2])

    def stage_far3():
        kept["three"] = norm(2, kept["rest"](), D, 2 * half, st3)
        if last:
            pooled[...] = jnp.zeros_like(pooled)

    def fifth(p, carry):
        for k in range(4):
            span = slice(k * MID, (k + 1) * MID)
            scale, shift = kept["three"]
            pre = h3v[p, :, span].astype(F32) * scale[:, span] + shift[:, span]
            pre = pre + xv[p, :, span].astype(F32)
            value = pre * jax.nn.sigmoid(pre)
            if last:
                pooled[:, span] += value * mask[...]
            else:
                xv[p, :, span] = value.astype(BF16)
        return carry

    def stage_fifth():
        lax.fori_loop(0, HW, fifth, 0)
        if last:
            classify()
        send_out(pooled if last else xv, out_hbm)

    def classify():
        clips = frames // SLOTS_HERE
        clip_sums[...] = jnp.zeros_like(clip_sums)
        for c in range(clips):
            rows = pooled[SLOTS_HERE * c : SLOTS_HERE * (c + 1), :]
            clip_sums[c : c + 1, :] = jnp.sum(rows, axis=0, keepdims=True)
        swap = links.remote(links.take(1), clip_sums, clip_other, links.other)
        swap.start()
        lane = lax.broadcasted_iota(jnp.int32, (1, 2 * LANES), 1)
        bias = jnp.zeros((1, 2 * LANES), F32)
        for d in range(SMALL_SHARDS):
            piece = small[d, 64:80, :].astype(F32)[4:5]
            piece = jnp.concatenate([piece, jnp.zeros_like(piece)], axis=1)
            own = jnp.logical_and(lane >= 6 * d, lane < 6 * d + 6)
            bias = bias + jnp.where(own, pltpu.roll(piece, 6 * d, 1) if d else piece, 0.0)
        need("cls")
        swap.wait()
        mean = (clip_sums[...] + clip_other[...]) * share[:, 0:1]
        low = jnp.concatenate([mean, jnp.zeros_like(mean)], axis=0).astype(BF16)
        scores = matmul(low, w_cls[...])[:8] + bias
        scores = jnp.where(lane < CLASSES, scores, -1e30)
        scores = jnp.exp(scores - jnp.max(scores, axis=1, keepdims=True))
        chance = scores / jnp.sum(scores, axis=1, keepdims=True)
        clips_total = clips * links.n_clip
        d_scores = jnp.where(share[:, 0:1] > 0.0, (chance - chosen[...]) / clips_total, 0.0)
        g_bias[...] = jnp.broadcast_to(jnp.sum(d_scores, axis=0, keepdims=True) / n_seg, g_bias.shape)
        d_low = jnp.concatenate([d_scores, jnp.zeros_like(d_scores)], axis=0).astype(BF16)
        grad = lax.dot_general(low, d_low, (((0,), (0,)), ((), ())), preferred_element_type=F32)
        g_cls[...] = (grad / n_seg).astype(BF16)
        d_mean = lax.dot_general(d_low, w_cls[...], (((1,), (1,)), ((), ())), preferred_element_type=F32)
        d_mean = d_mean[:8] * share[:, 0:1]
        for c in range(clips):
            rows = slice(SLOTS_HERE * c, SLOTS_HERE * (c + 1))
            here = mask[rows, 0:1]
            pooled[rows, :] = jnp.broadcast_to(d_mean[c : c + 1], (SLOTS_HERE, D)) * here

    stages = {
        "dpad": stage_dpad,
        "fpad": stage_fpad,
        "first": stage_first,
        "near1": stage_near1,
        "far1": stage_far1,
        "second": stage_second,
        "swap": stage_swap,
        "excite": stage_excite,
        "third": stage_third,
        "near2": stage_near2,
        "far2": stage_far2,
        "fourth": stage_fourth,
        "near3": stage_near3,
        "far3": stage_far3,
        "fifth": stage_fifth,
    }
    for item in STAGES[block]:
        if item[0] == "@":
            with jax.named_scope(item[1:]):
                stages[item[1:]]()
        elif item in gathers:
            push(item)
    for name in jobs:
        gathers[name].finish()
    for copy in outgoing:
        copy.wait()


def forward_block(block, x, mask, following, table, extra, shards, given):
    n_seg = lax.axis_size("seg")
    n_clip = lax.axis_size("clip")
    cells, frames, width = x.shape
    jobs = list(shards)
    plan = list(given)
    any_spec = pl.BlockSpec(memory_space=pl.ANY)
    vmem = pl.BlockSpec(memory_space=pltpu.VMEM)
    depth = n_clip // 4

    def grid_shape(columns):
        return (cells, frames, columns)

    last = block == 1
    devices = n_seg * n_clip
    outs = [jax.ShapeDtypeStruct((devices * shards[n].shape[0], shards[n].shape[1]), BF16) for n in jobs]
    outs += [
        jax.ShapeDtypeStruct(grid_shape(MID), F32),
        jax.ShapeDtypeStruct(grid_shape(MID), BF16),
        jax.ShapeDtypeStruct(grid_shape(MID), BF16),
        jax.ShapeDtypeStruct(grid_shape(GATE), BF16),
        jax.ShapeDtypeStruct((GRID, GRID, frames, MID), BF16),
        jax.ShapeDtypeStruct(grid_shape(MID), F32),
        jax.ShapeDtypeStruct(grid_shape(MID), BF16),
        jax.ShapeDtypeStruct(grid_shape(D), BF16),
        jax.ShapeDtypeStruct((frames, D), F32) if last else jax.ShapeDtypeStruct(x.shape, BF16),
        jax.ShapeDtypeStruct(TABLE, F32),
        jax.ShapeDtypeStruct((8, MID), F32),
        jax.ShapeDtypeStruct((8, MID), F32),
        jax.ShapeDtypeStruct((8, D), F32),
    ]
    out_specs = [any_spec] * (len(jobs) + 9) + [vmem] * 4
    if last:
        outs += [jax.ShapeDtypeStruct((D, 2 * LANES), BF16), jax.ShapeDtypeStruct((8, 2 * LANES), F32)]
        out_specs += [vmem] * 2

    shapes = [(D, MID), (9 * MID, MID), (MID, D), (SMALL_SHARDS, 80, LANES)]
    scratch = [pltpu.VMEM(x.shape, BF16)]
    scratch += [pltpu.VMEM(s, BF16) for s in shapes]
    scratch += [
        pltpu.VMEM(grid_shape(MID), F32),
        pltpu.VMEM(grid_shape(MID), F32),
        pltpu.VMEM(grid_shape(MID), BF16),
        pltpu.VMEM(grid_shape(GATE), BF16),
        pltpu.VMEM(grid_shape(GATE), BF16),
        pltpu.VMEM((GRID + 2, GRID + 2, frames, GATE), F32),
        pltpu.VMEM(grid_shape(GATE), BF16),
        pltpu.VMEM(grid_shape(MID), BF16),
        pltpu.VMEM((GRID + 2, GRID + 2, frames, MID), BF16),
        pltpu.VMEM(grid_shape(MID), F32),
        pltpu.VMEM(grid_shape(MID), BF16),
        pltpu.VMEM(grid_shape(D), BF16),
        pltpu.VMEM((8, D), F32),
        pltpu.VMEM((8, D), F32),
        pltpu.VMEM((GATE, MID), BF16),
    ]
    for shape in ((16, LANES), (8, LANES), (8, MID)):
        scratch += sum_scratch(n_seg, n_clip, shape)
    if last:
        scratch += [pltpu.VMEM((frames, D), F32), pltpu.VMEM((8, D), F32), pltpu.VMEM((8, D), F32)]
        scratch.append(pltpu.VMEM((D, 2 * LANES), BF16))
    count = 4 * (n_seg * 4 + depth) + len(jobs) * (depth + 4) + 48
    scratch += [pltpu.SemaphoreType.DMA((count,)), pltpu.SemaphoreType.DMA((count,))]
    results = pl.pallas_call(
        functools.partial(forward_kernel, n_seg, n_clip, block, jobs, plan),
        out_shape=outs,
        in_specs=[any_spec, vmem, vmem, vmem] + [vmem] * len(extra) + [any_spec] * (len(jobs) + len(plan)),
        out_specs=out_specs,
        scratch_shapes=scratch,
        compiler_params=pltpu.CompilerParams(
            collective_id=30 + block, has_side_effects=True, vmem_limit_bytes=60 * 1024 * 1024
        ),
        name="forward_block",
    )(x, mask, following, table, *extra, *[shards[n] for n in jobs], *[given[n] for n in plan])
    wholes = dict(zip(jobs, results[: len(jobs)]))
    return wholes, results[len(jobs) :]


def backward_kernel(n_seg, n_clip, block, *refs):
    refs = list(refs)

    def pop(count=1):
        taken = refs[:count]
        del refs[:count]
        return taken if count != 1 else taken[0]

    last = block == 1
    h3_hbm, x_hbm, d_in, h2_hbm, h1_hbm, gate_hbm = pop(6)
    in_a, in_b, mid_a, mid_b, mid_c, out_hbm, small_hbm = pop(7)
    table, st1, st2, st3, mask, present, following = pop(7)
    dh3_out, dh2_out, de_out, dr_out, dh1_out, dx_out, norm_grads = pop(7)
    dv, h3v, xv, h2v, h1v, gatev, dyv, pad2, dsv, edge, pad_s, pad_e = pop(12)
    drv, dh1v, w_in, w_mid, w_out, small, w_exp = pop(7)
    sum_gain, sum_shift = pop(2)
    sums = [pop(4) for _ in range(3)]
    send_sem, recv_sem = pop(2)
    links = Links(n_seg, n_clip, send_sem, recv_sem)
    frames = xv.shape[1]
    outgoing = []

    def send_out(source, target):
        copy = links.local(source, target)
        copy.start()
        outgoing.append(copy)

    def load(source, target):
        copy = links.local(source.reshape(target.shape), target)
        copy.start()
        return copy

    streams = [(h3_hbm, h3v), (x_hbm, xv)]
    if not last:
        streams.append((d_in, dv))
    wide_base = links.take(len(streams) * GRID)

    def wide_copies(i):
        rows = pl.ds(GRID * i, GRID)
        return [
            pltpu.make_async_copy(source.at[rows], target.at[rows], links.recv_sem.at[wide_base + GRID * k + i])
            for k, (source, target) in enumerate(streams)
        ]

    for i in range(GRID):
        for copy in wide_copies(i):
            copy.start()
    loads_two = [load(out_hbm, w_out), load(h2_hbm, h2v)]
    loads_three = [load(h1_hbm, h1v), load(gate_hbm, gatev), load(small_hbm, small)]
    loads_four = []
    for parts, target, waits in (
        ((mid_a, mid_b, mid_c), w_mid, loads_three),
        ((in_a, in_b), w_in, loads_four),
    ):
        rows = target.shape[0] // SMALL_SHARDS
        size = rows // len(parts)
        wide = target.reshape(SMALL_SHARDS, rows, MID)
        for k, source in enumerate(parts):
            waits.append(load(source, wide.at[:, k * size : (k + 1) * size]))
    links.meet()
    live_rows = table[TABLE[0] - 1, 0:1, 0:1]
    half = MID // LANES
    pad2[...] = jnp.zeros_like(pad2)
    pad_s[...] = jnp.zeros_like(pad_s)
    pad_e[...] = jnp.zeros_like(pad_e)
    sum_gain[...] = jnp.zeros_like(sum_gain)
    sum_shift[...] = jnp.zeros_like(sum_shift)

    def vectors(start, columns, stats):
        gain = row_vector(table, 2 * block, start, columns // LANES)
        shift = row_vector(table, 2 * block + 1, start, columns // LANES)
        return gain, shift, stats[0:1, :], stats[1:2, :]

    def totals(index, start, columns, gain_rows, shift_rows):
        stat = sums[index][0]
        put_rows(stat, 0, jnp.sum(gain_rows, axis=0, keepdims=True), 4)
        put_rows(stat, 4, jnp.sum(shift_rows, axis=0, keepdims=True), 4)
        tot = links.all_sum(*sums[index])
        gain = jnp.concatenate([tot[k : k + 1] for k in range(4)], axis=1)
        shift = jnp.concatenate([tot[4 + k : 5 + k] for k in range(4)], axis=1)
        put_rows(norm_grads, start, gain, columns // LANES)
        put_rows(norm_grads, 24 + start, shift, columns // LANES)
        return gain / live_rows, shift / live_rows

    def slope_of(values):
        sig = jax.nn.sigmoid(values)
        return sig, sig * (1.0 + values * (1.0 - sig))

    def dot_t(left, right):
        return lax.dot_general(left, right, (((1,), (1,)), ((), ())), preferred_element_type=F32)

    gain3, shift3, mean3, inv3 = vectors(2 * half, D, st3)

    def first_rows(i, carry):
        for copy in wide_copies(i):
            copy.wait()
        return lax.fori_loop(GRID * i, GRID * i + GRID, first, carry)

    def first(p, carry):
        for k in range(4):
            span = slice(k * MID, (k + 1) * MID)
            n = (h3v[p, :, span].astype(F32) - mean3[:, span]) * inv3[:, span]
            pre = n * gain3[:, span] + shift3[:, span] + xv[p, :, span].astype(F32)
            grad = d_in[:, span] if last else dv[p, :, span]
            grad = grad * slope_of(pre)[1]
            dv[p, :, span] = grad
            sum_gain[:, span] += fold(grad * n)
            sum_shift[:, span] += fold(grad)
        return carry

    lax.fori_loop(0, GRID, first_rows, 0)
    part_gain, part_shift = totals(0, 2 * half, D, sum_gain[...], sum_shift[...])
    factor3 = gain3 * inv3
    for copy in loads_two:
        copy.wait()
    gain2, shift2, mean2, inv2 = vectors(half, MID, st2)
    zeros = jnp.zeros((8, MID), F32)

    def second(i, carry):
        for j in range(GRID):
            p = GRID * i + j
            for k in range(4):
                span = slice(k * MID, (k + 1) * MID)
                n = (h3v[p, :, span].astype(F32) - mean3[:, span]) * inv3[:, span]
                rest = mask[...] * (part_shift[:, span] + n * part_gain[:, span])
                h3v[p, :, span] = (factor3[:, span] * (dv[p, :, span] - rest)).astype(BF16)
        d_a = dot_t(h3v[pl.ds(GRID * i, GRID)].reshape(GRID * frames, D), w_out[...])
        d_a = d_a.reshape(GRID, frames, MID)
        one, two = carry
        for j in range(GRID):
            n = (h2v[GRID * i + j] - mean2) * inv2
            grad = d_a[j] * slope_of(n * gain2 + shift2)[1]
            dyv[GRID * i + j] = grad
            one = one + fold(grad * n)
            two = two + fold(grad)
        return (one, two)

    one, two = lax.fori_loop(0, GRID, second, (zeros, zeros))
    send_out(h3v, dh3_out)
    part_gain2, part_shift2 = totals(1, half, MID, one, two)
    factor2 = gain2 * inv2

    def third(i, carry):
        for j in range(GRID):
            p = GRID * i + j
            n = (h2v[p] - mean2) * inv2
            rest = mask[...] * (part_shift2 + n * part_gain2)
            pad2[i + 1, j + 1] = (factor2 * (dyv[p] - rest)).astype(BF16)
        return carry

    lax.fori_loop(0, GRID, third, 0)
    send_out(pad2.at[pl.ds(1, GRID), pl.ds(1, GRID)], dh2_out)
    for copy in loads_three:
        copy.wait()
    w_exp[...] = excite_weights(small, block)
    red = small[:, 32 * block : 32 * block + 16].reshape(MID, GATE)
    gain1, shift1, mean1, inv1 = vectors(0, MID, st1)

    def fourth(i, carry):
        part = None
        for k in range(9):
            window = pad2[i + 2 - k // 3, pl.ds(2 - k % 3, GRID)].reshape(GRID * frames, MID)
            term = dot_t(window, w_mid[k * MID : (k + 1) * MID])
            part = term if part is None else part + term
        part = part.reshape(GRID, frames, MID)
        for j in range(GRID):
            p = GRID * i + j
            y = (h1v[p] - mean1) * inv1 * gain1 + shift1
            a = y * jax.nn.sigmoid(y)
            gate = gatev[p].astype(F32)
            dyv[p] = part[j] * (1.0 + gate)
            gatev[p] = (part[j] * a * gate * (1.0 - gate)).astype(BF16)
        d_s = dot_t(gatev[pl.ds(GRID * i, GRID)].reshape(GRID * frames, MID), w_exp[...])
        d_s = d_s.astype(BF16).reshape(GRID, frames, GATE)
        dsv[pl.ds(GRID * i, GRID)] = d_s
        for j in range(GRID):
            pad_s[i + 1, j + 1] = d_s[j].astype(F32)
        return carry

    lax.fori_loop(0, GRID, fourth, 0)
    swap = links.remote(links.take(1), dsv, edge, links.other)
    swap.start()
    send_out(gatev, de_out)
    swap.wait()

    def unpack(i, carry):
        for j in range(GRID):
            pad_e[i + 1, j + 1] = edge[GRID * i + j].astype(F32)
        return carry

    lax.fori_loop(0, GRID, unpack, 0)
    row = lax.rem(lax.broadcasted_iota(jnp.int32, (frames, GATE), 0), 8)
    from_other = links.seg.astype(F32)

    def fifth(i, carry):
        for j in range(GRID):
            near = jnp.zeros((frames, GATE), F32)
            far = jnp.zeros((frames, GATE), F32)
            for k in range(9):
                near = near + pad_s[i + k // 3, j + k % 3]
                far = far + pad_e[i + k // 3, j + k % 3]
            near = pad_s[i + 1, j + 1] + near / 9.0
            far = (pad_e[i + 1, j + 1] + far / 9.0) * from_other
            earlier = jnp.where(row > 0, pltpu.roll(near, 1, 0), pltpu.roll(far, frames - 7, 0))
            drv[GRID * i + j] = (present[...] * earlier - following[...] * near).astype(BF16)
        d_a = dot_t(drv[pl.ds(GRID * i, GRID)].reshape(GRID * frames, GATE), red)
        d_a = d_a.reshape(GRID, frames, MID)
        one, two = carry
        for j in range(GRID):
            p = GRID * i + j
            n = (h1v[p] - mean1) * inv1
            grad = (dyv[p] + d_a[j]) * slope_of(n * gain1 + shift1)[1]
            dyv[p] = grad
            one = one + fold(grad * n)
            two = two + fold(grad)
        return (one, two)

    one, two = lax.fori_loop(0, GRID, fifth, (zeros, zeros))
    send_out(drv, dr_out)
    part_gain1, part_shift1 = totals(2, 0, MID, one, two)
    factor1 = gain1 * inv1
    for copy in loads_four:
        copy.wait()

    def sixth(i, carry):
        for j in range(GRID):
            p = GRID * i + j
            n = (h1v[p] - mean1) * inv1
            rest = mask[...] * (part_shift1 + n * part_gain1)
            dh1v[p] = (factor1 * (dyv[p] - rest)).astype(BF16)
        rows = dh1v[pl.ds(GRID * i, GRID)].reshape(GRID * frames, MID)
        for k in range(4):
            span = slice(k * MID, (k + 1) * MID)
            part = dot_t(rows, w_in[span, :])
            dv[pl.ds(GRID * i, GRID), :, span] += part.reshape(GRID, frames, MID)
        dx_copy(i).start()
        return carry

    dx_base = links.take(GRID)

    def dx_copy(i):
        rows = pl.ds(GRID * i, GRID)
        return pltpu.make_async_copy(dv.at[rows], dx_out.at[rows], links.recv_sem.at[dx_base + i])

    lax.fori_loop(0, GRID, sixth, 0)
    send_out(dh1v, dh1_out)
    for i in range(GRID):
        dx_copy(i).wait()
    for copy in outgoing:
        copy.wait()


def backward_block(block, h3, x, d_in, h2, h1, gate, weights, table, stats, masks):
    n_seg = lax.axis_size("seg")
    n_clip = lax.axis_size("clip")
    cells, frames, width = x.shape
    any_spec = pl.BlockSpec(memory_space=pl.ANY)
    vmem = pl.BlockSpec(memory_space=pltpu.VMEM)
    last = block == 1

    def grid_shape(columns):
        return (cells, frames, columns)

    outs = [
        jax.ShapeDtypeStruct(grid_shape(D), BF16),
        jax.ShapeDtypeStruct((GRID, GRID, frames, MID), BF16),
        jax.ShapeDtypeStruct(grid_shape(MID), BF16),
        jax.ShapeDtypeStruct(grid_shape(GATE), BF16),
        jax.ShapeDtypeStruct(grid_shape(MID), BF16),
        jax.ShapeDtypeStruct(grid_shape(D), F32),
        jax.ShapeDtypeStruct((48, LANES), F32),
    ]
    scratch = [
        pltpu.VMEM(grid_shape(D), F32),
        pltpu.VMEM(grid_shape(D), BF16),
        pltpu.VMEM(grid_shape(D), BF16),
        pltpu.VMEM(grid_shape(MID), F32),
        pltpu.VMEM(grid_shape(MID), F32),
        pltpu.VMEM(grid_shape(MID), BF16),
        pltpu.VMEM(grid_shape(MID), F32),
        pltpu.VMEM((GRID + 2, GRID + 2, frames, MID), BF16),
        pltpu.VMEM(grid_shape(GATE), BF16),
        pltpu.VMEM(grid_shape(GATE), BF16),
        pltpu.VMEM((GRID + 2, GRID + 2, frames, GATE), F32),
        pltpu.VMEM((GRID + 2, GRID + 2, frames, GATE), F32),
        pltpu.VMEM(grid_shape(GATE), BF16),
        pltpu.VMEM(grid_shape(MID), BF16),
        pltpu.VMEM((D, MID), BF16),
        pltpu.VMEM((9 * MID, MID), BF16),
        pltpu.VMEM((MID, D), BF16),
        pltpu.VMEM((SMALL_SHARDS, 80, LANES), BF16),
        pltpu.VMEM((GATE, MID), BF16),
        pltpu.VMEM((8, D), F32),
        pltpu.VMEM((8, D), F32),
    ]
    for shape in ((8, MID), (8, LANES), (8, LANES)):
        scratch += sum_scratch(n_seg, n_clip, shape)
    count = 3 * (n_seg * 4 + n_clip // 4) + 64
    scratch += [pltpu.SemaphoreType.DMA((count,)), pltpu.SemaphoreType.DMA((count,))]
    d_spec = vmem if last else any_spec
    return pl.pallas_call(
        functools.partial(backward_kernel, n_seg, n_clip, block),
        out_shape=outs,
        in_specs=[any_spec, any_spec, d_spec] + [any_spec] * 10 + [vmem] * 7,
        out_specs=[any_spec] * 6 + [vmem],
        scratch_shapes=scratch,
        compiler_params=pltpu.CompilerParams(
            collective_id=40 + block, has_side_effects=True, vmem_limit_bytes=62 * 1024 * 1024
        ),
        name="backward_block",
    )(h3, x, d_in, h2, h1, gate, *weights, table, *stats, *masks)


class Scatter:
    def __init__(self, links, grad, rows, buffers, alternate, finish):
        self.links = links
        self.alternate = alternate
        self.grad = grad
        self.rows = rows
        self.one, self.two, self.three, self.four = buffers
        self.finish = finish
        self.depth = links.outer
        self.base = links.take(self.depth + 3)
        self.at = -1

    def copies(self):
        links, base, depth = self.links, self.base, self.depth
        if self.at == 0:
            source = self.grad.at[1 - links.seg, :, :, self.rows]
            return [links.remote(base, source, self.one, links.other)]
        found = []
        if self.at == 1:
            for k in range(2):
                source = self.one.at[:, links.jump * (1 - links.first) + links.step * k]
                found.append(links.remote(base + 1 + k, source, self.two.at[:, k], links.across_first))
            return found
        if self.alternate:
            if self.at == 2:
                for i in range(1, depth):
                    source = self.two.at[lax.rem(links.group + i, depth)]
                    found.append(links.remote(base + 2 + i, source, self.three.at[i - 1], links.far_peer(i)))
            else:
                source = self.four.at[1 - links.second]
                found.append(links.remote(base + depth + 2, source, self.four.at[2], links.across_second))
            return found
        if self.at == 2:
            source = self.two.at[:, 1 - links.second]
            return [links.remote(base + 3, source, self.three, links.across_second)]
        for i in range(1, depth):
            source = self.three.at[lax.rem(links.group + i, depth)]
            found.append(links.remote(base + 3 + i, source, self.four.at[i - 1], links.far_peer(i)))
        return found

    def add(self):
        links, depth = self.links, self.depth
        one, two, three, four = self.one, self.two, self.three, self.four
        if self.at == 0:

            def add_one(i, carry):
                z = i // 4
                w = lax.rem(i, 4)
                total = one[z, w].astype(F32) + self.grad[links.seg, z, w, self.rows].astype(F32)
                one[z, w] = total.astype(BF16)
                return carry

            lax.fori_loop(0, 4 * depth, add_one, 0)
        elif self.at == 1:

            def add_two(i, carry):
                z = i // 2
                k = lax.rem(i, 2)
                kept = one[z, links.jump * links.first + links.step * k]
                two[z, k] = (two[z, k].astype(F32) + kept.astype(F32)).astype(BF16)
                return carry

            lax.fori_loop(0, 2 * depth, add_two, 0)
        elif self.at == 2 and self.alternate:
            for k in range(2):
                total = two[links.group, k].astype(F32)
                for i in range(1, depth):
                    total = total + three[i - 1, k].astype(F32)
                four[k] = total.astype(BF16)
        elif self.at == 2:

            def add_three(z, carry):
                three[z] = (three[z].astype(F32) + two[z, links.second].astype(F32)).astype(BF16)
                return carry

            lax.fori_loop(0, depth, add_three, 0)
        elif self.alternate:
            self.finish(four[links.second].astype(F32) + four[2].astype(F32))
        else:
            total = three[links.group].astype(F32)
            for i in range(1, depth):
                total = total + four[i - 1].astype(F32)
            self.finish(total)

    def advance(self):
        if self.at > 3:
            return
        if self.at >= 0:
            for copy in self.copies():
                copy.wait()
            self.add()
        self.at += 1
        if self.at <= 3:
            for copy in self.copies():
                copy.start()


SCATTERED = {
    "cls": (64, 2 * LANES),
    "out1": (16, D),
    "mida1": (48, MID),
    "midb1": (48, MID),
    "midc1": (48, MID),
    "in1": (64, MID),
    "out0": (16, D),
    "mida0": (48, MID),
    "midb0": (48, MID),
    "midc0": (48, MID),
    "in0": (64, MID),
    "small": (80, LANES),
}


FLAT_MID = 256
FLAT_OUT = 832
FLAT_SMALL = 1088
FLAT_ROWS = 1122
FLAT_CLS = 2243
ORDER = (
    "cls", "@mid1a", "cls", "@mid1b", "mida1", "midb1", "midc1", "@mid1c", "cls", "mida1", "@in1a", "in1", "@in1b",
    "cls", "midb1", "@out1a", "mida1", "midc1", "@out1b", "out1", "cls", "@small1", "in1", "midb1", "out1",
    "@out0a", "midc1", "@out0b", "out0", "mida1", "@mid0a", "in1", "@mid0b", "mida0", "midb0", "midc0", "out0",
    "midb1", "out1", "@mid0c", "mida1", "midc1", "@small0", "small", "@in0a", "in0", "out0", "midb1", "@in0b",
    "in1", "out1", "mida0", "in0", "out0", "in1", "midc1", "mida0", "out1", "midb0", "in0", "out0", "mida0",
    "midc0", "midb0", "mida0", "in0", "small", "midc0", "midb0", "in0", "small", "midc0", "small", "midb0",
    "midc0", "small",
)
ALTERNATE = ("mida1", "midb1", "in1")

ORDER_FIRST = "mid1a"


def gradient_kernel(n_seg, n_clip, *refs):
    refs = list(refs)

    def pop(count=1):
        taken = refs[:count]
        del refs[:count]
        return taken if count != 1 else taken[0]

    sources = [pop(10) for _ in range(2)]
    cls_hbm, norm_rows_in, bias = pop(3)
    flat, tail = pop(2)
    big3, bigx, mid_a2, mid_d2, mid_d1, mid_low, mid_de, thin_dr, thin_s, fpad = pop(10)
    g_in, g_mid, g_out, g_small, g_cls, squares, turned = pop(7)
    sums = pop(4)
    buffers = {name: pop(4) for name in SCATTERED}
    send_sem, recv_sem = pop(2)
    links = Links(n_seg, n_clip, send_sem, recv_sem)
    cells, frames = bigx.shape[0], bigx.shape[1]
    rows_all = cells * frames
    devices = SMALL_SHARDS

    def load(source, target):
        copy = links.local(source.reshape(target.shape), target)
        copy.start()
        return copy

    interior = fpad.at[pl.ds(1, GRID), pl.ds(1, GRID)]
    names = ("x", "d1", "f", "d2", "a2", "d3", "low", "dr", "s", "de")
    targets = dict(zip(names, (bigx, mid_d1, interior, mid_d2, mid_a2, big3, mid_low, thin_dr, thin_s, mid_de)))
    hbm = [dict(zip(names, source)) for source in sources]

    def fetch(block, *keys):
        return [load(hbm[block][key], targets[key]) for key in keys]

    operands = {
        "out": ("a2", "d3"),
        "in": ("x", "d1"),
        "mid": ("f", "d2"),
        "small": ("low", "dr", "s", "de"),
    }
    load_cls = load(cls_hbm, g_cls)
    fpad[...] = jnp.zeros_like(fpad)
    waits = {"mid": fetch(1, *operands["mid"])}
    links.meet()
    squares[...] = jnp.zeros_like(squares)

    def folded(ref, rows):
        return ref.reshape(n_seg, links.outer, 4, rows, ref.shape[-1])

    grads = {"cls": g_cls, "small": g_small}
    jobs = {}

    def put(block, first, values, stride=1):
        count = values.shape[0]
        if block == 0:
            flat[pl.ds(first, count, stride), :] = values
        else:
            turned[pl.ds(first + 8, count, stride), :] = pltpu.roll(values, 64, 1)

    def put_small(total):
        lane = lax.broadcasted_iota(jnp.int32, (1, LANES), 1)
        for block in range(2):
            rows = total[32 * block : 32 * block + 32]
            put(block, FLAT_SMALL, rows[:16])
            for k in range(4):
                put(block, FLAT_SMALL + 16 + k, rows[16 + 4 * k : 20 + 4 * k], 4)
            gain = total[64 + 2 * block : 65 + 2 * block]
            shift = pltpu.roll(total[65 + 2 * block : 66 + 2 * block], 96, 1)
            put(block, FLAT_SMALL + 32, jnp.where(lane < 96, gain, shift))
            put(block, FLAT_SMALL + 33, shift)
        flat[FLAT_CLS + 87 : FLAT_CLS + 88, :] = total[68:69]

    def put_classifier(total):
        lane = lax.broadcasted_iota(jnp.int32, (1, LANES), 1)
        flat[FLAT_CLS:, :] = jnp.zeros_like(flat[FLAT_CLS:, :])
        for i in range(total.shape[0]):
            line, by = divmod(CLASSES * i, LANES)
            line += FLAT_CLS
            low, high = total[i : i + 1, :LANES], total[i : i + 1, LANES:]
            if by:
                low, high = pltpu.roll(low, by, 1), pltpu.roll(high, by, 1)
            here = lane >= by
            flat[line : line + 1, :] += jnp.where(here, low, 0.0)
            flat[line + 1 : line + 2, :] += jnp.where(here, high, low)
            if by + CLASSES - LANES > LANES:
                flat[line + 2 : line + 3, :] += jnp.where(here, 0.0, high)

    def make(name):
        kind = name[:-1] if name not in ("cls", "small") else name
        block = name[-1]
        rows, columns = SCATTERED[name]
        start = rows * "abc".index(kind[3]) if kind.startswith("mid") else 0
        ref = {"in": g_in, "out": g_out, "small": g_small, "cls": g_cls}.get(kind, g_mid)
        shard_rows = 3 * rows if kind.startswith("mid") else rows

        def finish(total):
            squares[:, :columns] += fold(total * total)
            if kind == "cls":
                put_classifier(total)
            elif kind == "small":
                put_small(total)
            else:
                lines = columns // LANES
                first = {"in": 0, "out": FLAT_OUT}.get(kind, FLAT_MID) + start * lines
                for k in range(lines):
                    put(int(block), first + k, total[:, k * LANES : (k + 1) * LANES], lines)

        jobs[name] = Scatter(links, folded(ref, shard_rows), pl.ds(start, rows), buffers[name], name in ALTERNATE, finish)

    for name in SCATTERED:
        make(name)

    def push(*wanted):
        for name in wanted:
            jobs[name].advance()

    def dot_tn(left, right):
        return lax.dot_general(left, right, (((0,), (0,)), ((), ())), preferred_element_type=F32)

    turn = 1 - links.seg

    def task_out(first, last):
        def body(k, carry):
            span = pl.ds(pl.multiple_of(k * MID, MID), MID)
            part = dot_tn(mid_a2[...].reshape(rows_all, MID), big3[:, :, span].reshape(rows_all, MID))
            g_out[:, span] = part.astype(BF16)
            return carry

        lax.fori_loop(first, last, body, 0)

    def task_in(first, last):
        def body(i, carry):
            k = i + turn * (3 - 2 * i)
            span = pl.ds(pl.multiple_of(k * MID, MID), MID)
            part = dot_tn(bigx[:, :, span].reshape(rows_all, MID), mid_d1[...].reshape(rows_all, MID))
            g_in[span, :] = part.astype(BF16)
            return carry

        lax.fori_loop(first, last, body, 0)

    def task_mid(first, last):
        def body(i, carry):
            k = i + turn * (8 - 2 * i)
            window = fpad[pl.ds(k // 3, GRID), pl.ds(lax.rem(k, 3), GRID)].reshape(rows_all, MID)
            part = dot_tn(window, mid_d2[...].reshape(rows_all, MID))
            g_mid[pl.ds(pl.multiple_of(k * MID, MID), MID), :] = part.astype(BF16)
            return carry

        lax.fori_loop(first, last, body, 0)

    def task_small(block):
        part = dot_tn(mid_low[...].reshape(rows_all, MID), thin_dr[...].reshape(rows_all, GATE))
        g_small[:, 32 * block : 32 * block + 16, :] = part.astype(BF16).reshape(devices, 16, LANES)
        part = dot_tn(thin_s[...].reshape(rows_all, GATE), mid_de[...].reshape(rows_all, MID)).astype(BF16)
        rows = jnp.zeros((devices * 16, LANES), F32)
        for k in range(MID // LANES):
            rows = rows + dot_tn(excite_pick(devices, k), part[:, k * LANES : (k + 1) * LANES])
        g_small[:, 32 * block + 16 : 32 * block + 32, :] = rows.astype(BF16).reshape(devices, 16, LANES)

    def run(piece):
        letter = piece[-1] if piece[-1] in "abc" else ""
        kind, block = piece[: len(piece) - 1 - len(letter)], int(piece[len(piece) - 1 - len(letter)])
        part = "abc".index(letter) if letter else 0
        if part == 0:
            for copy in waits[kind]:
                copy.wait()
            if block == 0 and kind != "small":
                for name in SCATTERED:
                    if name.startswith(kind) and name[-1] == "1":
                        while jobs[name].at < 1:
                            jobs[name].advance()
        if kind == "mid":
            task_mid((0, 3, 5)[part], (3, 5, 9)[part])
        elif kind == "in":
            task_in(2 * part, 2 * part + 2)
        elif kind == "out":
            task_out(2 * part, 2 * part + 2)
        else:
            task_small(block)
        if block == 1 and part == {"mid": 2, "in": 1, "out": 1, "small": 0}[kind]:
            waits[kind] = fetch(0, *operands[kind])
        if block == 1 and piece == ORDER_FIRST:
            for other in ("in", "out", "small"):
                waits[other] = fetch(1, *operands[other])

    g_small[:, 64:80, :] = norm_rows_in[...]
    load_cls.wait()
    for item in ORDER:
        if item[0] == "@":
            with jax.named_scope("product"):
                run(item[1:])
        else:
            push(item)
    for name in SCATTERED:
        while jobs[name].at <= 3:
            jobs[name].advance()
    lane = lax.broadcasted_iota(jnp.int32, (FLAT_ROWS, LANES), 1)
    now, before = turned[8 : 8 + FLAT_ROWS, :], turned[7 : 7 + FLAT_ROWS, :]
    old = flat[FLAT_SMALL + 33 : FLAT_SMALL + 34, :]
    flat[FLAT_ROWS - 1 : 2 * FLAT_ROWS - 1, :] = jnp.where(lane < 64, before, now)
    flat[FLAT_ROWS - 1 : FLAT_ROWS, :] = jnp.where(lane[:1] < 64, old, now[:1])
    total = jnp.sum(jnp.sum(squares[...], axis=0, keepdims=True), axis=1, keepdims=True)
    sums[0][0:8, :] = bias[...]
    sums[0][8:16, :] = jnp.broadcast_to(total, (8, LANES))
    tail[...] = links.all_sum(*sums)


def gradient_sums(sources, g_cls, norm_rows_in, bias):
    n_seg = lax.axis_size("seg")
    n_clip = lax.axis_size("clip")
    depth = n_clip // 4
    cells, frames, width = sources[0][0].shape
    any_spec = pl.BlockSpec(memory_space=pl.ANY)
    vmem = pl.BlockSpec(memory_space=pltpu.VMEM)

    def grid_shape(columns):
        return pltpu.VMEM((cells, frames, columns), BF16)

    outs = [(FLAT_CLS + 93, LANES), (16, LANES)]
    scratch = [grid_shape(D), grid_shape(D)] + [grid_shape(MID)] * 5 + [grid_shape(GATE)] * 2
    scratch += [
        pltpu.VMEM((GRID + 2, GRID + 2, frames, MID), BF16),
        pltpu.VMEM((D, MID), BF16),
        pltpu.VMEM((9 * MID, MID), BF16),
        pltpu.VMEM((MID, D), BF16),
        pltpu.VMEM((SMALL_SHARDS, 80, LANES), BF16),
        pltpu.VMEM((D, 2 * LANES), BF16),
        pltpu.VMEM((8, D), F32),
        pltpu.VMEM((FLAT_ROWS + 14, LANES), F32),
    ]
    scratch += sum_scratch(n_seg, n_clip, (16, LANES))
    for name, shape in SCATTERED.items():
        ends = ((depth - 1, 2), (3,)) if name in ALTERNATE else ((depth,), (depth - 1,))
        for lead in ((depth, 4), (depth, 2)) + ends:
            scratch.append(pltpu.VMEM(lead + shape, BF16))
    count = n_seg * 4 + depth + len(SCATTERED) * (depth + 3) + 40
    scratch += [pltpu.SemaphoreType.DMA((count,)), pltpu.SemaphoreType.DMA((count,))]
    return pl.pallas_call(
        functools.partial(gradient_kernel, n_seg, n_clip),
        out_shape=[jax.ShapeDtypeStruct(s, F32) for s in outs],
        in_specs=[any_spec] * 21 + [vmem, vmem],
        out_specs=[vmem] * len(outs),
        scratch_shapes=scratch,
        compiler_params=pltpu.CompilerParams(
            collective_id=50, has_side_effects=True, vmem_limit_bytes=62 * 1024 * 1024
        ),
        name="gradient_sums",
    )(*sources[0], *sources[1], g_cls, norm_rows_in, bias)


def weight_gradients(x, d_one, gated, d_two, a_two, d_three, a_low, d_reduced, mixed, d_excite):
    return [
        matmul(x.reshape(-1, D).T, d_one.reshape(-1, MID)),
        conv(gated, d_two, ("HWCN", "HWIO", "HWNC")).reshape(9 * MID, MID),
        matmul(a_two.reshape(-1, MID).T, d_three.reshape(-1, D)),
        matmul(a_low.reshape(-1, MID).T, d_reduced.reshape(-1, GATE)),
        matmul(mixed.reshape(-1, GATE).T, d_excite.reshape(-1, MID)),
    ]


def on_device(inputs, clip_counts, labels, master, first_moment, second_moment):
    seg_count = lax.axis_size("seg")
    clip_local, slot_local = inputs.shape[:2]
    frames = clip_local * slot_local
    slot_ids = lax.axis_index("seg") * slot_local + jnp.arange(slot_local, dtype=jnp.int32)
    present = (slot_ids[None, :] < clip_counts[:, None]).astype(F32)
    following = (slot_ids[None, :] + 1 < clip_counts[:, None]).astype(F32)
    frame_mask = jnp.broadcast_to(present.reshape(frames, 1), (frames, MID))
    frame_following = jnp.broadcast_to(following.reshape(frames, 1), (frames, GATE))
    table = jnp.zeros(TABLE, F32)
    x_low = inputs.reshape(frames, HW, D).transpose(1, 0, 2)
    shards = weight_shards(master)
    if shards is None:
        weights = whole_weights(master)
        jobs = ((), ())
    else:
        weights = {}
        jobs = JOBS
    rows = ((0, 8 - clip_local), (0, 0))
    share = jnp.pad(1.0 / (HW * clip_counts.astype(F32))[:, None], rows)
    share = jnp.broadcast_to(share, (8, LANES))
    onehot = (labels[:, None] == jnp.arange(2 * LANES, dtype=jnp.int32)[None, :]).astype(F32)
    target = jnp.pad(onehot, rows)
    kept = []
    flowing = x_low
    flows = []
    for block in range(2):
        flows.append(flowing)
        names = weight_names(block) + (["cls"] if block == 1 else [])
        given = {name: weights[name] for name in names if name not in jobs[block]}
        gathered, results = forward_block(
            block,
            flowing,
            frame_mask,
            frame_following,
            table,
            (share, target) if block == 1 else (),
            {name: shards[name] for name in jobs[block]},
            given,
        )
        weights.update(gathered)
        if block == 0:
            table = results[9]
        kept.append(results[:8] + results[10:13])
        flowing = results[8]
    d_flow = flowing
    g_cls, g_bias = results[13:]
    g_bias = g_bias[0, :CLASSES]
    masks = (frame_mask, frame_mask[:, :GATE], frame_following)
    sources = [None, None]
    norm_grads = [None, None]
    for block in (1, 0):
        h_one, a_low, gate, mixed, gated, h_two, a_two, h_three, st_one, st_two, st_three = kept[block]
        *steps, d_flow, norm_sums = backward_block(
            block,
            h_three,
            flows[block],
            d_flow,
            h_two,
            h_one,
            gate,
            [weights[name] for name in weight_names(block)],
            table,
            (st_one, st_two, st_three),
            masks,
        )
        sources[block] = (flows[block], steps[4], gated, steps[1], a_two, steps[0], a_low, steps[3], mixed, steps[2])
        norm_grads[block] = [norm_sums[:24].reshape(-1), norm_sums[24:].reshape(-1)]
    devices = seg_count * lax.axis_size("clip")
    bias_rows = jnp.pad(g_bias, (0, 8 * LANES - CLASSES)).reshape(8, LANES)
    if shards is None:
        grads = []
        for block in (0, 1):
            grads += weight_gradients(*sources[block]) + [v / devices for v in norm_grads[block]]
        grad_mine = scatter_gradients(grads + [g_cls[:, :CLASSES].astype(F32), g_bias])
        square = jnp.full((8, LANES), jnp.sum(grad_mine * grad_mine), F32)
        tail = lax.psum(jnp.concatenate([bias_rows, square]), AXES)
    else:
        vectors = [v.reshape(SMALL_SHARDS, -1) / devices for b in (0, 1) for v in norm_grads[b]]
        padded = jnp.pad(g_bias, (0, 6 * SMALL_SHARDS - CLASSES)).reshape(SMALL_SHARDS, 6)
        extra = norm_rows(vectors + [padded]).astype(BF16)
        flat, tail = gradient_sums(sources, g_cls, extra, bias_rows)
        grad_mine = flat.reshape(-1)[: master.shape[0]]
    norm = jnp.sqrt(tail[8, 0])
    bias_grad = tail[:8].reshape(-1)[:CLASSES]
    factor = jnp.minimum(1.0, CLIP_LIMIT / (norm + 1e-06))
    clipped = grad_mine * factor
    new_first = BETA_ONE * first_moment + (1.0 - BETA_ONE) * clipped
    new_second = BETA_TWO * second_moment + (1.0 - BETA_TWO) * clipped * clipped
    first_hat = new_first / (1.0 - BETA_ONE**STEP)
    second_hat = new_second / (1.0 - BETA_TWO**STEP)
    new_master = master - LEARN_RATE * (
        first_hat / (jnp.sqrt(second_hat) + ADAM_EPS) + WEIGHT_DECAY * master
    )
    grid_grad = d_flow.transpose(1, 0, 2).reshape(inputs.shape)
    return (
        new_master,
        new_first,
        new_second,
        new_master.astype(BF16),
        grid_grad.reshape(inputs.shape),
        norm.reshape(1),
        bias_grad,
    )


def solution(mesh):
    return jax.shard_map(
        on_device,
        mesh=mesh,
        in_specs=(
            P("clip", "seg", None, None),
            P("clip"),
            P("clip"),
            P(AXES),
            P(AXES),
            P(AXES),
        ),
        out_specs=(
            P(AXES),
            P(AXES),
            P(AXES),
            P(AXES),
            P("clip", "seg", None, None),
            P(),
            P(),
        ),
        check_vma=False,
    )
```

```python
import functools
import math

import jax
import jax.numpy as jnp
from jax import lax
from jax.experimental import pallas as pl
from jax.experimental.pallas import tpu as pltpu
from jax.sharding import PartitionSpec as P

D = 2048
MID = 512
GATE = 128
CLASSES = 174
GRID = 7
HW = 49
STEP = 7
LANES = 128

NORM_EPS = 1e-05
CLIP_LIMIT = 0.001
LEARN_RATE = 0.04
WEIGHT_DECAY = 0.05
BETA_ONE = 0.9
BETA_TWO = 0.999
ADAM_EPS = 1e-08

AXES = ("seg", "clip")
MESH_ID = pl.DeviceIdType.MESH
BF16 = jnp.bfloat16
F32 = jnp.float32


def matmul(left, right):
    return jnp.dot(left, right, preferred_element_type=F32)


def layout():
    block_layout = [
        (D, MID),
        (9, MID, MID),
        (MID, D),
        (MID, GATE),
        (GATE, MID),
        (2 * MID + D,),
        (2 * MID + D,),
    ]
    return block_layout + block_layout + [(D, CLASSES), (CLASSES,)]


def widths(devices):
    return [(math.prod(extent) + devices - 1) // devices for extent in layout()]


def pad_rows(flat, rows):
    return jnp.pad(flat, (0, rows * LANES - flat.shape[0])).reshape(rows, LANES)


def small_rows(devices):
    wide = widths(devices)
    amount = sum(wide[3:7]) + sum(wide[10:14])
    amount_cls = wide[14] + wide[15]
    return [16 * ((a + 16 * LANES - 1) // (16 * LANES)) for a in (amount, amount_cls)]


def gather_parameters(master):
    devices = lax.axis_size("seg") * lax.axis_size("clip")
    wide = widths(devices)
    starts = [sum(wide[:i]) for i in range(len(wide))]
    low = master.astype(BF16)

    def part(i):
        return low[starts[i] : starts[i] + wide[i]]

    def gather(values):
        return lax.all_gather(values, AXES, axis=0, tiled=True)

    big = {}
    for base in (0, 7):
        for i, columns in ((0, MID), (1, MID), (2, D)):
            big[base + i] = gather(part(base + i).reshape(-1, columns))
    rows, rows_cls = small_rows(devices)
    small = gather(pad_rows(jnp.concatenate([part(i) for i in (3, 4, 5, 6, 10, 11, 12, 13)]), rows))
    small_cls = gather(pad_rows(jnp.concatenate([part(14), part(15)]), rows_cls))
    small = small.reshape(devices, rows * LANES)
    small_cls = small_cls.reshape(devices, rows_cls * LANES)
    shapes = layout()
    pieces = dict(big)

    def take(source, ids):
        offset = 0
        for i in ids:
            amount = math.prod(shapes[i])
            pieces[i] = source[:, offset : offset + wide[i]].reshape(-1)[:amount].reshape(shapes[i])
            offset += wide[i]

    take(small, (3, 4, 5, 6, 10, 11, 12, 13))
    take(small_cls, (14, 15))
    return [pieces[i] for i in range(16)]


def part_of(master, index):
    devices = lax.axis_size("seg") * lax.axis_size("clip")
    wide = widths(devices)
    start = sum(wide[:index])
    return master[start : start + wide[index]]


def norm_rows(vectors):
    rows = jnp.stack([jnp.pad(v, ((0, 0), (0, LANES - v.shape[1]))) for v in vectors], axis=1)
    return jnp.pad(rows, ((0, 0), (0, 16 - rows.shape[1]), (0, 0)))


def lanes_first(values):
    lead = values.shape[:-2]
    rows, columns = values.shape[-2:]
    split = values.reshape(lead + (rows, columns // LANES, LANES))
    return jnp.swapaxes(split, -3, -2).reshape(lead + (-1, LANES))


def split_rows(target, kind, block, pieces, rows):
    size = rows.shape[1] // pieces
    for k, name in enumerate(piece_names(kind, block, pieces)):
        target[name] = rows[:, k * size : (k + 1) * size].reshape(-1, MID)


def piece_names(kind, block, pieces):
    return [kind + "abc"[k] + str(block) for k in range(pieces)]


def weight_names(block):
    return piece_names("in", block, 2) + piece_names("mid", block, 3) + ["out%d" % block, "small"]


def weight_shards(master):
    devices = lax.axis_size("seg") * lax.axis_size("clip")
    if lax.axis_size("seg") != 2 or devices != SMALL_SHARDS:
        return None
    low = master.astype(BF16)
    shards = {}
    small = []
    for block in range(2):
        base = 7 * block
        split_rows(shards, "in", block, 2, part_of(low, base).reshape(1, -1, MID))
        split_rows(shards, "mid", block, 3, part_of(low, base + 1).reshape(1, -1, MID))
        shards["out%d" % block] = part_of(low, base + 2).reshape(-1, D)
        small.append(part_of(low, base + 3).reshape(-1, GATE))
        small.append(lanes_first(part_of(low, base + 4).reshape(-1, MID)))
    small.append(norm_rows([part_of(low, i)[None] for i in (5, 6, 12, 13, 15)])[0])
    shards["small"] = jnp.concatenate(small)
    cls = part_of(low, 14).reshape(-1, CLASSES)
    shards["cls"] = jnp.pad(cls, ((0, 0), (0, 2 * LANES - CLASSES)))
    return shards


def whole_weights(master):
    pieces = gather_parameters(master)
    whole = {}
    small = []
    for block in range(2):
        w_in, w_mid, w_out, w_red, w_exp = pieces[7 * block : 7 * block + 5]
        split_rows(whole, "in", block, 2, w_in.reshape(SMALL_SHARDS, -1, MID))
        split_rows(whole, "mid", block, 3, w_mid.reshape(SMALL_SHARDS, -1, MID))
        whole["out%d" % block] = w_out
        small.append(w_red.reshape(SMALL_SHARDS, -1, GATE))
        small.append(lanes_first(w_exp.reshape(SMALL_SHARDS, -1, MID)))
    vectors = [pieces[i].reshape(SMALL_SHARDS, -1) for i in (5, 6, 12, 13)]
    bias = jnp.pad(pieces[15], (0, 6 * SMALL_SHARDS - CLASSES)).reshape(SMALL_SHARDS, 6)
    small.append(norm_rows(vectors + [bias]))
    whole["small"] = jnp.concatenate(small, axis=1).reshape(-1, LANES)
    whole["cls"] = jnp.pad(pieces[14], ((0, 0), (0, 2 * LANES - CLASSES)))
    return whole


def scatter_gradients(grads):
    devices = lax.axis_size("seg") * lax.axis_size("clip")
    wide = widths(devices)
    columns = []
    for values, width in zip(grads, wide):
        flat = values.reshape(-1)
        columns.append(jnp.pad(flat, (0, devices * width - flat.shape[0])).reshape(devices, width))
    packed = jnp.concatenate(columns, axis=1)
    return lax.psum_scatter(packed, AXES, scatter_dimension=0, tiled=True)[0]


def conv(values, kernel, numbers):
    return lax.conv_general_dilated(
        values, kernel, (1, 1), ((1, 1), (1, 1)), dimension_numbers=numbers, preferred_element_type=F32
    )


class Links:
    def __init__(self, n_seg, n_clip, send_sem, recv_sem):
        self.n_seg = n_seg
        self.n_clip = n_clip
        self.inner = 4
        self.outer = n_clip // 4
        self.seg = lax.axis_index("seg")
        self.clip = lax.axis_index("clip")
        self.group = self.clip // 4
        self.place = lax.rem(self.clip, 4)
        y = self.place // 2
        x = lax.rem(self.place, 2)
        self.first = (1 - self.seg) * y + self.seg * x
        self.second = (1 - self.seg) * x + self.seg * y
        self.step = 1 + self.seg
        self.jump = 2 - self.seg
        self.across_first = (self.seg, self.clip + self.jump * (1 - 2 * self.first))
        self.across_second = (self.seg, self.clip + self.step * (1 - 2 * self.second))
        self.other = (1 - self.seg, self.clip)
        self.send_sem = send_sem
        self.recv_sem = recv_sem
        self.used = 0

    def take(self, count):
        base = self.used
        self.used += count
        return base

    def near_peer(self, i):
        return (
            lax.rem(self.seg + i // 4, self.n_seg),
            self.group * 4 + lax.rem(self.place + lax.rem(i, 4), 4),
        )

    def far_peer(self, i):
        return (self.seg, lax.rem(self.group + i, self.outer) * 4 + self.place)

    def remote(self, index, source, target, peer):
        return pltpu.make_async_remote_copy(
            src_ref=source,
            dst_ref=target,
            send_sem=self.send_sem.at[index],
            recv_sem=self.recv_sem.at[index],
            device_id=peer,
            device_id_type=MESH_ID,
        )

    def local(self, source, target):
        return pltpu.make_async_copy(source, target, self.recv_sem.at[self.take(1)])

    def meet(self):
        barrier = pltpu.get_barrier_semaphore()
        n_near = self.n_seg * 4 - 1
        n_far = self.outer - 1

        def greet(peer):
            pl.semaphore_signal(barrier, inc=1, device_id=peer, device_id_type=MESH_ID)

        repeat(1, n_near + 1, lambda i: greet(self.near_peer(i)))
        repeat(1, n_far + 1, lambda i: greet(self.far_peer(i)))
        pl.semaphore_wait(barrier, n_near + n_far)

    def sum_near(self, source, middle, near, far):
        n_near = self.n_seg * 4 - 1
        n_far = self.outer - 1
        base = self.take(n_near + n_far)

        def close(i):
            return self.remote(base + i - 1, source, near.at[i - 1], self.near_peer(i))

        def distant(i):
            return self.remote(base + n_near + i - 1, middle, far.at[i - 1], self.far_peer(i))

        repeat(1, n_near + 1, lambda i: close(i).start())
        repeat(1, n_near + 1, lambda i: close(i).wait())
        middle[...] = source[...] + jnp.sum(near[...], axis=0)
        repeat(1, n_far + 1, lambda i: distant(i).start())

        def rest():
            repeat(1, n_far + 1, lambda i: distant(i).wait())
            return middle[...] + jnp.sum(far[...], axis=0)

        return rest

    def all_sum(self, source, middle, near, far):
        return self.sum_near(source, middle, near, far)()


def repeat(first, last, action):
    if last - first <= 8:
        for i in range(first, last):
            action(i)
    else:

        def body(i, carry):
            action(i)
            return carry

        lax.fori_loop(first, last, body, 0)


def sum_scratch(n_seg, n_clip, shape):
    return [
        pltpu.VMEM(shape, F32),
        pltpu.VMEM(shape, F32),
        pltpu.VMEM((n_seg * 4 - 1,) + shape, F32),
        pltpu.VMEM((n_clip // 4 - 1,) + shape, F32),
    ]


class Gather:
    def __init__(self, links, shard, whole):
        depth = links.outer
        whole = whole.reshape((links.n_seg, depth, 4) + shard.shape)
        base = links.take(depth + 3)
        seg, z, place = links.seg, links.group, links.place
        self.own = links.local(shard, whole.at[seg, z, place])
        self.steps = [
            [
                links.remote(base + i - 1, shard, whole.at[seg, z, place], links.far_peer(i))
                for i in range(1, depth)
            ],
            [
                links.remote(
                    base + depth - 1, whole.at[seg, :, place], whole.at[seg, :, place], links.across_second
                )
            ],
            [],
            [links.remote(base + depth + 2, whole.at[seg], whole.at[seg], links.other)],
        ]
        for k in range(2):
            index = links.jump * links.first + links.step * k
            self.steps[2].append(
                links.remote(
                    base + depth + k, whole.at[seg, :, index], whole.at[seg, :, index], links.across_first
                )
            )
        self.at = -1

    def advance(self, last=3):
        if self.at >= 0:
            for copy in self.steps[self.at]:
                copy.wait()
            if self.at == 0:
                self.own.wait()
        self.at += 1
        if self.at == 0:
            self.own.start()
        if self.at <= 3:
            for copy in self.steps[self.at]:
                copy.start()

    def finish(self):
        while self.at <= 3:
            self.advance()


def row_vector(table, row, start, count):
    return jnp.concatenate([table[start + k, row : row + 1, :] for k in range(count)], axis=1)


def build_table(small, table):
    lane = lax.broadcasted_iota(jnp.int32, (8, LANES), 1)
    for q in range(SMALL_SHARDS // 4):
        rows = [small[4 * q + j, 64:80, :].astype(F32)[:8] for j in range(4)]
        one = pltpu.roll(rows[1], 96, 1)
        two = pltpu.roll(rows[2], 64, 1)
        three = pltpu.roll(rows[3], 32, 1)
        table[3 * q] = jnp.where(lane < 96, rows[0], one)
        table[3 * q + 1] = jnp.where(lane < 64, one, two)
        table[3 * q + 2] = jnp.where(lane < 32, two, three)


def put_rows(target, start, vector, count):
    width = vector.shape[1] // count
    for k in range(count):
        target[start + k : start + k + 1, :] = vector[:, k * width : (k + 1) * width]


def fold(values):
    return jnp.sum(values.reshape(-1, 8, values.shape[-1]), axis=0)


def excite_pick(shards, k):
    deep = GATE // shards
    line = lax.broadcasted_iota(jnp.int32, (GATE, shards * 16), 0)
    column = lax.broadcasted_iota(jnp.int32, (GATE, shards * 16), 1)
    wanted = (line // deep) * 16 + k * deep + lax.rem(line, deep)
    return (column == wanted).astype(F32).astype(BF16)


def excite_weights(small, block):
    shards = small.shape[0]
    rows = small[:, 32 * block + 16 : 32 * block + 32].reshape(shards * 16, LANES)
    parts = [matmul(excite_pick(shards, k), rows) for k in range(MID // LANES)]
    return jnp.concatenate(parts, axis=1).astype(BF16)


SMALL_SHARDS = 32
SLOTS_HERE = 8
TABLE = ((2 * MID + D) // LANES + 1, 8, LANES)


STAGES = (
    (
        "ina0", "small", "@dpad", "@fpad", "@turn0", "inb0", "@turn1", "@turn2", "@turn3", "@turn4", "mida0",
        "@turn5", "@turn6", "ina0", "small", "ina0", "midb0", "inb0", "small", "mida0", "midc0", "ina0", "inb0",
        "small", "out0", "ina0", "midb0", "mida0", "small", "midc0", "ina1", "inb0", "midb0", "inb1", "inb0",
        "@first", "mida1", "mida0", "midc0", "out0", "ina1", "@near1", "midb1", "mida0", "midb0", "inb1", "@far1",
        "midc1", "midb0", "midc0", "out0", "ina1", "mida1", "@second", "inb1", "@swap", "@excite", "midc0",
        "midb1", "@third", "out0", "ina1", "mida1", "midc1", "@near2", "out0", "ina1", "inb1", "midb1", "@far2",
        "mida1", "midc1", "@fourth", "inb1", "mida1", "midb1", "@near3", "midc1", "@far3", "midb1", "@fifth",
        "midc1",
    ),
    (
        "out1", "@dpad", "@fpad", "@first", "cls", "@near1", "out1", "@far1", "cls", "@second", "@swap", "out1",
        "@excite", "cls", "@third", "out1", "@near2", "cls", "@far2", "out1", "@fourth", "cls", "@near3", "@far3",
        "@fifth",
    ),
)
JOBS = tuple(tuple(dict.fromkeys(item for item in order if item[0] != "@")) for order in STAGES)


def forward_kernel(n_seg, n_clip, block, jobs, plan, *refs):
    refs = list(refs)

    def pop(count=1):
        taken = refs[:count]
        del refs[:count]
        return taken if count != 1 else taken[0]

    last = block == 1
    x_hbm, mask, following, table_in = pop(4)
    share, chosen = pop(2) if last else (None, None)
    shards = dict(zip(jobs, [pop() for _ in jobs]))
    given = dict(zip(plan, [pop() for _ in plan]))
    wholes = dict(zip(jobs, [pop() for _ in jobs]))
    h1_out, low_out, gate_out, mix_out, f_out, h2_out, a2_out, h3_out = pop(8)
    out_hbm, table_out, st1, st2, st3 = pop(5)
    g_cls, g_bias = pop(2) if last else (None, None)
    x_out = None if last else pop()
    xv, w_in, w_mid, w_out, small = pop(5)
    h1v, a1v, lowv, rv, edge, dpad, mixv, gatev, fpad, h2v, a2v, h3v = pop(12)
    wide_sum, wide_square, w_exp = pop(3)
    sums = [pop(4) for _ in range(3)]
    pooled, clip_sums, clip_other, w_cls = pop(4) if last else [None] * 4
    frames_first = None if last else pop()
    send_sem, recv_sem = pop(2)
    links = Links(n_seg, n_clip, send_sem, recv_sem)
    frames = xv.shape[1]
    table = table_in if last else table_out
    outgoing = []

    def send_out(source, target):
        copy = links.local(source, target)
        copy.start()
        outgoing.append(copy)

    links.meet()
    x_base = links.take(GRID)

    def load_x(i):
        rows = pl.ds(GRID * i, GRID)
        return pltpu.make_async_copy(x_hbm.at[rows], xv.at[rows], links.recv_sem.at[x_base + i])

    if last:
        for i in range(GRID):
            load_x(i).start()
    else:
        load_frames = links.local(x_hbm, frames_first)
        load_frames.start()
    gathers = {name: Gather(links, shards[name], wholes[name]) for name in jobs}

    targets = {"out%d" % block: w_out, "small": small}
    if last:
        targets["cls"] = w_cls
    for kind, target, count in (("in", w_in, 2), ("mid", w_mid, 3)):
        rows = target.shape[0] // SMALL_SHARDS
        size = rows // count
        wide = target.reshape(SMALL_SHARDS, rows, MID)
        for k, name in enumerate(piece_names(kind, block, count)):
            targets[name] = wide.at[:, k * size : (k + 1) * size]
    loads = {}

    def load(name):
        source = wholes[name] if name in gathers else given[name]
        loads[name] = links.local(source.reshape(targets[name].shape), targets[name])
        loads[name].start()

    def push(name):
        if gathers[name].at <= 3:
            gathers[name].advance()
            if gathers[name].at > 3 and name in targets:
                load(name)

    def need(*names):
        for name in names:
            while name not in loads:
                push(name)
        for name in names:
            loads[name].wait()

    for name in targets:
        if name not in gathers:
            load(name)
    table = table_in if last else table_out
    half = MID // LANES

    def norm(index, tot, columns, start, out):
        live_rows = table[TABLE[0] - 1, 0:1, 0:1]
        mean = jnp.concatenate([tot[k : k + 1] for k in range(4)], axis=1) / live_rows
        square = jnp.concatenate([tot[4 + k : 5 + k] for k in range(4)], axis=1) / live_rows
        inv = lax.rsqrt(square - mean * mean + NORM_EPS)
        out[0:1, :] = mean
        out[1:2, :] = inv
        gain = row_vector(table, 2 * block, start, columns // LANES)
        shift = row_vector(table, 2 * block + 1, start, columns // LANES)
        scale = gain * inv
        return scale, shift - mean * scale

    def masked_sums(values):
        shaped = values.reshape(-1, frames, values.shape[-1])
        masked = shaped * mask[...][None]
        return fold(masked), fold(masked * shaped)

    zeros = jnp.zeros((8, MID), F32)
    kept = {}

    def first(i, carry):
        if last:
            load_x(i).wait()
        part = matmul(xv[pl.ds(GRID * i, GRID)].reshape(GRID * frames, D), w_in[...])
        h1v[pl.ds(GRID * i, GRID)] = part.reshape(GRID, frames, MID)
        one, two = masked_sums(part)
        return (carry[0] + one, carry[1] + two)

    def put_sums(index, one, two):
        stat = sums[index][0]
        put_rows(stat, 0, jnp.sum(one, axis=0, keepdims=True), 4)
        put_rows(stat, 4, jnp.sum(two, axis=0, keepdims=True), 4)
        return stat

    def stage_dpad():
        dpad[...] = jnp.zeros_like(dpad)

    def stage_fpad():
        fpad[...] = jnp.zeros_like(fpad)
        if last:
            table_out[...] = table_in[...]
        else:
            table_out[...] = jnp.zeros_like(table_out)

    def turn(step):
        if step == 0:
            load_frames.wait()

        def body(p, carry):
            for k in range(4):
                span = slice(k * MID, (k + 1) * MID)
                parts = [frames_first[c, p, :, span].astype(F32) for c in range(frames_first.shape[0])]
                xv[p, :, span] = jnp.concatenate(parts, axis=0).astype(BF16)
            return carry

        lax.fori_loop(GRID * step, GRID * step + GRID, body, 0)
        if step == GRID - 1:
            kept["x"] = links.local(xv, x_out)
            kept["x"].start()

    def stage_first():
        need(*piece_names("in", block, 2))
        stat = put_sums(0, *lax.fori_loop(0, GRID, first, (zeros, zeros)))
        present = HW * jnp.sum(mask[:, :LANES], axis=0, keepdims=True)
        stat[8:16, :] = jnp.broadcast_to(present, (8, LANES))
        send_out(h1v, h1_out)

    def stage_near1():
        kept["rest"] = links.sum_near(*sums[0])

    def stage_far1():
        need("small")
        total = kept["rest"]()
        if not last:
            build_table(small, table_out)
            table_out[TABLE[0] - 1] = total[8:16]
        kept["one"] = norm(0, total, MID, 0, st1)

    def second(i, carry):
        for j in range(GRID):
            y = h1v[GRID * i + j] * kept["one"][0] + kept["one"][1]
            a = y * jax.nn.sigmoid(y)
            a1v[GRID * i + j] = a
            lowv[GRID * i + j] = a.astype(BF16)
        part = matmul(lowv[pl.ds(GRID * i, GRID)].reshape(GRID * frames, MID), kept["red"])
        rv[pl.ds(GRID * i, GRID)] = part.astype(BF16).reshape(GRID, frames, GATE)
        return carry

    def stage_second():
        w_exp[...] = excite_weights(small, block)
        kept["red"] = small[:, 32 * block : 32 * block + 16].reshape(MID, GATE)
        lax.fori_loop(0, GRID, second, 0)
        send_out(lowv, low_out)
        kept["swap"] = links.remote(links.take(1), rv, edge, links.other)
        kept["swap"].start()

    row = lax.rem(lax.broadcasted_iota(jnp.int32, (frames, GATE), 0), 8)

    def change(i, carry):
        for j in range(GRID):
            now = rv[GRID * i + j].astype(F32)
            rest = edge[GRID * i + j].astype(F32)
            later = jnp.where(row < 7, pltpu.roll(now, frames - 1, 0), pltpu.roll(rest, 7, 0))
            dpad[i + 1, j + 1] = following[...] * (later - now)
        return carry

    def stage_swap():
        kept["swap"].wait()
        lax.fori_loop(0, GRID, change, 0)

    def excite(i, carry):
        for j in range(GRID):
            total = jnp.zeros((frames, GATE), F32)
            for k in range(9):
                total = total + dpad[i + k // 3, j + k % 3]
            mixv[GRID * i + j] = (dpad[i + 1, j + 1] + total / 9.0).astype(BF16)
        e = matmul(mixv[pl.ds(GRID * i, GRID)].reshape(GRID * frames, GATE), w_exp[...])
        e = e.reshape(GRID, frames, MID)
        for j in range(GRID):
            gate = jax.nn.sigmoid(e[j])
            gatev[GRID * i + j] = gate.astype(BF16)
            fpad[i + 1, j + 1] = (a1v[GRID * i + j] * (1.0 + gate)).astype(BF16)
        return carry

    def stage_excite():
        lax.fori_loop(0, GRID, excite, 0)
        send_out(mixv, mix_out)
        send_out(gatev, gate_out)
        send_out(fpad.at[pl.ds(1, GRID), pl.ds(1, GRID)], f_out)

    def third(i, carry):
        part = None
        for k in range(9):
            window = fpad[i + k // 3, pl.ds(k % 3, GRID)].reshape(GRID * frames, MID)
            term = matmul(window, w_mid[k * MID : (k + 1) * MID])
            part = term if part is None else part + term
        h2v[pl.ds(GRID * i, GRID)] = part.reshape(GRID, frames, MID)
        one, two = masked_sums(part)
        return (carry[0] + one, carry[1] + two)

    def stage_third():
        need(*piece_names("mid", block, 3))
        put_sums(1, *lax.fori_loop(0, GRID, third, (zeros, zeros)))
        send_out(h2v, h2_out)

    def stage_near2():
        kept["rest"] = links.sum_near(*sums[1])

    def stage_far2():
        kept["two"] = norm(1, kept["rest"](), MID, half, st2)
        wide_sum[...] = jnp.zeros_like(wide_sum)
        wide_square[...] = jnp.zeros_like(wide_square)

    def fourth(i, carry):
        for j in range(GRID):
            y = h2v[GRID * i + j] * kept["two"][0] + kept["two"][1]
            a2v[GRID * i + j] = (y * jax.nn.sigmoid(y)).astype(BF16)
        rows = a2v[pl.ds(GRID * i, GRID)].reshape(GRID * frames, MID)
        for k in range(4):
            part = matmul(rows, w_out[:, k * MID : (k + 1) * MID])
            h3v[pl.ds(GRID * i, GRID), :, k * MID : (k + 1) * MID] = part.astype(BF16).reshape(
                GRID, frames, MID
            )
            one, two = masked_sums(part)
            wide_sum[:, k * MID : (k + 1) * MID] += one
            wide_square[:, k * MID : (k + 1) * MID] += two
        return carry

    def stage_fourth():
        need("out%d" % block)
        lax.fori_loop(0, GRID, fourth, 0)
        put_sums(2, wide_sum[...], wide_square[...])
        send_out(a2v, a2_out)
        send_out(h3v, h3_out)

    def stage_near3():
        kept["rest"] = links.sum_near(*sums[2])

    def stage_far3():
        kept["three"] = norm(2, kept["rest"](), D, 2 * half, st3)
        if last:
            pooled[...] = jnp.zeros_like(pooled)

    def fifth(p, carry):
        for k in range(4):
            span = slice(k * MID, (k + 1) * MID)
            scale, shift = kept["three"]
            pre = h3v[p, :, span].astype(F32) * scale[:, span] + shift[:, span]
            pre = pre + xv[p, :, span].astype(F32)
            value = pre * jax.nn.sigmoid(pre)
            if last:
                pooled[:, span] += value * mask[...]
            else:
                xv[p, :, span] = value.astype(BF16)
        return carry

    def stage_fifth():
        if not last:
            kept["x"].wait()
        lax.fori_loop(0, HW, fifth, 0)
        if last:
            classify()
        send_out(pooled if last else xv, out_hbm)

    def classify():
        clips = frames // SLOTS_HERE
        clip_sums[...] = jnp.zeros_like(clip_sums)
        for c in range(clips):
            rows = pooled[SLOTS_HERE * c : SLOTS_HERE * (c + 1), :]
            clip_sums[c : c + 1, :] = jnp.sum(rows, axis=0, keepdims=True)
        swap = links.remote(links.take(1), clip_sums, clip_other, links.other)
        swap.start()
        lane = lax.broadcasted_iota(jnp.int32, (1, 2 * LANES), 1)
        bias = jnp.zeros((1, 2 * LANES), F32)
        for d in range(SMALL_SHARDS):
            piece = small[d, 64:80, :].astype(F32)[4:5]
            piece = jnp.concatenate([piece, jnp.zeros_like(piece)], axis=1)
            own = jnp.logical_and(lane >= 6 * d, lane < 6 * d + 6)
            bias = bias + jnp.where(own, pltpu.roll(piece, 6 * d, 1) if d else piece, 0.0)
        need("cls")
        swap.wait()
        mean = (clip_sums[...] + clip_other[...]) * share[:, 0:1]
        low = jnp.concatenate([mean, jnp.zeros_like(mean)], axis=0).astype(BF16)
        scores = matmul(low, w_cls[...])[:8] + bias
        scores = jnp.where(lane < CLASSES, scores, -1e30)
        scores = jnp.exp(scores - jnp.max(scores, axis=1, keepdims=True))
        chance = scores / jnp.sum(scores, axis=1, keepdims=True)
        clips_total = clips * links.n_clip
        d_scores = jnp.where(share[:, 0:1] > 0.0, (chance - chosen[...]) / clips_total, 0.0)
        g_bias[...] = jnp.broadcast_to(jnp.sum(d_scores, axis=0, keepdims=True) / n_seg, g_bias.shape)
        d_low = jnp.concatenate([d_scores, jnp.zeros_like(d_scores)], axis=0).astype(BF16)
        grad = lax.dot_general(low, d_low, (((0,), (0,)), ((), ())), preferred_element_type=F32)
        g_cls[...] = (grad / n_seg).astype(BF16)
        d_mean = lax.dot_general(d_low, w_cls[...], (((1,), (1,)), ((), ())), preferred_element_type=F32)
        d_mean = d_mean[:8] * share[:, 0:1]
        for c in range(clips):
            rows = slice(SLOTS_HERE * c, SLOTS_HERE * (c + 1))
            here = mask[rows, 0:1]
            pooled[rows, :] = jnp.broadcast_to(d_mean[c : c + 1], (SLOTS_HERE, D)) * here

    stages = {
        "dpad": stage_dpad,
        "fpad": stage_fpad,
        "first": stage_first,
        "near1": stage_near1,
        "far1": stage_far1,
        "second": stage_second,
        "swap": stage_swap,
        "excite": stage_excite,
        "third": stage_third,
        "near2": stage_near2,
        "far2": stage_far2,
        "fourth": stage_fourth,
        "near3": stage_near3,
        "far3": stage_far3,
        "fifth": stage_fifth,
    }
    for k in range(GRID):
        stages["turn%d" % k] = functools.partial(turn, k)
    for item in STAGES[block]:
        if item[0] == "@":
            with jax.named_scope(item[1:]):
                stages[item[1:]]()
        elif item in gathers:
            push(item)
    for name in jobs:
        gathers[name].finish()
    for copy in outgoing:
        copy.wait()


def forward_block(block, x, mask, following, table, extra, shards, given):
    n_seg = lax.axis_size("seg")
    n_clip = lax.axis_size("clip")
    last = block == 1
    cells = x.shape[0] if last else x.shape[1]
    frames = x.shape[1] if last else x.shape[0] * x.shape[2]
    jobs = list(shards)
    plan = list(given)
    any_spec = pl.BlockSpec(memory_space=pl.ANY)
    vmem = pl.BlockSpec(memory_space=pltpu.VMEM)
    depth = n_clip // 4

    def grid_shape(columns):
        return (cells, frames, columns)

    devices = n_seg * n_clip
    outs = [jax.ShapeDtypeStruct((devices * shards[n].shape[0], shards[n].shape[1]), BF16) for n in jobs]
    outs += [
        jax.ShapeDtypeStruct(grid_shape(MID), F32),
        jax.ShapeDtypeStruct(grid_shape(MID), BF16),
        jax.ShapeDtypeStruct(grid_shape(MID), BF16),
        jax.ShapeDtypeStruct(grid_shape(GATE), BF16),
        jax.ShapeDtypeStruct((GRID, GRID, frames, MID), BF16),
        jax.ShapeDtypeStruct(grid_shape(MID), F32),
        jax.ShapeDtypeStruct(grid_shape(MID), BF16),
        jax.ShapeDtypeStruct(grid_shape(D), BF16),
        jax.ShapeDtypeStruct((frames, D), F32) if last else jax.ShapeDtypeStruct(grid_shape(D), BF16),
        jax.ShapeDtypeStruct(TABLE, F32),
        jax.ShapeDtypeStruct((8, MID), F32),
        jax.ShapeDtypeStruct((8, MID), F32),
        jax.ShapeDtypeStruct((8, D), F32),
    ]
    out_specs = [any_spec] * (len(jobs) + 9) + [vmem] * 4
    if last:
        outs += [jax.ShapeDtypeStruct((D, 2 * LANES), BF16), jax.ShapeDtypeStruct((8, 2 * LANES), F32)]
        out_specs += [vmem] * 2
    else:
        outs.append(jax.ShapeDtypeStruct(grid_shape(D), BF16))
        out_specs.append(any_spec)

    shapes = [(D, MID), (9 * MID, MID), (MID, D), (SMALL_SHARDS, 80, LANES)]
    scratch = [pltpu.VMEM(grid_shape(D), BF16)]
    scratch += [pltpu.VMEM(s, BF16) for s in shapes]
    scratch += [
        pltpu.VMEM(grid_shape(MID), F32),
        pltpu.VMEM(grid_shape(MID), F32),
        pltpu.VMEM(grid_shape(MID), BF16),
        pltpu.VMEM(grid_shape(GATE), BF16),
        pltpu.VMEM(grid_shape(GATE), BF16),
        pltpu.VMEM((GRID + 2, GRID + 2, frames, GATE), F32),
        pltpu.VMEM(grid_shape(GATE), BF16),
        pltpu.VMEM(grid_shape(MID), BF16),
        pltpu.VMEM((GRID + 2, GRID + 2, frames, MID), BF16),
        pltpu.VMEM(grid_shape(MID), F32),
        pltpu.VMEM(grid_shape(MID), BF16),
        pltpu.VMEM(grid_shape(D), BF16),
        pltpu.VMEM((8, D), F32),
        pltpu.VMEM((8, D), F32),
        pltpu.VMEM((GATE, MID), BF16),
    ]
    for shape in ((16, LANES), (8, LANES), (8, MID)):
        scratch += sum_scratch(n_seg, n_clip, shape)
    if last:
        scratch += [pltpu.VMEM((frames, D), F32), pltpu.VMEM((8, D), F32), pltpu.VMEM((8, D), F32)]
        scratch.append(pltpu.VMEM((D, 2 * LANES), BF16))
    else:
        scratch.append(pltpu.VMEM(x.shape, BF16))
    count = 4 * (n_seg * 4 + depth) + len(jobs) * (depth + 4) + 48
    scratch += [pltpu.SemaphoreType.DMA((count,)), pltpu.SemaphoreType.DMA((count,))]
    results = pl.pallas_call(
        functools.partial(forward_kernel, n_seg, n_clip, block, jobs, plan),
        out_shape=outs,
        in_specs=[any_spec, vmem, vmem, vmem] + [vmem] * len(extra) + [any_spec] * (len(jobs) + len(plan)),
        out_specs=out_specs,
        scratch_shapes=scratch,
        compiler_params=pltpu.CompilerParams(
            collective_id=30 + block, has_side_effects=True, vmem_limit_bytes=60 * 1024 * 1024
        ),
        name="forward_block",
    )(x, mask, following, table, *extra, *[shards[n] for n in jobs], *[given[n] for n in plan])
    wholes = dict(zip(jobs, results[: len(jobs)]))
    return wholes, results[len(jobs) :]


def backward_kernel(n_seg, n_clip, block, *refs):
    refs = list(refs)

    def pop(count=1):
        taken = refs[:count]
        del refs[:count]
        return taken if count != 1 else taken[0]

    last = block == 1
    h3_hbm, x_hbm, d_in, h2_hbm, h1_hbm, gate_hbm = pop(6)
    in_a, in_b, mid_a, mid_b, mid_c, out_hbm, small_hbm = pop(7)
    table, st1, st2, st3, mask, present, following = pop(7)
    dh3_out, dh2_out, de_out, dr_out, dh1_out, dx_out, norm_grads = pop(7)
    dv, h3v, xv, h2v, h1v, gatev, dyv, pad2, dsv, edge, pad_s, pad_e = pop(12)
    drv, dh1v, w_in, w_mid, w_out, small, w_exp = pop(7)
    sum_gain, sum_shift = pop(2)
    sums = [pop(4) for _ in range(3)]
    send_sem, recv_sem = pop(2)
    links = Links(n_seg, n_clip, send_sem, recv_sem)
    frames = xv.shape[1]
    outgoing = []

    def send_out(source, target):
        copy = links.local(source, target)
        copy.start()
        outgoing.append(copy)

    def load(source, target):
        copy = links.local(source.reshape(target.shape), target)
        copy.start()
        return copy

    streams = [(h3_hbm, h3v), (x_hbm, xv)]
    if not last:
        streams.append((d_in, dv))
    wide_base = links.take(len(streams) * GRID)

    def wide_copies(i):
        rows = pl.ds(GRID * i, GRID)
        return [
            pltpu.make_async_copy(source.at[rows], target.at[rows], links.recv_sem.at[wide_base + GRID * k + i])
            for k, (source, target) in enumerate(streams)
        ]

    for i in range(GRID):
        for copy in wide_copies(i):
            copy.start()
    loads_two = [load(out_hbm, w_out), load(h2_hbm, h2v)]
    loads_three = [load(h1_hbm, h1v), load(gate_hbm, gatev), load(small_hbm, small)]
    loads_four = []
    for parts, target, waits in (
        ((mid_a, mid_b, mid_c), w_mid, loads_three),
        ((in_a, in_b), w_in, loads_four),
    ):
        rows = target.shape[0] // SMALL_SHARDS
        size = rows // len(parts)
        wide = target.reshape(SMALL_SHARDS, rows, MID)
        for k, source in enumerate(parts):
            waits.append(load(source, wide.at[:, k * size : (k + 1) * size]))
    links.meet()
    live_rows = table[TABLE[0] - 1, 0:1, 0:1]
    half = MID // LANES
    pad2[...] = jnp.zeros_like(pad2)
    pad_s[...] = jnp.zeros_like(pad_s)
    pad_e[...] = jnp.zeros_like(pad_e)
    sum_gain[...] = jnp.zeros_like(sum_gain)
    sum_shift[...] = jnp.zeros_like(sum_shift)

    def vectors(start, columns, stats):
        gain = row_vector(table, 2 * block, start, columns // LANES)
        shift = row_vector(table, 2 * block + 1, start, columns // LANES)
        return gain, shift, stats[0:1, :], stats[1:2, :]

    def totals(index, start, columns, gain_rows, shift_rows):
        stat = sums[index][0]
        put_rows(stat, 0, jnp.sum(gain_rows, axis=0, keepdims=True), 4)
        put_rows(stat, 4, jnp.sum(shift_rows, axis=0, keepdims=True), 4)
        tot = links.all_sum(*sums[index])
        gain = jnp.concatenate([tot[k : k + 1] for k in range(4)], axis=1)
        shift = jnp.concatenate([tot[4 + k : 5 + k] for k in range(4)], axis=1)
        put_rows(norm_grads, start, gain, columns // LANES)
        put_rows(norm_grads, 24 + start, shift, columns // LANES)
        return gain / live_rows, shift / live_rows

    def slope_of(values):
        sig = jax.nn.sigmoid(values)
        return sig, sig * (1.0 + values * (1.0 - sig))

    def dot_t(left, right):
        return lax.dot_general(left, right, (((1,), (1,)), ((), ())), preferred_element_type=F32)

    gain3, shift3, mean3, inv3 = vectors(2 * half, D, st3)
    dx_base = links.take(GRID)

    def dx_copy(i):
        rows = pl.ds(GRID * i, GRID)
        return pltpu.make_async_copy(dv.at[rows], dx_out.at[rows], links.recv_sem.at[dx_base + i])


    def first_rows(i, carry):
        for copy in wide_copies(i):
            copy.wait()
        lax.fori_loop(GRID * i, GRID * i + GRID, first, carry)
        if not last:
            dx_copy(i).start()
        return carry

    def first(p, carry):
        for k in range(4):
            span = slice(k * MID, (k + 1) * MID)
            n = (h3v[p, :, span].astype(F32) - mean3[:, span]) * inv3[:, span]
            pre = n * gain3[:, span] + shift3[:, span] + xv[p, :, span].astype(F32)
            grad = d_in[:, span] if last else dv[p, :, span]
            grad = grad * slope_of(pre)[1]
            dv[p, :, span] = grad
            sum_gain[:, span] += fold(grad * n)
            sum_shift[:, span] += fold(grad)
        return carry

    lax.fori_loop(0, GRID, first_rows, 0)
    part_gain, part_shift = totals(0, 2 * half, D, sum_gain[...], sum_shift[...])
    factor3 = gain3 * inv3
    for copy in loads_two:
        copy.wait()
    gain2, shift2, mean2, inv2 = vectors(half, MID, st2)
    zeros = jnp.zeros((8, MID), F32)

    def second(i, carry):
        for j in range(GRID):
            p = GRID * i + j
            for k in range(4):
                span = slice(k * MID, (k + 1) * MID)
                n = (h3v[p, :, span].astype(F32) - mean3[:, span]) * inv3[:, span]
                rest = mask[...] * (part_shift[:, span] + n * part_gain[:, span])
                h3v[p, :, span] = (factor3[:, span] * (dv[p, :, span] - rest)).astype(BF16)
        d_a = dot_t(h3v[pl.ds(GRID * i, GRID)].reshape(GRID * frames, D), w_out[...])
        d_a = d_a.reshape(GRID, frames, MID)
        one, two = carry
        for j in range(GRID):
            n = (h2v[GRID * i + j] - mean2) * inv2
            grad = d_a[j] * slope_of(n * gain2 + shift2)[1]
            dyv[GRID * i + j] = grad
            one = one + fold(grad * n)
            two = two + fold(grad)
        return (one, two)

    one, two = lax.fori_loop(0, GRID, second, (zeros, zeros))
    send_out(h3v, dh3_out)
    part_gain2, part_shift2 = totals(1, half, MID, one, two)
    factor2 = gain2 * inv2

    def third(i, carry):
        for j in range(GRID):
            p = GRID * i + j
            n = (h2v[p] - mean2) * inv2
            rest = mask[...] * (part_shift2 + n * part_gain2)
            pad2[i + 1, j + 1] = (factor2 * (dyv[p] - rest)).astype(BF16)
        return carry

    lax.fori_loop(0, GRID, third, 0)
    send_out(pad2.at[pl.ds(1, GRID), pl.ds(1, GRID)], dh2_out)
    for copy in loads_three:
        copy.wait()
    w_exp[...] = excite_weights(small, block)
    red = small[:, 32 * block : 32 * block + 16].reshape(MID, GATE)
    gain1, shift1, mean1, inv1 = vectors(0, MID, st1)

    def fourth(i, carry):
        part = None
        for k in range(9):
            window = pad2[i + 2 - k // 3, pl.ds(2 - k % 3, GRID)].reshape(GRID * frames, MID)
            term = dot_t(window, w_mid[k * MID : (k + 1) * MID])
            part = term if part is None else part + term
        part = part.reshape(GRID, frames, MID)
        for j in range(GRID):
            p = GRID * i + j
            y = (h1v[p] - mean1) * inv1 * gain1 + shift1
            a = y * jax.nn.sigmoid(y)
            gate = gatev[p].astype(F32)
            dyv[p] = part[j] * (1.0 + gate)
            gatev[p] = (part[j] * a * gate * (1.0 - gate)).astype(BF16)
        d_s = dot_t(gatev[pl.ds(GRID * i, GRID)].reshape(GRID * frames, MID), w_exp[...])
        d_s = d_s.astype(BF16).reshape(GRID, frames, GATE)
        dsv[pl.ds(GRID * i, GRID)] = d_s
        for j in range(GRID):
            pad_s[i + 1, j + 1] = d_s[j].astype(F32)
        return carry

    lax.fori_loop(0, GRID, fourth, 0)
    swap = links.remote(links.take(1), dsv, edge, links.other)
    swap.start()
    send_out(gatev, de_out)
    swap.wait()

    def unpack(i, carry):
        for j in range(GRID):
            pad_e[i + 1, j + 1] = edge[GRID * i + j].astype(F32)
        return carry

    lax.fori_loop(0, GRID, unpack, 0)
    row = lax.rem(lax.broadcasted_iota(jnp.int32, (frames, GATE), 0), 8)
    from_other = links.seg.astype(F32)

    def fifth(i, carry):
        for j in range(GRID):
            near = jnp.zeros((frames, GATE), F32)
            far = jnp.zeros((frames, GATE), F32)
            for k in range(9):
                near = near + pad_s[i + k // 3, j + k % 3]
                far = far + pad_e[i + k // 3, j + k % 3]
            near = pad_s[i + 1, j + 1] + near / 9.0
            far = (pad_e[i + 1, j + 1] + far / 9.0) * from_other
            earlier = jnp.where(row > 0, pltpu.roll(near, 1, 0), pltpu.roll(far, frames - 7, 0))
            drv[GRID * i + j] = (present[...] * earlier - following[...] * near).astype(BF16)
        d_a = dot_t(drv[pl.ds(GRID * i, GRID)].reshape(GRID * frames, GATE), red)
        d_a = d_a.reshape(GRID, frames, MID)
        one, two = carry
        for j in range(GRID):
            p = GRID * i + j
            n = (h1v[p] - mean1) * inv1
            grad = (dyv[p] + d_a[j]) * slope_of(n * gain1 + shift1)[1]
            dyv[p] = grad
            one = one + fold(grad * n)
            two = two + fold(grad)
        return (one, two)

    one, two = lax.fori_loop(0, GRID, fifth, (zeros, zeros))
    send_out(drv, dr_out)
    part_gain1, part_shift1 = totals(2, 0, MID, one, two)
    factor1 = gain1 * inv1
    for copy in loads_four:
        copy.wait()

    def sixth(i, carry):
        for j in range(GRID):
            p = GRID * i + j
            n = (h1v[p] - mean1) * inv1
            rest = mask[...] * (part_shift1 + n * part_gain1)
            dh1v[p] = (factor1 * (dyv[p] - rest)).astype(BF16)
        if last:
            rows = dh1v[pl.ds(GRID * i, GRID)].reshape(GRID * frames, MID)
            for k in range(4):
                span = slice(k * MID, (k + 1) * MID)
                part = dot_t(rows, w_in[span, :])
                dv[pl.ds(GRID * i, GRID), :, span] += part.reshape(GRID, frames, MID)
            dx_copy(i).start()
        return carry

    lax.fori_loop(0, GRID, sixth, 0)
    send_out(dh1v, dh1_out)
    for i in range(GRID):
        dx_copy(i).wait()
    for copy in outgoing:
        copy.wait()


def backward_block(block, h3, x, d_in, h2, h1, gate, weights, table, stats, masks):
    n_seg = lax.axis_size("seg")
    n_clip = lax.axis_size("clip")
    cells, frames, width = x.shape
    any_spec = pl.BlockSpec(memory_space=pl.ANY)
    vmem = pl.BlockSpec(memory_space=pltpu.VMEM)
    last = block == 1

    def grid_shape(columns):
        return (cells, frames, columns)

    outs = [
        jax.ShapeDtypeStruct(grid_shape(D), BF16),
        jax.ShapeDtypeStruct((GRID, GRID, frames, MID), BF16),
        jax.ShapeDtypeStruct(grid_shape(MID), BF16),
        jax.ShapeDtypeStruct(grid_shape(GATE), BF16),
        jax.ShapeDtypeStruct(grid_shape(MID), BF16),
        jax.ShapeDtypeStruct(grid_shape(D), F32),
        jax.ShapeDtypeStruct((48, LANES), F32),
    ]
    scratch = [
        pltpu.VMEM(grid_shape(D), F32),
        pltpu.VMEM(grid_shape(D), BF16),
        pltpu.VMEM(grid_shape(D), BF16),
        pltpu.VMEM(grid_shape(MID), F32),
        pltpu.VMEM(grid_shape(MID), F32),
        pltpu.VMEM(grid_shape(MID), BF16),
        pltpu.VMEM(grid_shape(MID), F32),
        pltpu.VMEM((GRID + 2, GRID + 2, frames, MID), BF16),
        pltpu.VMEM(grid_shape(GATE), BF16),
        pltpu.VMEM(grid_shape(GATE), BF16),
        pltpu.VMEM((GRID + 2, GRID + 2, frames, GATE), F32),
        pltpu.VMEM((GRID + 2, GRID + 2, frames, GATE), F32),
        pltpu.VMEM(grid_shape(GATE), BF16),
        pltpu.VMEM(grid_shape(MID), BF16),
        pltpu.VMEM((D, MID), BF16),
        pltpu.VMEM((9 * MID, MID), BF16),
        pltpu.VMEM((MID, D), BF16),
        pltpu.VMEM((SMALL_SHARDS, 80, LANES), BF16),
        pltpu.VMEM((GATE, MID), BF16),
        pltpu.VMEM((8, D), F32),
        pltpu.VMEM((8, D), F32),
    ]
    for shape in ((8, MID), (8, LANES), (8, LANES)):
        scratch += sum_scratch(n_seg, n_clip, shape)
    count = 3 * (n_seg * 4 + n_clip // 4) + 64
    scratch += [pltpu.SemaphoreType.DMA((count,)), pltpu.SemaphoreType.DMA((count,))]
    d_spec = vmem if last else any_spec
    return pl.pallas_call(
        functools.partial(backward_kernel, n_seg, n_clip, block),
        out_shape=outs,
        in_specs=[any_spec, any_spec, d_spec] + [any_spec] * 10 + [vmem] * 7,
        out_specs=[any_spec] * 6 + [vmem],
        scratch_shapes=scratch,
        compiler_params=pltpu.CompilerParams(
            collective_id=40 + block, has_side_effects=True, vmem_limit_bytes=62 * 1024 * 1024
        ),
        name="backward_block",
    )(h3, x, d_in, h2, h1, gate, *weights, table, *stats, *masks)


class Scatter:
    def __init__(self, links, grad, rows, buffers, alternate, finish):
        self.links = links
        self.alternate = alternate
        self.grad = grad
        self.rows = rows
        self.one, self.two, self.three, self.four = buffers
        self.finish = finish
        self.depth = links.outer
        self.base = links.take(self.depth + 3)
        self.at = -1

    def copies(self):
        links, base, depth = self.links, self.base, self.depth
        if self.at == 0:
            source = self.grad.at[1 - links.seg, :, :, self.rows]
            return [links.remote(base, source, self.one, links.other)]
        found = []
        if self.at == 1:
            for k in range(2):
                source = self.one.at[:, links.jump * (1 - links.first) + links.step * k]
                found.append(links.remote(base + 1 + k, source, self.two.at[:, k], links.across_first))
            return found
        if self.alternate:
            if self.at == 2:
                for i in range(1, depth):
                    source = self.two.at[lax.rem(links.group + i, depth)]
                    found.append(links.remote(base + 2 + i, source, self.three.at[i - 1], links.far_peer(i)))
            else:
                source = self.four.at[1 - links.second]
                found.append(links.remote(base + depth + 2, source, self.four.at[2], links.across_second))
            return found
        if self.at == 2:
            source = self.two.at[:, 1 - links.second]
            return [links.remote(base + 3, source, self.three, links.across_second)]
        for i in range(1, depth):
            source = self.three.at[lax.rem(links.group + i, depth)]
            found.append(links.remote(base + 3 + i, source, self.four.at[i - 1], links.far_peer(i)))
        return found

    def add(self):
        links, depth = self.links, self.depth
        one, two, three, four = self.one, self.two, self.three, self.four
        if self.at == 0:

            def add_one(i, carry):
                z = i // 4
                w = lax.rem(i, 4)
                total = one[z, w].astype(F32) + self.grad[links.seg, z, w, self.rows].astype(F32)
                one[z, w] = total.astype(BF16)
                return carry

            lax.fori_loop(0, 4 * depth, add_one, 0)
        elif self.at == 1:

            def add_two(i, carry):
                z = i // 2
                k = lax.rem(i, 2)
                kept = one[z, links.jump * links.first + links.step * k]
                two[z, k] = (two[z, k].astype(F32) + kept.astype(F32)).astype(BF16)
                return carry

            lax.fori_loop(0, 2 * depth, add_two, 0)
        elif self.at == 2 and self.alternate:
            for k in range(2):
                total = two[links.group, k].astype(F32)
                for i in range(1, depth):
                    total = total + three[i - 1, k].astype(F32)
                four[k] = total.astype(BF16)
        elif self.at == 2:

            def add_three(z, carry):
                three[z] = (three[z].astype(F32) + two[z, links.second].astype(F32)).astype(BF16)
                return carry

            lax.fori_loop(0, depth, add_three, 0)
        elif self.alternate:
            self.finish(four[links.second].astype(F32) + four[2].astype(F32))
        else:
            total = three[links.group].astype(F32)
            for i in range(1, depth):
                total = total + four[i - 1].astype(F32)
            self.finish(total)

    def advance(self):
        if self.at > 3:
            return
        if self.at >= 0:
            for copy in self.copies():
                copy.wait()
            self.add()
        self.at += 1
        if self.at <= 3:
            for copy in self.copies():
                copy.start()


SCATTERED = {
    "cls": (64, 2 * LANES),
    "out1": (16, D),
    "mida1": (48, MID),
    "midb1": (48, MID),
    "midc1": (48, MID),
    "in1": (64, MID),
    "out0": (16, D),
    "mida0": (48, MID),
    "midb0": (48, MID),
    "midc0": (48, MID),
    "in0": (64, MID),
    "small": (80, LANES),
}


FLAT_MID = 256
FLAT_OUT = 832
FLAT_SMALL = 1088
FLAT_ROWS = 1122
FLAT_CLS = 2243
ORDER = (
    "cls", "@mid1a", "cls", "@mid1b", "mida1", "midb1", "midc1", "@mid1c", "cls", "mida1", "@in1a", "in1", "midb1",
    "@in1b", "cls", "@out1a", "mida1", "midc1", "@out1b", "out1", "cls", "in1", "@small1", "midb1", "out1",
    "@out0a", "midc1", "@out0b", "out0", "mida1", "@in0a", "in0", "in1", "@in0b", "out0", "@mid0a", "midb1",
    "midc1", "mida1", "out1", "@mid0b", "mida0", "midb0", "midc0", "in0", "@mid0c", "midb1", "out0", "@small0",
    "small", "in1", "out1", "@dx0", "@dx1", "mida0", "midc1", "@dx2", "in0", "@dx3", "@dx4", "out0", "@dx5", "in1",
    "out1", "midb0", "@dx6", "mida0", "in0", "out0", "midc0", "midb0", "mida0", "small", "in0", "midc0", "mida0",
    "midb0", "small", "midc0", "small", "midb0", "midc0", "small",
)
ALTERNATE = ("mida1", "midb1", "in1")

ORDER_FIRST = "mid1a"


def gradient_kernel(n_seg, n_clip, *refs):
    refs = list(refs)

    def pop(count=1):
        taken = refs[:count]
        del refs[:count]
        return taken if count != 1 else taken[0]

    sources = [pop(10) for _ in range(2)]
    cls_hbm, norm_rows_in, bias = pop(3)
    d_pre, *in_parts = pop(3)
    flat, tail, dx_out = pop(3)
    big3, bigx, mid_a2, mid_d2, mid_d1, mid_low, mid_de, thin_dr, thin_s, fpad = pop(10)
    g_in, g_mid, g_out, g_small, g_cls, squares, turned, rows_x = pop(8)
    sums = pop(4)
    buffers = {name: pop(4) for name in SCATTERED}
    send_sem, recv_sem = pop(2)
    links = Links(n_seg, n_clip, send_sem, recv_sem)
    cells, frames = bigx.shape[0], bigx.shape[1]
    rows_all = cells * frames
    devices = SMALL_SHARDS

    def load(source, target):
        copy = links.local(source.reshape(target.shape), target)
        copy.start()
        return copy

    interior = fpad.at[pl.ds(1, GRID), pl.ds(1, GRID)]
    names = ("x", "d1", "f", "d2", "a2", "d3", "low", "dr", "s", "de")
    targets = dict(zip(names, (bigx, mid_d1, interior, mid_d2, mid_a2, big3, mid_low, thin_dr, thin_s, mid_de)))
    hbm = [dict(zip(names, source)) for source in sources]

    def fetch(block, *keys):
        return [load(hbm[block][key], targets[key]) for key in keys]

    operands = {
        "out": ("a2", "d3"),
        "in": ("x", "d1"),
        "mid": ("f", "d2"),
        "small": ("low", "dr", "s", "de"),
    }
    load_cls = load(cls_hbm, g_cls)
    fpad[...] = jnp.zeros_like(fpad)
    waits = {"mid": fetch(1, *operands["mid"])}
    links.meet()
    squares[...] = jnp.zeros_like(squares)

    def folded(ref, rows):
        return ref.reshape(n_seg, links.outer, 4, rows, ref.shape[-1])

    grads = {"cls": g_cls, "small": g_small}
    jobs = {}

    def put(block, first, values, stride=1):
        count = values.shape[0]
        if block == 0:
            flat[pl.ds(first, count, stride), :] = values
        else:
            turned[pl.ds(first + 8, count, stride), :] = pltpu.roll(values, 64, 1)

    def put_small(total):
        lane = lax.broadcasted_iota(jnp.int32, (1, LANES), 1)
        for block in range(2):
            rows = total[32 * block : 32 * block + 32]
            put(block, FLAT_SMALL, rows[:16])
            for k in range(4):
                put(block, FLAT_SMALL + 16 + k, rows[16 + 4 * k : 20 + 4 * k], 4)
            gain = total[64 + 2 * block : 65 + 2 * block]
            shift = pltpu.roll(total[65 + 2 * block : 66 + 2 * block], 96, 1)
            put(block, FLAT_SMALL + 32, jnp.where(lane < 96, gain, shift))
            put(block, FLAT_SMALL + 33, shift)
        flat[FLAT_CLS + 87 : FLAT_CLS + 88, :] = total[68:69]

    def put_classifier(total):
        lane = lax.broadcasted_iota(jnp.int32, (1, LANES), 1)
        flat[FLAT_CLS:, :] = jnp.zeros_like(flat[FLAT_CLS:, :])
        for i in range(total.shape[0]):
            line, by = divmod(CLASSES * i, LANES)
            line += FLAT_CLS
            low, high = total[i : i + 1, :LANES], total[i : i + 1, LANES:]
            if by:
                low, high = pltpu.roll(low, by, 1), pltpu.roll(high, by, 1)
            here = lane >= by
            flat[line : line + 1, :] += jnp.where(here, low, 0.0)
            flat[line + 1 : line + 2, :] += jnp.where(here, high, low)
            if by + CLASSES - LANES > LANES:
                flat[line + 2 : line + 3, :] += jnp.where(here, 0.0, high)

    def make(name):
        kind = name[:-1] if name not in ("cls", "small") else name
        block = name[-1]
        rows, columns = SCATTERED[name]
        start = rows * "abc".index(kind[3]) if kind.startswith("mid") else 0
        ref = {"in": g_in, "out": g_out, "small": g_small, "cls": g_cls}.get(kind, g_mid)
        shard_rows = 3 * rows if kind.startswith("mid") else rows

        def finish(total):
            squares[:, :columns] += fold(total * total)
            if kind == "cls":
                put_classifier(total)
            elif kind == "small":
                put_small(total)
            else:
                lines = columns // LANES
                first = {"in": 0, "out": FLAT_OUT}.get(kind, FLAT_MID) + start * lines
                for k in range(lines):
                    put(int(block), first + k, total[:, k * LANES : (k + 1) * LANES], lines)

        jobs[name] = Scatter(links, folded(ref, shard_rows), pl.ds(start, rows), buffers[name], name in ALTERNATE, finish)

    for name in SCATTERED:
        make(name)

    def push(*wanted):
        for name in wanted:
            jobs[name].advance()

    def dot_tn(left, right):
        return lax.dot_general(left, right, (((0,), (0,)), ((), ())), preferred_element_type=F32)

    turn = 1 - links.seg

    def task_out(first, last):
        def body(k, carry):
            span = pl.ds(pl.multiple_of(k * MID, MID), MID)
            part = dot_tn(mid_a2[...].reshape(rows_all, MID), big3[:, :, span].reshape(rows_all, MID))
            g_out[:, span] = part.astype(BF16)
            return carry

        lax.fori_loop(first, last, body, 0)

    def task_in(first, last):
        def body(i, carry):
            k = i + turn * (3 - 2 * i)
            span = pl.ds(pl.multiple_of(k * MID, MID), MID)
            part = dot_tn(bigx[:, :, span].reshape(rows_all, MID), mid_d1[...].reshape(rows_all, MID))
            g_in[span, :] = part.astype(BF16)
            return carry

        lax.fori_loop(first, last, body, 0)

    def task_mid(first, last):
        def body(i, carry):
            k = i + turn * (8 - 2 * i)
            window = fpad[pl.ds(k // 3, GRID), pl.ds(lax.rem(k, 3), GRID)].reshape(rows_all, MID)
            part = dot_tn(window, mid_d2[...].reshape(rows_all, MID))
            g_mid[pl.ds(pl.multiple_of(k * MID, MID), MID), :] = part.astype(BF16)
            return carry

        lax.fori_loop(first, last, body, 0)

    def task_small(block):
        part = dot_tn(mid_low[...].reshape(rows_all, MID), thin_dr[...].reshape(rows_all, GATE))
        g_small[:, 32 * block : 32 * block + 16, :] = part.astype(BF16).reshape(devices, 16, LANES)
        part = dot_tn(thin_s[...].reshape(rows_all, GATE), mid_de[...].reshape(rows_all, MID)).astype(BF16)
        rows = jnp.zeros((devices * 16, LANES), F32)
        for k in range(MID // LANES):
            rows = rows + dot_tn(excite_pick(devices, k), part[:, k * LANES : (k + 1) * LANES])
        g_small[:, 32 * block + 16 : 32 * block + 32, :] = rows.astype(BF16).reshape(devices, 16, LANES)

    dx_base = links.take(2 * GRID)
    w_in = big3.at[0 : 2 * 8].reshape(8, 2, SMALL_SHARDS, D)
    in_loads = []

    def load_w_in():
        for half, part in enumerate(in_parts):
            quarters = part.reshape(4, 8, SMALL_SHARDS, MID)
            for k in range(4):
                copy = links.local(quarters.at[k], w_in.at[:, half, :, k * MID : (k + 1) * MID])
                copy.start()
                in_loads.append(copy)
        dx_load(0).start()

    def dx_load(i):
        return pltpu.make_async_copy(
            d_pre.at[pl.ds(GRID * i, GRID)], rows_x.at[i % 2], links.recv_sem.at[dx_base + i]
        )

    def dx_store(i):
        slots = frames // dx_out.shape[0]
        return [
            pltpu.make_async_copy(
                rows_x.at[i % 2, :, slots * c : slots * (c + 1)],
                dx_out.at[c, pl.ds(GRID * i, GRID)],
                links.recv_sem.at[store_base + dx_out.shape[0] * i + c],
            )
            for c in range(dx_out.shape[0])
        ]

    store_base = links.take(dx_out.shape[0] * GRID)

    def task_dx(i):
        if i == 0:
            for copy in in_loads:
                copy.wait()
        dx_load(i).wait()
        rows = mid_d1[GRID * i : GRID * (i + 1)].reshape(GRID * frames, MID)
        for k in range(4):
            span = slice(k * MID, (k + 1) * MID)
            right = big3[0:16, :, span].reshape(MID, MID)
            part = lax.dot_general(rows, right, (((1,), (1,)), ((), ())), preferred_element_type=F32)
            rows_x[i % 2, :, :, span] += part.reshape(GRID, frames, MID)
        for copy in dx_store(i):
            copy.start()
        if i:
            for copy in dx_store(i - 1):
                copy.wait()
        if i < GRID - 1:
            dx_load(i + 1).start()

    def run(piece):
        if piece[:2] == "dx":
            task_dx(int(piece[2:]))
            return
        letter = piece[-1] if piece[-1] in "abc" else ""
        kind, block = piece[: len(piece) - 1 - len(letter)], int(piece[len(piece) - 1 - len(letter)])
        part = "abc".index(letter) if letter else 0
        if part == 0:
            for copy in waits[kind]:
                copy.wait()
            if block == 0 and kind != "small":
                for name in SCATTERED:
                    if name.startswith(kind) and name[-1] == "1":
                        while jobs[name].at < 1:
                            jobs[name].advance()
        if kind == "mid":
            task_mid((0, 3, 5)[part], (3, 5, 9)[part])
        elif kind == "in":
            task_in(2 * part, 2 * part + 2)
        elif kind == "out":
            task_out(2 * part, 2 * part + 2)
        else:
            task_small(block)
        if block == 1 and part == {"mid": 2, "in": 1, "out": 1, "small": 0}[kind]:
            waits[kind] = fetch(0, *operands[kind])
        if piece == "out0b":
            load_w_in()
        if block == 1 and piece == ORDER_FIRST:
            for other in ("in", "out", "small"):
                waits[other] = fetch(1, *operands[other])

    g_small[:, 64:80, :] = norm_rows_in[...]
    load_cls.wait()
    for item in ORDER:
        if item[0] == "@":
            with jax.named_scope("product"):
                run(item[1:])
        else:
            push(item)
    for name in SCATTERED:
        while jobs[name].at <= 3:
            jobs[name].advance()
    for copy in dx_store(GRID - 1):
        copy.wait()
    lane = lax.broadcasted_iota(jnp.int32, (FLAT_ROWS, LANES), 1)
    now, before = turned[8 : 8 + FLAT_ROWS, :], turned[7 : 7 + FLAT_ROWS, :]
    old = flat[FLAT_SMALL + 33 : FLAT_SMALL + 34, :]
    flat[FLAT_ROWS - 1 : 2 * FLAT_ROWS - 1, :] = jnp.where(lane < 64, before, now)
    flat[FLAT_ROWS - 1 : FLAT_ROWS, :] = jnp.where(lane[:1] < 64, old, now[:1])
    total = jnp.sum(jnp.sum(squares[...], axis=0, keepdims=True), axis=1, keepdims=True)
    sums[0][0:8, :] = bias[...]
    sums[0][8:16, :] = jnp.broadcast_to(total, (8, LANES))
    tail[...] = links.all_sum(*sums)


def gradient_sums(sources, g_cls, norm_rows_in, bias, d_pre, in_a, in_b, clips):
    n_seg = lax.axis_size("seg")
    n_clip = lax.axis_size("clip")
    depth = n_clip // 4
    cells, frames, width = sources[0][0].shape
    any_spec = pl.BlockSpec(memory_space=pl.ANY)
    vmem = pl.BlockSpec(memory_space=pltpu.VMEM)

    def grid_shape(columns):
        return pltpu.VMEM((cells, frames, columns), BF16)

    outs = [(FLAT_CLS + 93, LANES), (16, LANES)]
    scratch = [grid_shape(D), grid_shape(D)] + [grid_shape(MID)] * 5 + [grid_shape(GATE)] * 2
    scratch += [
        pltpu.VMEM((GRID + 2, GRID + 2, frames, MID), BF16),
        pltpu.VMEM((D, MID), BF16),
        pltpu.VMEM((9 * MID, MID), BF16),
        pltpu.VMEM((MID, D), BF16),
        pltpu.VMEM((SMALL_SHARDS, 80, LANES), BF16),
        pltpu.VMEM((D, 2 * LANES), BF16),
        pltpu.VMEM((8, D), F32),
        pltpu.VMEM((FLAT_ROWS + 14, LANES), F32),
        pltpu.VMEM((2, GRID, frames, D), F32),
    ]
    scratch += sum_scratch(n_seg, n_clip, (16, LANES))
    for name, shape in SCATTERED.items():
        ends = ((depth - 1, 2), (3,)) if name in ALTERNATE else ((depth,), (depth - 1,))
        for lead in ((depth, 4), (depth, 2)) + ends:
            scratch.append(pltpu.VMEM(lead + shape, BF16))
    count = n_seg * 4 + depth + len(SCATTERED) * (depth + 3) + 100
    scratch += [pltpu.SemaphoreType.DMA((count,)), pltpu.SemaphoreType.DMA((count,))]
    return pl.pallas_call(
        functools.partial(gradient_kernel, n_seg, n_clip),
        out_shape=[jax.ShapeDtypeStruct(s, F32) for s in outs + [(clips, cells, frames // clips, D)]],
        in_specs=[any_spec] * 21 + [vmem, vmem] + [any_spec] * 3,
        out_specs=[vmem] * len(outs) + [any_spec],
        scratch_shapes=scratch,
        compiler_params=pltpu.CompilerParams(
            collective_id=50, has_side_effects=True, vmem_limit_bytes=62 * 1024 * 1024
        ),
        name="gradient_sums",
    )(*sources[0], *sources[1], g_cls, norm_rows_in, bias, d_pre, in_a, in_b)


def input_gradient_kernel(d_pre, d_one, in_a, in_b, out, w_in):
    rows = w_in.shape[0] // SMALL_SHARDS // 2

    @pl.when(pl.program_id(0) == 0)
    def _():
        wide = w_in.reshape(SMALL_SHARDS, 2 * rows, MID)
        wide[:, :rows] = in_a[...].reshape(SMALL_SHARDS, rows, MID)
        wide[:, rows:] = in_b[...].reshape(SMALL_SHARDS, rows, MID)

    cells, frames = d_one.shape[:2]
    clips = out.shape[0]
    slots = frames // clips
    left = d_one[...].reshape(cells * frames, MID)
    for k in range(4):
        span = slice(k * MID, (k + 1) * MID)
        part = lax.dot_general(left, w_in[span, :], (((1,), (1,)), ((), ())), preferred_element_type=F32)
        part = part.reshape(cells, frames, MID) + d_pre[:, :, span]
        for c in range(clips):
            out[c, :, :, span] = part[:, slots * c : slots * (c + 1), :]


def input_gradient(d_pre, d_one, in_a, in_b, clips):
    cells, frames, width = d_pre.shape
    slots = frames // clips
    whole = pl.BlockSpec(in_a.shape, lambda i: (0, 0))
    return pl.pallas_call(
        input_gradient_kernel,
        grid=(GRID,),
        out_shape=jax.ShapeDtypeStruct((clips, cells, slots, width), F32),
        in_specs=[
            pl.BlockSpec((GRID, frames, width), lambda i: (i, 0, 0)),
            pl.BlockSpec((GRID, frames, MID), lambda i: (i, 0, 0)),
            whole,
            whole,
        ],
        out_specs=pl.BlockSpec((clips, GRID, slots, width), lambda i: (0, i, 0, 0)),
        scratch_shapes=[pltpu.VMEM((D, MID), BF16)],
        compiler_params=pltpu.CompilerParams(vmem_limit_bytes=48 * 1024 * 1024),
        name="input_gradient",
    )(d_pre, d_one, in_a, in_b)


def weight_gradients(x, d_one, gated, d_two, a_two, d_three, a_low, d_reduced, mixed, d_excite):
    return [
        matmul(x.reshape(-1, D).T, d_one.reshape(-1, MID)),
        conv(gated, d_two, ("HWCN", "HWIO", "HWNC")).reshape(9 * MID, MID),
        matmul(a_two.reshape(-1, MID).T, d_three.reshape(-1, D)),
        matmul(a_low.reshape(-1, MID).T, d_reduced.reshape(-1, GATE)),
        matmul(mixed.reshape(-1, GATE).T, d_excite.reshape(-1, MID)),
    ]


def on_device(inputs, clip_counts, labels, master, first_moment, second_moment):
    seg_count = lax.axis_size("seg")
    clip_local, slot_local = inputs.shape[:2]
    frames = clip_local * slot_local
    slot_ids = lax.axis_index("seg") * slot_local + jnp.arange(slot_local, dtype=jnp.int32)
    present = (slot_ids[None, :] < clip_counts[:, None]).astype(F32)
    following = (slot_ids[None, :] + 1 < clip_counts[:, None]).astype(F32)
    frame_mask = jnp.broadcast_to(present.reshape(frames, 1), (frames, MID))
    frame_following = jnp.broadcast_to(following.reshape(frames, 1), (frames, GATE))
    table = jnp.zeros(TABLE, F32)
    x_low = inputs.transpose(0, 2, 1, 3)
    shards = weight_shards(master)
    if shards is None:
        weights = whole_weights(master)
        jobs = ((), ())
    else:
        weights = {}
        jobs = JOBS
    rows = ((0, 8 - clip_local), (0, 0))
    share = jnp.pad(1.0 / (HW * clip_counts.astype(F32))[:, None], rows)
    share = jnp.broadcast_to(share, (8, LANES))
    onehot = (labels[:, None] == jnp.arange(2 * LANES, dtype=jnp.int32)[None, :]).astype(F32)
    target = jnp.pad(onehot, rows)
    kept = []
    flowing = x_low
    flows = []
    for block in range(2):
        flows.append(flowing)
        names = weight_names(block) + (["cls"] if block == 1 else [])
        given = {name: weights[name] for name in names if name not in jobs[block]}
        gathered, results = forward_block(
            block,
            flowing,
            frame_mask,
            frame_following,
            table,
            (share, target) if block == 1 else (),
            {name: shards[name] for name in jobs[block]},
            given,
        )
        weights.update(gathered)
        if block == 0:
            table = results[9]
        kept.append(results[:8] + results[10:13])
        if block == 0:
            flows[0] = results[13]
        flowing = results[8]
    d_flow = flowing
    g_cls, g_bias = results[13:]
    g_bias = g_bias[0, :CLASSES]
    masks = (frame_mask, frame_mask[:, :GATE], frame_following)
    sources = [None, None]
    norm_grads = [None, None]
    for block in (1, 0):
        h_one, a_low, gate, mixed, gated, h_two, a_two, h_three, st_one, st_two, st_three = kept[block]
        *steps, d_flow, norm_sums = backward_block(
            block,
            h_three,
            flows[block],
            d_flow,
            h_two,
            h_one,
            gate,
            [weights[name] for name in weight_names(block)],
            table,
            (st_one, st_two, st_three),
            masks,
        )
        sources[block] = (flows[block], steps[4], gated, steps[1], a_two, steps[0], a_low, steps[3], mixed, steps[2])
        norm_grads[block] = [norm_sums[:24].reshape(-1), norm_sums[24:].reshape(-1)]
    devices = seg_count * lax.axis_size("clip")
    bias_rows = jnp.pad(g_bias, (0, 8 * LANES - CLASSES)).reshape(8, LANES)
    if shards is None:
        grads = []
        for block in (0, 1):
            grads += weight_gradients(*sources[block]) + [v / devices for v in norm_grads[block]]
        d_input = input_gradient(d_flow, steps[4], weights["ina0"], weights["inb0"], clip_local)
        grad_mine = scatter_gradients(grads + [g_cls[:, :CLASSES].astype(F32), g_bias])
        square = jnp.full((8, LANES), jnp.sum(grad_mine * grad_mine), F32)
        tail = lax.psum(jnp.concatenate([bias_rows, square]), AXES)
    else:
        vectors = [v.reshape(SMALL_SHARDS, -1) / devices for b in (0, 1) for v in norm_grads[b]]
        padded = jnp.pad(g_bias, (0, 6 * SMALL_SHARDS - CLASSES)).reshape(SMALL_SHARDS, 6)
        extra = norm_rows(vectors + [padded]).astype(BF16)
        flat, tail, d_input = gradient_sums(
            sources, g_cls, extra, bias_rows, d_flow, weights["ina0"], weights["inb0"], clip_local
        )
        grad_mine = flat.reshape(-1)[: master.shape[0]]
    norm = jnp.sqrt(tail[8, 0])
    bias_grad = tail[:8].reshape(-1)[:CLASSES]
    factor = jnp.minimum(1.0, CLIP_LIMIT / (norm + 1e-06))
    clipped = grad_mine * factor
    new_first = BETA_ONE * first_moment + (1.0 - BETA_ONE) * clipped
    new_second = BETA_TWO * second_moment + (1.0 - BETA_TWO) * clipped * clipped
    first_hat = new_first / (1.0 - BETA_ONE**STEP)
    second_hat = new_second / (1.0 - BETA_TWO**STEP)
    new_master = master - LEARN_RATE * (
        first_hat / (jnp.sqrt(second_hat) + ADAM_EPS) + WEIGHT_DECAY * master
    )
    grid_grad = d_input.transpose(0, 2, 1, 3)
    return (
        new_master,
        new_first,
        new_second,
        new_master.astype(BF16),
        grid_grad,
        norm.reshape(1),
        bias_grad,
    )


def solution(mesh):
    return jax.shard_map(
        on_device,
        mesh=mesh,
        in_specs=(
            P("clip", "seg", None, None),
            P("clip"),
            P("clip"),
            P(AXES),
            P(AXES),
            P(AXES),
        ),
        out_specs=(
            P(AXES),
            P(AXES),
            P(AXES),
            P(AXES),
            P("clip", "seg", None, None),
            P(),
            P(),
        ),
        check_vma=False,
    )
```

```python
import functools
import math

import jax
import jax.numpy as jnp
from jax import lax
from jax.experimental import pallas as pl
from jax.experimental.pallas import tpu as pltpu
from jax.sharding import PartitionSpec as P

D = 2048
MID = 512
GATE = 128
CLASSES = 174
GRID = 7
HW = 49
STEP = 7
LANES = 128

NORM_EPS = 1e-05
CLIP_LIMIT = 0.001
LEARN_RATE = 0.04
WEIGHT_DECAY = 0.05
BETA_ONE = 0.9
BETA_TWO = 0.999
ADAM_EPS = 1e-08

AXES = ("seg", "clip")
MESH_ID = pl.DeviceIdType.MESH
BF16 = jnp.bfloat16
F32 = jnp.float32


def matmul(left, right):
    return jnp.dot(left, right, preferred_element_type=F32)


def layout():
    block_layout = [
        (D, MID),
        (9, MID, MID),
        (MID, D),
        (MID, GATE),
        (GATE, MID),
        (2 * MID + D,),
        (2 * MID + D,),
    ]
    return block_layout + block_layout + [(D, CLASSES), (CLASSES,)]


def widths(devices):
    return [(math.prod(extent) + devices - 1) // devices for extent in layout()]


def pad_rows(flat, rows):
    return jnp.pad(flat, (0, rows * LANES - flat.shape[0])).reshape(rows, LANES)


def small_rows(devices):
    wide = widths(devices)
    amount = sum(wide[3:7]) + sum(wide[10:14])
    amount_cls = wide[14] + wide[15]
    return [16 * ((a + 16 * LANES - 1) // (16 * LANES)) for a in (amount, amount_cls)]


def gather_parameters(master):
    devices = lax.axis_size("seg") * lax.axis_size("clip")
    wide = widths(devices)
    starts = [sum(wide[:i]) for i in range(len(wide))]
    low = master.astype(BF16)

    def part(i):
        return low[starts[i] : starts[i] + wide[i]]

    def gather(values):
        return lax.all_gather(values, AXES, axis=0, tiled=True)

    big = {}
    for base in (0, 7):
        for i, columns in ((0, MID), (1, MID), (2, D)):
            big[base + i] = gather(part(base + i).reshape(-1, columns))
    rows, rows_cls = small_rows(devices)
    small = gather(pad_rows(jnp.concatenate([part(i) for i in (3, 4, 5, 6, 10, 11, 12, 13)]), rows))
    small_cls = gather(pad_rows(jnp.concatenate([part(14), part(15)]), rows_cls))
    small = small.reshape(devices, rows * LANES)
    small_cls = small_cls.reshape(devices, rows_cls * LANES)
    shapes = layout()
    pieces = dict(big)

    def take(source, ids):
        offset = 0
        for i in ids:
            amount = math.prod(shapes[i])
            pieces[i] = source[:, offset : offset + wide[i]].reshape(-1)[:amount].reshape(shapes[i])
            offset += wide[i]

    take(small, (3, 4, 5, 6, 10, 11, 12, 13))
    take(small_cls, (14, 15))
    return [pieces[i] for i in range(16)]


def part_of(master, index):
    devices = lax.axis_size("seg") * lax.axis_size("clip")
    wide = widths(devices)
    start = sum(wide[:index])
    return master[start : start + wide[index]]


def norm_rows(vectors):
    rows = jnp.stack([jnp.pad(v, ((0, 0), (0, LANES - v.shape[1]))) for v in vectors], axis=1)
    return jnp.pad(rows, ((0, 0), (0, 16 - rows.shape[1]), (0, 0)))


def lanes_first(values):
    lead = values.shape[:-2]
    rows, columns = values.shape[-2:]
    split = values.reshape(lead + (rows, columns // LANES, LANES))
    return jnp.swapaxes(split, -3, -2).reshape(lead + (-1, LANES))


def split_rows(target, kind, block, pieces, rows):
    size = rows.shape[1] // pieces
    for k, name in enumerate(piece_names(kind, block, pieces)):
        target[name] = rows[:, k * size : (k + 1) * size].reshape(-1, MID)


def piece_names(kind, block, pieces):
    return [kind + "abc"[k] + str(block) for k in range(pieces)]


def weight_names(block):
    return piece_names("in", block, 2) + piece_names("mid", block, 3) + ["out%d" % block, "small"]


def weight_shards(master):
    devices = lax.axis_size("seg") * lax.axis_size("clip")
    if lax.axis_size("seg") != 2 or devices != SMALL_SHARDS:
        return None
    low = master.astype(BF16)
    shards = {}
    small = []
    for block in range(2):
        base = 7 * block
        split_rows(shards, "in", block, 2, part_of(low, base).reshape(1, -1, MID))
        split_rows(shards, "mid", block, 3, part_of(low, base + 1).reshape(1, -1, MID))
        shards["out%d" % block] = part_of(low, base + 2).reshape(-1, D)
        small.append(part_of(low, base + 3).reshape(-1, GATE))
        small.append(lanes_first(part_of(low, base + 4).reshape(-1, MID)))
    small.append(norm_rows([part_of(low, i)[None] for i in (5, 6, 12, 13, 15)])[0])
    shards["small"] = jnp.concatenate(small)
    cls = part_of(low, 14).reshape(-1, CLASSES)
    shards["cls"] = jnp.pad(cls, ((0, 0), (0, 2 * LANES - CLASSES)))
    return shards


def whole_weights(master):
    pieces = gather_parameters(master)
    whole = {}
    small = []
    for block in range(2):
        w_in, w_mid, w_out, w_red, w_exp = pieces[7 * block : 7 * block + 5]
        split_rows(whole, "in", block, 2, w_in.reshape(SMALL_SHARDS, -1, MID))
        split_rows(whole, "mid", block, 3, w_mid.reshape(SMALL_SHARDS, -1, MID))
        whole["out%d" % block] = w_out
        small.append(w_red.reshape(SMALL_SHARDS, -1, GATE))
        small.append(lanes_first(w_exp.reshape(SMALL_SHARDS, -1, MID)))
    vectors = [pieces[i].reshape(SMALL_SHARDS, -1) for i in (5, 6, 12, 13)]
    bias = jnp.pad(pieces[15], (0, 6 * SMALL_SHARDS - CLASSES)).reshape(SMALL_SHARDS, 6)
    small.append(norm_rows(vectors + [bias]))
    whole["small"] = jnp.concatenate(small, axis=1).reshape(-1, LANES)
    whole["cls"] = jnp.pad(pieces[14], ((0, 0), (0, 2 * LANES - CLASSES)))
    return whole


def scatter_gradients(grads):
    devices = lax.axis_size("seg") * lax.axis_size("clip")
    wide = widths(devices)
    columns = []
    for values, width in zip(grads, wide):
        flat = values.reshape(-1)
        columns.append(jnp.pad(flat, (0, devices * width - flat.shape[0])).reshape(devices, width))
    packed = jnp.concatenate(columns, axis=1)
    return lax.psum_scatter(packed, AXES, scatter_dimension=0, tiled=True)[0]


def conv(values, kernel, numbers):
    return lax.conv_general_dilated(
        values, kernel, (1, 1), ((1, 1), (1, 1)), dimension_numbers=numbers, preferred_element_type=F32
    )


class Links:
    def __init__(self, n_seg, n_clip, send_sem, recv_sem):
        self.n_seg = n_seg
        self.n_clip = n_clip
        self.inner = 4
        self.outer = n_clip // 4
        self.seg = lax.axis_index("seg")
        self.clip = lax.axis_index("clip")
        self.group = self.clip // 4
        self.place = lax.rem(self.clip, 4)
        y = self.place // 2
        x = lax.rem(self.place, 2)
        self.first = (1 - self.seg) * y + self.seg * x
        self.second = (1 - self.seg) * x + self.seg * y
        self.step = 1 + self.seg
        self.jump = 2 - self.seg
        self.across_first = (self.seg, self.clip + self.jump * (1 - 2 * self.first))
        self.across_second = (self.seg, self.clip + self.step * (1 - 2 * self.second))
        self.other = (1 - self.seg, self.clip)
        self.send_sem = send_sem
        self.recv_sem = recv_sem
        self.used = 0

    def take(self, count):
        base = self.used
        self.used += count
        return base

    def near_peer(self, i):
        return (
            lax.rem(self.seg + i // 4, self.n_seg),
            self.group * 4 + lax.rem(self.place + lax.rem(i, 4), 4),
        )

    def far_peer(self, i):
        return (self.seg, lax.rem(self.group + i, self.outer) * 4 + self.place)

    def remote(self, index, source, target, peer):
        return pltpu.make_async_remote_copy(
            src_ref=source,
            dst_ref=target,
            send_sem=self.send_sem.at[index],
            recv_sem=self.recv_sem.at[index],
            device_id=peer,
            device_id_type=MESH_ID,
        )

    def local(self, source, target):
        return pltpu.make_async_copy(source, target, self.recv_sem.at[self.take(1)])

    def meet(self):
        barrier = pltpu.get_barrier_semaphore()
        n_near = self.n_seg * 4 - 1
        n_far = self.outer - 1

        def greet(peer):
            pl.semaphore_signal(barrier, inc=1, device_id=peer, device_id_type=MESH_ID)

        repeat(1, n_near + 1, lambda i: greet(self.near_peer(i)))
        repeat(1, n_far + 1, lambda i: greet(self.far_peer(i)))
        pl.semaphore_wait(barrier, n_near + n_far)

    def sum_near(self, source, middle, near, far):
        n_near = self.n_seg * 4 - 1
        n_far = self.outer - 1
        base = self.take(n_near + n_far)

        def close(i):
            return self.remote(base + i - 1, source, near.at[i - 1], self.near_peer(i))

        def distant(i):
            return self.remote(base + n_near + i - 1, middle, far.at[i - 1], self.far_peer(i))

        repeat(1, n_near + 1, lambda i: close(i).start())
        repeat(1, n_near + 1, lambda i: close(i).wait())
        middle[...] = source[...] + jnp.sum(near[...], axis=0)
        repeat(1, n_far + 1, lambda i: distant(i).start())

        def rest():
            repeat(1, n_far + 1, lambda i: distant(i).wait())
            return middle[...] + jnp.sum(far[...], axis=0)

        return rest

    def all_sum(self, source, middle, near, far):
        return self.sum_near(source, middle, near, far)()


def repeat(first, last, action):
    if last - first <= 8:
        for i in range(first, last):
            action(i)
    else:

        def body(i, carry):
            action(i)
            return carry

        lax.fori_loop(first, last, body, 0)


def sum_scratch(n_seg, n_clip, shape):
    return [
        pltpu.VMEM(shape, F32),
        pltpu.VMEM(shape, F32),
        pltpu.VMEM((n_seg * 4 - 1,) + shape, F32),
        pltpu.VMEM((n_clip // 4 - 1,) + shape, F32),
    ]


class Gather:
    def __init__(self, links, shard, whole):
        depth = links.outer
        whole = whole.reshape((links.n_seg, depth, 4) + shard.shape)
        base = links.take(depth + 3)
        seg, z, place = links.seg, links.group, links.place
        self.own = links.local(shard, whole.at[seg, z, place])
        self.steps = [
            [
                links.remote(base + i - 1, shard, whole.at[seg, z, place], links.far_peer(i))
                for i in range(1, depth)
            ],
            [
                links.remote(
                    base + depth - 1, whole.at[seg, :, place], whole.at[seg, :, place], links.across_second
                )
            ],
            [],
            [links.remote(base + depth + 2, whole.at[seg], whole.at[seg], links.other)],
        ]
        for k in range(2):
            index = links.jump * links.first + links.step * k
            self.steps[2].append(
                links.remote(
                    base + depth + k, whole.at[seg, :, index], whole.at[seg, :, index], links.across_first
                )
            )
        self.at = -1

    def advance(self, last=3):
        if self.at >= 0:
            for copy in self.steps[self.at]:
                copy.wait()
            if self.at == 0:
                self.own.wait()
        self.at += 1
        if self.at == 0:
            self.own.start()
        if self.at <= 3:
            for copy in self.steps[self.at]:
                copy.start()

    def finish(self):
        while self.at <= 3:
            self.advance()


def row_vector(table, row, start, count):
    return jnp.concatenate([table[start + k, row : row + 1, :] for k in range(count)], axis=1)


def build_table(small, table):
    lane = lax.broadcasted_iota(jnp.int32, (8, LANES), 1)
    for q in range(SMALL_SHARDS // 4):
        rows = [small[4 * q + j, 64:80, :].astype(F32)[:8] for j in range(4)]
        one = pltpu.roll(rows[1], 96, 1)
        two = pltpu.roll(rows[2], 64, 1)
        three = pltpu.roll(rows[3], 32, 1)
        table[3 * q] = jnp.where(lane < 96, rows[0], one)
        table[3 * q + 1] = jnp.where(lane < 64, one, two)
        table[3 * q + 2] = jnp.where(lane < 32, two, three)


def put_rows(target, start, vector, count):
    width = vector.shape[1] // count
    for k in range(count):
        target[start + k : start + k + 1, :] = vector[:, k * width : (k + 1) * width]


def fold(values):
    return jnp.sum(values.reshape(-1, 8, values.shape[-1]), axis=0)


def excite_pick(shards, k):
    deep = GATE // shards
    line = lax.broadcasted_iota(jnp.int32, (GATE, shards * 16), 0)
    column = lax.broadcasted_iota(jnp.int32, (GATE, shards * 16), 1)
    wanted = (line // deep) * 16 + k * deep + lax.rem(line, deep)
    return (column == wanted).astype(F32).astype(BF16)


def excite_weights(small, block):
    shards = small.shape[0]
    rows = small[:, 32 * block + 16 : 32 * block + 32].reshape(shards * 16, LANES)
    parts = [matmul(excite_pick(shards, k), rows) for k in range(MID // LANES)]
    return jnp.concatenate(parts, axis=1).astype(BF16)


SMALL_SHARDS = 32
SLOTS_HERE = 8
TABLE = ((2 * MID + D) // LANES + 1, 8, LANES)


STAGES = (
    (
        "ina0", "small", "@dpad", "@fpad", "@turn0", "inb0", "@turn1", "@turn2", "@turn3", "@turn4", "mida0",
        "@turn5", "@turn6", "ina0", "small", "ina0", "midb0", "inb0", "small", "mida0", "midc0", "ina0", "inb0",
        "small", "out0", "ina0", "midb0", "mida0", "small", "midc0", "ina1", "inb0", "midb0", "inb1", "inb0",
        "@first", "mida1", "mida0", "midc0", "out0", "ina1", "@near1", "midb1", "mida0", "midb0", "inb1", "@far1",
        "midc1", "midb0", "midc0", "out0", "ina1", "mida1", "@second", "inb1", "@swap", "@excite", "midc0",
        "midb1", "@third", "out0", "ina1", "mida1", "midc1", "@near2", "out0", "ina1", "inb1", "midb1", "@far2",
        "mida1", "midc1", "@fourth", "inb1", "mida1", "midb1", "@near3", "midc1", "@far3", "midb1", "@fifth",
        "midc1",
    ),
    (
        "out1", "@dpad", "@fpad", "@first", "cls", "@near1", "out1", "@far1", "cls", "@second", "@swap", "out1",
        "@excite", "cls", "@third", "out1", "@near2", "cls", "@far2", "out1", "@fourth", "cls", "@near3", "@far3",
        "@fifth",
    ),
)
JOBS = tuple(tuple(dict.fromkeys(item for item in order if item[0] != "@")) for order in STAGES)


def forward_kernel(n_seg, n_clip, block, jobs, plan, *refs):
    refs = list(refs)

    def pop(count=1):
        taken = refs[:count]
        del refs[:count]
        return taken if count != 1 else taken[0]

    last = block == 1
    x_hbm, mask, following, table_in = pop(4)
    share, chosen = pop(2) if last else (None, None)
    shards = dict(zip(jobs, [pop() for _ in jobs]))
    given = dict(zip(plan, [pop() for _ in plan]))
    wholes = dict(zip(jobs, [pop() for _ in jobs]))
    h1_out, low_out, gate_out, mix_out, f_out, h2_out, a2_out, h3_out = pop(8)
    out_hbm, table_out, st1, st2, st3 = pop(5)
    g_cls, g_bias = pop(2) if last else (None, None)
    x_out = None if last else pop()
    xv, w_in, w_mid, w_out, small = pop(5)
    h1v, a1v, lowv, rv, edge, dpad, mixv, gatev, fpad, h2v, a2v, h3v = pop(12)
    wide_sum, wide_square, w_exp = pop(3)
    sums = [pop(4) for _ in range(3)]
    pooled, clip_sums, clip_other, w_cls = pop(4) if last else [None] * 4
    frames_first = None if last else pop()
    send_sem, recv_sem = pop(2)
    links = Links(n_seg, n_clip, send_sem, recv_sem)
    frames = xv.shape[1]
    table = table_in if last else table_out
    outgoing = []

    def send_out(source, target):
        copy = links.local(source, target)
        copy.start()
        outgoing.append(copy)

    x_base = links.take(GRID)

    def load_x(i):
        rows = pl.ds(GRID * i, GRID)
        return pltpu.make_async_copy(x_hbm.at[rows], xv.at[rows], links.recv_sem.at[x_base + i])

    if last:
        for i in range(GRID):
            load_x(i).start()
    else:
        load_frames = links.local(x_hbm, frames_first)
        load_frames.start()
    gathers = {name: Gather(links, shards[name], wholes[name]) for name in jobs}

    targets = {"out%d" % block: w_out, "small": small}
    if last:
        targets["cls"] = w_cls
    for kind, target, count in (("in", w_in, 2), ("mid", w_mid, 3)):
        rows = target.shape[0] // SMALL_SHARDS
        size = rows // count
        wide = target.reshape(SMALL_SHARDS, rows, MID)
        for k, name in enumerate(piece_names(kind, block, count)):
            targets[name] = wide.at[:, k * size : (k + 1) * size]
    loads = {}

    def load(name):
        source = wholes[name] if name in gathers else given[name]
        loads[name] = links.local(source.reshape(targets[name].shape), targets[name])
        loads[name].start()

    def push(name):
        if gathers[name].at <= 3:
            gathers[name].advance()
            if gathers[name].at > 3 and name in targets:
                load(name)

    def need(*names):
        for name in names:
            while name not in loads:
                push(name)
        for name in names:
            loads[name].wait()

    early = piece_names("in", block, 2)
    for name in early:
        if name not in gathers:
            load(name)
    table = table_in if last else table_out
    half = MID // LANES

    def norm(index, tot, columns, start, out):
        live_rows = table[TABLE[0] - 1, 0:1, 0:1]
        mean = jnp.concatenate([tot[k : k + 1] for k in range(4)], axis=1) / live_rows
        square = jnp.concatenate([tot[4 + k : 5 + k] for k in range(4)], axis=1) / live_rows
        inv = lax.rsqrt(square - mean * mean + NORM_EPS)
        out[0:1, :] = mean
        out[1:2, :] = inv
        gain = row_vector(table, 2 * block, start, columns // LANES)
        shift = row_vector(table, 2 * block + 1, start, columns // LANES)
        scale = gain * inv
        return scale, shift - mean * scale

    def masked_sums(values):
        shaped = values.reshape(-1, frames, values.shape[-1])
        masked = shaped * mask[...][None]
        return fold(masked), fold(masked * shaped)

    zeros = jnp.zeros((8, MID), F32)
    kept = {}

    def first(i, carry):
        if last:
            load_x(i).wait()
        part = matmul(xv[pl.ds(GRID * i, GRID)].reshape(GRID * frames, D), w_in[...])
        h1v[pl.ds(GRID * i, GRID)] = part.reshape(GRID, frames, MID)
        one, two = masked_sums(part)
        return (carry[0] + one, carry[1] + two)

    def put_sums(index, one, two):
        stat = sums[index][0]
        put_rows(stat, 0, jnp.sum(one, axis=0, keepdims=True), 4)
        put_rows(stat, 4, jnp.sum(two, axis=0, keepdims=True), 4)
        return stat

    def stage_dpad():
        dpad[...] = jnp.zeros_like(dpad)

    def stage_fpad():
        fpad[...] = jnp.zeros_like(fpad)
        if last:
            table_out[...] = table_in[...]
        else:
            table_out[...] = jnp.zeros_like(table_out)

    def turn(step):
        if step == 0:
            load_frames.wait()

        def body(p, carry):
            for k in range(4):
                span = slice(k * MID, (k + 1) * MID)
                parts = [frames_first[c, p, :, span].astype(F32) for c in range(frames_first.shape[0])]
                xv[p, :, span] = jnp.concatenate(parts, axis=0).astype(BF16)
            return carry

        lax.fori_loop(GRID * step, GRID * step + GRID, body, 0)
        if step == GRID - 1:
            kept["x"] = links.local(xv, x_out)
            kept["x"].start()

    def stage_first():
        need(*piece_names("in", block, 2))
        for name in targets:
            if name not in gathers and name not in early:
                load(name)
        stat = put_sums(0, *lax.fori_loop(0, GRID, first, (zeros, zeros)))
        present = HW * jnp.sum(mask[:, :LANES], axis=0, keepdims=True)
        stat[8:16, :] = jnp.broadcast_to(present, (8, LANES))
        send_out(h1v, h1_out)

    def stage_near1():
        kept["rest"] = links.sum_near(*sums[0])

    def stage_far1():
        need("small")
        total = kept["rest"]()
        if not last:
            build_table(small, table_out)
            table_out[TABLE[0] - 1] = total[8:16]
        kept["one"] = norm(0, total, MID, 0, st1)

    def second(i, carry):
        for j in range(GRID):
            y = h1v[GRID * i + j] * kept["one"][0] + kept["one"][1]
            a = y * jax.nn.sigmoid(y)
            a1v[GRID * i + j] = a
            lowv[GRID * i + j] = a.astype(BF16)
        part = matmul(lowv[pl.ds(GRID * i, GRID)].reshape(GRID * frames, MID), kept["red"])
        rv[pl.ds(GRID * i, GRID)] = part.astype(BF16).reshape(GRID, frames, GATE)
        return carry

    def stage_second():
        w_exp[...] = excite_weights(small, block)
        kept["red"] = small[:, 32 * block : 32 * block + 16].reshape(MID, GATE)
        lax.fori_loop(0, GRID, second, 0)
        send_out(lowv, low_out)
        kept["swap"] = links.remote(links.take(1), rv, edge, links.other)
        kept["swap"].start()

    row = lax.rem(lax.broadcasted_iota(jnp.int32, (frames, GATE), 0), 8)

    def change(i, carry):
        for j in range(GRID):
            now = rv[GRID * i + j].astype(F32)
            rest = edge[GRID * i + j].astype(F32)
            later = jnp.where(row < 7, pltpu.roll(now, frames - 1, 0), pltpu.roll(rest, 7, 0))
            dpad[i + 1, j + 1] = following[...] * (later - now)
        return carry

    def stage_swap():
        kept["swap"].wait()
        lax.fori_loop(0, GRID, change, 0)

    def excite(i, carry):
        for j in range(GRID):
            total = jnp.zeros((frames, GATE), F32)
            for k in range(9):
                total = total + dpad[i + k // 3, j + k % 3]
            mixv[GRID * i + j] = (dpad[i + 1, j + 1] + total / 9.0).astype(BF16)
        e = matmul(mixv[pl.ds(GRID * i, GRID)].reshape(GRID * frames, GATE), w_exp[...])
        e = e.reshape(GRID, frames, MID)
        for j in range(GRID):
            gate = jax.nn.sigmoid(e[j])
            gatev[GRID * i + j] = gate.astype(BF16)
            fpad[i + 1, j + 1] = (a1v[GRID * i + j] * (1.0 + gate)).astype(BF16)
        return carry

    def stage_excite():
        lax.fori_loop(0, GRID, excite, 0)
        send_out(mixv, mix_out)
        send_out(gatev, gate_out)
        send_out(fpad.at[pl.ds(1, GRID), pl.ds(1, GRID)], f_out)

    def third(i, carry):
        part = None
        for k in range(9):
            window = fpad[i + k // 3, pl.ds(k % 3, GRID)].reshape(GRID * frames, MID)
            term = matmul(window, w_mid[k * MID : (k + 1) * MID])
            part = term if part is None else part + term
        h2v[pl.ds(GRID * i, GRID)] = part.reshape(GRID, frames, MID)
        one, two = masked_sums(part)
        return (carry[0] + one, carry[1] + two)

    def stage_third():
        need(*piece_names("mid", block, 3))
        put_sums(1, *lax.fori_loop(0, GRID, third, (zeros, zeros)))
        send_out(h2v, h2_out)

    def stage_near2():
        kept["rest"] = links.sum_near(*sums[1])

    def stage_far2():
        kept["two"] = norm(1, kept["rest"](), MID, half, st2)
        wide_sum[...] = jnp.zeros_like(wide_sum)
        wide_square[...] = jnp.zeros_like(wide_square)

    def fourth(i, carry):
        for j in range(GRID):
            y = h2v[GRID * i + j] * kept["two"][0] + kept["two"][1]
            a2v[GRID * i + j] = (y * jax.nn.sigmoid(y)).astype(BF16)
        rows = a2v[pl.ds(GRID * i, GRID)].reshape(GRID * frames, MID)
        for k in range(4):
            part = matmul(rows, w_out[:, k * MID : (k + 1) * MID])
            h3v[pl.ds(GRID * i, GRID), :, k * MID : (k + 1) * MID] = part.astype(BF16).reshape(
                GRID, frames, MID
            )
            one, two = masked_sums(part)
            wide_sum[:, k * MID : (k + 1) * MID] += one
            wide_square[:, k * MID : (k + 1) * MID] += two
        return carry

    def stage_fourth():
        need("out%d" % block)
        lax.fori_loop(0, GRID, fourth, 0)
        put_sums(2, wide_sum[...], wide_square[...])
        send_out(a2v, a2_out)
        send_out(h3v, h3_out)

    def stage_near3():
        kept["rest"] = links.sum_near(*sums[2])

    def stage_far3():
        kept["three"] = norm(2, kept["rest"](), D, 2 * half, st3)
        if last:
            pooled[...] = jnp.zeros_like(pooled)

    def fifth(p, carry):
        for k in range(4):
            span = slice(k * MID, (k + 1) * MID)
            scale, shift = kept["three"]
            pre = h3v[p, :, span].astype(F32) * scale[:, span] + shift[:, span]
            pre = pre + xv[p, :, span].astype(F32)
            value = pre * jax.nn.sigmoid(pre)
            if last:
                pooled[:, span] += value * mask[...]
            else:
                xv[p, :, span] = value.astype(BF16)
        return carry

    def stage_fifth():
        if not last:
            kept["x"].wait()
        lax.fori_loop(0, HW, fifth, 0)
        if last:
            classify()
        send_out(pooled if last else xv, out_hbm)

    def classify():
        clips = frames // SLOTS_HERE
        clip_sums[...] = jnp.zeros_like(clip_sums)
        for c in range(clips):
            rows = pooled[SLOTS_HERE * c : SLOTS_HERE * (c + 1), :]
            clip_sums[c : c + 1, :] = jnp.sum(rows, axis=0, keepdims=True)
        swap = links.remote(links.take(1), clip_sums, clip_other, links.other)
        swap.start()
        lane = lax.broadcasted_iota(jnp.int32, (1, 2 * LANES), 1)
        bias = jnp.zeros((1, 2 * LANES), F32)
        for d in range(SMALL_SHARDS):
            piece = small[d, 64:80, :].astype(F32)[4:5]
            piece = jnp.concatenate([piece, jnp.zeros_like(piece)], axis=1)
            own = jnp.logical_and(lane >= 6 * d, lane < 6 * d + 6)
            bias = bias + jnp.where(own, pltpu.roll(piece, 6 * d, 1) if d else piece, 0.0)
        need("cls")
        swap.wait()
        mean = (clip_sums[...] + clip_other[...]) * share[:, 0:1]
        low = jnp.concatenate([mean, jnp.zeros_like(mean)], axis=0).astype(BF16)
        scores = matmul(low, w_cls[...])[:8] + bias
        scores = jnp.where(lane < CLASSES, scores, -1e30)
        scores = jnp.exp(scores - jnp.max(scores, axis=1, keepdims=True))
        chance = scores / jnp.sum(scores, axis=1, keepdims=True)
        clips_total = clips * links.n_clip
        d_scores = jnp.where(share[:, 0:1] > 0.0, (chance - chosen[...]) / clips_total, 0.0)
        g_bias[...] = jnp.broadcast_to(jnp.sum(d_scores, axis=0, keepdims=True) / n_seg, g_bias.shape)
        d_low = jnp.concatenate([d_scores, jnp.zeros_like(d_scores)], axis=0).astype(BF16)
        grad = lax.dot_general(low, d_low, (((0,), (0,)), ((), ())), preferred_element_type=F32)
        g_cls[...] = (grad / n_seg).astype(BF16)
        d_mean = lax.dot_general(d_low, w_cls[...], (((1,), (1,)), ((), ())), preferred_element_type=F32)
        d_mean = d_mean[:8] * share[:, 0:1]
        for c in range(clips):
            rows = slice(SLOTS_HERE * c, SLOTS_HERE * (c + 1))
            here = mask[rows, 0:1]
            pooled[rows, :] = jnp.broadcast_to(d_mean[c : c + 1], (SLOTS_HERE, D)) * here

    stages = {
        "dpad": stage_dpad,
        "fpad": stage_fpad,
        "first": stage_first,
        "near1": stage_near1,
        "far1": stage_far1,
        "second": stage_second,
        "swap": stage_swap,
        "excite": stage_excite,
        "third": stage_third,
        "near2": stage_near2,
        "far2": stage_far2,
        "fourth": stage_fourth,
        "near3": stage_near3,
        "far3": stage_far3,
        "fifth": stage_fifth,
    }
    for k in range(GRID):
        stages["turn%d" % k] = functools.partial(turn, k)
    links.meet()
    for item in STAGES[block]:
        if item[0] == "@":
            with jax.named_scope(item[1:]):
                stages[item[1:]]()
        elif item in gathers:
            push(item)
    for name in jobs:
        gathers[name].finish()
    for copy in outgoing:
        copy.wait()


def forward_block(block, x, mask, following, table, extra, shards, given):
    n_seg = lax.axis_size("seg")
    n_clip = lax.axis_size("clip")
    last = block == 1
    cells = x.shape[0] if last else x.shape[1]
    frames = x.shape[1] if last else x.shape[0] * x.shape[2]
    jobs = list(shards)
    plan = list(given)
    any_spec = pl.BlockSpec(memory_space=pl.ANY)
    vmem = pl.BlockSpec(memory_space=pltpu.VMEM)
    depth = n_clip // 4

    def grid_shape(columns):
        return (cells, frames, columns)

    devices = n_seg * n_clip
    outs = [jax.ShapeDtypeStruct((devices * shards[n].shape[0], shards[n].shape[1]), BF16) for n in jobs]
    outs += [
        jax.ShapeDtypeStruct(grid_shape(MID), F32),
        jax.ShapeDtypeStruct(grid_shape(MID), BF16),
        jax.ShapeDtypeStruct(grid_shape(MID), BF16),
        jax.ShapeDtypeStruct(grid_shape(GATE), BF16),
        jax.ShapeDtypeStruct((GRID, GRID, frames, MID), BF16),
        jax.ShapeDtypeStruct(grid_shape(MID), F32),
        jax.ShapeDtypeStruct(grid_shape(MID), BF16),
        jax.ShapeDtypeStruct(grid_shape(D), BF16),
        jax.ShapeDtypeStruct((frames, D), F32) if last else jax.ShapeDtypeStruct(grid_shape(D), BF16),
        jax.ShapeDtypeStruct(TABLE, F32),
        jax.ShapeDtypeStruct((8, MID), F32),
        jax.ShapeDtypeStruct((8, MID), F32),
        jax.ShapeDtypeStruct((8, D), F32),
    ]
    out_specs = [any_spec] * (len(jobs) + 9) + [vmem] * 4
    if last:
        outs += [jax.ShapeDtypeStruct((D, 2 * LANES), BF16), jax.ShapeDtypeStruct((8, 2 * LANES), F32)]
        out_specs += [vmem] * 2
    else:
        outs.append(jax.ShapeDtypeStruct(grid_shape(D), BF16))
        out_specs.append(any_spec)

    shapes = [(D, MID), (9 * MID, MID), (MID, D), (SMALL_SHARDS, 80, LANES)]
    scratch = [pltpu.VMEM(grid_shape(D), BF16)]
    scratch += [pltpu.VMEM(s, BF16) for s in shapes]
    scratch += [
        pltpu.VMEM(grid_shape(MID), F32),
        pltpu.VMEM(grid_shape(MID), F32),
        pltpu.VMEM(grid_shape(MID), BF16),
        pltpu.VMEM(grid_shape(GATE), BF16),
        pltpu.VMEM(grid_shape(GATE), BF16),
        pltpu.VMEM((GRID + 2, GRID + 2, frames, GATE), F32),
        pltpu.VMEM(grid_shape(GATE), BF16),
        pltpu.VMEM(grid_shape(MID), BF16),
        pltpu.VMEM((GRID + 2, GRID + 2, frames, MID), BF16),
        pltpu.VMEM(grid_shape(MID), F32),
        pltpu.VMEM(grid_shape(MID), BF16),
        pltpu.VMEM(grid_shape(D), BF16),
        pltpu.VMEM((8, D), F32),
        pltpu.VMEM((8, D), F32),
        pltpu.VMEM((GATE, MID), BF16),
    ]
    for shape in ((16, LANES), (8, LANES), (8, MID)):
        scratch += sum_scratch(n_seg, n_clip, shape)
    if last:
        scratch += [pltpu.VMEM((frames, D), F32), pltpu.VMEM((8, D), F32), pltpu.VMEM((8, D), F32)]
        scratch.append(pltpu.VMEM((D, 2 * LANES), BF16))
    else:
        scratch.append(pltpu.VMEM(x.shape, BF16))
    count = 4 * (n_seg * 4 + depth) + len(jobs) * (depth + 4) + 48
    scratch += [pltpu.SemaphoreType.DMA((count,)), pltpu.SemaphoreType.DMA((count,))]
    results = pl.pallas_call(
        functools.partial(forward_kernel, n_seg, n_clip, block, jobs, plan),
        out_shape=outs,
        in_specs=[any_spec, vmem, vmem, vmem] + [vmem] * len(extra) + [any_spec] * (len(jobs) + len(plan)),
        out_specs=out_specs,
        scratch_shapes=scratch,
        compiler_params=pltpu.CompilerParams(
            collective_id=30 + block, has_side_effects=True, vmem_limit_bytes=60 * 1024 * 1024
        ),
        name="forward_block",
    )(x, mask, following, table, *extra, *[shards[n] for n in jobs], *[given[n] for n in plan])
    wholes = dict(zip(jobs, results[: len(jobs)]))
    return wholes, results[len(jobs) :]


def backward_kernel(n_seg, n_clip, block, *refs):
    refs = list(refs)

    def pop(count=1):
        taken = refs[:count]
        del refs[:count]
        return taken if count != 1 else taken[0]

    last = block == 1
    h3_hbm, x_hbm, d_in, h2_hbm, h1_hbm, gate_hbm = pop(6)
    in_a, in_b, mid_a, mid_b, mid_c, out_hbm, small_hbm = pop(7)
    table, st1, st2, st3, mask, present, following = pop(7)
    dh3_out, dh2_out, de_out, dr_out, dh1_out, dx_out, norm_grads = pop(7)
    dv, h3v, xv, h2v, h1v, gatev, dyv, pad2, dsv, edge, pad_s, pad_e = pop(12)
    drv, dh1v, w_in, w_mid, w_out, small, w_exp = pop(7)
    sum_gain, sum_shift = pop(2)
    sums = [pop(4) for _ in range(3)]
    send_sem, recv_sem = pop(2)
    links = Links(n_seg, n_clip, send_sem, recv_sem)
    frames = xv.shape[1]
    outgoing = []

    def send_out(source, target):
        copy = links.local(source, target)
        copy.start()
        outgoing.append(copy)

    def load(source, target):
        copy = links.local(source.reshape(target.shape), target)
        copy.start()
        return copy

    streams = [(h3_hbm, h3v), (x_hbm, xv)]
    if not last:
        streams.append((d_in, dv))
    wide_base = links.take(len(streams) * GRID)

    def wide_copies(i):
        rows = pl.ds(GRID * i, GRID)
        return [
            pltpu.make_async_copy(source.at[rows], target.at[rows], links.recv_sem.at[wide_base + GRID * k + i])
            for k, (source, target) in enumerate(streams)
        ]

    for i in range(GRID):
        for copy in wide_copies(i):
            copy.start()
    loads_two = [load(out_hbm, w_out), load(h2_hbm, h2v)]
    loads_three = [load(h1_hbm, h1v), load(gate_hbm, gatev), load(small_hbm, small)]
    loads_four = []
    for parts, target, waits in (
        ((mid_a, mid_b, mid_c), w_mid, loads_three),
        ((in_a, in_b), w_in, loads_four),
    ):
        rows = target.shape[0] // SMALL_SHARDS
        size = rows // len(parts)
        wide = target.reshape(SMALL_SHARDS, rows, MID)
        for k, source in enumerate(parts):
            waits.append(load(source, wide.at[:, k * size : (k + 1) * size]))
    links.meet()
    live_rows = table[TABLE[0] - 1, 0:1, 0:1]
    half = MID // LANES
    pad2[...] = jnp.zeros_like(pad2)
    pad_s[...] = jnp.zeros_like(pad_s)
    pad_e[...] = jnp.zeros_like(pad_e)
    sum_gain[...] = jnp.zeros_like(sum_gain)
    sum_shift[...] = jnp.zeros_like(sum_shift)

    def vectors(start, columns, stats):
        gain = row_vector(table, 2 * block, start, columns // LANES)
        shift = row_vector(table, 2 * block + 1, start, columns // LANES)
        return gain, shift, stats[0:1, :], stats[1:2, :]

    def totals(index, start, columns, gain_rows, shift_rows):
        stat = sums[index][0]
        put_rows(stat, 0, jnp.sum(gain_rows, axis=0, keepdims=True), 4)
        put_rows(stat, 4, jnp.sum(shift_rows, axis=0, keepdims=True), 4)
        tot = links.all_sum(*sums[index])
        gain = jnp.concatenate([tot[k : k + 1] for k in range(4)], axis=1)
        shift = jnp.concatenate([tot[4 + k : 5 + k] for k in range(4)], axis=1)
        put_rows(norm_grads, start, gain, columns // LANES)
        put_rows(norm_grads, 24 + start, shift, columns // LANES)
        return gain / live_rows, shift / live_rows

    def slope_of(values):
        sig = jax.nn.sigmoid(values)
        return sig, sig * (1.0 + values * (1.0 - sig))

    def dot_t(left, right):
        return lax.dot_general(left, right, (((1,), (1,)), ((), ())), preferred_element_type=F32)

    gain3, shift3, mean3, inv3 = vectors(2 * half, D, st3)
    dx_base = links.take(GRID)

    def dx_copy(i):
        rows = pl.ds(GRID * i, GRID)
        return pltpu.make_async_copy(dv.at[rows], dx_out.at[rows], links.recv_sem.at[dx_base + i])


    def first_rows(i, carry):
        for copy in wide_copies(i):
            copy.wait()
        lax.fori_loop(GRID * i, GRID * i + GRID, first, carry)
        if not last:
            dx_copy(i).start()
        return carry

    def first(p, carry):
        for k in range(4):
            span = slice(k * MID, (k + 1) * MID)
            n = (h3v[p, :, span].astype(F32) - mean3[:, span]) * inv3[:, span]
            pre = n * gain3[:, span] + shift3[:, span] + xv[p, :, span].astype(F32)
            grad = d_in[:, span] if last else dv[p, :, span]
            grad = grad * slope_of(pre)[1]
            dv[p, :, span] = grad
            sum_gain[:, span] += fold(grad * n)
            sum_shift[:, span] += fold(grad)
        return carry

    lax.fori_loop(0, GRID, first_rows, 0)
    part_gain, part_shift = totals(0, 2 * half, D, sum_gain[...], sum_shift[...])
    factor3 = gain3 * inv3
    for copy in loads_two:
        copy.wait()
    gain2, shift2, mean2, inv2 = vectors(half, MID, st2)
    zeros = jnp.zeros((8, MID), F32)

    def second(i, carry):
        for j in range(GRID):
            p = GRID * i + j
            for k in range(4):
                span = slice(k * MID, (k + 1) * MID)
                n = (h3v[p, :, span].astype(F32) - mean3[:, span]) * inv3[:, span]
                rest = mask[...] * (part_shift[:, span] + n * part_gain[:, span])
                h3v[p, :, span] = (factor3[:, span] * (dv[p, :, span] - rest)).astype(BF16)
        d_a = dot_t(h3v[pl.ds(GRID * i, GRID)].reshape(GRID * frames, D), w_out[...])
        d_a = d_a.reshape(GRID, frames, MID)
        one, two = carry
        for j in range(GRID):
            n = (h2v[GRID * i + j] - mean2) * inv2
            grad = d_a[j] * slope_of(n * gain2 + shift2)[1]
            dyv[GRID * i + j] = grad
            one = one + fold(grad * n)
            two = two + fold(grad)
        return (one, two)

    one, two = lax.fori_loop(0, GRID, second, (zeros, zeros))
    send_out(h3v, dh3_out)
    part_gain2, part_shift2 = totals(1, half, MID, one, two)
    factor2 = gain2 * inv2

    def third(i, carry):
        for j in range(GRID):
            p = GRID * i + j
            n = (h2v[p] - mean2) * inv2
            rest = mask[...] * (part_shift2 + n * part_gain2)
            pad2[i + 1, j + 1] = (factor2 * (dyv[p] - rest)).astype(BF16)
        return carry

    lax.fori_loop(0, GRID, third, 0)
    send_out(pad2.at[pl.ds(1, GRID), pl.ds(1, GRID)], dh2_out)
    for copy in loads_three:
        copy.wait()
    w_exp[...] = excite_weights(small, block)
    red = small[:, 32 * block : 32 * block + 16].reshape(MID, GATE)
    gain1, shift1, mean1, inv1 = vectors(0, MID, st1)

    def fourth(i, carry):
        part = None
        for k in range(9):
            window = pad2[i + 2 - k // 3, pl.ds(2 - k % 3, GRID)].reshape(GRID * frames, MID)
            term = dot_t(window, w_mid[k * MID : (k + 1) * MID])
            part = term if part is None else part + term
        part = part.reshape(GRID, frames, MID)
        for j in range(GRID):
            p = GRID * i + j
            y = (h1v[p] - mean1) * inv1 * gain1 + shift1
            a = y * jax.nn.sigmoid(y)
            gate = gatev[p].astype(F32)
            dyv[p] = part[j] * (1.0 + gate)
            gatev[p] = (part[j] * a * gate * (1.0 - gate)).astype(BF16)
        d_s = dot_t(gatev[pl.ds(GRID * i, GRID)].reshape(GRID * frames, MID), w_exp[...])
        d_s = d_s.astype(BF16).reshape(GRID, frames, GATE)
        dsv[pl.ds(GRID * i, GRID)] = d_s
        for j in range(GRID):
            pad_s[i + 1, j + 1] = d_s[j].astype(F32)
        return carry

    lax.fori_loop(0, GRID, fourth, 0)
    swap = links.remote(links.take(1), dsv, edge, links.other)
    swap.start()
    send_out(gatev, de_out)
    swap.wait()

    def unpack(i, carry):
        for j in range(GRID):
            pad_e[i + 1, j + 1] = edge[GRID * i + j].astype(F32)
        return carry

    lax.fori_loop(0, GRID, unpack, 0)
    row = lax.rem(lax.broadcasted_iota(jnp.int32, (frames, GATE), 0), 8)
    from_other = links.seg.astype(F32)

    def fifth(i, carry):
        for j in range(GRID):
            near = jnp.zeros((frames, GATE), F32)
            far = jnp.zeros((frames, GATE), F32)
            for k in range(9):
                near = near + pad_s[i + k // 3, j + k % 3]
                far = far + pad_e[i + k // 3, j + k % 3]
            near = pad_s[i + 1, j + 1] + near / 9.0
            far = (pad_e[i + 1, j + 1] + far / 9.0) * from_other
            earlier = jnp.where(row > 0, pltpu.roll(near, 1, 0), pltpu.roll(far, frames - 7, 0))
            drv[GRID * i + j] = (present[...] * earlier - following[...] * near).astype(BF16)
        d_a = dot_t(drv[pl.ds(GRID * i, GRID)].reshape(GRID * frames, GATE), red)
        d_a = d_a.reshape(GRID, frames, MID)
        one, two = carry
        for j in range(GRID):
            p = GRID * i + j
            n = (h1v[p] - mean1) * inv1
            grad = (dyv[p] + d_a[j]) * slope_of(n * gain1 + shift1)[1]
            dyv[p] = grad
            one = one + fold(grad * n)
            two = two + fold(grad)
        return (one, two)

    one, two = lax.fori_loop(0, GRID, fifth, (zeros, zeros))
    send_out(drv, dr_out)
    part_gain1, part_shift1 = totals(2, 0, MID, one, two)
    factor1 = gain1 * inv1
    for copy in loads_four:
        copy.wait()

    def sixth(i, carry):
        for j in range(GRID):
            p = GRID * i + j
            n = (h1v[p] - mean1) * inv1
            rest = mask[...] * (part_shift1 + n * part_gain1)
            dh1v[p] = (factor1 * (dyv[p] - rest)).astype(BF16)
        if last:
            rows = dh1v[pl.ds(GRID * i, GRID)].reshape(GRID * frames, MID)
            for k in range(4):
                span = slice(k * MID, (k + 1) * MID)
                part = dot_t(rows, w_in[span, :])
                dv[pl.ds(GRID * i, GRID), :, span] += part.reshape(GRID, frames, MID)
            dx_copy(i).start()
        return carry

    lax.fori_loop(0, GRID, sixth, 0)
    send_out(dh1v, dh1_out)
    for i in range(GRID):
        dx_copy(i).wait()
    for copy in outgoing:
        copy.wait()


def backward_block(block, h3, x, d_in, h2, h1, gate, weights, table, stats, masks):
    n_seg = lax.axis_size("seg")
    n_clip = lax.axis_size("clip")
    cells, frames, width = x.shape
    any_spec = pl.BlockSpec(memory_space=pl.ANY)
    vmem = pl.BlockSpec(memory_space=pltpu.VMEM)
    last = block == 1

    def grid_shape(columns):
        return (cells, frames, columns)

    outs = [
        jax.ShapeDtypeStruct(grid_shape(D), BF16),
        jax.ShapeDtypeStruct((GRID, GRID, frames, MID), BF16),
        jax.ShapeDtypeStruct(grid_shape(MID), BF16),
        jax.ShapeDtypeStruct(grid_shape(GATE), BF16),
        jax.ShapeDtypeStruct(grid_shape(MID), BF16),
        jax.ShapeDtypeStruct(grid_shape(D), F32),
        jax.ShapeDtypeStruct((48, LANES), F32),
    ]
    scratch = [
        pltpu.VMEM(grid_shape(D), F32),
        pltpu.VMEM(grid_shape(D), BF16),
        pltpu.VMEM(grid_shape(D), BF16),
        pltpu.VMEM(grid_shape(MID), F32),
        pltpu.VMEM(grid_shape(MID), F32),
        pltpu.VMEM(grid_shape(MID), BF16),
        pltpu.VMEM(grid_shape(MID), F32),
        pltpu.VMEM((GRID + 2, GRID + 2, frames, MID), BF16),
        pltpu.VMEM(grid_shape(GATE), BF16),
        pltpu.VMEM(grid_shape(GATE), BF16),
        pltpu.VMEM((GRID + 2, GRID + 2, frames, GATE), F32),
        pltpu.VMEM((GRID + 2, GRID + 2, frames, GATE), F32),
        pltpu.VMEM(grid_shape(GATE), BF16),
        pltpu.VMEM(grid_shape(MID), BF16),
        pltpu.VMEM((D, MID), BF16),
        pltpu.VMEM((9 * MID, MID), BF16),
        pltpu.VMEM((MID, D), BF16),
        pltpu.VMEM((SMALL_SHARDS, 80, LANES), BF16),
        pltpu.VMEM((GATE, MID), BF16),
        pltpu.VMEM((8, D), F32),
        pltpu.VMEM((8, D), F32),
    ]
    for shape in ((8, MID), (8, LANES), (8, LANES)):
        scratch += sum_scratch(n_seg, n_clip, shape)
    count = 3 * (n_seg * 4 + n_clip // 4) + 64
    scratch += [pltpu.SemaphoreType.DMA((count,)), pltpu.SemaphoreType.DMA((count,))]
    d_spec = vmem if last else any_spec
    return pl.pallas_call(
        functools.partial(backward_kernel, n_seg, n_clip, block),
        out_shape=outs,
        in_specs=[any_spec, any_spec, d_spec] + [any_spec] * 10 + [vmem] * 7,
        out_specs=[any_spec] * 6 + [vmem],
        scratch_shapes=scratch,
        compiler_params=pltpu.CompilerParams(
            collective_id=40 + block, has_side_effects=True, vmem_limit_bytes=62 * 1024 * 1024
        ),
        name="backward_block",
    )(h3, x, d_in, h2, h1, gate, *weights, table, *stats, *masks)


class Scatter:
    def __init__(self, links, grad, rows, buffers, alternate, finish):
        self.links = links
        self.alternate = alternate
        self.grad = grad
        self.rows = rows
        self.one, self.two, self.three, self.four = buffers
        self.finish = finish
        self.depth = links.outer
        self.base = links.take(self.depth + 3)
        self.at = -1

    def copies(self):
        links, base, depth = self.links, self.base, self.depth
        if self.at == 0:
            source = self.grad.at[1 - links.seg, :, :, self.rows]
            return [links.remote(base, source, self.one, links.other)]
        found = []
        if self.at == 1:
            for k in range(2):
                source = self.one.at[:, links.jump * (1 - links.first) + links.step * k]
                found.append(links.remote(base + 1 + k, source, self.two.at[:, k], links.across_first))
            return found
        if self.alternate:
            if self.at == 2:
                for i in range(1, depth):
                    source = self.two.at[lax.rem(links.group + i, depth)]
                    found.append(links.remote(base + 2 + i, source, self.three.at[i - 1], links.far_peer(i)))
            else:
                source = self.four.at[1 - links.second]
                found.append(links.remote(base + depth + 2, source, self.four.at[2], links.across_second))
            return found
        if self.at == 2:
            source = self.two.at[:, 1 - links.second]
            return [links.remote(base + 3, source, self.three, links.across_second)]
        for i in range(1, depth):
            source = self.three.at[lax.rem(links.group + i, depth)]
            found.append(links.remote(base + 3 + i, source, self.four.at[i - 1], links.far_peer(i)))
        return found

    def add(self):
        links, depth = self.links, self.depth
        one, two, three, four = self.one, self.two, self.three, self.four
        if self.at == 0:

            def add_one(i, carry):
                z = i // 4
                w = lax.rem(i, 4)
                total = one[z, w].astype(F32) + self.grad[links.seg, z, w, self.rows].astype(F32)
                one[z, w] = total.astype(BF16)
                return carry

            lax.fori_loop(0, 4 * depth, add_one, 0)
        elif self.at == 1:

            def add_two(i, carry):
                z = i // 2
                k = lax.rem(i, 2)
                kept = one[z, links.jump * links.first + links.step * k]
                two[z, k] = (two[z, k].astype(F32) + kept.astype(F32)).astype(BF16)
                return carry

            lax.fori_loop(0, 2 * depth, add_two, 0)
        elif self.at == 2 and self.alternate:
            for k in range(2):
                total = two[links.group, k].astype(F32)
                for i in range(1, depth):
                    total = total + three[i - 1, k].astype(F32)
                four[k] = total.astype(BF16)
        elif self.at == 2:

            def add_three(z, carry):
                three[z] = (three[z].astype(F32) + two[z, links.second].astype(F32)).astype(BF16)
                return carry

            lax.fori_loop(0, depth, add_three, 0)
        elif self.alternate:
            self.finish(four[links.second].astype(F32) + four[2].astype(F32))
        else:
            total = three[links.group].astype(F32)
            for i in range(1, depth):
                total = total + four[i - 1].astype(F32)
            self.finish(total)

    def advance(self):
        if self.at > 3:
            return
        if self.at >= 0:
            for copy in self.copies():
                copy.wait()
            self.add()
        self.at += 1
        if self.at <= 3:
            for copy in self.copies():
                copy.start()


SCATTERED = {
    "cls": (64, 2 * LANES),
    "out1": (16, D),
    "mida1": (48, MID),
    "midb1": (48, MID),
    "midc1": (48, MID),
    "in1": (64, MID),
    "out0": (16, D),
    "mida0": (48, MID),
    "midb0": (48, MID),
    "midc0": (48, MID),
    "in0": (64, MID),
    "small": (80, LANES),
}


FLAT_MID = 256
FLAT_OUT = 832
FLAT_SMALL = 1088
FLAT_ROWS = 1122
FLAT_CLS = 2243
ORDER = (
    "cls", "@mid1a", "cls", "@mid1b", "mida1", "midb1", "midc1", "@mid1c", "cls", "mida1", "@in1a", "in1", "midb1",
    "@in1b", "cls", "@out1a", "mida1", "midc1", "@out1b", "out1", "cls", "in1", "@small1", "midb1", "out1",
    "@out0a", "midc1", "@out0b", "out0", "mida1", "@in0a", "in0", "in1", "@in0b", "out0", "@mid0a", "midb1",
    "midc1", "mida1", "out1", "@mid0b", "mida0", "midb0", "midc0", "in0", "@mid0c", "midb1", "out0", "@small0",
    "small", "in1", "out1", "@dx0", "@dx1", "mida0", "midc1", "@dx2", "in0", "@dx3", "@dx4", "out0", "@dx5", "in1",
    "out1", "midb0", "@dx6", "mida0", "in0", "out0", "midc0", "midb0", "mida0", "small", "in0", "midc0", "mida0",
    "midb0", "small", "midc0", "small", "midb0", "midc0", "small",
)
ALTERNATE = ("mida1", "midb1", "in1")

ORDER_FIRST = "mid1a"


def gradient_kernel(n_seg, n_clip, *refs):
    refs = list(refs)

    def pop(count=1):
        taken = refs[:count]
        del refs[:count]
        return taken if count != 1 else taken[0]

    sources = [pop(10) for _ in range(2)]
    cls_hbm, norm_rows_in, bias = pop(3)
    d_pre, *in_parts = pop(3)
    flat, tail, dx_out = pop(3)
    big3, bigx, mid_a2, mid_d2, mid_d1, mid_low, mid_de, thin_dr, thin_s, fpad = pop(10)
    g_in, g_mid, g_out, g_small, g_cls, squares, turned, rows_x = pop(8)
    sums = pop(4)
    buffers = {name: pop(4) for name in SCATTERED}
    send_sem, recv_sem = pop(2)
    links = Links(n_seg, n_clip, send_sem, recv_sem)
    cells, frames = bigx.shape[0], bigx.shape[1]
    rows_all = cells * frames
    devices = SMALL_SHARDS

    def load(source, target):
        copy = links.local(source.reshape(target.shape), target)
        copy.start()
        return copy

    interior = fpad.at[pl.ds(1, GRID), pl.ds(1, GRID)]
    names = ("x", "d1", "f", "d2", "a2", "d3", "low", "dr", "s", "de")
    targets = dict(zip(names, (bigx, mid_d1, interior, mid_d2, mid_a2, big3, mid_low, thin_dr, thin_s, mid_de)))
    hbm = [dict(zip(names, source)) for source in sources]

    def fetch(block, *keys):
        return [load(hbm[block][key], targets[key]) for key in keys]

    operands = {
        "out": ("a2", "d3"),
        "in": ("x", "d1"),
        "mid": ("f", "d2"),
        "small": ("low", "dr", "s", "de"),
    }
    load_cls = load(cls_hbm, g_cls)
    fpad[...] = jnp.zeros_like(fpad)
    waits = {"mid": fetch(1, *operands["mid"])}
    links.meet()
    squares[...] = jnp.zeros_like(squares)

    def folded(ref, rows):
        return ref.reshape(n_seg, links.outer, 4, rows, ref.shape[-1])

    grads = {"cls": g_cls, "small": g_small}
    jobs = {}

    def put(block, first, values, stride=1):
        count = values.shape[0]
        if block == 0:
            flat[pl.ds(first, count, stride), :] = values
        else:
            turned[pl.ds(first + 8, count, stride), :] = pltpu.roll(values, 64, 1)

    def put_small(total):
        lane = lax.broadcasted_iota(jnp.int32, (1, LANES), 1)
        for block in range(2):
            rows = total[32 * block : 32 * block + 32]
            put(block, FLAT_SMALL, rows[:16])
            for k in range(4):
                put(block, FLAT_SMALL + 16 + k, rows[16 + 4 * k : 20 + 4 * k], 4)
            gain = total[64 + 2 * block : 65 + 2 * block]
            shift = pltpu.roll(total[65 + 2 * block : 66 + 2 * block], 96, 1)
            put(block, FLAT_SMALL + 32, jnp.where(lane < 96, gain, shift))
            put(block, FLAT_SMALL + 33, shift)
        flat[FLAT_CLS + 87 : FLAT_CLS + 88, :] = total[68:69]

    def put_classifier(total):
        lane = lax.broadcasted_iota(jnp.int32, (1, LANES), 1)
        flat[FLAT_CLS:, :] = jnp.zeros_like(flat[FLAT_CLS:, :])
        for i in range(total.shape[0]):
            line, by = divmod(CLASSES * i, LANES)
            line += FLAT_CLS
            low, high = total[i : i + 1, :LANES], total[i : i + 1, LANES:]
            if by:
                low, high = pltpu.roll(low, by, 1), pltpu.roll(high, by, 1)
            here = lane >= by
            flat[line : line + 1, :] += jnp.where(here, low, 0.0)
            flat[line + 1 : line + 2, :] += jnp.where(here, high, low)
            if by + CLASSES - LANES > LANES:
                flat[line + 2 : line + 3, :] += jnp.where(here, 0.0, high)

    def make(name):
        kind = name[:-1] if name not in ("cls", "small") else name
        block = name[-1]
        rows, columns = SCATTERED[name]
        start = rows * "abc".index(kind[3]) if kind.startswith("mid") else 0
        ref = {"in": g_in, "out": g_out, "small": g_small, "cls": g_cls}.get(kind, g_mid)
        shard_rows = 3 * rows if kind.startswith("mid") else rows

        def finish(total):
            squares[:, :columns] += fold(total * total)
            if kind == "cls":
                put_classifier(total)
            elif kind == "small":
                put_small(total)
            else:
                lines = columns // LANES
                first = {"in": 0, "out": FLAT_OUT}.get(kind, FLAT_MID) + start * lines
                for k in range(lines):
                    put(int(block), first + k, total[:, k * LANES : (k + 1) * LANES], lines)

        jobs[name] = Scatter(links, folded(ref, shard_rows), pl.ds(start, rows), buffers[name], name in ALTERNATE, finish)

    for name in SCATTERED:
        make(name)

    def push(*wanted):
        for name in wanted:
            jobs[name].advance()

    def dot_tn(left, right):
        return lax.dot_general(left, right, (((0,), (0,)), ((), ())), preferred_element_type=F32)

    turn = 1 - links.seg

    def task_out(first, last):
        def body(k, carry):
            span = pl.ds(pl.multiple_of(k * MID, MID), MID)
            part = dot_tn(mid_a2[...].reshape(rows_all, MID), big3[:, :, span].reshape(rows_all, MID))
            g_out[:, span] = part.astype(BF16)
            return carry

        lax.fori_loop(first, last, body, 0)

    def task_in(first, last):
        def body(i, carry):
            k = i + turn * (3 - 2 * i)
            span = pl.ds(pl.multiple_of(k * MID, MID), MID)
            part = dot_tn(bigx[:, :, span].reshape(rows_all, MID), mid_d1[...].reshape(rows_all, MID))
            g_in[span, :] = part.astype(BF16)
            return carry

        lax.fori_loop(first, last, body, 0)

    def task_mid(first, last):
        def body(i, carry):
            k = i + turn * (8 - 2 * i)
            window = fpad[pl.ds(k // 3, GRID), pl.ds(lax.rem(k, 3), GRID)].reshape(rows_all, MID)
            part = dot_tn(window, mid_d2[...].reshape(rows_all, MID))
            g_mid[pl.ds(pl.multiple_of(k * MID, MID), MID), :] = part.astype(BF16)
            return carry

        lax.fori_loop(first, last, body, 0)

    def task_small(block):
        part = dot_tn(mid_low[...].reshape(rows_all, MID), thin_dr[...].reshape(rows_all, GATE))
        g_small[:, 32 * block : 32 * block + 16, :] = part.astype(BF16).reshape(devices, 16, LANES)
        part = dot_tn(thin_s[...].reshape(rows_all, GATE), mid_de[...].reshape(rows_all, MID)).astype(BF16)
        rows = jnp.zeros((devices * 16, LANES), F32)
        for k in range(MID // LANES):
            rows = rows + dot_tn(excite_pick(devices, k), part[:, k * LANES : (k + 1) * LANES])
        g_small[:, 32 * block + 16 : 32 * block + 32, :] = rows.astype(BF16).reshape(devices, 16, LANES)

    dx_base = links.take(2 * GRID)
    w_in = big3.at[0 : 2 * 8].reshape(8, 2, SMALL_SHARDS, D)
    in_loads = []

    def load_w_in():
        for half, part in enumerate(in_parts):
            quarters = part.reshape(4, 8, SMALL_SHARDS, MID)
            for k in range(4):
                copy = links.local(quarters.at[k], w_in.at[:, half, :, k * MID : (k + 1) * MID])
                copy.start()
                in_loads.append(copy)
        dx_load(0).start()

    def dx_load(i):
        return pltpu.make_async_copy(
            d_pre.at[pl.ds(GRID * i, GRID)], rows_x.at[i % 2], links.recv_sem.at[dx_base + i]
        )

    def dx_store(i):
        slots = frames // dx_out.shape[0]
        return [
            pltpu.make_async_copy(
                rows_x.at[i % 2, :, slots * c : slots * (c + 1)],
                dx_out.at[c, pl.ds(GRID * i, GRID)],
                links.recv_sem.at[store_base + dx_out.shape[0] * i + c],
            )
            for c in range(dx_out.shape[0])
        ]

    store_base = links.take(dx_out.shape[0] * GRID)

    def task_dx(i):
        if i == 0:
            for copy in in_loads:
                copy.wait()
        dx_load(i).wait()
        rows = mid_d1[GRID * i : GRID * (i + 1)].reshape(GRID * frames, MID)
        for k in range(4):
            span = slice(k * MID, (k + 1) * MID)
            right = big3[0:16, :, span].reshape(MID, MID)
            part = lax.dot_general(rows, right, (((1,), (1,)), ((), ())), preferred_element_type=F32)
            rows_x[i % 2, :, :, span] += part.reshape(GRID, frames, MID)
        for copy in dx_store(i):
            copy.start()
        if i:
            for copy in dx_store(i - 1):
                copy.wait()
        if i < GRID - 1:
            dx_load(i + 1).start()

    def run(piece):
        if piece[:2] == "dx":
            task_dx(int(piece[2:]))
            return
        letter = piece[-1] if piece[-1] in "abc" else ""
        kind, block = piece[: len(piece) - 1 - len(letter)], int(piece[len(piece) - 1 - len(letter)])
        part = "abc".index(letter) if letter else 0
        if part == 0:
            for copy in waits[kind]:
                copy.wait()
            if block == 0 and kind != "small":
                for name in SCATTERED:
                    if name.startswith(kind) and name[-1] == "1":
                        while jobs[name].at < 1:
                            jobs[name].advance()
        if kind == "mid":
            task_mid((0, 3, 5)[part], (3, 5, 9)[part])
        elif kind == "in":
            task_in(2 * part, 2 * part + 2)
        elif kind == "out":
            task_out(2 * part, 2 * part + 2)
        else:
            task_small(block)
        if block == 1 and part == {"mid": 2, "in": 1, "out": 1, "small": 0}[kind]:
            waits[kind] = fetch(0, *operands[kind])
        if piece == "out0b":
            load_w_in()
        if block == 1 and piece == ORDER_FIRST:
            for other in ("in", "out", "small"):
                waits[other] = fetch(1, *operands[other])

    g_small[:, 64:80, :] = norm_rows_in[...]
    load_cls.wait()
    for item in ORDER:
        if item[0] == "@":
            with jax.named_scope("product"):
                run(item[1:])
        else:
            push(item)
    for name in SCATTERED:
        while jobs[name].at <= 3:
            jobs[name].advance()
    for copy in dx_store(GRID - 1):
        copy.wait()
    lane = lax.broadcasted_iota(jnp.int32, (FLAT_ROWS, LANES), 1)
    now, before = turned[8 : 8 + FLAT_ROWS, :], turned[7 : 7 + FLAT_ROWS, :]
    old = flat[FLAT_SMALL + 33 : FLAT_SMALL + 34, :]
    flat[FLAT_ROWS - 1 : 2 * FLAT_ROWS - 1, :] = jnp.where(lane < 64, before, now)
    flat[FLAT_ROWS - 1 : FLAT_ROWS, :] = jnp.where(lane[:1] < 64, old, now[:1])
    total = jnp.sum(jnp.sum(squares[...], axis=0, keepdims=True), axis=1, keepdims=True)
    sums[0][0:8, :] = bias[...]
    sums[0][8:16, :] = jnp.broadcast_to(total, (8, LANES))
    tail[...] = links.all_sum(*sums)


def gradient_sums(sources, g_cls, norm_rows_in, bias, d_pre, in_a, in_b, clips):
    n_seg = lax.axis_size("seg")
    n_clip = lax.axis_size("clip")
    depth = n_clip // 4
    cells, frames, width = sources[0][0].shape
    any_spec = pl.BlockSpec(memory_space=pl.ANY)
    vmem = pl.BlockSpec(memory_space=pltpu.VMEM)

    def grid_shape(columns):
        return pltpu.VMEM((cells, frames, columns), BF16)

    outs = [(FLAT_CLS + 93, LANES), (16, LANES)]
    scratch = [grid_shape(D), grid_shape(D)] + [grid_shape(MID)] * 5 + [grid_shape(GATE)] * 2
    scratch += [
        pltpu.VMEM((GRID + 2, GRID + 2, frames, MID), BF16),
        pltpu.VMEM((D, MID), BF16),
        pltpu.VMEM((9 * MID, MID), BF16),
        pltpu.VMEM((MID, D), BF16),
        pltpu.VMEM((SMALL_SHARDS, 80, LANES), BF16),
        pltpu.VMEM((D, 2 * LANES), BF16),
        pltpu.VMEM((8, D), F32),
        pltpu.VMEM((FLAT_ROWS + 14, LANES), F32),
        pltpu.VMEM((2, GRID, frames, D), F32),
    ]
    scratch += sum_scratch(n_seg, n_clip, (16, LANES))
    for name, shape in SCATTERED.items():
        ends = ((depth - 1, 2), (3,)) if name in ALTERNATE else ((depth,), (depth - 1,))
        for lead in ((depth, 4), (depth, 2)) + ends:
            scratch.append(pltpu.VMEM(lead + shape, BF16))
    count = n_seg * 4 + depth + len(SCATTERED) * (depth + 3) + 100
    scratch += [pltpu.SemaphoreType.DMA((count,)), pltpu.SemaphoreType.DMA((count,))]
    return pl.pallas_call(
        functools.partial(gradient_kernel, n_seg, n_clip),
        out_shape=[jax.ShapeDtypeStruct(s, F32) for s in outs + [(clips, cells, frames // clips, D)]],
        in_specs=[any_spec] * 21 + [vmem, vmem] + [any_spec] * 3,
        out_specs=[vmem] * len(outs) + [any_spec],
        scratch_shapes=scratch,
        compiler_params=pltpu.CompilerParams(
            collective_id=50, has_side_effects=True, vmem_limit_bytes=62 * 1024 * 1024
        ),
        name="gradient_sums",
    )(*sources[0], *sources[1], g_cls, norm_rows_in, bias, d_pre, in_a, in_b)


def input_gradient_kernel(d_pre, d_one, in_a, in_b, out, w_in):
    rows = w_in.shape[0] // SMALL_SHARDS // 2

    @pl.when(pl.program_id(0) == 0)
    def _():
        wide = w_in.reshape(SMALL_SHARDS, 2 * rows, MID)
        wide[:, :rows] = in_a[...].reshape(SMALL_SHARDS, rows, MID)
        wide[:, rows:] = in_b[...].reshape(SMALL_SHARDS, rows, MID)

    cells, frames = d_one.shape[:2]
    clips = out.shape[0]
    slots = frames // clips
    left = d_one[...].reshape(cells * frames, MID)
    for k in range(4):
        span = slice(k * MID, (k + 1) * MID)
        part = lax.dot_general(left, w_in[span, :], (((1,), (1,)), ((), ())), preferred_element_type=F32)
        part = part.reshape(cells, frames, MID) + d_pre[:, :, span]
        for c in range(clips):
            out[c, :, :, span] = part[:, slots * c : slots * (c + 1), :]


def input_gradient(d_pre, d_one, in_a, in_b, clips):
    cells, frames, width = d_pre.shape
    slots = frames // clips
    whole = pl.BlockSpec(in_a.shape, lambda i: (0, 0))
    return pl.pallas_call(
        input_gradient_kernel,
        grid=(GRID,),
        out_shape=jax.ShapeDtypeStruct((clips, cells, slots, width), F32),
        in_specs=[
            pl.BlockSpec((GRID, frames, width), lambda i: (i, 0, 0)),
            pl.BlockSpec((GRID, frames, MID), lambda i: (i, 0, 0)),
            whole,
            whole,
        ],
        out_specs=pl.BlockSpec((clips, GRID, slots, width), lambda i: (0, i, 0, 0)),
        scratch_shapes=[pltpu.VMEM((D, MID), BF16)],
        compiler_params=pltpu.CompilerParams(vmem_limit_bytes=48 * 1024 * 1024),
        name="input_gradient",
    )(d_pre, d_one, in_a, in_b)


def weight_gradients(x, d_one, gated, d_two, a_two, d_three, a_low, d_reduced, mixed, d_excite):
    return [
        matmul(x.reshape(-1, D).T, d_one.reshape(-1, MID)),
        conv(gated, d_two, ("HWCN", "HWIO", "HWNC")).reshape(9 * MID, MID),
        matmul(a_two.reshape(-1, MID).T, d_three.reshape(-1, D)),
        matmul(a_low.reshape(-1, MID).T, d_reduced.reshape(-1, GATE)),
        matmul(mixed.reshape(-1, GATE).T, d_excite.reshape(-1, MID)),
    ]


def on_device(inputs, clip_counts, labels, master, first_moment, second_moment):
    seg_count = lax.axis_size("seg")
    clip_local, slot_local = inputs.shape[:2]
    frames = clip_local * slot_local
    slot_ids = lax.axis_index("seg") * slot_local + jnp.arange(slot_local, dtype=jnp.int32)
    present = (slot_ids[None, :] < clip_counts[:, None]).astype(F32)
    following = (slot_ids[None, :] + 1 < clip_counts[:, None]).astype(F32)
    frame_mask = jnp.broadcast_to(present.reshape(frames, 1), (frames, MID))
    frame_following = jnp.broadcast_to(following.reshape(frames, 1), (frames, GATE))
    table = jnp.zeros(TABLE, F32)
    x_low = inputs.transpose(0, 2, 1, 3)
    shards = weight_shards(master)
    if shards is None:
        weights = whole_weights(master)
        jobs = ((), ())
    else:
        weights = {}
        jobs = JOBS
    rows = ((0, 8 - clip_local), (0, 0))
    share = jnp.pad(1.0 / (HW * clip_counts.astype(F32))[:, None], rows)
    share = jnp.broadcast_to(share, (8, LANES))
    onehot = (labels[:, None] == jnp.arange(2 * LANES, dtype=jnp.int32)[None, :]).astype(F32)
    target = jnp.pad(onehot, rows)
    kept = []
    flowing = x_low
    flows = []
    for block in range(2):
        flows.append(flowing)
        names = weight_names(block) + (["cls"] if block == 1 else [])
        given = {name: weights[name] for name in names if name not in jobs[block]}
        gathered, results = forward_block(
            block,
            flowing,
            frame_mask,
            frame_following,
            table,
            (share, target) if block == 1 else (),
            {name: shards[name] for name in jobs[block]},
            given,
        )
        weights.update(gathered)
        if block == 0:
            table = results[9]
        kept.append(results[:8] + results[10:13])
        if block == 0:
            flows[0] = results[13]
        flowing = results[8]
    d_flow = flowing
    g_cls, g_bias = results[13:]
    g_bias = g_bias[0, :CLASSES]
    masks = (frame_mask, frame_mask[:, :GATE], frame_following)
    sources = [None, None]
    norm_grads = [None, None]
    for block in (1, 0):
        h_one, a_low, gate, mixed, gated, h_two, a_two, h_three, st_one, st_two, st_three = kept[block]
        *steps, d_flow, norm_sums = backward_block(
            block,
            h_three,
            flows[block],
            d_flow,
            h_two,
            h_one,
            gate,
            [weights[name] for name in weight_names(block)],
            table,
            (st_one, st_two, st_three),
            masks,
        )
        sources[block] = (flows[block], steps[4], gated, steps[1], a_two, steps[0], a_low, steps[3], mixed, steps[2])
        norm_grads[block] = [norm_sums[:24].reshape(-1), norm_sums[24:].reshape(-1)]
    devices = seg_count * lax.axis_size("clip")
    bias_rows = jnp.pad(g_bias, (0, 8 * LANES - CLASSES)).reshape(8, LANES)
    if shards is None:
        grads = []
        for block in (0, 1):
            grads += weight_gradients(*sources[block]) + [v / devices for v in norm_grads[block]]
        d_input = input_gradient(d_flow, steps[4], weights["ina0"], weights["inb0"], clip_local)
        grad_mine = scatter_gradients(grads + [g_cls[:, :CLASSES].astype(F32), g_bias])
        square = jnp.full((8, LANES), jnp.sum(grad_mine * grad_mine), F32)
        tail = lax.psum(jnp.concatenate([bias_rows, square]), AXES)
    else:
        vectors = [v.reshape(SMALL_SHARDS, -1) / devices for b in (0, 1) for v in norm_grads[b]]
        padded = jnp.pad(g_bias, (0, 6 * SMALL_SHARDS - CLASSES)).reshape(SMALL_SHARDS, 6)
        extra = norm_rows(vectors + [padded]).astype(BF16)
        flat, tail, d_input = gradient_sums(
            sources, g_cls, extra, bias_rows, d_flow, weights["ina0"], weights["inb0"], clip_local
        )
        grad_mine = flat.reshape(-1)[: master.shape[0]]
    norm = jnp.sqrt(tail[8, 0])
    bias_grad = tail[:8].reshape(-1)[:CLASSES]
    factor = jnp.minimum(1.0, CLIP_LIMIT / (norm + 1e-06))
    clipped = grad_mine * factor
    new_first = BETA_ONE * first_moment + (1.0 - BETA_ONE) * clipped
    new_second = BETA_TWO * second_moment + (1.0 - BETA_TWO) * clipped * clipped
    first_hat = new_first / (1.0 - BETA_ONE**STEP)
    second_hat = new_second / (1.0 - BETA_TWO**STEP)
    new_master = master - LEARN_RATE * (
        first_hat / (jnp.sqrt(second_hat) + ADAM_EPS) + WEIGHT_DECAY * master
    )
    grid_grad = d_input.transpose(0, 2, 1, 3)
    return (
        new_master,
        new_first,
        new_second,
        new_master.astype(BF16),
        grid_grad,
        norm.reshape(1),
        bias_grad,
    )


def solution(mesh):
    return jax.shard_map(
        on_device,
        mesh=mesh,
        in_specs=(
            P("clip", "seg", None, None),
            P("clip"),
            P("clip"),
            P(AXES),
            P(AXES),
            P(AXES),
        ),
        out_specs=(
            P(AXES),
            P(AXES),
            P(AXES),
            P(AXES),
            P("clip", "seg", None, None),
            P(),
            P(),
        ),
        check_vma=False,
    )
```

```python
import functools
import math

import jax
import jax.numpy as jnp
from jax import lax
from jax.experimental import pallas as pl
from jax.experimental.pallas import tpu as pltpu
from jax.sharding import PartitionSpec as P

D = 2048
MID = 512
GATE = 128
CLASSES = 174
GRID = 7
HW = 49
STEP = 7
LANES = 128

NORM_EPS = 1e-05
CLIP_LIMIT = 0.001
LEARN_RATE = 0.04
WEIGHT_DECAY = 0.05
BETA_ONE = 0.9
BETA_TWO = 0.999
ADAM_EPS = 1e-08

AXES = ("seg", "clip")
MESH_ID = pl.DeviceIdType.MESH
BF16 = jnp.bfloat16
F32 = jnp.float32


def matmul(left, right):
    return jnp.dot(left, right, preferred_element_type=F32)


def layout():
    block_layout = [
        (D, MID),
        (9, MID, MID),
        (MID, D),
        (MID, GATE),
        (GATE, MID),
        (2 * MID + D,),
        (2 * MID + D,),
    ]
    return block_layout + block_layout + [(D, CLASSES), (CLASSES,)]


def widths(devices):
    return [(math.prod(extent) + devices - 1) // devices for extent in layout()]


def pad_rows(flat, rows):
    return jnp.pad(flat, (0, rows * LANES - flat.shape[0])).reshape(rows, LANES)


def small_rows(devices):
    wide = widths(devices)
    amount = sum(wide[3:7]) + sum(wide[10:14])
    amount_cls = wide[14] + wide[15]
    return [16 * ((a + 16 * LANES - 1) // (16 * LANES)) for a in (amount, amount_cls)]


def gather_parameters(master):
    devices = lax.axis_size("seg") * lax.axis_size("clip")
    wide = widths(devices)
    starts = [sum(wide[:i]) for i in range(len(wide))]
    low = master.astype(BF16)

    def part(i):
        return low[starts[i] : starts[i] + wide[i]]

    def gather(values):
        return lax.all_gather(values, AXES, axis=0, tiled=True)

    big = {}
    for base in (0, 7):
        for i, columns in ((0, MID), (1, MID), (2, D)):
            big[base + i] = gather(part(base + i).reshape(-1, columns))
    rows, rows_cls = small_rows(devices)
    small = gather(pad_rows(jnp.concatenate([part(i) for i in (3, 4, 5, 6, 10, 11, 12, 13)]), rows))
    small_cls = gather(pad_rows(jnp.concatenate([part(14), part(15)]), rows_cls))
    small = small.reshape(devices, rows * LANES)
    small_cls = small_cls.reshape(devices, rows_cls * LANES)
    shapes = layout()
    pieces = dict(big)

    def take(source, ids):
        offset = 0
        for i in ids:
            amount = math.prod(shapes[i])
            pieces[i] = source[:, offset : offset + wide[i]].reshape(-1)[:amount].reshape(shapes[i])
            offset += wide[i]

    take(small, (3, 4, 5, 6, 10, 11, 12, 13))
    take(small_cls, (14, 15))
    return [pieces[i] for i in range(16)]


def part_of(master, index):
    devices = lax.axis_size("seg") * lax.axis_size("clip")
    wide = widths(devices)
    start = sum(wide[:index])
    return master[start : start + wide[index]]


def norm_rows(vectors):
    rows = jnp.stack([jnp.pad(v, ((0, 0), (0, LANES - v.shape[1]))) for v in vectors], axis=1)
    return jnp.pad(rows, ((0, 0), (0, 16 - rows.shape[1]), (0, 0)))


def lanes_first(values):
    lead = values.shape[:-2]
    rows, columns = values.shape[-2:]
    split = values.reshape(lead + (rows, columns // LANES, LANES))
    return jnp.swapaxes(split, -3, -2).reshape(lead + (-1, LANES))


def split_rows(target, kind, block, pieces, rows):
    size = rows.shape[1] // pieces
    for k, name in enumerate(piece_names(kind, block, pieces)):
        target[name] = rows[:, k * size : (k + 1) * size].reshape(-1, MID)


def piece_names(kind, block, pieces):
    return [kind + "abc"[k] + str(block) for k in range(pieces)]


def weight_names(block):
    return piece_names("in", block, 2) + piece_names("mid", block, 3) + ["out%d" % block, "small"]


def weight_shards(master):
    devices = lax.axis_size("seg") * lax.axis_size("clip")
    if lax.axis_size("seg") != 2 or devices != SMALL_SHARDS:
        return None
    low = master.astype(BF16)
    shards = {}
    small = []
    for block in range(2):
        base = 7 * block
        split_rows(shards, "in", block, 2, part_of(low, base).reshape(1, -1, MID))
        split_rows(shards, "mid", block, 3, part_of(low, base + 1).reshape(1, -1, MID))
        shards["out%d" % block] = part_of(low, base + 2).reshape(-1, D)
        small.append(part_of(low, base + 3).reshape(-1, GATE))
        small.append(lanes_first(part_of(low, base + 4).reshape(-1, MID)))
    small.append(norm_rows([part_of(low, i)[None] for i in (5, 6, 12, 13, 15)])[0])
    shards["small"] = jnp.concatenate(small)
    cls = part_of(low, 14).reshape(-1, CLASSES)
    shards["cls"] = jnp.pad(cls, ((0, 0), (0, 2 * LANES - CLASSES)))
    return shards


def whole_weights(master):
    pieces = gather_parameters(master)
    whole = {}
    small = []
    for block in range(2):
        w_in, w_mid, w_out, w_red, w_exp = pieces[7 * block : 7 * block + 5]
        split_rows(whole, "in", block, 2, w_in.reshape(SMALL_SHARDS, -1, MID))
        split_rows(whole, "mid", block, 3, w_mid.reshape(SMALL_SHARDS, -1, MID))
        whole["out%d" % block] = w_out
        small.append(w_red.reshape(SMALL_SHARDS, -1, GATE))
        small.append(lanes_first(w_exp.reshape(SMALL_SHARDS, -1, MID)))
    vectors = [pieces[i].reshape(SMALL_SHARDS, -1) for i in (5, 6, 12, 13)]
    bias = jnp.pad(pieces[15], (0, 6 * SMALL_SHARDS - CLASSES)).reshape(SMALL_SHARDS, 6)
    small.append(norm_rows(vectors + [bias]))
    whole["small"] = jnp.concatenate(small, axis=1).reshape(-1, LANES)
    whole["cls"] = jnp.pad(pieces[14], ((0, 0), (0, 2 * LANES - CLASSES)))
    return whole


def scatter_gradients(grads):
    devices = lax.axis_size("seg") * lax.axis_size("clip")
    wide = widths(devices)
    columns = []
    for values, width in zip(grads, wide):
        flat = values.reshape(-1)
        columns.append(jnp.pad(flat, (0, devices * width - flat.shape[0])).reshape(devices, width))
    packed = jnp.concatenate(columns, axis=1)
    return lax.psum_scatter(packed, AXES, scatter_dimension=0, tiled=True)[0]


def conv(values, kernel, numbers):
    return lax.conv_general_dilated(
        values, kernel, (1, 1), ((1, 1), (1, 1)), dimension_numbers=numbers, preferred_element_type=F32
    )


class Links:
    def __init__(self, n_seg, n_clip, send_sem, recv_sem):
        self.n_seg = n_seg
        self.n_clip = n_clip
        self.inner = 4
        self.outer = n_clip // 4
        self.seg = lax.axis_index("seg")
        self.clip = lax.axis_index("clip")
        self.group = self.clip // 4
        self.place = lax.rem(self.clip, 4)
        y = self.place // 2
        x = lax.rem(self.place, 2)
        self.first = (1 - self.seg) * y + self.seg * x
        self.second = (1 - self.seg) * x + self.seg * y
        self.step = 1 + self.seg
        self.jump = 2 - self.seg
        self.across_first = (self.seg, self.clip + self.jump * (1 - 2 * self.first))
        self.across_second = (self.seg, self.clip + self.step * (1 - 2 * self.second))
        self.other = (1 - self.seg, self.clip)
        self.send_sem = send_sem
        self.recv_sem = recv_sem
        self.used = 0

    def take(self, count):
        base = self.used
        self.used += count
        return base

    def near_peer(self, i):
        return (
            lax.rem(self.seg + i // 4, self.n_seg),
            self.group * 4 + lax.rem(self.place + lax.rem(i, 4), 4),
        )

    def far_peer(self, i):
        return (self.seg, lax.rem(self.group + i, self.outer) * 4 + self.place)

    def remote(self, index, source, target, peer):
        return pltpu.make_async_remote_copy(
            src_ref=source,
            dst_ref=target,
            send_sem=self.send_sem.at[index],
            recv_sem=self.recv_sem.at[index],
            device_id=peer,
            device_id_type=MESH_ID,
        )

    def local(self, source, target):
        return pltpu.make_async_copy(source, target, self.recv_sem.at[self.take(1)])

    def meet(self):
        self.greet()
        self.wait_for_all()

    def wait_for_all(self):
        pl.semaphore_wait(pltpu.get_barrier_semaphore(), self.n_seg * 4 + self.outer - 2)

    def greet(self):
        barrier = pltpu.get_barrier_semaphore()
        n_near = self.n_seg * 4 - 1
        n_far = self.outer - 1

        def greet(peer):
            pl.semaphore_signal(barrier, inc=1, device_id=peer, device_id_type=MESH_ID)

        repeat(1, n_near + 1, lambda i: greet(self.near_peer(i)))
        repeat(1, n_far + 1, lambda i: greet(self.far_peer(i)))

    def sum_near(self, source, middle, near, far):
        n_near = self.n_seg * 4 - 1
        n_far = self.outer - 1
        base = self.take(n_near + n_far)

        def close(i):
            return self.remote(base + i - 1, source, near.at[i - 1], self.near_peer(i))

        def distant(i):
            return self.remote(base + n_near + i - 1, middle, far.at[i - 1], self.far_peer(i))

        repeat(1, n_near + 1, lambda i: close(i).start())
        repeat(1, n_near + 1, lambda i: close(i).wait())
        middle[...] = source[...] + jnp.sum(near[...], axis=0)
        repeat(1, n_far + 1, lambda i: distant(i).start())

        def rest():
            repeat(1, n_far + 1, lambda i: distant(i).wait())
            return middle[...] + jnp.sum(far[...], axis=0)

        return rest

    def all_sum(self, source, middle, near, far):
        return self.sum_near(source, middle, near, far)()


def repeat(first, last, action):
    if last - first <= 8:
        for i in range(first, last):
            action(i)
    else:

        def body(i, carry):
            action(i)
            return carry

        lax.fori_loop(first, last, body, 0)


def sum_scratch(n_seg, n_clip, shape):
    return [
        pltpu.VMEM(shape, F32),
        pltpu.VMEM(shape, F32),
        pltpu.VMEM((n_seg * 4 - 1,) + shape, F32),
        pltpu.VMEM((n_clip // 4 - 1,) + shape, F32),
    ]


class Gather:
    def __init__(self, links, shard, whole):
        depth = links.outer
        whole = whole.reshape((links.n_seg, depth, 4) + shard.shape)
        base = links.take(depth + 3)
        seg, z, place = links.seg, links.group, links.place
        self.own = links.local(shard, whole.at[seg, z, place])
        self.steps = [
            [
                links.remote(base + i - 1, shard, whole.at[seg, z, place], links.far_peer(i))
                for i in range(1, depth)
            ],
            [
                links.remote(
                    base + depth - 1, whole.at[seg, :, place], whole.at[seg, :, place], links.across_second
                )
            ],
            [],
            [links.remote(base + depth + 2, whole.at[seg], whole.at[seg], links.other)],
        ]
        for k in range(2):
            index = links.jump * links.first + links.step * k
            self.steps[2].append(
                links.remote(
                    base + depth + k, whole.at[seg, :, index], whole.at[seg, :, index], links.across_first
                )
            )
        self.at = -1

    def advance(self, last=3):
        if self.at >= 0:
            for copy in self.steps[self.at]:
                copy.wait()
            if self.at == 0:
                self.own.wait()
        self.at += 1
        if self.at == 0:
            self.own.start()
        if self.at <= 3:
            for copy in self.steps[self.at]:
                copy.start()

    def finish(self):
        while self.at <= 3:
            self.advance()


def row_vector(table, row, start, count):
    return jnp.concatenate([table[start + k, row : row + 1, :] for k in range(count)], axis=1)


def build_table(small, table):
    lane = lax.broadcasted_iota(jnp.int32, (8, LANES), 1)
    for q in range(SMALL_SHARDS // 4):
        rows = [small[4 * q + j, 64:80, :].astype(F32)[:8] for j in range(4)]
        one = pltpu.roll(rows[1], 96, 1)
        two = pltpu.roll(rows[2], 64, 1)
        three = pltpu.roll(rows[3], 32, 1)
        table[3 * q] = jnp.where(lane < 96, rows[0], one)
        table[3 * q + 1] = jnp.where(lane < 64, one, two)
        table[3 * q + 2] = jnp.where(lane < 32, two, three)


def put_rows(target, start, vector, count):
    width = vector.shape[1] // count
    for k in range(count):
        target[start + k : start + k + 1, :] = vector[:, k * width : (k + 1) * width]


def fold(values):
    return jnp.sum(values.reshape(-1, 8, values.shape[-1]), axis=0)


def excite_pick(shards, k):
    deep = GATE // shards
    line = lax.broadcasted_iota(jnp.int32, (GATE, shards * 16), 0)
    column = lax.broadcasted_iota(jnp.int32, (GATE, shards * 16), 1)
    wanted = (line // deep) * 16 + k * deep + lax.rem(line, deep)
    return (column == wanted).astype(F32).astype(BF16)


def excite_weights(small, block):
    shards = small.shape[0]
    rows = small[:, 32 * block + 16 : 32 * block + 32].reshape(shards * 16, LANES)
    parts = [matmul(excite_pick(shards, k), rows) for k in range(MID // LANES)]
    return jnp.concatenate(parts, axis=1).astype(BF16)


SMALL_SHARDS = 32
SLOTS_HERE = 8
TABLE = ((2 * MID + D) // LANES + 1, 8, LANES)


STAGES = (
    (
        "ina0", "small", "@dpad", "@fpad", "@turn0", "inb0", "@turn1", "@turn2", "@turn3", "@turn4", "mida0",
        "@turn5", "@turn6", "ina0", "small", "ina0", "midb0", "inb0", "small", "mida0", "midc0", "ina0", "inb0",
        "small", "out0", "ina0", "midb0", "mida0", "small", "midc0", "ina1", "inb0", "midb0", "inb1", "inb0",
        "@first", "mida1", "mida0", "midc0", "out0", "ina1", "@near1", "midb1", "mida0", "midb0", "inb1", "@far1",
        "midc1", "midb0", "midc0", "out0", "ina1", "mida1", "@second", "inb1", "@swap", "@excite", "midc0",
        "midb1", "@third", "out0", "ina1", "mida1", "midc1", "@near2", "out0", "ina1", "inb1", "midb1", "@far2",
        "mida1", "midc1", "@fourth", "inb1", "mida1", "midb1", "@near3", "midc1", "@far3", "midb1", "@fifth",
        "midc1",
    ),
    (
        "out1", "@dpad", "@fpad", "@first", "cls", "@near1", "out1", "@far1", "cls", "@second", "@swap", "out1",
        "@excite", "cls", "@third", "out1", "@near2", "cls", "@far2", "out1", "@fourth", "cls", "@near3", "@far3",
        "@fifth",
    ),
)
JOBS = tuple(tuple(dict.fromkeys(item for item in order if item[0] != "@")) for order in STAGES)


def forward_kernel(n_seg, n_clip, block, jobs, plan, *refs):
    refs = list(refs)

    def pop(count=1):
        taken = refs[:count]
        del refs[:count]
        return taken if count != 1 else taken[0]

    last = block == 1
    x_hbm, mask, following, table_in = pop(4)
    share, chosen = pop(2) if last else (None, None)
    shards = dict(zip(jobs, [pop() for _ in jobs]))
    given = dict(zip(plan, [pop() for _ in plan]))
    wholes = dict(zip(jobs, [pop() for _ in jobs]))
    h1_out, low_out, gate_out, mix_out, f_out, h2_out, a2_out, h3_out = pop(8)
    out_hbm, table_out, st1, st2, st3 = pop(5)
    g_cls, g_bias = pop(2) if last else (None, None)
    x_out = None if last else pop()
    xv, w_in, w_mid, w_out, small = pop(5)
    h1v, a1v, lowv, rv, edge, dpad, mixv, gatev, fpad, h2v, a2v, h3v = pop(12)
    wide_sum, wide_square, w_exp = pop(3)
    sums = [pop(4) for _ in range(3)]
    pooled, clip_sums, clip_other, w_cls = pop(4) if last else [None] * 4
    frames_first = None if last else pop()
    send_sem, recv_sem = pop(2)
    links = Links(n_seg, n_clip, send_sem, recv_sem)
    frames = xv.shape[1]
    table = table_in if last else table_out
    outgoing = []

    def send_out(source, target):
        copy = links.local(source, target)
        copy.start()
        outgoing.append(copy)

    x_base = links.take(GRID)

    def load_x(i):
        rows = pl.ds(GRID * i, GRID)
        return pltpu.make_async_copy(x_hbm.at[rows], xv.at[rows], links.recv_sem.at[x_base + i])

    if last:
        for i in range(GRID):
            load_x(i).start()
    else:
        load_frames = links.local(x_hbm, frames_first)
        load_frames.start()
    gathers = {name: Gather(links, shards[name], wholes[name]) for name in jobs}

    targets = {"out%d" % block: w_out, "small": small}
    if last:
        targets["cls"] = w_cls
    for kind, target, count in (("in", w_in, 2), ("mid", w_mid, 3)):
        rows = target.shape[0] // SMALL_SHARDS
        size = rows // count
        wide = target.reshape(SMALL_SHARDS, rows, MID)
        for k, name in enumerate(piece_names(kind, block, count)):
            targets[name] = wide.at[:, k * size : (k + 1) * size]
    loads = {}

    def load(name):
        source = wholes[name] if name in gathers else given[name]
        loads[name] = links.local(source.reshape(targets[name].shape), targets[name])
        loads[name].start()

    def push(name):
        if gathers[name].at <= 3:
            gathers[name].advance()
            if gathers[name].at > 3 and name in targets:
                load(name)

    def need(*names):
        for name in names:
            while name not in loads:
                push(name)
        for name in names:
            loads[name].wait()

    early = piece_names("in", block, 2)
    for name in early:
        if name not in gathers:
            load(name)
    table = table_in if last else table_out
    half = MID // LANES

    def norm(index, tot, columns, start, out):
        live_rows = table[TABLE[0] - 1, 0:1, 0:1]
        mean = jnp.concatenate([tot[k : k + 1] for k in range(4)], axis=1) / live_rows
        square = jnp.concatenate([tot[4 + k : 5 + k] for k in range(4)], axis=1) / live_rows
        inv = lax.rsqrt(square - mean * mean + NORM_EPS)
        out[0:1, :] = mean
        out[1:2, :] = inv
        gain = row_vector(table, 2 * block, start, columns // LANES)
        shift = row_vector(table, 2 * block + 1, start, columns // LANES)
        scale = gain * inv
        return scale, shift - mean * scale

    def masked_sums(values):
        shaped = values.reshape(-1, frames, values.shape[-1])
        masked = shaped * mask[...][None]
        return fold(masked), fold(masked * shaped)

    zeros = jnp.zeros((8, MID), F32)
    kept = {}

    def first(i, carry):
        if last:
            load_x(i).wait()
        part = matmul(xv[pl.ds(GRID * i, GRID)].reshape(GRID * frames, D), w_in[...])
        h1v[pl.ds(GRID * i, GRID)] = part.reshape(GRID, frames, MID)
        one, two = masked_sums(part)
        return (carry[0] + one, carry[1] + two)

    def put_sums(index, one, two):
        stat = sums[index][0]
        put_rows(stat, 0, jnp.sum(one, axis=0, keepdims=True), 4)
        put_rows(stat, 4, jnp.sum(two, axis=0, keepdims=True), 4)
        return stat

    def stage_dpad():
        dpad[...] = jnp.zeros_like(dpad)

    def stage_fpad():
        fpad[...] = jnp.zeros_like(fpad)
        if last:
            table_out[...] = table_in[...]
        else:
            table_out[...] = jnp.zeros_like(table_out)

    def turn(step):
        if step == 0:
            load_frames.wait()

        def body(p, carry):
            for k in range(4):
                span = slice(k * MID, (k + 1) * MID)
                parts = [frames_first[c, p, :, span].astype(F32) for c in range(frames_first.shape[0])]
                xv[p, :, span] = jnp.concatenate(parts, axis=0).astype(BF16)
            return carry

        lax.fori_loop(GRID * step, GRID * step + GRID, body, 0)
        if step == GRID - 1:
            kept["x"] = links.local(xv, x_out)
            kept["x"].start()

    def stage_first():
        need(*piece_names("in", block, 2))
        for name in targets:
            if name not in gathers and name not in early:
                load(name)
        stat = put_sums(0, *lax.fori_loop(0, GRID, first, (zeros, zeros)))
        present = HW * jnp.sum(mask[:, :LANES], axis=0, keepdims=True)
        stat[8:16, :] = jnp.broadcast_to(present, (8, LANES))
        send_out(h1v, h1_out)

    def stage_near1():
        kept["rest"] = links.sum_near(*sums[0])

    def stage_far1():
        need("small")
        total = kept["rest"]()
        if not last:
            build_table(small, table_out)
            table_out[TABLE[0] - 1] = total[8:16]
        kept["one"] = norm(0, total, MID, 0, st1)

    def second(i, carry):
        for j in range(GRID):
            y = h1v[GRID * i + j] * kept["one"][0] + kept["one"][1]
            a = y * jax.nn.sigmoid(y)
            a1v[GRID * i + j] = a
            lowv[GRID * i + j] = a.astype(BF16)
        part = matmul(lowv[pl.ds(GRID * i, GRID)].reshape(GRID * frames, MID), kept["red"])
        rv[pl.ds(GRID * i, GRID)] = part.astype(BF16).reshape(GRID, frames, GATE)
        return carry

    def stage_second():
        w_exp[...] = excite_weights(small, block)
        kept["red"] = small[:, 32 * block : 32 * block + 16].reshape(MID, GATE)
        lax.fori_loop(0, GRID, second, 0)
        send_out(lowv, low_out)
        kept["swap"] = links.remote(links.take(1), rv, edge, links.other)
        kept["swap"].start()

    row = lax.rem(lax.broadcasted_iota(jnp.int32, (frames, GATE), 0), 8)

    def change(i, carry):
        for j in range(GRID):
            now = rv[GRID * i + j].astype(F32)
            rest = edge[GRID * i + j].astype(F32)
            later = jnp.where(row < 7, pltpu.roll(now, frames - 1, 0), pltpu.roll(rest, 7, 0))
            dpad[i + 1, j + 1] = following[...] * (later - now)
        return carry

    def stage_swap():
        kept["swap"].wait()
        lax.fori_loop(0, GRID, change, 0)

    def excite(i, carry):
        for j in range(GRID):
            total = jnp.zeros((frames, GATE), F32)
            for k in range(9):
                total = total + dpad[i + k // 3, j + k % 3]
            mixv[GRID * i + j] = (dpad[i + 1, j + 1] + total / 9.0).astype(BF16)
        e = matmul(mixv[pl.ds(GRID * i, GRID)].reshape(GRID * frames, GATE), w_exp[...])
        e = e.reshape(GRID, frames, MID)
        for j in range(GRID):
            gate = jax.nn.sigmoid(e[j])
            gatev[GRID * i + j] = gate.astype(BF16)
            fpad[i + 1, j + 1] = (a1v[GRID * i + j] * (1.0 + gate)).astype(BF16)
        return carry

    def stage_excite():
        lax.fori_loop(0, GRID, excite, 0)
        send_out(mixv, mix_out)
        send_out(gatev, gate_out)
        send_out(fpad.at[pl.ds(1, GRID), pl.ds(1, GRID)], f_out)

    def third(i, carry):
        part = None
        for k in range(9):
            window = fpad[i + k // 3, pl.ds(k % 3, GRID)].reshape(GRID * frames, MID)
            term = matmul(window, w_mid[k * MID : (k + 1) * MID])
            part = term if part is None else part + term
        h2v[pl.ds(GRID * i, GRID)] = part.reshape(GRID, frames, MID)
        one, two = masked_sums(part)
        return (carry[0] + one, carry[1] + two)

    def stage_third():
        need(*piece_names("mid", block, 3))
        put_sums(1, *lax.fori_loop(0, GRID, third, (zeros, zeros)))
        send_out(h2v, h2_out)

    def stage_near2():
        kept["rest"] = links.sum_near(*sums[1])

    def stage_far2():
        kept["two"] = norm(1, kept["rest"](), MID, half, st2)
        wide_sum[...] = jnp.zeros_like(wide_sum)
        wide_square[...] = jnp.zeros_like(wide_square)

    def fourth(i, carry):
        for j in range(GRID):
            y = h2v[GRID * i + j] * kept["two"][0] + kept["two"][1]
            a2v[GRID * i + j] = (y * jax.nn.sigmoid(y)).astype(BF16)
        rows = a2v[pl.ds(GRID * i, GRID)].reshape(GRID * frames, MID)
        for k in range(4):
            part = matmul(rows, w_out[:, k * MID : (k + 1) * MID])
            h3v[pl.ds(GRID * i, GRID), :, k * MID : (k + 1) * MID] = part.astype(BF16).reshape(
                GRID, frames, MID
            )
            one, two = masked_sums(part)
            wide_sum[:, k * MID : (k + 1) * MID] += one
            wide_square[:, k * MID : (k + 1) * MID] += two
        return carry

    def stage_fourth():
        need("out%d" % block)
        lax.fori_loop(0, GRID, fourth, 0)
        put_sums(2, wide_sum[...], wide_square[...])
        send_out(a2v, a2_out)
        send_out(h3v, h3_out)

    def stage_near3():
        kept["rest"] = links.sum_near(*sums[2])

    def stage_far3():
        kept["three"] = norm(2, kept["rest"](), D, 2 * half, st3)
        if last:
            pooled[...] = jnp.zeros_like(pooled)

    def fifth(p, carry):
        for k in range(4):
            span = slice(k * MID, (k + 1) * MID)
            scale, shift = kept["three"]
            pre = h3v[p, :, span].astype(F32) * scale[:, span] + shift[:, span]
            pre = pre + xv[p, :, span].astype(F32)
            value = pre * jax.nn.sigmoid(pre)
            if last:
                pooled[:, span] += value * mask[...]
            else:
                xv[p, :, span] = value.astype(BF16)
        return carry

    def stage_fifth():
        if not last:
            kept["x"].wait()
        lax.fori_loop(0, HW, fifth, 0)
        if last:
            classify()
        send_out(pooled if last else xv, out_hbm)

    def classify():
        clips = frames // SLOTS_HERE
        clip_sums[...] = jnp.zeros_like(clip_sums)
        for c in range(clips):
            rows = pooled[SLOTS_HERE * c : SLOTS_HERE * (c + 1), :]
            clip_sums[c : c + 1, :] = jnp.sum(rows, axis=0, keepdims=True)
        swap = links.remote(links.take(1), clip_sums, clip_other, links.other)
        swap.start()
        lane = lax.broadcasted_iota(jnp.int32, (1, 2 * LANES), 1)
        bias = jnp.zeros((1, 2 * LANES), F32)
        for d in range(SMALL_SHARDS):
            piece = small[d, 64:80, :].astype(F32)[4:5]
            piece = jnp.concatenate([piece, jnp.zeros_like(piece)], axis=1)
            own = jnp.logical_and(lane >= 6 * d, lane < 6 * d + 6)
            bias = bias + jnp.where(own, pltpu.roll(piece, 6 * d, 1) if d else piece, 0.0)
        need("cls")
        swap.wait()
        mean = (clip_sums[...] + clip_other[...]) * share[:, 0:1]
        low = jnp.concatenate([mean, jnp.zeros_like(mean)], axis=0).astype(BF16)
        scores = matmul(low, w_cls[...])[:8] + bias
        scores = jnp.where(lane < CLASSES, scores, -1e30)
        scores = jnp.exp(scores - jnp.max(scores, axis=1, keepdims=True))
        chance = scores / jnp.sum(scores, axis=1, keepdims=True)
        clips_total = clips * links.n_clip
        d_scores = jnp.where(share[:, 0:1] > 0.0, (chance - chosen[...]) / clips_total, 0.0)
        g_bias[...] = jnp.broadcast_to(jnp.sum(d_scores, axis=0, keepdims=True) / n_seg, g_bias.shape)
        d_low = jnp.concatenate([d_scores, jnp.zeros_like(d_scores)], axis=0).astype(BF16)
        grad = lax.dot_general(low, d_low, (((0,), (0,)), ((), ())), preferred_element_type=F32)
        g_cls[...] = (grad / n_seg).astype(BF16)
        d_mean = lax.dot_general(d_low, w_cls[...], (((1,), (1,)), ((), ())), preferred_element_type=F32)
        d_mean = d_mean[:8] * share[:, 0:1]
        for c in range(clips):
            rows = slice(SLOTS_HERE * c, SLOTS_HERE * (c + 1))
            here = mask[rows, 0:1]
            pooled[rows, :] = jnp.broadcast_to(d_mean[c : c + 1], (SLOTS_HERE, D)) * here

    stages = {
        "dpad": stage_dpad,
        "fpad": stage_fpad,
        "first": stage_first,
        "near1": stage_near1,
        "far1": stage_far1,
        "second": stage_second,
        "swap": stage_swap,
        "excite": stage_excite,
        "third": stage_third,
        "near2": stage_near2,
        "far2": stage_far2,
        "fourth": stage_fourth,
        "near3": stage_near3,
        "far3": stage_far3,
        "fifth": stage_fifth,
    }
    for k in range(GRID):
        stages["turn%d" % k] = functools.partial(turn, k)
    links.meet()
    for item in STAGES[block]:
        if item[0] == "@":
            with jax.named_scope(item[1:]):
                stages[item[1:]]()
        elif item in gathers:
            push(item)
    for name in jobs:
        gathers[name].finish()
    for copy in outgoing:
        copy.wait()


def forward_block(block, x, mask, following, table, extra, shards, given):
    n_seg = lax.axis_size("seg")
    n_clip = lax.axis_size("clip")
    last = block == 1
    cells = x.shape[0] if last else x.shape[1]
    frames = x.shape[1] if last else x.shape[0] * x.shape[2]
    jobs = list(shards)
    plan = list(given)
    any_spec = pl.BlockSpec(memory_space=pl.ANY)
    vmem = pl.BlockSpec(memory_space=pltpu.VMEM)
    depth = n_clip // 4

    def grid_shape(columns):
        return (cells, frames, columns)

    devices = n_seg * n_clip
    outs = [jax.ShapeDtypeStruct((devices * shards[n].shape[0], shards[n].shape[1]), BF16) for n in jobs]
    outs += [
        jax.ShapeDtypeStruct(grid_shape(MID), F32),
        jax.ShapeDtypeStruct(grid_shape(MID), BF16),
        jax.ShapeDtypeStruct(grid_shape(MID), BF16),
        jax.ShapeDtypeStruct(grid_shape(GATE), BF16),
        jax.ShapeDtypeStruct((GRID, GRID, frames, MID), BF16),
        jax.ShapeDtypeStruct(grid_shape(MID), F32),
        jax.ShapeDtypeStruct(grid_shape(MID), BF16),
        jax.ShapeDtypeStruct(grid_shape(D), BF16),
        jax.ShapeDtypeStruct((frames, D), F32) if last else jax.ShapeDtypeStruct(grid_shape(D), BF16),
        jax.ShapeDtypeStruct(TABLE, F32),
        jax.ShapeDtypeStruct((8, MID), F32),
        jax.ShapeDtypeStruct((8, MID), F32),
        jax.ShapeDtypeStruct((8, D), F32),
    ]
    out_specs = [any_spec] * (len(jobs) + 9) + [vmem] * 4
    if last:
        outs += [jax.ShapeDtypeStruct((D, 2 * LANES), BF16), jax.ShapeDtypeStruct((8, 2 * LANES), F32)]
        out_specs += [vmem] * 2
    else:
        outs.append(jax.ShapeDtypeStruct(grid_shape(D), BF16))
        out_specs.append(any_spec)

    shapes = [(D, MID), (9 * MID, MID), (MID, D), (SMALL_SHARDS, 80, LANES)]
    scratch = [pltpu.VMEM(grid_shape(D), BF16)]
    scratch += [pltpu.VMEM(s, BF16) for s in shapes]
    scratch += [
        pltpu.VMEM(grid_shape(MID), F32),
        pltpu.VMEM(grid_shape(MID), F32),
        pltpu.VMEM(grid_shape(MID), BF16),
        pltpu.VMEM(grid_shape(GATE), BF16),
        pltpu.VMEM(grid_shape(GATE), BF16),
        pltpu.VMEM((GRID + 2, GRID + 2, frames, GATE), F32),
        pltpu.VMEM(grid_shape(GATE), BF16),
        pltpu.VMEM(grid_shape(MID), BF16),
        pltpu.VMEM((GRID + 2, GRID + 2, frames, MID), BF16),
        pltpu.VMEM(grid_shape(MID), F32),
        pltpu.VMEM(grid_shape(MID), BF16),
        pltpu.VMEM(grid_shape(D), BF16),
        pltpu.VMEM((8, D), F32),
        pltpu.VMEM((8, D), F32),
        pltpu.VMEM((GATE, MID), BF16),
    ]
    for shape in ((16, LANES), (8, LANES), (8, MID)):
        scratch += sum_scratch(n_seg, n_clip, shape)
    if last:
        scratch += [pltpu.VMEM((frames, D), F32), pltpu.VMEM((8, D), F32), pltpu.VMEM((8, D), F32)]
        scratch.append(pltpu.VMEM((D, 2 * LANES), BF16))
    else:
        scratch.append(pltpu.VMEM(x.shape, BF16))
    count = 4 * (n_seg * 4 + depth) + len(jobs) * (depth + 4) + 48
    scratch += [pltpu.SemaphoreType.DMA((count,)), pltpu.SemaphoreType.DMA((count,))]
    results = pl.pallas_call(
        functools.partial(forward_kernel, n_seg, n_clip, block, jobs, plan),
        out_shape=outs,
        in_specs=[any_spec, vmem, vmem, vmem] + [vmem] * len(extra) + [any_spec] * (len(jobs) + len(plan)),
        out_specs=out_specs,
        scratch_shapes=scratch,
        compiler_params=pltpu.CompilerParams(
            collective_id=30 + block, has_side_effects=True, vmem_limit_bytes=60 * 1024 * 1024
        ),
        name="forward_block",
    )(x, mask, following, table, *extra, *[shards[n] for n in jobs], *[given[n] for n in plan])
    wholes = dict(zip(jobs, results[: len(jobs)]))
    return wholes, results[len(jobs) :]


def backward_kernel(n_seg, n_clip, block, *refs):
    refs = list(refs)

    def pop(count=1):
        taken = refs[:count]
        del refs[:count]
        return taken if count != 1 else taken[0]

    last = block == 1
    h3_hbm, x_hbm, d_in, h2_hbm, h1_hbm, gate_hbm = pop(6)
    in_a, in_b, mid_a, mid_b, mid_c, out_hbm, small_hbm = pop(7)
    table, st1, st2, st3, mask, present, following = pop(7)
    dh3_out, dh2_out, de_out, dr_out, dh1_out, dx_out, norm_grads = pop(7)
    dv, h3v, xv, h2v, h1v, gatev, dyv, pad2, dsv, edge, pad_s, pad_e = pop(12)
    drv, dh1v, w_in, w_mid, w_out, small, w_exp = pop(7)
    sum_gain, sum_shift = pop(2)
    sums = [pop(4) for _ in range(3)]
    send_sem, recv_sem = pop(2)
    links = Links(n_seg, n_clip, send_sem, recv_sem)
    frames = xv.shape[1]
    outgoing = []

    def send_out(source, target):
        copy = links.local(source, target)
        copy.start()
        outgoing.append(copy)

    def load(source, target):
        copy = links.local(source.reshape(target.shape), target)
        copy.start()
        return copy

    streams = [(h3_hbm, h3v), (x_hbm, xv)]
    if not last:
        streams.append((d_in, dv))
    wide_base = links.take(len(streams) * GRID)

    def wide_copies(i):
        rows = pl.ds(GRID * i, GRID)
        return [
            pltpu.make_async_copy(source.at[rows], target.at[rows], links.recv_sem.at[wide_base + GRID * k + i])
            for k, (source, target) in enumerate(streams)
        ]

    for i in range(GRID):
        for copy in wide_copies(i):
            copy.start()
    loads_two = [load(out_hbm, w_out), load(h2_hbm, h2v)]
    loads_three = [load(h1_hbm, h1v), load(gate_hbm, gatev), load(small_hbm, small)]
    loads_four = []
    for parts, target, waits in (
        ((mid_a, mid_b, mid_c), w_mid, loads_three),
        ((in_a, in_b), w_in, loads_four),
    ):
        rows = target.shape[0] // SMALL_SHARDS
        size = rows // len(parts)
        wide = target.reshape(SMALL_SHARDS, rows, MID)
        for k, source in enumerate(parts):
            waits.append(load(source, wide.at[:, k * size : (k + 1) * size]))
    links.greet()
    live_rows = table[TABLE[0] - 1, 0:1, 0:1]
    half = MID // LANES
    pad2[...] = jnp.zeros_like(pad2)
    pad_s[...] = jnp.zeros_like(pad_s)
    pad_e[...] = jnp.zeros_like(pad_e)
    sum_gain[...] = jnp.zeros_like(sum_gain)
    sum_shift[...] = jnp.zeros_like(sum_shift)

    def vectors(start, columns, stats):
        gain = row_vector(table, 2 * block, start, columns // LANES)
        shift = row_vector(table, 2 * block + 1, start, columns // LANES)
        return gain, shift, stats[0:1, :], stats[1:2, :]

    def totals(index, start, columns, gain_rows, shift_rows):
        stat = sums[index][0]
        put_rows(stat, 0, jnp.sum(gain_rows, axis=0, keepdims=True), 4)
        put_rows(stat, 4, jnp.sum(shift_rows, axis=0, keepdims=True), 4)
        tot = links.all_sum(*sums[index])
        gain = jnp.concatenate([tot[k : k + 1] for k in range(4)], axis=1)
        shift = jnp.concatenate([tot[4 + k : 5 + k] for k in range(4)], axis=1)
        put_rows(norm_grads, start, gain, columns // LANES)
        put_rows(norm_grads, 24 + start, shift, columns // LANES)
        return gain / live_rows, shift / live_rows

    def slope_of(values):
        sig = jax.nn.sigmoid(values)
        return sig, sig * (1.0 + values * (1.0 - sig))

    def dot_t(left, right):
        return lax.dot_general(left, right, (((1,), (1,)), ((), ())), preferred_element_type=F32)

    gain3, shift3, mean3, inv3 = vectors(2 * half, D, st3)
    dx_base = links.take(GRID)

    def dx_copy(i):
        rows = pl.ds(GRID * i, GRID)
        return pltpu.make_async_copy(dv.at[rows], dx_out.at[rows], links.recv_sem.at[dx_base + i])


    def first_rows(i, carry):
        for copy in wide_copies(i):
            copy.wait()
        lax.fori_loop(GRID * i, GRID * i + GRID, first, carry)
        if not last:
            dx_copy(i).start()
        return carry

    def first(p, carry):
        for k in range(4):
            span = slice(k * MID, (k + 1) * MID)
            n = (h3v[p, :, span].astype(F32) - mean3[:, span]) * inv3[:, span]
            pre = n * gain3[:, span] + shift3[:, span] + xv[p, :, span].astype(F32)
            grad = d_in[:, span] if last else dv[p, :, span]
            grad = grad * slope_of(pre)[1]
            dv[p, :, span] = grad
            sum_gain[:, span] += fold(grad * n)
            sum_shift[:, span] += fold(grad)
        return carry

    lax.fori_loop(0, GRID, first_rows, 0)
    links.wait_for_all()
    part_gain, part_shift = totals(0, 2 * half, D, sum_gain[...], sum_shift[...])
    factor3 = gain3 * inv3
    for copy in loads_two:
        copy.wait()
    gain2, shift2, mean2, inv2 = vectors(half, MID, st2)
    zeros = jnp.zeros((8, MID), F32)

    def second(i, carry):
        for j in range(GRID):
            p = GRID * i + j
            for k in range(4):
                span = slice(k * MID, (k + 1) * MID)
                n = (h3v[p, :, span].astype(F32) - mean3[:, span]) * inv3[:, span]
                rest = mask[...] * (part_shift[:, span] + n * part_gain[:, span])
                h3v[p, :, span] = (factor3[:, span] * (dv[p, :, span] - rest)).astype(BF16)
        d_a = dot_t(h3v[pl.ds(GRID * i, GRID)].reshape(GRID * frames, D), w_out[...])
        d_a = d_a.reshape(GRID, frames, MID)
        one, two = carry
        for j in range(GRID):
            n = (h2v[GRID * i + j] - mean2) * inv2
            grad = d_a[j] * slope_of(n * gain2 + shift2)[1]
            dyv[GRID * i + j] = grad
            one = one + fold(grad * n)
            two = two + fold(grad)
        return (one, two)

    one, two = lax.fori_loop(0, GRID, second, (zeros, zeros))
    send_out(h3v, dh3_out)
    part_gain2, part_shift2 = totals(1, half, MID, one, two)
    factor2 = gain2 * inv2

    def third(i, carry):
        for j in range(GRID):
            p = GRID * i + j
            n = (h2v[p] - mean2) * inv2
            rest = mask[...] * (part_shift2 + n * part_gain2)
            pad2[i + 1, j + 1] = (factor2 * (dyv[p] - rest)).astype(BF16)
        return carry

    lax.fori_loop(0, GRID, third, 0)
    send_out(pad2.at[pl.ds(1, GRID), pl.ds(1, GRID)], dh2_out)
    for copy in loads_three:
        copy.wait()
    w_exp[...] = excite_weights(small, block)
    red = small[:, 32 * block : 32 * block + 16].reshape(MID, GATE)
    gain1, shift1, mean1, inv1 = vectors(0, MID, st1)

    def fourth(i, carry):
        part = None
        for k in range(9):
            window = pad2[i + 2 - k // 3, pl.ds(2 - k % 3, GRID)].reshape(GRID * frames, MID)
            term = dot_t(window, w_mid[k * MID : (k + 1) * MID])
            part = term if part is None else part + term
        part = part.reshape(GRID, frames, MID)
        for j in range(GRID):
            p = GRID * i + j
            y = (h1v[p] - mean1) * inv1 * gain1 + shift1
            a = y * jax.nn.sigmoid(y)
            gate = gatev[p].astype(F32)
            dyv[p] = part[j] * (1.0 + gate)
            gatev[p] = (part[j] * a * gate * (1.0 - gate)).astype(BF16)
        d_s = dot_t(gatev[pl.ds(GRID * i, GRID)].reshape(GRID * frames, MID), w_exp[...])
        d_s = d_s.astype(BF16).reshape(GRID, frames, GATE)
        dsv[pl.ds(GRID * i, GRID)] = d_s
        for j in range(GRID):
            pad_s[i + 1, j + 1] = d_s[j].astype(F32)
        return carry

    lax.fori_loop(0, GRID, fourth, 0)
    swap = links.remote(links.take(1), dsv, edge, links.other)
    swap.start()
    send_out(gatev, de_out)
    swap.wait()

    def unpack(i, carry):
        for j in range(GRID):
            pad_e[i + 1, j + 1] = edge[GRID * i + j].astype(F32)
        return carry

    lax.fori_loop(0, GRID, unpack, 0)
    row = lax.rem(lax.broadcasted_iota(jnp.int32, (frames, GATE), 0), 8)
    from_other = links.seg.astype(F32)

    def fifth(i, carry):
        for j in range(GRID):
            near = jnp.zeros((frames, GATE), F32)
            far = jnp.zeros((frames, GATE), F32)
            for k in range(9):
                near = near + pad_s[i + k // 3, j + k % 3]
                far = far + pad_e[i + k // 3, j + k % 3]
            near = pad_s[i + 1, j + 1] + near / 9.0
            far = (pad_e[i + 1, j + 1] + far / 9.0) * from_other
            earlier = jnp.where(row > 0, pltpu.roll(near, 1, 0), pltpu.roll(far, frames - 7, 0))
            drv[GRID * i + j] = (present[...] * earlier - following[...] * near).astype(BF16)
        d_a = dot_t(drv[pl.ds(GRID * i, GRID)].reshape(GRID * frames, GATE), red)
        d_a = d_a.reshape(GRID, frames, MID)
        one, two = carry
        for j in range(GRID):
            p = GRID * i + j
            n = (h1v[p] - mean1) * inv1
            grad = (dyv[p] + d_a[j]) * slope_of(n * gain1 + shift1)[1]
            dyv[p] = grad
            one = one + fold(grad * n)
            two = two + fold(grad)
        return (one, two)

    one, two = lax.fori_loop(0, GRID, fifth, (zeros, zeros))
    send_out(drv, dr_out)
    part_gain1, part_shift1 = totals(2, 0, MID, one, two)
    factor1 = gain1 * inv1
    for copy in loads_four:
        copy.wait()

    def sixth(i, carry):
        for j in range(GRID):
            p = GRID * i + j
            n = (h1v[p] - mean1) * inv1
            rest = mask[...] * (part_shift1 + n * part_gain1)
            dh1v[p] = (factor1 * (dyv[p] - rest)).astype(BF16)
        if last:
            rows = dh1v[pl.ds(GRID * i, GRID)].reshape(GRID * frames, MID)
            for k in range(4):
                span = slice(k * MID, (k + 1) * MID)
                part = dot_t(rows, w_in[span, :])
                dv[pl.ds(GRID * i, GRID), :, span] += part.reshape(GRID, frames, MID)
            dx_copy(i).start()
        return carry

    lax.fori_loop(0, GRID, sixth, 0)
    send_out(dh1v, dh1_out)
    for i in range(GRID):
        dx_copy(i).wait()
    for copy in outgoing:
        copy.wait()


def backward_block(block, h3, x, d_in, h2, h1, gate, weights, table, stats, masks):
    n_seg = lax.axis_size("seg")
    n_clip = lax.axis_size("clip")
    cells, frames, width = x.shape
    any_spec = pl.BlockSpec(memory_space=pl.ANY)
    vmem = pl.BlockSpec(memory_space=pltpu.VMEM)
    last = block == 1

    def grid_shape(columns):
        return (cells, frames, columns)

    outs = [
        jax.ShapeDtypeStruct(grid_shape(D), BF16),
        jax.ShapeDtypeStruct((GRID, GRID, frames, MID), BF16),
        jax.ShapeDtypeStruct(grid_shape(MID), BF16),
        jax.ShapeDtypeStruct(grid_shape(GATE), BF16),
        jax.ShapeDtypeStruct(grid_shape(MID), BF16),
        jax.ShapeDtypeStruct(grid_shape(D), F32),
        jax.ShapeDtypeStruct((48, LANES), F32),
    ]
    scratch = [
        pltpu.VMEM(grid_shape(D), F32),
        pltpu.VMEM(grid_shape(D), BF16),
        pltpu.VMEM(grid_shape(D), BF16),
        pltpu.VMEM(grid_shape(MID), F32),
        pltpu.VMEM(grid_shape(MID), F32),
        pltpu.VMEM(grid_shape(MID), BF16),
        pltpu.VMEM(grid_shape(MID), F32),
        pltpu.VMEM((GRID + 2, GRID + 2, frames, MID), BF16),
        pltpu.VMEM(grid_shape(GATE), BF16),
        pltpu.VMEM(grid_shape(GATE), BF16),
        pltpu.VMEM((GRID + 2, GRID + 2, frames, GATE), F32),
        pltpu.VMEM((GRID + 2, GRID + 2, frames, GATE), F32),
        pltpu.VMEM(grid_shape(GATE), BF16),
        pltpu.VMEM(grid_shape(MID), BF16),
        pltpu.VMEM((D, MID), BF16),
        pltpu.VMEM((9 * MID, MID), BF16),
        pltpu.VMEM((MID, D), BF16),
        pltpu.VMEM((SMALL_SHARDS, 80, LANES), BF16),
        pltpu.VMEM((GATE, MID), BF16),
        pltpu.VMEM((8, D), F32),
        pltpu.VMEM((8, D), F32),
    ]
    for shape in ((8, MID), (8, LANES), (8, LANES)):
        scratch += sum_scratch(n_seg, n_clip, shape)
    count = 3 * (n_seg * 4 + n_clip // 4) + 64
    scratch += [pltpu.SemaphoreType.DMA((count,)), pltpu.SemaphoreType.DMA((count,))]
    d_spec = vmem if last else any_spec
    return pl.pallas_call(
        functools.partial(backward_kernel, n_seg, n_clip, block),
        out_shape=outs,
        in_specs=[any_spec, any_spec, d_spec] + [any_spec] * 10 + [vmem] * 7,
        out_specs=[any_spec] * 6 + [vmem],
        scratch_shapes=scratch,
        compiler_params=pltpu.CompilerParams(
            collective_id=40 + block, has_side_effects=True, vmem_limit_bytes=62 * 1024 * 1024
        ),
        name="backward_block",
    )(h3, x, d_in, h2, h1, gate, *weights, table, *stats, *masks)


class Scatter:
    def __init__(self, links, grad, rows, buffers, alternate, finish):
        self.links = links
        self.alternate = alternate
        self.grad = grad
        self.rows = rows
        self.one, self.two, self.three, self.four = buffers
        self.finish = finish
        self.depth = links.outer
        self.base = links.take(self.depth + 3)
        self.at = -1

    def copies(self):
        links, base, depth = self.links, self.base, self.depth
        if self.at == 0:
            source = self.grad.at[1 - links.seg, :, :, self.rows]
            return [links.remote(base, source, self.one, links.other)]
        found = []
        if self.at == 1:
            for k in range(2):
                source = self.one.at[:, links.jump * (1 - links.first) + links.step * k]
                found.append(links.remote(base + 1 + k, source, self.two.at[:, k], links.across_first))
            return found
        if self.alternate:
            if self.at == 2:
                for i in range(1, depth):
                    source = self.two.at[lax.rem(links.group + i, depth)]
                    found.append(links.remote(base + 2 + i, source, self.three.at[i - 1], links.far_peer(i)))
            else:
                source = self.four.at[1 - links.second]
                found.append(links.remote(base + depth + 2, source, self.four.at[2], links.across_second))
            return found
        if self.at == 2:
            source = self.two.at[:, 1 - links.second]
            return [links.remote(base + 3, source, self.three, links.across_second)]
        for i in range(1, depth):
            source = self.three.at[lax.rem(links.group + i, depth)]
            found.append(links.remote(base + 3 + i, source, self.four.at[i - 1], links.far_peer(i)))
        return found

    def add(self):
        links, depth = self.links, self.depth
        one, two, three, four = self.one, self.two, self.three, self.four
        if self.at == 0:

            def add_one(i, carry):
                z = i // 4
                w = lax.rem(i, 4)
                total = one[z, w].astype(F32) + self.grad[links.seg, z, w, self.rows].astype(F32)
                one[z, w] = total.astype(BF16)
                return carry

            lax.fori_loop(0, 4 * depth, add_one, 0)
        elif self.at == 1:

            def add_two(i, carry):
                z = i // 2
                k = lax.rem(i, 2)
                kept = one[z, links.jump * links.first + links.step * k]
                two[z, k] = (two[z, k].astype(F32) + kept.astype(F32)).astype(BF16)
                return carry

            lax.fori_loop(0, 2 * depth, add_two, 0)
        elif self.at == 2 and self.alternate:
            for k in range(2):
                total = two[links.group, k].astype(F32)
                for i in range(1, depth):
                    total = total + three[i - 1, k].astype(F32)
                four[k] = total.astype(BF16)
        elif self.at == 2:

            def add_three(z, carry):
                three[z] = (three[z].astype(F32) + two[z, links.second].astype(F32)).astype(BF16)
                return carry

            lax.fori_loop(0, depth, add_three, 0)
        elif self.alternate:
            self.finish(four[links.second].astype(F32) + four[2].astype(F32))
        else:
            total = three[links.group].astype(F32)
            for i in range(1, depth):
                total = total + four[i - 1].astype(F32)
            self.finish(total)

    def advance(self):
        if self.at > 3:
            return
        if self.at >= 0:
            for copy in self.copies():
                copy.wait()
            self.add()
        self.at += 1
        if self.at <= 3:
            for copy in self.copies():
                copy.start()


SCATTERED = {
    "cls": (64, 2 * LANES),
    "out1": (16, D),
    "mida1": (48, MID),
    "midb1": (48, MID),
    "midc1": (48, MID),
    "in1": (64, MID),
    "out0": (16, D),
    "mida0": (48, MID),
    "midb0": (48, MID),
    "midc0": (48, MID),
    "in0": (64, MID),
    "small": (80, LANES),
}


FLAT_MID = 256
FLAT_OUT = 832
FLAT_SMALL = 1088
FLAT_ROWS = 1122
FLAT_CLS = 2243
ORDER = (
    "cls", "@mid1a", "cls", "@mid1b", "mida1", "midb1", "midc1", "@mid1c", "cls", "mida1", "@in1a", "in1", "midb1",
    "@in1b", "cls", "@out1a", "mida1", "midc1", "@out1b", "out1", "cls", "in1", "@small1", "midb1", "out1",
    "@out0a", "midc1", "@out0b", "out0", "mida1", "@in0a", "in0", "in1", "@in0b", "out0", "@mid0a", "midb1",
    "midc1", "mida1", "out1", "@mid0b", "mida0", "midb0", "midc0", "in0", "@mid0c", "midb1", "out0", "@small0",
    "small", "in1", "out1", "@dx0", "@dx1", "mida0", "midc1", "@dx2", "in0", "@dx3", "@dx4", "out0", "@dx5", "in1",
    "out1", "midb0", "@dx6", "mida0", "in0", "out0", "midc0", "midb0", "mida0", "small", "in0", "midc0", "mida0",
    "midb0", "small", "midc0", "small", "midb0", "midc0", "small",
)
ALTERNATE = ("mida1", "midb1", "in1")

ORDER_FIRST = "mid1a"


def gradient_kernel(n_seg, n_clip, *refs):
    refs = list(refs)

    def pop(count=1):
        taken = refs[:count]
        del refs[:count]
        return taken if count != 1 else taken[0]

    sources = [pop(10) for _ in range(2)]
    cls_hbm, norm_rows_in, bias = pop(3)
    d_pre, *in_parts = pop(3)
    flat, tail, dx_out = pop(3)
    big3, bigx, mid_a2, mid_d2, mid_d1, mid_low, mid_de, thin_dr, thin_s, fpad = pop(10)
    g_in, g_mid, g_out, g_small, g_cls, squares, turned, rows_x = pop(8)
    sums = pop(4)
    buffers = {name: pop(4) for name in SCATTERED}
    send_sem, recv_sem = pop(2)
    links = Links(n_seg, n_clip, send_sem, recv_sem)
    cells, frames = bigx.shape[0], bigx.shape[1]
    rows_all = cells * frames
    devices = SMALL_SHARDS

    def load(source, target):
        copy = links.local(source.reshape(target.shape), target)
        copy.start()
        return copy

    interior = fpad.at[pl.ds(1, GRID), pl.ds(1, GRID)]
    names = ("x", "d1", "f", "d2", "a2", "d3", "low", "dr", "s", "de")
    targets = dict(zip(names, (bigx, mid_d1, interior, mid_d2, mid_a2, big3, mid_low, thin_dr, thin_s, mid_de)))
    hbm = [dict(zip(names, source)) for source in sources]

    def fetch(block, *keys):
        return [load(hbm[block][key], targets[key]) for key in keys]

    operands = {
        "out": ("a2", "d3"),
        "in": ("x", "d1"),
        "mid": ("f", "d2"),
        "small": ("low", "dr", "s", "de"),
    }
    load_cls = load(cls_hbm, g_cls)
    fpad[...] = jnp.zeros_like(fpad)
    waits = {"mid": fetch(1, *operands["mid"])}
    links.meet()
    squares[...] = jnp.zeros_like(squares)

    def folded(ref, rows):
        return ref.reshape(n_seg, links.outer, 4, rows, ref.shape[-1])

    grads = {"cls": g_cls, "small": g_small}
    jobs = {}

    def put(block, first, values, stride=1):
        count = values.shape[0]
        if block == 0:
            flat[pl.ds(first, count, stride), :] = values
        else:
            turned[pl.ds(first + 8, count, stride), :] = pltpu.roll(values, 64, 1)

    def put_small(total):
        lane = lax.broadcasted_iota(jnp.int32, (1, LANES), 1)
        for block in range(2):
            rows = total[32 * block : 32 * block + 32]
            put(block, FLAT_SMALL, rows[:16])
            for k in range(4):
                put(block, FLAT_SMALL + 16 + k, rows[16 + 4 * k : 20 + 4 * k], 4)
            gain = total[64 + 2 * block : 65 + 2 * block]
            shift = pltpu.roll(total[65 + 2 * block : 66 + 2 * block], 96, 1)
            put(block, FLAT_SMALL + 32, jnp.where(lane < 96, gain, shift))
            put(block, FLAT_SMALL + 33, shift)
        flat[FLAT_CLS + 87 : FLAT_CLS + 88, :] = total[68:69]

    def put_classifier(total):
        lane = lax.broadcasted_iota(jnp.int32, (1, LANES), 1)
        flat[FLAT_CLS:, :] = jnp.zeros_like(flat[FLAT_CLS:, :])
        for i in range(total.shape[0]):
            line, by = divmod(CLASSES * i, LANES)
            line += FLAT_CLS
            low, high = total[i : i + 1, :LANES], total[i : i + 1, LANES:]
            if by:
                low, high = pltpu.roll(low, by, 1), pltpu.roll(high, by, 1)
            here = lane >= by
            flat[line : line + 1, :] += jnp.where(here, low, 0.0)
            flat[line + 1 : line + 2, :] += jnp.where(here, high, low)
            if by + CLASSES - LANES > LANES:
                flat[line + 2 : line + 3, :] += jnp.where(here, 0.0, high)

    def make(name):
        kind = name[:-1] if name not in ("cls", "small") else name
        block = name[-1]
        rows, columns = SCATTERED[name]
        start = rows * "abc".index(kind[3]) if kind.startswith("mid") else 0
        ref = {"in": g_in, "out": g_out, "small": g_small, "cls": g_cls}.get(kind, g_mid)
        shard_rows = 3 * rows if kind.startswith("mid") else rows

        def finish(total):
            squares[:, :columns] += fold(total * total)
            if kind == "cls":
                put_classifier(total)
            elif kind == "small":
                put_small(total)
            else:
                lines = columns // LANES
                first = {"in": 0, "out": FLAT_OUT}.get(kind, FLAT_MID) + start * lines
                for k in range(lines):
                    put(int(block), first + k, total[:, k * LANES : (k + 1) * LANES], lines)

        jobs[name] = Scatter(links, folded(ref, shard_rows), pl.ds(start, rows), buffers[name], name in ALTERNATE, finish)

    for name in SCATTERED:
        make(name)

    def push(*wanted):
        for name in wanted:
            jobs[name].advance()

    def dot_tn(left, right):
        return lax.dot_general(left, right, (((0,), (0,)), ((), ())), preferred_element_type=F32)

    turn = 1 - links.seg

    def task_out(first, last):
        def body(k, carry):
            span = pl.ds(pl.multiple_of(k * MID, MID), MID)
            part = dot_tn(mid_a2[...].reshape(rows_all, MID), big3[:, :, span].reshape(rows_all, MID))
            g_out[:, span] = part.astype(BF16)
            return carry

        lax.fori_loop(first, last, body, 0)

    def task_in(first, last):
        def body(i, carry):
            k = i + turn * (3 - 2 * i)
            span = pl.ds(pl.multiple_of(k * MID, MID), MID)
            part = dot_tn(bigx[:, :, span].reshape(rows_all, MID), mid_d1[...].reshape(rows_all, MID))
            g_in[span, :] = part.astype(BF16)
            return carry

        lax.fori_loop(first, last, body, 0)

    def task_mid(first, last):
        def body(i, carry):
            k = i + turn * (8 - 2 * i)
            window = fpad[pl.ds(k // 3, GRID), pl.ds(lax.rem(k, 3), GRID)].reshape(rows_all, MID)
            part = dot_tn(window, mid_d2[...].reshape(rows_all, MID))
            g_mid[pl.ds(pl.multiple_of(k * MID, MID), MID), :] = part.astype(BF16)
            return carry

        lax.fori_loop(first, last, body, 0)

    def task_small(block):
        part = dot_tn(mid_low[...].reshape(rows_all, MID), thin_dr[...].reshape(rows_all, GATE))
        g_small[:, 32 * block : 32 * block + 16, :] = part.astype(BF16).reshape(devices, 16, LANES)
        part = dot_tn(thin_s[...].reshape(rows_all, GATE), mid_de[...].reshape(rows_all, MID)).astype(BF16)
        rows = jnp.zeros((devices * 16, LANES), F32)
        for k in range(MID // LANES):
            rows = rows + dot_tn(excite_pick(devices, k), part[:, k * LANES : (k + 1) * LANES])
        g_small[:, 32 * block + 16 : 32 * block + 32, :] = rows.astype(BF16).reshape(devices, 16, LANES)

    dx_base = links.take(2 * GRID)
    w_in = big3.at[0 : 2 * 8].reshape(8, 2, SMALL_SHARDS, D)
    in_loads = []

    def load_w_in():
        for half, part in enumerate(in_parts):
            quarters = part.reshape(4, 8, SMALL_SHARDS, MID)
            for k in range(4):
                copy = links.local(quarters.at[k], w_in.at[:, half, :, k * MID : (k + 1) * MID])
                copy.start()
                in_loads.append(copy)
        dx_load(0).start()

    def dx_load(i):
        return pltpu.make_async_copy(
            d_pre.at[pl.ds(GRID * i, GRID)], rows_x.at[i % 2], links.recv_sem.at[dx_base + i]
        )

    def dx_store(i):
        slots = frames // dx_out.shape[0]
        return [
            pltpu.make_async_copy(
                rows_x.at[i % 2, :, slots * c : slots * (c + 1)],
                dx_out.at[c, pl.ds(GRID * i, GRID)],
                links.recv_sem.at[store_base + dx_out.shape[0] * i + c],
            )
            for c in range(dx_out.shape[0])
        ]

    store_base = links.take(dx_out.shape[0] * GRID)

    def task_dx(i):
        if i == 0:
            for copy in in_loads:
                copy.wait()
        dx_load(i).wait()
        rows = mid_d1[GRID * i : GRID * (i + 1)].reshape(GRID * frames, MID)
        for k in range(4):
            span = slice(k * MID, (k + 1) * MID)
            right = big3[0:16, :, span].reshape(MID, MID)
            part = lax.dot_general(rows, right, (((1,), (1,)), ((), ())), preferred_element_type=F32)
            rows_x[i % 2, :, :, span] += part.reshape(GRID, frames, MID)
        for copy in dx_store(i):
            copy.start()
        if i:
            for copy in dx_store(i - 1):
                copy.wait()
        if i < GRID - 1:
            dx_load(i + 1).start()

    def run(piece):
        if piece[:2] == "dx":
            task_dx(int(piece[2:]))
            return
        letter = piece[-1] if piece[-1] in "abc" else ""
        kind, block = piece[: len(piece) - 1 - len(letter)], int(piece[len(piece) - 1 - len(letter)])
        part = "abc".index(letter) if letter else 0
        if part == 0:
            for copy in waits[kind]:
                copy.wait()
            if block == 0 and kind != "small":
                for name in SCATTERED:
                    if name.startswith(kind) and name[-1] == "1":
                        while jobs[name].at < 1:
                            jobs[name].advance()
        if kind == "mid":
            task_mid((0, 3, 5)[part], (3, 5, 9)[part])
        elif kind == "in":
            task_in(2 * part, 2 * part + 2)
        elif kind == "out":
            task_out(2 * part, 2 * part + 2)
        else:
            task_small(block)
        if block == 1 and part == {"mid": 2, "in": 1, "out": 1, "small": 0}[kind]:
            waits[kind] = fetch(0, *operands[kind])
        if piece == "out0b":
            load_w_in()
        if block == 1 and piece == ORDER_FIRST:
            for other in ("in", "out", "small"):
                waits[other] = fetch(1, *operands[other])

    g_small[:, 64:80, :] = norm_rows_in[...]
    load_cls.wait()
    for item in ORDER:
        if item[0] == "@":
            with jax.named_scope("product"):
                run(item[1:])
        else:
            push(item)
    for name in SCATTERED:
        while jobs[name].at <= 3:
            jobs[name].advance()
    for copy in dx_store(GRID - 1):
        copy.wait()
    lane = lax.broadcasted_iota(jnp.int32, (FLAT_ROWS, LANES), 1)
    now, before = turned[8 : 8 + FLAT_ROWS, :], turned[7 : 7 + FLAT_ROWS, :]
    old = flat[FLAT_SMALL + 33 : FLAT_SMALL + 34, :]
    flat[FLAT_ROWS - 1 : 2 * FLAT_ROWS - 1, :] = jnp.where(lane < 64, before, now)
    flat[FLAT_ROWS - 1 : FLAT_ROWS, :] = jnp.where(lane[:1] < 64, old, now[:1])
    total = jnp.sum(jnp.sum(squares[...], axis=0, keepdims=True), axis=1, keepdims=True)
    sums[0][0:8, :] = bias[...]
    sums[0][8:16, :] = jnp.broadcast_to(total, (8, LANES))
    tail[...] = links.all_sum(*sums)


def gradient_sums(sources, g_cls, norm_rows_in, bias, d_pre, in_a, in_b, clips):
    n_seg = lax.axis_size("seg")
    n_clip = lax.axis_size("clip")
    depth = n_clip // 4
    cells, frames, width = sources[0][0].shape
    any_spec = pl.BlockSpec(memory_space=pl.ANY)
    vmem = pl.BlockSpec(memory_space=pltpu.VMEM)

    def grid_shape(columns):
        return pltpu.VMEM((cells, frames, columns), BF16)

    outs = [(FLAT_CLS + 93, LANES), (16, LANES)]
    scratch = [grid_shape(D), grid_shape(D)] + [grid_shape(MID)] * 5 + [grid_shape(GATE)] * 2
    scratch += [
        pltpu.VMEM((GRID + 2, GRID + 2, frames, MID), BF16),
        pltpu.VMEM((D, MID), BF16),
        pltpu.VMEM((9 * MID, MID), BF16),
        pltpu.VMEM((MID, D), BF16),
        pltpu.VMEM((SMALL_SHARDS, 80, LANES), BF16),
        pltpu.VMEM((D, 2 * LANES), BF16),
        pltpu.VMEM((8, D), F32),
        pltpu.VMEM((FLAT_ROWS + 14, LANES), F32),
        pltpu.VMEM((2, GRID, frames, D), F32),
    ]
    scratch += sum_scratch(n_seg, n_clip, (16, LANES))
    for name, shape in SCATTERED.items():
        ends = ((depth - 1, 2), (3,)) if name in ALTERNATE else ((depth,), (depth - 1,))
        for lead in ((depth, 4), (depth, 2)) + ends:
            scratch.append(pltpu.VMEM(lead + shape, BF16))
    count = n_seg * 4 + depth + len(SCATTERED) * (depth + 3) + 100
    scratch += [pltpu.SemaphoreType.DMA((count,)), pltpu.SemaphoreType.DMA((count,))]
    return pl.pallas_call(
        functools.partial(gradient_kernel, n_seg, n_clip),
        out_shape=[jax.ShapeDtypeStruct(s, F32) for s in outs + [(clips, cells, frames // clips, D)]],
        in_specs=[any_spec] * 21 + [vmem, vmem] + [any_spec] * 3,
        out_specs=[vmem] * len(outs) + [any_spec],
        scratch_shapes=scratch,
        compiler_params=pltpu.CompilerParams(
            collective_id=50, has_side_effects=True, vmem_limit_bytes=62 * 1024 * 1024
        ),
        name="gradient_sums",
    )(*sources[0], *sources[1], g_cls, norm_rows_in, bias, d_pre, in_a, in_b)


def input_gradient_kernel(d_pre, d_one, in_a, in_b, out, w_in):
    rows = w_in.shape[0] // SMALL_SHARDS // 2

    @pl.when(pl.program_id(0) == 0)
    def _():
        wide = w_in.reshape(SMALL_SHARDS, 2 * rows, MID)
        wide[:, :rows] = in_a[...].reshape(SMALL_SHARDS, rows, MID)
        wide[:, rows:] = in_b[...].reshape(SMALL_SHARDS, rows, MID)

    cells, frames = d_one.shape[:2]
    clips = out.shape[0]
    slots = frames // clips
    left = d_one[...].reshape(cells * frames, MID)
    for k in range(4):
        span = slice(k * MID, (k + 1) * MID)
        part = lax.dot_general(left, w_in[span, :], (((1,), (1,)), ((), ())), preferred_element_type=F32)
        part = part.reshape(cells, frames, MID) + d_pre[:, :, span]
        for c in range(clips):
            out[c, :, :, span] = part[:, slots * c : slots * (c + 1), :]


def input_gradient(d_pre, d_one, in_a, in_b, clips):
    cells, frames, width = d_pre.shape
    slots = frames // clips
    whole = pl.BlockSpec(in_a.shape, lambda i: (0, 0))
    return pl.pallas_call(
        input_gradient_kernel,
        grid=(GRID,),
        out_shape=jax.ShapeDtypeStruct((clips, cells, slots, width), F32),
        in_specs=[
            pl.BlockSpec((GRID, frames, width), lambda i: (i, 0, 0)),
            pl.BlockSpec((GRID, frames, MID), lambda i: (i, 0, 0)),
            whole,
            whole,
        ],
        out_specs=pl.BlockSpec((clips, GRID, slots, width), lambda i: (0, i, 0, 0)),
        scratch_shapes=[pltpu.VMEM((D, MID), BF16)],
        compiler_params=pltpu.CompilerParams(vmem_limit_bytes=48 * 1024 * 1024),
        name="input_gradient",
    )(d_pre, d_one, in_a, in_b)


def weight_gradients(x, d_one, gated, d_two, a_two, d_three, a_low, d_reduced, mixed, d_excite):
    return [
        matmul(x.reshape(-1, D).T, d_one.reshape(-1, MID)),
        conv(gated, d_two, ("HWCN", "HWIO", "HWNC")).reshape(9 * MID, MID),
        matmul(a_two.reshape(-1, MID).T, d_three.reshape(-1, D)),
        matmul(a_low.reshape(-1, MID).T, d_reduced.reshape(-1, GATE)),
        matmul(mixed.reshape(-1, GATE).T, d_excite.reshape(-1, MID)),
    ]


def on_device(inputs, clip_counts, labels, master, first_moment, second_moment):
    seg_count = lax.axis_size("seg")
    clip_local, slot_local = inputs.shape[:2]
    frames = clip_local * slot_local
    slot_ids = lax.axis_index("seg") * slot_local + jnp.arange(slot_local, dtype=jnp.int32)
    present = (slot_ids[None, :] < clip_counts[:, None]).astype(F32)
    following = (slot_ids[None, :] + 1 < clip_counts[:, None]).astype(F32)
    frame_mask = jnp.broadcast_to(present.reshape(frames, 1), (frames, MID))
    frame_following = jnp.broadcast_to(following.reshape(frames, 1), (frames, GATE))
    table = jnp.zeros(TABLE, F32)
    x_low = inputs.transpose(0, 2, 1, 3)
    shards = weight_shards(master)
    if shards is None:
        weights = whole_weights(master)
        jobs = ((), ())
    else:
        weights = {}
        jobs = JOBS
    rows = ((0, 8 - clip_local), (0, 0))
    share = jnp.pad(1.0 / (HW * clip_counts.astype(F32))[:, None], rows)
    share = jnp.broadcast_to(share, (8, LANES))
    onehot = (labels[:, None] == jnp.arange(2 * LANES, dtype=jnp.int32)[None, :]).astype(F32)
    target = jnp.pad(onehot, rows)
    kept = []
    flowing = x_low
    flows = []
    for block in range(2):
        flows.append(flowing)
        names = weight_names(block) + (["cls"] if block == 1 else [])
        given = {name: weights[name] for name in names if name not in jobs[block]}
        gathered, results = forward_block(
            block,
            flowing,
            frame_mask,
            frame_following,
            table,
            (share, target) if block == 1 else (),
            {name: shards[name] for name in jobs[block]},
            given,
        )
        weights.update(gathered)
        if block == 0:
            table = results[9]
        kept.append(results[:8] + results[10:13])
        if block == 0:
            flows[0] = results[13]
        flowing = results[8]
    d_flow = flowing
    g_cls, g_bias = results[13:]
    g_bias = g_bias[0, :CLASSES]
    masks = (frame_mask, frame_mask[:, :GATE], frame_following)
    sources = [None, None]
    norm_grads = [None, None]
    for block in (1, 0):
        h_one, a_low, gate, mixed, gated, h_two, a_two, h_three, st_one, st_two, st_three = kept[block]
        *steps, d_flow, norm_sums = backward_block(
            block,
            h_three,
            flows[block],
            d_flow,
            h_two,
            h_one,
            gate,
            [weights[name] for name in weight_names(block)],
            table,
            (st_one, st_two, st_three),
            masks,
        )
        sources[block] = (flows[block], steps[4], gated, steps[1], a_two, steps[0], a_low, steps[3], mixed, steps[2])
        norm_grads[block] = [norm_sums[:24].reshape(-1), norm_sums[24:].reshape(-1)]
    devices = seg_count * lax.axis_size("clip")
    bias_rows = jnp.pad(g_bias, (0, 8 * LANES - CLASSES)).reshape(8, LANES)
    if shards is None:
        grads = []
        for block in (0, 1):
            grads += weight_gradients(*sources[block]) + [v / devices for v in norm_grads[block]]
        d_input = input_gradient(d_flow, steps[4], weights["ina0"], weights["inb0"], clip_local)
        grad_mine = scatter_gradients(grads + [g_cls[:, :CLASSES].astype(F32), g_bias])
        square = jnp.full((8, LANES), jnp.sum(grad_mine * grad_mine), F32)
        tail = lax.psum(jnp.concatenate([bias_rows, square]), AXES)
    else:
        vectors = [v.reshape(SMALL_SHARDS, -1) / devices for b in (0, 1) for v in norm_grads[b]]
        padded = jnp.pad(g_bias, (0, 6 * SMALL_SHARDS - CLASSES)).reshape(SMALL_SHARDS, 6)
        extra = norm_rows(vectors + [padded]).astype(BF16)
        flat, tail, d_input = gradient_sums(
            sources, g_cls, extra, bias_rows, d_flow, weights["ina0"], weights["inb0"], clip_local
        )
        grad_mine = flat.reshape(-1)[: master.shape[0]]
    norm = jnp.sqrt(tail[8, 0])
    bias_grad = tail[:8].reshape(-1)[:CLASSES]
    factor = jnp.minimum(1.0, CLIP_LIMIT / (norm + 1e-06))
    clipped = grad_mine * factor
    new_first = BETA_ONE * first_moment + (1.0 - BETA_ONE) * clipped
    new_second = BETA_TWO * second_moment + (1.0 - BETA_TWO) * clipped * clipped
    first_hat = new_first / (1.0 - BETA_ONE**STEP)
    second_hat = new_second / (1.0 - BETA_TWO**STEP)
    new_master = master - LEARN_RATE * (
        first_hat / (jnp.sqrt(second_hat) + ADAM_EPS) + WEIGHT_DECAY * master
    )
    grid_grad = d_input.transpose(0, 2, 1, 3)
    return (
        new_master,
        new_first,
        new_second,
        new_master.astype(BF16),
        grid_grad,
        norm.reshape(1),
        bias_grad,
    )


def solution(mesh):
    return jax.shard_map(
        on_device,
        mesh=mesh,
        in_specs=(
            P("clip", "seg", None, None),
            P("clip"),
            P("clip"),
            P(AXES),
            P(AXES),
            P(AXES),
        ),
        out_specs=(
            P(AXES),
            P(AXES),
            P(AXES),
            P(AXES),
            P("clip", "seg", None, None),
            P(),
            P(),
        ),
        check_vma=False,
    )
```
